512 devices in a mesh: wide: 64 (over x, y, core), narrow: 8 (over z).
Axes of the slice: x: 4, y: 8, z: 8, core: 2. Of those that a mesh axis runs over, the one named last changes fastest.
Arguments:
- node_coords: float32 [3, 64, 8, 9, 256], P(None, 'wide', 'narrow'), may hold values from -192 to 192, as said below
- solution: float32 [2, 64, 8, 9, 256], P(None, 'wide', 'narrow'), may hold values from -6 to 6
- residual: float32 [2, 64, 8, 9, 256], P(None, 'wide', 'narrow'), may hold values from -6 to 6
- direction: float32 [2, 64, 8, 9, 256], P(None, 'wide', 'narrow'), may hold values from -6 to 6
- tile_pairs: int32 [64, 8, 2, 61], P('wide', 'narrow'), may hold values from 0 to 80, as said below
- tile_counts: int32 [64, 8], P('wide', 'narrow'), may hold values from 1 to 61
Outputs:
- new_solution: float32 [2, 64, 8, 9, 256], P(None, 'wide', 'narrow')
- new_residual: float32 [2, 64, 8, 9, 256], P(None, 'wide', 'narrow')
- new_direction: float32 [2, 64, 8, 9, 256], P(None, 'wide', 'narrow')
The draws below stay inside these ranges and needn't reach their ends.
Inputs may be any that keep to these rules, and one draw needn't show every extreme that they name: `tile_pairs`: neighbourhood indices lie in 0 to 80. In live slots every unordered pair of blocks appears at most once over all devices, one of its two blocks is owned by the device that holds the slot, the two blocks lie on devices at most one step apart along each direction (wide taken around its loop), and no live index points past the bounded ends of the narrow direction. Slots past a device's count hold arbitrary indices. `node_coords`: distinct nodes; the operator M built from the live tiles is symmetric positive definite.
All inputs are finite; a program needn't handle non-finite values.
Results may differ from the reference program's by a relative error of at most 0.00095.
Values sent between devices are 32-bit elements; how exact they have to be, the bound alone decides.
A program may use at most 64 MiB of HBM per device.

```python
import math
import jax
import jax.numpy as jnp
import numpy as np
from jax import lax

BLOCK = 256
BSIDE = 3
FIELDS = 2
ITERS = 3
BLK_DEV = 9
TILE_CAP = 61
N_WIDE = 64
N_NARROW = 8


def tile_layout(key):
    devices_total = N_WIDE * N_NARROW
    wide_cells = BSIDE * N_WIDE
    narrow_cells = BSIDE * N_NARROW
    cell_wide, cell_narrow = np.meshgrid(np.arange(wide_cells), np.arange(narrow_cells), indexing='ij')
    directions = np.array([[0, 0], [1, 0], [0, 1], [1, 1], [1, -1]])
    left_wide = np.repeat(cell_wide.reshape(-1), 5)
    left_narrow = np.repeat(cell_narrow.reshape(-1), 5)
    right_wide = (left_wide + np.tile(directions[:, 0], wide_cells * narrow_cells)) % wide_cells
    right_narrow = left_narrow + np.tile(directions[:, 1], wide_cells * narrow_cells)
    inside = (right_narrow >= 0) & (right_narrow < narrow_cells)
    left_wide = left_wide[inside]
    left_narrow = left_narrow[inside]
    right_wide = right_wide[inside]
    right_narrow = right_narrow[inside]
    pair_total = left_wide.shape[0]
    left_dev = jnp.asarray(left_wide // BSIDE * N_NARROW + left_narrow // BSIDE, jnp.int32)
    right_dev = jnp.asarray(right_wide // BSIDE * N_NARROW + right_narrow // BSIDE, jnp.int32)
    priority = jax.random.permutation(jax.random.fold_in(key, 11), devices_total).astype(jnp.int32)
    forced = min(1, N_NARROW - 1)
    priority = jnp.where(jnp.arange(devices_total) == forced, devices_total, priority)
    owner_dev = jnp.where(priority[left_dev] >= priority[right_dev], left_dev, right_dev)
    owner_wide = owner_dev // N_NARROW
    owner_narrow = owner_dev % N_NARROW

    def local_index(cell_w, cell_n):
        dev_wide = jnp.asarray(cell_w // BSIDE, jnp.int32)
        dev_narrow = jnp.asarray(cell_n // BSIDE, jnp.int32)
        step_wide = (dev_wide - owner_wide + 1) % N_WIDE
        step_narrow = dev_narrow - owner_narrow + 1
        within = jnp.asarray(cell_w % BSIDE * BSIDE + cell_n % BSIDE, jnp.int32)
        return step_wide * 3 * BLK_DEV + step_narrow * BLK_DEV + within
    left_local = local_index(left_wide, left_narrow)
    right_local = local_index(right_wide, right_narrow)
    shuffle = jax.random.permutation(jax.random.fold_in(key, 12), pair_total).astype(jnp.int32)
    sort_key = owner_dev * pair_total + shuffle
    ordering = jnp.argsort(sort_key)
    sorted_owner = owner_dev[ordering]
    tile_total = jnp.zeros((devices_total,), jnp.int32).at[owner_dev].add(1)
    starts = jnp.cumsum(tile_total) - tile_total
    slot_index = jnp.arange(pair_total, dtype=jnp.int32) - starts[sorted_owner]
    filler = jax.random.randint(jax.random.fold_in(key, 13), (devices_total, 2, TILE_CAP), 0, 9 * BLK_DEV).astype(jnp.int32)
    slot_table = filler.at[sorted_owner, 0, slot_index].set(left_local[ordering])
    slot_table = slot_table.at[sorted_owner, 1, slot_index].set(right_local[ordering])
    return (slot_table.reshape(N_WIDE, N_NARROW, 2, TILE_CAP), tile_total.reshape(N_WIDE, N_NARROW))


def draw_tile_pairs(key, part):
    return tile_layout(key)[0]


def draw_tile_counts(key, part):
    return tile_layout(key)[1]


def draw_node_coords(key, part):
    key = jax.random.fold_in(key, 7)
    first_key, second_key = jax.random.split(key)
    along_wide = jax.random.uniform(first_key, (N_WIDE, N_NARROW, BLK_DEV, BLOCK), jnp.float32)
    across = jax.random.uniform(second_key, (N_WIDE, N_NARROW, BLK_DEV, BLOCK), jnp.float32)
    wide_cells = BSIDE * N_WIDE
    block_index = jnp.arange(BLK_DEV)
    wide_pos = (jnp.arange(N_WIDE)[:, None, None, None] * BSIDE + (block_index // BSIDE)[None, None, :, None]).astype(jnp.float32) + along_wide
    narrow_pos = (jnp.arange(N_NARROW)[None, :, None, None] * BSIDE + (block_index % BSIDE)[None, None, :, None]).astype(jnp.float32) + across
    cycle_radius = wide_cells / (2.0 * math.pi)
    turn_angle = 2.0 * math.pi * wide_pos / wide_cells
    return jnp.stack([cycle_radius * jnp.cos(turn_angle), cycle_radius * jnp.sin(turn_angle), narrow_pos]).astype(jnp.float32)


def steps_of(rng, shape, pieces, low, top_value):
    def one(axis_at, blocks):
        heights = jax.random.uniform(jax.random.fold_in(jax.random.fold_in(rng, 6), axis_at), (blocks,), jnp.float32, low / len(pieces), top_value / len(pieces))
        return jnp.repeat(jnp.exp(heights), shape[axis_at] // blocks).reshape((-1,) + (1,) * (len(shape) - axis_at - 1))

    factor_of = one(*pieces[0])
    for cut in pieces[1:]:
        factor_of = factor_of * one(*cut)
    return factor_of


def gaussian(rng, extent, spread, most, cuts=(), held_as=jnp.bfloat16):
    values = spread * jax.random.normal(rng, extent, jnp.float32)
    if cuts:
        values = values * steps_of(rng, extent, cuts, -0.22, 0.18)
    return jnp.clip(values, -most, most).astype(held_as)


def setup_inputs(seed: int = 0) -> dict:
    streams_of = jax.random.split(jax.random.key(seed), 7)
    node_coords = draw_node_coords(jax.random.fold_in(streams_of[6], 71), 0)
    solution = gaussian(streams_of[1], (FIELDS, N_WIDE, N_NARROW, BLK_DEV, BLOCK), 1.0, 6.0, ((1, 64), (2, 8)), jnp.float32)
    residual = gaussian(streams_of[2], (FIELDS, N_WIDE, N_NARROW, BLK_DEV, BLOCK), 1.0, 6.0, ((1, 64), (2, 8)), jnp.float32)
    direction = gaussian(streams_of[3], (FIELDS, N_WIDE, N_NARROW, BLK_DEV, BLOCK), 1.0, 6.0, ((1, 64), (2, 8)), jnp.float32)
    tile_pairs = draw_tile_pairs(jax.random.fold_in(streams_of[6], 71), 0)
    tile_counts = draw_tile_counts(jax.random.fold_in(streams_of[6], 71), 0)
    return dict(node_coords=node_coords, solution=solution, residual=residual, direction=direction, tile_pairs=tile_pairs, tile_counts=tile_counts)


radius = 0.9

def wendland(left_coords, right_coords):
    offset = left_coords[:, :, :, None] - right_coords[:, :, None, :]
    distance = jnp.sqrt(lax.optimization_barrier(jnp.sum(offset * offset, axis=1)))
    scaled = jnp.minimum(distance / radius, 1.0)
    return (1.0 - scaled) ** 4 * (4.0 * scaled + 1.0)

def tile_terms(coord_rows, field_rows, left_index, right_index, active, buffer):
    left_coords = jnp.take(coord_rows, left_index, axis=1).transpose(1, 0, 2)
    right_coords = jnp.take(coord_rows, right_index, axis=1).transpose(1, 0, 2)
    weights = wendland(left_coords, right_coords)
    left_field = jnp.take(field_rows, left_index, axis=1)
    right_field = jnp.take(field_rows, right_index, axis=1)
    toward_left = jnp.einsum('fgj,gij->fgi', right_field, weights, precision=lax.Precision.HIGHEST)
    toward_right = jnp.einsum('fgi,gij->fgj', left_field, weights, precision=lax.Precision.HIGHEST)
    mirror = active * (left_index != right_index).astype(jnp.float32)
    buffer = buffer.at[:, left_index].add(toward_left * active[None, :, None])
    buffer = buffer.at[:, right_index].add(toward_right * mirror[None, :, None])
    return buffer

def neighbour_lists(tile_pairs, tile_counts):
    wide_count = tile_pairs.shape[0]
    narrow_count = tile_pairs.shape[1]
    capacity = tile_pairs.shape[3]
    wide_at = jnp.arange(wide_count, dtype=jnp.int32)[:, None, None, None]
    narrow_at = jnp.arange(narrow_count, dtype=jnp.int32)[None, :, None, None]
    step_wide = tile_pairs // (3 * BLK_DEV) - 1
    step_narrow = tile_pairs // BLK_DEV % 3 - 1
    within = tile_pairs % BLK_DEV
    owner_wide = (wide_at + step_wide) % wide_count
    owner_narrow = (narrow_at + step_narrow) % narrow_count
    global_ids = ((owner_wide * narrow_count + owner_narrow) * BLK_DEV + within).astype(jnp.int32)
    slot_index = jnp.arange(capacity, dtype=jnp.int32)[None, None, :]
    active = (slot_index < tile_counts[:, :, None]).astype(jnp.float32)
    return (global_ids[:, :, 0, :].reshape(-1), global_ids[:, :, 1, :].reshape(-1), active.reshape(-1))

def full_operator(coord_rows, field_rows, left_index, right_index, active):
    batch_rows = 64
    tile_total = left_index.shape[0]
    padding = -(-tile_total // batch_rows) * batch_rows - tile_total
    left_groups = jnp.pad(left_index, (0, padding)).reshape(-1, batch_rows)
    right_groups = jnp.pad(right_index, (0, padding)).reshape(-1, batch_rows)
    active_groups = jnp.pad(active, (0, padding)).reshape(-1, batch_rows)

    def one_group(buffer, group_items):
        left_part, right_part, active_part = group_items
        return (tile_terms(coord_rows, field_rows, left_part, right_part, active_part, buffer), None)
    zeroed = jnp.zeros(field_rows.shape, jnp.float32)
    result, unused = lax.scan(one_group, zeroed, (left_groups, right_groups, active_groups))
    return result

def field_sum(left_field, right_field):
    return lax.optimization_barrier(jnp.sum(left_field * right_field, axis=(1, 2)))

def reference(node_coords, solution, residual, direction, tile_pairs, tile_counts):
    full_shape = solution.shape
    coord_rows = node_coords.reshape(3, -1, BLOCK)
    left_index, right_index, active = neighbour_lists(tile_pairs, tile_counts)
    current_x = solution.reshape(FIELDS, -1, BLOCK)
    current_r = residual.reshape(FIELDS, -1, BLOCK)
    current_p = direction.reshape(FIELDS, -1, BLOCK)
    norm_now = field_sum(current_r, current_r)
    for iteration in range(ITERS):
        image_field = full_operator(coord_rows, current_p, left_index, right_index, active)
        step_size = norm_now / field_sum(current_p, image_field)
        current_x = current_x + step_size[:, None, None] * current_p
        current_r = current_r - step_size[:, None, None] * image_field
        norm_next = field_sum(current_r, current_r)
        current_p = current_r + (norm_next / norm_now)[:, None, None] * current_p
        norm_now = norm_next
    return (current_x.reshape(full_shape), current_r.reshape(full_shape), current_p.reshape(full_shape))
```

```python
import functools

import jax
import jax.numpy as jnp
from jax import lax
from jax.experimental import pallas as pl
from jax.experimental.pallas import tpu as pltpu
from jax.sharding import PartitionSpec as P

ITERS = 3
RADIUS = 0.9
MESH = pl.DeviceIdType.MESH
F32 = jnp.float32
BF16 = jnp.bfloat16

BLOCKS = 9
NODES = 256
SLOTS = 61
ROWS = 40
TABLE = 368
CHUNK = 16

PHI_SLOPE = 4.0 / RADIUS**5
PHI_CONST = 1.0 / RADIUS**4


def dot_bf16(left, right, transposed):
    dims = (((1,), (1 if transposed else 0,)), ((), ()))
    return lax.dot_general(left, right, dims, preferred_element_type=F32)


def split(value):
    high = value.astype(BF16)
    return high, (value - high.astype(F32)).astype(BF16)


def stage_peers(wide, narrow, stages):
    peers = []
    for axis, places in stages:
        here = wide if axis == "wide" else narrow
        rank, size = 0, 1
        for stride, count in places:
            rank = rank * count + here // stride % count
            size *= count
        group = []
        for step in range(1, size):
            other = (rank + step) % size
            position = here
            left = other
            for stride, count in reversed(places):
                position = position + (left % count - here // stride % count) * stride
                left = left // count
            group.append((position, narrow) if axis == "wide" else (wide, position))
        peers.append(group)
    return peers


def body(
    sizes,
    stages,
    coord_ref,
    sol_ref,
    res_ref,
    dir_ref,
    pairs_ref,
    pairs_vec_ref,
    count_ref,
    new_sol_ref,
    new_res_ref,
    new_dir_ref,
    near0,
    nearq,
    part,
    got,
    khi,
    klo,
    pieces,
    slot_out,
    onehot,
    basis,
    sums,
    sum_in,
    near_send,
    near_recv,
    q_send,
    q_recv,
    fold_send,
    fold_recv,
    sum_send,
    sum_recv,
):
    wide_size, narrow_size = sizes
    wide = lax.axis_index("wide")
    narrow = lax.axis_index("narrow")
    neighbours = []
    for d in range(9):
        if d != 4:
            to_wide = (wide + (d // 3 - 1) + wide_size) % wide_size
            to_narrow = (narrow + (d % 3 - 1) + narrow_size) % narrow_size
            neighbours.append((d, (to_wide, to_narrow)))
    peers = stage_peers(wide, narrow, stages)

    barrier = pltpu.get_barrier_semaphore()
    targets = [device for _, device in neighbours] + [device for group in peers for device in group]
    for device in targets:
        pl.semaphore_signal(barrier, inc=1, device_id=device, device_id_type=MESH)

    for k in range(BLOCKS):
        own = 4 * BLOCKS + k
        for f in range(2):
            near0[own, f : f + 1, :] = dir_ref[f, k : k + 1, :]
            near0[own, 2 + f : 3 + f, :] = res_ref[f, k : k + 1, :]
        for axis in range(3):
            near0[own, 4 + axis : 5 + axis, :] = coord_ref[axis, k : k + 1, :]
        near0[own, 7:8, :] = jnp.zeros((1, NODES), F32)

    pl.semaphore_wait(barrier, len(targets))

    pending = []

    def exchange(source, landing, send_sem, recv_sem):
        copies = []
        for at, (d, device) in enumerate(neighbours):
            copy = pltpu.make_async_remote_copy(
                src_ref=source(d),
                dst_ref=landing(8 - d, 7 - at),
                send_sem=send_sem.at[at],
                recv_sem=recv_sem.at[7 - at],
                device_id=device,
                device_id_type=MESH,
            )
            copy.start()
            copies.append(copy)
        pending.extend(copies)
        arrivals = []
        for at, (d, device) in enumerate(neighbours):
            arrivals.append(
                pltpu.make_async_remote_copy(
                    src_ref=source(d),
                    dst_ref=landing(d, at),
                    send_sem=send_sem.at[at],
                    recv_sem=recv_sem.at[at],
                    device_id=device,
                    device_id_type=MESH,
                )
            )
        return arrivals

    arrivals = exchange(
        lambda d: near0.at[pl.ds(4 * BLOCKS, BLOCKS)],
        lambda d, at: near0.at[pl.ds(d * BLOCKS, BLOCKS)],
        near_send,
        near_recv,
    )

    slot_of = lax.broadcasted_iota(jnp.int32, (64, 512), 0)
    lane_slot = lax.broadcasted_iota(jnp.int32, (64, 512), 1) // 8
    spread = jnp.where(slot_of == lane_slot, 1.0, 0.0).astype(BF16)
    left_id = pairs_vec_ref[0:1, :]
    right_id = pairs_vec_ref[1:2, :]
    live = lax.broadcasted_iota(jnp.int32, (1, SLOTS), 1) < count_ref[0:1, 0:1]
    toward_left = jnp.where(live, left_id, 255)
    toward_right = jnp.where(live & (left_id != right_id), right_id, 255)
    ids = jnp.concatenate([toward_right, toward_left] + [toward_left] * 6, axis=0).astype(F32)
    ids = jnp.concatenate([ids, jnp.full((8, 64 - SLOTS), 255.0, F32)], axis=1)
    wanted = dot_bf16(ids.astype(BF16), spread, False)
    lane = lax.broadcasted_iota(jnp.int32, (8, 512), 1)
    target = jnp.where(lane % 8 < 4, wanted[0:1, :], wanted[1:2, :]).astype(jnp.int32)
    for first in range(0, TABLE, CHUNK):
        row = lax.broadcasted_iota(jnp.int32, (CHUNK, 512), 0) + first
        place = row % ROWS
        block = jnp.where(place < 4 * BLOCKS, row // ROWS * BLOCKS + place // 4, 200)
        match = (block == target[0:1, :]) & (
            row % 4 == lax.broadcasted_iota(jnp.int32, (CHUNK, 512), 1) % 4
        )
        onehot[pl.ds(first, CHUNK), :] = jnp.where(match, 1.0, 0.0).astype(BF16)

    slot_out[pl.ds(8 * SLOTS, 512 - 8 * SLOTS), :] = jnp.zeros((512 - 8 * SLOTS, NODES), F32)
    half = lax.broadcasted_iota(jnp.int32, (8, NODES), 0) < 4

    def put_pieces(j, rows_at, value):
        high = value.astype(BF16).astype(F32)
        low = value - high
        if rows_at == 0:
            rows = jnp.where(half, high, pltpu.roll(low, 4, 0))
        else:
            rows = jnp.where(half, pltpu.roll(high, 4, 0), low)
        pieces[j] = jnp.concatenate([rows, rows], axis=0).astype(BF16)

    for arrival in arrivals:
        arrival.wait_recv()

    for h in range(2):
        for k in range(BLOCKS):
            basis[0, h, 4 * k : 4 * k + 4, :] = near0[4 * BLOCKS + k, 0:4, 128 * h : 128 * h + 128]
        basis[0, h, 4 * BLOCKS : ROWS, :] = jnp.zeros((ROWS - 4 * BLOCKS, 128), F32)

    def first_pieces(j, carry):
        put_pieces(j, 0, near0[j])
        return carry

    lax.fori_loop(0, 9 * BLOCKS, first_pieces, 0)

    def evaluate(s, carry):
        left = jnp.transpose(near0[pairs_ref[0, s]])
        right = near0[pairs_ref[1, s]]
        for first in range(0, NODES, CHUNK):
            squared = None
            for axis in range(3):
                offset = left[first : first + CHUNK, 4 + axis : 5 + axis] - right[4 + axis : 5 + axis, :]
                squared = offset * offset if squared is None else squared + offset * offset
            squared = jnp.minimum(squared, RADIUS * RADIUS)
            distance = squared * lax.rsqrt(jnp.maximum(squared, 1e-36))
            rest = jnp.maximum(RADIUS - distance, 0.0)
            rest = rest * rest
            rest = rest * rest
            high, low = split(rest * (PHI_SLOPE * distance + PHI_CONST))
            khi[s, first : first + CHUNK, :] = high
            klo[s, first : first + CHUNK, :] = low
        return carry

    lax.fori_loop(0, SLOTS, evaluate, 0)

    def product(s):
        left = pieces[pairs_ref[0, s]]
        right = pieces[pairs_ref[1, s]]
        to_right = dot_bf16(left, khi[s], False) + dot_bf16(left, klo[s], False)
        to_left = dot_bf16(right, khi[s], True) + dot_bf16(right, klo[s], True)
        to_right = to_right[0:8]
        to_left = to_left[0:8]
        to_right = to_right + pltpu.roll(to_right, 4, 0)
        to_left = to_left + pltpu.roll(to_left, 4, 0)
        slot_out[pl.ds(pl.multiple_of(s * 8, 8), 8), :] = jnp.where(half, to_right, to_left)

    group = 4

    def products(g, carry):
        for u in range(group):
            product(g * group + u)
        return carry

    for it in range(ITERS):
        lax.fori_loop(0, SLOTS // group, products, 0)
        for s in range(SLOTS // group * group, SLOTS):
            product(s)
        high, low = split(slot_out[...])
        table = onehot[...]
        added = dot_bf16(table, high, False) + dot_bf16(table, low, False)
        for d in range(9):
            part[it, d] = added[d * ROWS : (d + 1) * ROWS]
        arrivals = exchange(
            lambda d: part.at[it, d],
            lambda d, at: got.at[it, at],
            fold_send.at[it],
            fold_recv.at[it],
        )
        image = part[it, 4]
        for at, arrival in enumerate(arrivals):
            arrival.wait_recv()
            image = image + got[it, at]
        for h in range(2):
            basis[it + 1, h] = image[:, 128 * h : 128 * h + 128]
        if it + 1 < ITERS:
            nearq[it, 4] = image
            arrivals = exchange(
                lambda d: nearq.at[it, 4],
                lambda d, at: nearq.at[it, d],
                q_send.at[it],
                q_recv.at[it],
            )
            for arrival in arrivals:
                arrival.wait_recv()
            for d in range(9):
                for k in range(0, BLOCKS, 2):
                    value = nearq[it, d, 4 * k : 4 * k + 8, :]
                    put_pieces(d * BLOCKS + k, 0, value)
                    if k + 1 < BLOCKS:
                        put_pieces(d * BLOCKS + k + 1, 4, value)

    lane = lax.broadcasted_iota(jnp.int32, (8, 128), 1)
    forward = lax.broadcasted_iota(jnp.int32, (8, 128), 0) % 4 < 2

    def swapped(value):
        return jnp.where(forward, pltpu.roll(value, 6, 0), pltpu.roll(value, 2, 0))

    tiles = [
        [basis[i, h, g : g + 8, :] for h in range(2) for g in range(0, ROWS, 8)]
        for i in range(ITERS + 1)
    ]
    crossed = [[swapped(tile) for tile in row] for row in tiles]
    places = {}
    gram = jnp.zeros((8, 128), F32)
    for i in range(ITERS + 1):
        for j in range(i, ITERS + 1):
            for kind, other in (("same", tiles), ("cross", crossed)):
                total = None
                for mine, theirs in zip(tiles[i], other[j]):
                    term = mine * theirs
                    total = term if total is None else total + term
                column = jnp.sum(total, axis=1, keepdims=True)
                places[kind, i, j] = len(places)
                gram = jnp.where(lane == places[kind, i, j], column, gram)

    for stage, group_peers in enumerate(peers):
        sums[stage] = gram
        copies = []
        for at, device in enumerate(group_peers):
            copy = pltpu.make_async_remote_copy(
                src_ref=sums.at[stage],
                dst_ref=sum_in.at[stage, at],
                send_sem=sum_send.at[stage, at],
                recv_sem=sum_recv.at[stage, at],
                device_id=device,
                device_id_type=MESH,
            )
            copy.start()
            copies.append(copy)
        pending.extend(copies)
        for at, copy in enumerate(copies):
            copy.wait_recv()
            gram = gram + sum_in[stage, at]
    gram = gram + pltpu.roll(gram, 4, 0)

    def entry(kind, i, j, second):
        value = jnp.broadcast_to(gram[:, places[kind, i, j] : places[kind, i, j] + 1], (8, 128))
        return pltpu.roll(value, 6, 0) if second else value

    chain = ITERS + 1
    inner = {}
    for i in range(chain):
        for j in range(chain):
            inner[i, j] = entry("same", min(i, j), max(i, j), False)
            if i < ITERS and j < ITERS:
                inner[chain + i, chain + j] = entry("same", min(i, j), max(i, j), True)
            if j < ITERS:
                cross = entry("cross", min(i, j), max(i, j), i > j)
                inner[i, chain + j] = cross
                inner[chain + j, i] = cross

    def bilinear(first, second):
        total = None
        for i, a in first.items():
            inside = None
            for j, b in second.items():
                term = b * inner[i, j]
                inside = term if inside is None else inside + term
            inside = a * inside
            total = inside if total is None else total + inside
        return total

    def combine(base, scale, other):
        result = dict(base)
        for i, value in other.items():
            result[i] = result[i] + scale * value if i in result else scale * value
        return result

    one = jnp.ones((8, 128), F32)
    in_x, in_r, in_p = {}, {chain: one}, {0: one}
    norm_now = inner[chain, chain]
    for it in range(ITERS):
        image = {i + 1: value for i, value in in_p.items()}
        step = norm_now / bilinear(in_p, image)
        in_x = combine(in_x, step, in_p)
        in_r = combine(in_r, -step, image)
        norm_next = bilinear(in_r, in_r)
        in_p = combine(in_r, norm_next / norm_now, in_p)
        norm_now = norm_next

    for f, h in ((0, 0), (0, 1), (1, 0), (1, 1)):
        lanes = slice(128 * h, 128 * h + 128)
        vectors = {}
        for i in range(chain):
            vectors[i] = basis[i, h, pl.ds(f, BLOCKS, stride=4), :]
            if i < ITERS:
                vectors[chain + i] = basis[i, h, pl.ds(2 + f, BLOCKS, stride=4), :]

        def mixed(total, coefficients):
            for i, value in coefficients.items():
                term = value[f : f + 1, :] * vectors[i]
                total = term if total is None else total + term
            return total

        new_sol_ref[f, :, lanes] = mixed(sol_ref[f, :, lanes], in_x)
        new_res_ref[f, :, lanes] = mixed(None, in_r)
        new_dir_ref[f, :, lanes] = mixed(None, in_p)

    for copy in pending:
        copy.wait_send()


def solution(mesh):
    sizes = (mesh.shape["wide"], mesh.shape["narrow"])
    if sizes[0] == 64:
        stages = (
            ("narrow", ((1, sizes[1]),)),
            ("wide", ((2, 8),)),
            ("wide", ((16, 4), (1, 2))),
        )
    else:
        stages = (("narrow", ((1, sizes[1]),)), ("wide", ((1, sizes[0]),)))
    most = 0
    for _, places in stages:
        size = 1
        for _, count in places:
            size *= count
        most = max(most, size - 1)

    def on_device(node_coords, solution, residual, direction, tile_pairs, tile_counts):
        full_shape = direction.shape
        fields = jax.ShapeDtypeStruct((2, BLOCKS, NODES), F32)
        pairs = tile_pairs.reshape(2, SLOTS)
        vmem = pl.BlockSpec(memory_space=pltpu.VMEM)
        smem = pl.BlockSpec(memory_space=pltpu.SMEM)
        dma = pltpu.SemaphoreType.DMA
        outs = pl.pallas_call(
            functools.partial(body, sizes, stages),
            out_shape=(fields, fields, fields),
            in_specs=[vmem, vmem, vmem, vmem, smem, vmem, vmem],
            out_specs=(vmem, vmem, vmem),
            scratch_shapes=[
                pltpu.VMEM((9 * BLOCKS, 8, NODES), F32),
                pltpu.VMEM((ITERS - 1, 9, ROWS, NODES), F32),
                pltpu.VMEM((ITERS, 9, ROWS, NODES), F32),
                pltpu.VMEM((ITERS, 8, ROWS, NODES), F32),
                pltpu.VMEM((SLOTS, NODES, NODES), BF16),
                pltpu.VMEM((SLOTS, NODES, NODES), BF16),
                pltpu.VMEM((9 * BLOCKS, 16, NODES), BF16),
                pltpu.VMEM((512, NODES), F32),
                pltpu.VMEM((TABLE, 512), BF16),
                pltpu.VMEM((ITERS + 1, 2, ROWS, 128), F32),
                pltpu.VMEM((len(stages), 8, 128), F32),
                pltpu.VMEM((len(stages), most, 8, 128), F32),
                dma((8,)),
                dma((8,)),
                dma((ITERS - 1, 8)),
                dma((ITERS - 1, 8)),
                dma((ITERS, 8)),
                dma((ITERS, 8)),
                dma((len(stages), most)),
                dma((len(stages), most)),
            ],
            compiler_params=pltpu.CompilerParams(
                collective_id=0, has_side_effects=True, vmem_limit_bytes=48 * 1024 * 1024
            ),
            cost_estimate=pl.CostEstimate(
                flops=61 * 65536 * 40, bytes_accessed=200000, transcendentals=61 * 65536
            ),
        )(
            node_coords.reshape(3, BLOCKS, NODES),
            solution.reshape(2, BLOCKS, NODES),
            residual.reshape(2, BLOCKS, NODES),
            direction.reshape(2, BLOCKS, NODES),
            pairs,
            pairs,
            tile_counts,
        )
        return tuple(out.reshape(full_shape) for out in outs)

    fields_spec = P(None, "wide", "narrow", None, None)
    return jax.shard_map(
        on_device,
        mesh=mesh,
        in_specs=(
            fields_spec,
            fields_spec,
            fields_spec,
            fields_spec,
            P("wide", "narrow", None, None),
            P("wide", "narrow"),
        ),
        out_specs=(fields_spec, fields_spec, fields_spec),
        check_vma=False,
    )
```

```python
import functools

import jax
import jax.numpy as jnp
from jax import lax
from jax.experimental import pallas as pl
from jax.experimental.pallas import tpu as pltpu
from jax.sharding import PartitionSpec as P

ITERS = 3
RADIUS = 0.9
MESH = pl.DeviceIdType.MESH
F32 = jnp.float32
BF16 = jnp.bfloat16

BLOCKS = 9
NODES = 256
SLOTS = 61
ROWS = 40
TABLE = 368
GROUP = 3
CHUNK = 16

PHI_SLOPE = 4.0 / RADIUS**5
PHI_CONST = 1.0 / RADIUS**4


def dot_bf16(left, right, transposed):
    dims = (((1,), (1 if transposed else 0,)), ((), ()))
    return lax.dot_general(left, right, dims, preferred_element_type=F32)


def split(value):
    high = value.astype(BF16)
    return high, (value - high.astype(F32)).astype(BF16)


def stage_peers(wide, narrow, stages):
    peers = []
    for axis, places in stages:
        here = wide if axis == "wide" else narrow
        rank, size = 0, 1
        for stride, count in places:
            rank = rank * count + here // stride % count
            size *= count
        group = []
        for step in range(1, size):
            other = (rank + step) % size
            position = here
            left = other
            for stride, count in reversed(places):
                position = position + (left % count - here // stride % count) * stride
                left = left // count
            group.append((position, narrow) if axis == "wide" else (wide, position))
        peers.append(group)
    return peers


def body(
    sizes,
    stages,
    coord_ref,
    sol_ref,
    res_ref,
    dir_ref,
    pairs_hbm_ref,
    count_ref,
    new_sol_ref,
    new_res_ref,
    new_dir_ref,
    near0,
    nearq,
    part,
    got,
    khi_even,
    klo_even,
    khi_odd,
    klo_odd,
    pieces,
    slot_out,
    onehot,
    basis,
    sums,
    sum_in,
    raw,
    sol_rows,
    pairs_ref,
    pairs_vec_ref,
    cols,
    load_sems,
    near_send,
    near_recv,
    q_send,
    q_recv,
    fold_send,
    fold_recv,
    sum_send,
    sum_recv,
):
    wide_size, narrow_size = sizes
    wide = lax.axis_index("wide")
    narrow = lax.axis_index("narrow")
    neighbours = []
    for d in range(9):
        if d != 4:
            to_wide = (wide + (d // 3 - 1) + wide_size) % wide_size
            to_narrow = (narrow + (d % 3 - 1) + narrow_size) % narrow_size
            neighbours.append((d, (to_wide, to_narrow)))
    peers = stage_peers(wide, narrow, stages)

    loads = [
        pltpu.make_async_copy(source, landing, load_sems.at[at])
        for at, (source, landing) in enumerate(
            (
                (dir_ref, raw.at[pl.ds(0, 2 * BLOCKS)]),
                (res_ref, raw.at[pl.ds(2 * BLOCKS, 2 * BLOCKS)]),
                (coord_ref, raw.at[pl.ds(4 * BLOCKS, 3 * BLOCKS)]),
                (pairs_hbm_ref, pairs_ref),
                (pairs_hbm_ref, pairs_vec_ref),
                (sol_ref, sol_rows),
            )
        )
    ]
    for load in loads:
        load.start()

    barrier = pltpu.get_barrier_semaphore()
    targets = [device for _, device in neighbours] + [device for group in peers for device in group]
    for device in targets:
        pl.semaphore_signal(barrier, inc=1, device_id=device, device_id_type=MESH)

    for load in loads:
        load.wait()
    for k in range(BLOCKS):
        own = 4 * BLOCKS + k
        for c in range(7):
            near0[own, c : c + 1, :] = raw[c * BLOCKS + k]
        near0[own, 7:8, :] = jnp.zeros((1, NODES), F32)

    pl.semaphore_wait(barrier, len(targets))

    pending = []

    def exchange(source, landing, send_sem, recv_sem):
        copies = []
        for at, (d, device) in enumerate(neighbours):
            copy = pltpu.make_async_remote_copy(
                src_ref=source(d),
                dst_ref=landing(8 - d, 7 - at),
                send_sem=send_sem.at[at],
                recv_sem=recv_sem.at[7 - at],
                device_id=device,
                device_id_type=MESH,
            )
            copy.start()
            copies.append(copy)
        pending.extend(copies)

        def wait(at):
            pltpu.make_async_remote_copy(
                src_ref=source(4),
                dst_ref=landing(at + at // 4, at),
                send_sem=send_sem.at[at],
                recv_sem=recv_sem.at[at],
                device_id=neighbours[0][1],
                device_id_type=MESH,
            ).wait_recv()

        return wait

    arrive = exchange(
        lambda d: near0.at[pl.ds(4 * BLOCKS, BLOCKS)],
        lambda d, at: near0.at[pl.ds(d * BLOCKS, BLOCKS)],
        near_send,
        near_recv,
    )

    slot_of = lax.broadcasted_iota(jnp.int32, (64, 512), 0)
    lane_slot = lax.broadcasted_iota(jnp.int32, (64, 512), 1) // 8
    spread = jnp.where(slot_of == lane_slot, 1.0, 0.0).astype(BF16)
    left_id = pairs_vec_ref[0:1, :]
    right_id = pairs_vec_ref[1:2, :]
    live = lax.broadcasted_iota(jnp.int32, (1, SLOTS), 1) < count_ref[0:1, 0:1]
    toward_left = jnp.where(live, left_id, 255)
    toward_right = jnp.where(live & (left_id != right_id), right_id, 255)
    ids = jnp.concatenate([toward_right, toward_left] + [toward_left] * 6, axis=0).astype(F32)
    ids = jnp.concatenate([ids, jnp.full((8, 64 - SLOTS), 255.0, F32)], axis=1)
    wanted = dot_bf16(ids.astype(BF16), spread, False)
    lane = lax.broadcasted_iota(jnp.int32, (8, 512), 1)
    target = jnp.where(lane % 8 < 4, wanted[0:1, :], wanted[1:2, :]).astype(jnp.int32)
    for first in range(0, TABLE, CHUNK):
        row = lax.broadcasted_iota(jnp.int32, (CHUNK, 512), 0) + first
        place = row % ROWS
        block = jnp.where(place < 4 * BLOCKS, row // ROWS * BLOCKS + place // 4, 200)
        match = (block == target[0:1, :]) & (
            row % 4 == lax.broadcasted_iota(jnp.int32, (CHUNK, 512), 1) % 4
        )
        onehot[pl.ds(first, CHUNK), :] = jnp.where(match, 1.0, 0.0).astype(BF16)

    slot_out[pl.ds(8 * SLOTS, 512 - 8 * SLOTS), :] = jnp.zeros((512 - 8 * SLOTS, NODES), F32)
    half = lax.broadcasted_iota(jnp.int32, (8, NODES), 0) < 4

    def put_pieces(j, rows_at, value):
        high = value.astype(BF16).astype(F32)
        low = value - high
        if rows_at == 0:
            rows = jnp.where(half, high, pltpu.roll(low, 4, 0))
        else:
            rows = jnp.where(half, pltpu.roll(high, 4, 0), low)
        pieces[j] = jnp.concatenate([rows, rows], axis=0).astype(BF16)

    for h in range(2):
        for k in range(BLOCKS):
            basis[0, h, 4 * k : 4 * k + 4, :] = near0[4 * BLOCKS + k, 0:4, 128 * h : 128 * h + 128]
        basis[0, h, 4 * BLOCKS : ROWS, :] = jnp.zeros((ROWS - 4 * BLOCKS, 128), F32)

    def prepare(d):
        for k in range(BLOCKS):
            j = d * BLOCKS + k
            value = near0[j]
            put_pieces(j, 0, value)
            cols[j] = jnp.transpose(value)

    def prepare_next(at, carry):
        arrive(at)
        prepare(at + at // 4)
        return carry

    prepare(4)
    lax.fori_loop(0, 8, prepare_next, 0)

    def evaluate(s, high_ref, low_ref, at):
        left = cols.at[pairs_ref[0, s]]
        right = near0[pairs_ref[1, s]]
        for first in range(0, NODES, CHUNK):
            column = left[first : first + CHUNK, :]
            squared = None
            for axis in range(3):
                offset = column[:, 4 + axis : 5 + axis] - right[4 + axis : 5 + axis, :]
                squared = offset * offset if squared is None else squared + offset * offset
            squared = jnp.minimum(squared, RADIUS * RADIUS)
            distance = squared * lax.rsqrt(jnp.maximum(squared, 1e-36))
            rest = RADIUS - distance
            rest = rest * rest
            rest = rest * rest
            high, low = split(rest * (PHI_SLOPE * distance + PHI_CONST))
            high_ref[at, first : first + CHUNK, :] = high
            low_ref[at, first : first + CHUNK, :] = low

    def product(s, high_ref, low_ref, at):
        left = pieces[pairs_ref[0, s]]
        right = pieces[pairs_ref[1, s]]
        high = high_ref[at]
        low = low_ref[at]
        to_right = dot_bf16(left, high, False) + dot_bf16(left, low, False)
        to_left = dot_bf16(right, high, True) + dot_bf16(right, low, True)
        to_right = to_right[0:8]
        to_left = to_left[0:8]
        to_right = to_right + pltpu.roll(to_right, 4, 0)
        to_left = to_left + pltpu.roll(to_left, 4, 0)
        slot_out[pl.ds(pl.multiple_of(s * 8, 8), 8), :] = jnp.where(half, to_right, to_left)

    def evaluate_and_multiply(t, carry):
        before = jnp.maximum(t - 1, 0)
        product(2 * before, khi_even, klo_even, before)
        evaluate(2 * t, khi_even, klo_even, t)
        product(2 * before + 1, khi_odd, klo_odd, before)
        evaluate(jnp.minimum(2 * t + 1, SLOTS - 1), khi_odd, klo_odd, t)
        return carry

    def products(g, carry):
        for u in range(GROUP):
            at = g * GROUP + u
            product(2 * at, khi_even, klo_even, at)
            product(2 * at + 1, khi_odd, klo_odd, at)
        return carry

    for it in range(ITERS):
        if it == 0:
            lax.fori_loop(0, SLOTS // 2 + 1, evaluate_and_multiply, 0)
        else:
            lax.fori_loop(0, SLOTS // 2 // GROUP, products, 0)
        product(SLOTS - 1, khi_even, klo_even, SLOTS // 2)
        high, low = split(slot_out[...])
        table = onehot[...]
        added = dot_bf16(table, high, False) + dot_bf16(table, low, False)
        for d in range(9):
            part[it, d] = added[d * ROWS : (d + 1) * ROWS]
        arrive = exchange(
            lambda d: part.at[it, d],
            lambda d, at: got.at[it, at],
            fold_send.at[it],
            fold_recv.at[it],
        )
        image = part[it, 4]
        for at in range(8):
            arrive(at)
            image = image + got[it, at]
        for h in range(2):
            basis[it + 1, h] = image[:, 128 * h : 128 * h + 128]
        if it + 1 < ITERS:
            nearq[it, 4] = image
            arrive = exchange(
                lambda d: nearq.at[it, 4],
                lambda d, at: nearq.at[it, d],
                q_send.at[it],
                q_recv.at[it],
            )

            def refresh(d):
                for k in range(0, BLOCKS, 2):
                    value = nearq[it, d, 4 * k : 4 * k + 8, :]
                    put_pieces(d * BLOCKS + k, 0, value)
                    if k + 1 < BLOCKS:
                        put_pieces(d * BLOCKS + k + 1, 4, value)

            def refresh_next(at, carry):
                arrive(at)
                refresh(at + at // 4)
                return carry

            refresh(4)
            lax.fori_loop(0, 8, refresh_next, 0)

    lane = lax.broadcasted_iota(jnp.int32, (8, 128), 1)
    forward = lax.broadcasted_iota(jnp.int32, (8, 128), 0) % 4 < 2

    def swapped(value):
        return jnp.where(forward, pltpu.roll(value, 6, 0), pltpu.roll(value, 2, 0))

    tiles = [
        [basis[i, h, g : g + 8, :] for h in range(2) for g in range(0, ROWS, 8)]
        for i in range(ITERS + 1)
    ]
    crossed = [[swapped(tile) for tile in row] for row in tiles]
    places = {}
    gram = jnp.zeros((8, 128), F32)
    for i in range(ITERS + 1):
        for j in range(i, ITERS + 1):
            for kind, other in (("same", tiles), ("cross", crossed)):
                total = None
                for mine, theirs in zip(tiles[i], other[j]):
                    term = mine * theirs
                    total = term if total is None else total + term
                column = jnp.sum(total, axis=1, keepdims=True)
                places[kind, i, j] = len(places)
                gram = jnp.where(lane == places[kind, i, j], column, gram)

    for stage, group_peers in enumerate(peers):
        sums[stage] = gram
        copies = []
        for at, device in enumerate(group_peers):
            copy = pltpu.make_async_remote_copy(
                src_ref=sums.at[stage],
                dst_ref=sum_in.at[stage, at],
                send_sem=sum_send.at[stage, at],
                recv_sem=sum_recv.at[stage, at],
                device_id=device,
                device_id_type=MESH,
            )
            copy.start()
            copies.append(copy)
        pending.extend(copies)
        for at, copy in enumerate(copies):
            copy.wait_recv()
            gram = gram + sum_in[stage, at]
    gram = gram + pltpu.roll(gram, 4, 0)

    def entry(kind, i, j, second):
        value = jnp.broadcast_to(gram[:, places[kind, i, j] : places[kind, i, j] + 1], (8, 128))
        return pltpu.roll(value, 6, 0) if second else value

    chain = ITERS + 1
    inner = {}
    for i in range(chain):
        for j in range(chain):
            inner[i, j] = entry("same", min(i, j), max(i, j), False)
            if i < ITERS and j < ITERS:
                inner[chain + i, chain + j] = entry("same", min(i, j), max(i, j), True)
            if j < ITERS:
                cross = entry("cross", min(i, j), max(i, j), i > j)
                inner[i, chain + j] = cross
                inner[chain + j, i] = cross

    def bilinear(first, second):
        total = None
        for i, a in first.items():
            inside = None
            for j, b in second.items():
                term = b * inner[i, j]
                inside = term if inside is None else inside + term
            inside = a * inside
            total = inside if total is None else total + inside
        return total

    def combine(base, scale, other):
        result = dict(base)
        for i, value in other.items():
            result[i] = result[i] + scale * value if i in result else scale * value
        return result

    one = jnp.ones((8, 128), F32)
    in_x, in_r, in_p = {}, {chain: one}, {0: one}
    norm_now = inner[chain, chain]
    for it in range(ITERS):
        image = {i + 1: value for i, value in in_p.items()}
        step = norm_now / bilinear(in_p, image)
        in_x = combine(in_x, step, in_p)
        in_r = combine(in_r, -step, image)
        norm_next = bilinear(in_r, in_r)
        in_p = combine(in_r, norm_next / norm_now, in_p)
        norm_now = norm_next

    for f, h in ((0, 0), (0, 1), (1, 0), (1, 1)):
        lanes = slice(128 * h, 128 * h + 128)
        vectors = {}
        for i in range(chain):
            vectors[i] = basis[i, h, pl.ds(f, BLOCKS, stride=4), :]
            if i < ITERS:
                vectors[chain + i] = basis[i, h, pl.ds(2 + f, BLOCKS, stride=4), :]

        def mixed(total, coefficients):
            for i, value in coefficients.items():
                term = value[f : f + 1, :] * vectors[i]
                total = term if total is None else total + term
            return total

        results = (mixed(None, in_x), mixed(None, in_r), mixed(None, in_p))
        for k in range(BLOCKS):
            at = f * BLOCKS + k
            new_sol_ref[at, :, lanes] = sol_rows[at, :, lanes] + results[0][k : k + 1, :]
            new_res_ref[at, :, lanes] = results[1][k : k + 1, :]
            new_dir_ref[at, :, lanes] = results[2][k : k + 1, :]

    for copy in pending:
        copy.wait_send()


def solution(mesh):
    sizes = (mesh.shape["wide"], mesh.shape["narrow"])
    if sizes[0] == 64:
        stages = (
            ("narrow", ((1, sizes[1]),)),
            ("wide", ((2, 8),)),
            ("wide", ((16, 4), (1, 2))),
        )
    else:
        stages = (("narrow", ((1, sizes[1]),)), ("wide", ((1, sizes[0]),)))
    most = 0
    for _, places in stages:
        size = 1
        for _, count in places:
            size *= count
        most = max(most, size - 1)

    def on_device(node_coords, solution, residual, direction, tile_pairs, tile_counts):
        full_shape = direction.shape
        fields = jax.ShapeDtypeStruct((2 * BLOCKS, 1, NODES), F32)
        vmem = pl.BlockSpec(memory_space=pltpu.VMEM)
        anywhere = pl.BlockSpec(memory_space=pl.ANY)
        dma = pltpu.SemaphoreType.DMA
        outs = pl.pallas_call(
            functools.partial(body, sizes, stages),
            out_shape=(fields, fields, fields),
            in_specs=[anywhere] * 5 + [vmem],
            out_specs=(vmem, vmem, vmem),
            scratch_shapes=[
                pltpu.VMEM((9 * BLOCKS, 8, NODES), F32),
                pltpu.VMEM((ITERS - 1, 9, ROWS, NODES), F32),
                pltpu.VMEM((ITERS, 9, ROWS, NODES), F32),
                pltpu.VMEM((ITERS, 8, ROWS, NODES), F32),
                pltpu.VMEM((SLOTS // 2 + 1, NODES, NODES), BF16),
                pltpu.VMEM((SLOTS // 2 + 1, NODES, NODES), BF16),
                pltpu.VMEM((SLOTS // 2 + 1, NODES, NODES), BF16),
                pltpu.VMEM((SLOTS // 2 + 1, NODES, NODES), BF16),
                pltpu.VMEM((9 * BLOCKS, 16, NODES), BF16),
                pltpu.VMEM((512, NODES), F32),
                pltpu.VMEM((TABLE, 512), BF16),
                pltpu.VMEM((ITERS + 1, 2, ROWS, 128), F32),
                pltpu.VMEM((len(stages), 8, 128), F32),
                pltpu.VMEM((len(stages), most, 8, 128), F32),
                pltpu.VMEM((7 * BLOCKS, 1, NODES), F32),
                pltpu.VMEM((2 * BLOCKS, 1, NODES), F32),
                pltpu.SMEM((2, SLOTS), jnp.int32),
                pltpu.VMEM((2, SLOTS), jnp.int32),
                pltpu.VMEM((9 * BLOCKS, NODES, 8), F32),
                dma((6,)),
                dma((8,)),
                dma((8,)),
                dma((ITERS - 1, 8)),
                dma((ITERS - 1, 8)),
                dma((ITERS, 8)),
                dma((ITERS, 8)),
                dma((len(stages), most)),
                dma((len(stages), most)),
            ],
            compiler_params=pltpu.CompilerParams(
                collective_id=0, has_side_effects=True, vmem_limit_bytes=60 * 1024 * 1024
            ),
            cost_estimate=pl.CostEstimate(
                flops=61 * 65536 * 40, bytes_accessed=200000, transcendentals=61 * 65536
            ),
        )(
            node_coords.reshape(3 * BLOCKS, 1, NODES),
            solution.reshape(2 * BLOCKS, 1, NODES),
            residual.reshape(2 * BLOCKS, 1, NODES),
            direction.reshape(2 * BLOCKS, 1, NODES),
            tile_pairs.reshape(2, SLOTS),
            tile_counts,
        )
        return tuple(out.reshape(full_shape) for out in outs)

    fields_spec = P(None, "wide", "narrow", None, None)
    return jax.shard_map(
        on_device,
        mesh=mesh,
        in_specs=(
            fields_spec,
            fields_spec,
            fields_spec,
            fields_spec,
            P("wide", "narrow", None, None),
            P("wide", "narrow"),
        ),
        out_specs=(fields_spec, fields_spec, fields_spec),
        check_vma=False,
    )
```

```python
import functools

import jax
import jax.numpy as jnp
from jax import lax
from jax.experimental import pallas as pl
from jax.experimental.pallas import tpu as pltpu
from jax.sharding import PartitionSpec as P

ITERS = 3
RADIUS = 0.9
MESH = pl.DeviceIdType.MESH
F32 = jnp.float32
BF16 = jnp.bfloat16

BLOCKS = 9
NODES = 256
SLOTS = 61
PAIRS = SLOTS // 2 + 1
ROWS = 24
TABLE = 224
WIDTH = 1024

PHI_SLOPE = 4.0 / RADIUS**5
PHI_CONST = 1.0 / RADIUS**4


def dot_bf16(left, right):
    return lax.dot_general(left, right, (((1,), (0,)), ((), ())), preferred_element_type=F32)


def split(value):
    high = value.astype(BF16)
    return high, (value - high.astype(F32)).astype(BF16)


def stage_peers(wide, narrow, stages):
    peers = []
    for axis, places in stages:
        here = wide if axis == "wide" else narrow
        rank, size = 0, 1
        for stride, count in places:
            rank = rank * count + here // stride % count
            size *= count
        group = []
        for step in range(1, size):
            other = (rank + step) % size
            position = here
            left = other
            for stride, count in reversed(places):
                position = position + (left % count - here // stride % count) * stride
                left = left // count
            group.append((position, narrow) if axis == "wide" else (wide, position))
        peers.append(group)
    return peers


def body(
    sizes,
    stages,
    coord_ref,
    sol_ref,
    res_ref,
    dir_ref,
    pairs_hbm_ref,
    count_ref,
    new_sol_ref,
    new_res_ref,
    new_dir_ref,
    near,
    nearq,
    part,
    got,
    tile_even,
    tile_odd,
    turned,
    slot_out,
    onehot,
    current_x,
    sums,
    sum_in,
    raw,
    sol_rows,
    pairs_ref,
    pairs_vec_ref,
    cols,
    load_sems,
    near_send,
    near_recv,
    q_send,
    q_recv,
    fold_send,
    fold_recv,
    sum_send,
    sum_recv,
):
    wide_size, narrow_size = sizes
    wide = lax.axis_index("wide")
    narrow = lax.axis_index("narrow")
    neighbours = []
    for d in range(9):
        if d != 4:
            to_wide = (wide + (d // 3 - 1) + wide_size) % wide_size
            to_narrow = (narrow + (d % 3 - 1) + narrow_size) % narrow_size
            neighbours.append((d, (to_wide, to_narrow)))
    peers = stage_peers(wide, narrow, stages)

    loads = [
        pltpu.make_async_copy(source, landing, load_sems.at[at])
        for at, (source, landing) in enumerate(
            (
                (dir_ref, raw.at[pl.ds(0, 2 * BLOCKS)]),
                (res_ref, raw.at[pl.ds(2 * BLOCKS, 2 * BLOCKS)]),
                (coord_ref, raw.at[pl.ds(4 * BLOCKS, 3 * BLOCKS)]),
                (pairs_hbm_ref, pairs_ref),
                (pairs_hbm_ref, pairs_vec_ref),
                (sol_ref, sol_rows),
            )
        )
    ]
    for load in loads:
        load.start()

    barrier = pltpu.get_barrier_semaphore()
    targets = [device for _, device in neighbours] + [device for group in peers for device in group]
    for device in targets:
        pl.semaphore_signal(barrier, inc=1, device_id=device, device_id_type=MESH)

    for load in loads:
        load.wait()
    for k in range(BLOCKS):
        own = 4 * BLOCKS + k
        for c in range(7):
            near[own, c : c + 1, :] = raw[c * BLOCKS + k]
        near[own, 7:8, :] = jnp.zeros((1, NODES), F32)
        current_x[k] = jnp.zeros((8, NODES), F32)
        for f in range(2):
            current_x[k, f : f + 1, :] = sol_rows[f * BLOCKS + k]

    pl.semaphore_wait(barrier, len(targets))

    pending = []

    def exchange(source, landing, send_sem, recv_sem):
        copies = []
        for at, (d, device) in enumerate(neighbours):
            copy = pltpu.make_async_remote_copy(
                src_ref=source(d),
                dst_ref=landing(8 - d, 7 - at),
                send_sem=send_sem.at[at],
                recv_sem=recv_sem.at[7 - at],
                device_id=device,
                device_id_type=MESH,
            )
            copy.start()
            copies.append(copy)

        def wait(at):
            pltpu.make_async_remote_copy(
                src_ref=source(4),
                dst_ref=landing(at + at // 4, at),
                send_sem=send_sem.at[at],
                recv_sem=recv_sem.at[at],
                device_id=neighbours[0][1],
                device_id_type=MESH,
            ).wait_recv()

        return wait, copies

    arrive, first_copies = exchange(
        lambda d: near.at[pl.ds(4 * BLOCKS, BLOCKS)],
        lambda d, at: near.at[pl.ds(d * BLOCKS, BLOCKS)],
        near_send,
        near_recv,
    )

    slot_of = lax.broadcasted_iota(jnp.int32, (64, WIDTH), 0)
    lane_slot = lax.broadcasted_iota(jnp.int32, (64, WIDTH), 1) // 16
    spread = jnp.where(slot_of == lane_slot, 1.0, 0.0).astype(BF16)
    left_id = pairs_vec_ref[0:1, :]
    right_id = pairs_vec_ref[1:2, :]
    live = lax.broadcasted_iota(jnp.int32, (1, SLOTS), 1) < count_ref[0:1, 0:1]
    toward_left = jnp.where(live, left_id, 255)
    toward_right = jnp.where(live & (left_id != right_id), right_id, 255)
    ids = jnp.concatenate([toward_right, toward_left] + [toward_left] * 6, axis=0).astype(F32)
    ids = jnp.concatenate([ids, jnp.full((8, 64 - SLOTS), 255.0, F32)], axis=1)
    wanted = dot_bf16(ids.astype(BF16), spread)
    lane = lax.broadcasted_iota(jnp.int32, (1, WIDTH), 1)
    target = jnp.where(lane % 16 < 8, wanted[0:1, :], wanted[1:2, :]).astype(jnp.int32)
    target = target * 2 + lane % 8 // 4

    def fill_onehot(g, carry):
        row = lax.broadcasted_iota(jnp.int32, (16, WIDTH), 0) + g * 16
        place = row % ROWS
        block = jnp.where(place < 2 * BLOCKS, row // ROWS * (2 * BLOCKS) + place, 600)
        onehot[pl.ds(pl.multiple_of(g * 16, 16), 16), :] = jnp.where(
            block == target, 1.0, 0.0
        ).astype(BF16)
        return carry

    lax.fori_loop(0, TABLE // 16, fill_onehot, 0)
    slot_out[pl.ds(32 * PAIRS, WIDTH - 32 * PAIRS), :] = jnp.zeros((WIDTH - 32 * PAIRS, NODES), F32)

    row8 = lax.broadcasted_iota(jnp.int32, (8, NODES), 0)
    half = row8 < 4

    def prepare(d):
        for k in range(BLOCKS):
            cols[d * BLOCKS + k] = jnp.transpose(near[d * BLOCKS + k])

    def prepare_next(at, carry):
        arrive(at)
        prepare(at + at // 4)
        return carry

    prepare(4)
    lax.fori_loop(0, 8, prepare_next, 0)

    def evaluate(s, tile_ref, at):
        left = cols.at[pairs_ref[0, s]]
        right = near[pairs_ref[1, s]]
        for first in range(0, NODES, 8):
            column = left[first : first + 8, :]
            squared = None
            for axis in range(3):
                offset = column[:, 4 + axis : 5 + axis] - right[4 + axis : 5 + axis, :]
                squared = offset * offset if squared is None else squared + offset * offset
            squared = jnp.minimum(squared, RADIUS * RADIUS)
            distance = squared * lax.rsqrt(jnp.maximum(squared, 1e-36))
            rest = RADIUS - distance
            rest = rest * rest
            rest = rest * rest
            tile_ref[at, first : first + 8, :] = rest * (PHI_SLOPE * distance + PHI_CONST)

    def turn(s, tile_ref, at):
        for first in range(0, NODES, 128):
            turned[s, :, first : first + 128] = jnp.transpose(tile_ref[at, first : first + 128, :])

    def evaluate_two(t, carry):
        evaluate(2 * t, tile_even, t)
        turn(2 * t, tile_even, t)
        evaluate(jnp.minimum(2 * t + 1, SLOTS - 1), tile_odd, t)
        turn(2 * t + 1, tile_odd, t)
        return carry

    lax.fori_loop(0, PAIRS, evaluate_two, 0)

    def weighted(block, tile):
        column_ref = cols.at[block]
        totals = [None, None]
        for first in range(0, NODES, 8):
            column = column_ref[first : first + 8, :]
            values = tile(first)
            for f in range(2):
                term = column[:, f : f + 1] * values
                totals[f] = term if totals[f] is None else totals[f] + term
        return jnp.where(half, totals[0], totals[1]) + pltpu.roll(
            jnp.where(half, totals[1], totals[0]), 4, 0
        )

    def product(s, from_slot, tile_ref, at):
        start = pl.multiple_of(s * 16, 16)
        slot_out[pl.ds(start, 8), :] = weighted(
            pairs_ref[0, from_slot], lambda first: tile_ref[at, first : first + 8, :]
        )
        slot_out[pl.ds(start + 8, 8), :] = weighted(
            pairs_ref[1, from_slot], lambda first: turned[s, first : first + 8, :]
        )

    def products(t, carry):
        product(2 * t, 2 * t, tile_even, t)
        product(2 * t + 1, jnp.minimum(2 * t + 1, SLOTS - 1), tile_odd, t)
        return carry

    row = lax.broadcasted_iota(jnp.int32, (8, 128), 0)

    def both(value):
        return jnp.concatenate([value, value], axis=1)

    for it in range(ITERS):
        lax.fori_loop(0, PAIRS, products, 0)
        high, low = split(slot_out[...])
        table = onehot[...]
        added = dot_bf16(table, high) + dot_bf16(table, low)
        for d in range(9):
            part[it, d] = added[d * ROWS : (d + 1) * ROWS]
        arrive, copies = exchange(
            lambda d: part.at[it, d],
            lambda d, at: got.at[it, at],
            fold_send.at[it],
            fold_recv.at[it],
        )
        pending.extend(copies)
        image = part[it, 4]
        for at in range(8):
            arrive(at)
            image = image + got[it, at]
        last = it + 1 == ITERS
        if not last:
            nearq[it, 4] = image
            arrive, copies = exchange(
                lambda d: nearq.at[it, 4],
                lambda d, at: nearq.at[it, d],
                q_send.at[it],
                q_recv.at[it],
            )
            pending.extend(copies)

        total = jnp.zeros((8, 128), F32)
        for k in range(BLOCKS):
            at = k * 2 // 8 * 8
            tile = pltpu.roll(image[at : at + 8, :], (8 - k * 2 % 8) % 8, 0)
            own = near[4 * BLOCKS + k]
            first = jnp.where(row8 < 4, own, jnp.where(row8 < 6, pltpu.roll(tile, 4, 0), pltpu.roll(own, 4, 0)))
            second = jnp.where(
                row8 < 2,
                tile,
                jnp.where(
                    row8 < 4,
                    pltpu.roll(tile, 2, 0),
                    jnp.where(row8 < 6, pltpu.roll(tile, 4, 0), pltpu.roll(own, 4, 0)),
                ),
            )
            term = first * second
            total = total + (term[:, 0:128] + term[:, 128:256])

        for stage, group_peers in enumerate(peers):
            sums[it, stage] = total
            copies = []
            for at, device in enumerate(group_peers):
                copy = pltpu.make_async_remote_copy(
                    src_ref=sums.at[it, stage],
                    dst_ref=sum_in.at[it, stage, at],
                    send_sem=sum_send.at[it, stage, at],
                    recv_sem=sum_recv.at[it, stage, at],
                    device_id=device,
                    device_id_type=MESH,
                )
                copy.start()
                copies.append(copy)
            pending.extend(copies)
            for at, copy in enumerate(copies):
                copy.wait_recv()
                total = total + sum_in[it, stage, at]
        totals = jnp.broadcast_to(jnp.sum(total, axis=1, keepdims=True), (8, 128))

        norm_now = pltpu.roll(totals, 2, 0)
        step = norm_now / totals
        norm_next = norm_now + step * (step * pltpu.roll(totals, 4, 0) - 2.0 * pltpu.roll(totals, 6, 0))
        ratio = norm_next / norm_now
        step_x = both(jnp.where(row < 2, step, 0.0))
        step_r = both(jnp.where((row >= 2) & (row < 4), pltpu.roll(step, 2, 0), 0.0))
        ratio = both(jnp.where(row < 2, ratio, 0.0))

        def renew(j, k, tile):
            value = near[j]
            changed = value - step_r * pltpu.roll(tile, (8 - k * 2 % 8 + 2) % 8, 0)
            value = jnp.where(row8 < 2, pltpu.roll(changed, 6, 0) + ratio * value, changed)
            near[j] = value
            return value

        if it == 0:
            for copy in first_copies:
                copy.wait_send()
        for k in range(BLOCKS):
            at = k * 2 // 8 * 8
            current_x[k] = current_x[k] + step_x * near[4 * BLOCKS + k]
            value = renew(4 * BLOCKS + k, k, image[at : at + 8, :])
            if last:
                for f in range(2):
                    new_sol_ref[f * BLOCKS + k] = current_x[k, f : f + 1, :]
                    new_res_ref[f * BLOCKS + k] = value[2 + f : 3 + f, :]
                    new_dir_ref[f * BLOCKS + k] = value[f : f + 1, :]
            else:
                cols[4 * BLOCKS + k] = jnp.transpose(value)
        if not last:

            def renew_next(at, carry):
                arrive(at)
                d = at + at // 4
                for k in range(BLOCKS):
                    tile = nearq[it, d, k * 2 // 8 * 8 : k * 2 // 8 * 8 + 8, :]
                    j = d * BLOCKS + k
                    cols[j] = jnp.transpose(renew(j, k, tile))
                return carry

            lax.fori_loop(0, 8, renew_next, 0)

    for copy in pending:
        copy.wait_send()


def solution(mesh):
    sizes = (mesh.shape["wide"], mesh.shape["narrow"])
    if sizes[0] == 64:
        stages = (
            ("narrow", ((1, sizes[1]),)),
            ("wide", ((2, 8),)),
            ("wide", ((16, 4), (1, 2))),
        )
    else:
        stages = (("narrow", ((1, sizes[1]),)), ("wide", ((1, sizes[0]),)))
    most = 0
    for _, places in stages:
        size = 1
        for _, count in places:
            size *= count
        most = max(most, size - 1)

    def on_device(node_coords, solution, residual, direction, tile_pairs, tile_counts):
        full_shape = direction.shape
        fields = jax.ShapeDtypeStruct((2 * BLOCKS, 1, NODES), F32)
        vmem = pl.BlockSpec(memory_space=pltpu.VMEM)
        anywhere = pl.BlockSpec(memory_space=pl.ANY)
        dma = pltpu.SemaphoreType.DMA
        outs = pl.pallas_call(
            functools.partial(body, sizes, stages),
            out_shape=(fields, fields, fields),
            in_specs=[anywhere] * 5 + [vmem],
            out_specs=(vmem, vmem, vmem),
            scratch_shapes=[
                pltpu.VMEM((9 * BLOCKS, 8, NODES), F32),
                pltpu.VMEM((ITERS - 1, 9, ROWS, NODES), F32),
                pltpu.VMEM((ITERS, 9, ROWS, NODES), F32),
                pltpu.VMEM((ITERS, 8, ROWS, NODES), F32),
                pltpu.VMEM((PAIRS, NODES, NODES), F32),
                pltpu.VMEM((PAIRS, NODES, NODES), F32),
                pltpu.VMEM((2 * PAIRS, NODES, NODES), F32),
                pltpu.VMEM((WIDTH, NODES), F32),
                pltpu.VMEM((TABLE, WIDTH), BF16),
                pltpu.VMEM((BLOCKS, 8, NODES), F32),
                pltpu.VMEM((ITERS, len(stages), 8, 128), F32),
                pltpu.VMEM((ITERS, len(stages), most, 8, 128), F32),
                pltpu.VMEM((7 * BLOCKS, 1, NODES), F32),
                pltpu.VMEM((2 * BLOCKS, 1, NODES), F32),
                pltpu.SMEM((2, SLOTS), jnp.int32),
                pltpu.VMEM((2, SLOTS), jnp.int32),
                pltpu.VMEM((9 * BLOCKS, NODES, 8), F32),
                dma((6,)),
                dma((8,)),
                dma((8,)),
                dma((ITERS - 1, 8)),
                dma((ITERS - 1, 8)),
                dma((ITERS, 8)),
                dma((ITERS, 8)),
                dma((ITERS, len(stages), most)),
                dma((ITERS, len(stages), most)),
            ],
            compiler_params=pltpu.CompilerParams(
                collective_id=0, has_side_effects=True, vmem_limit_bytes=60 * 1024 * 1024
            ),
            cost_estimate=pl.CostEstimate(
                flops=61 * 65536 * 40, bytes_accessed=200000, transcendentals=61 * 65536
            ),
        )(
            node_coords.reshape(3 * BLOCKS, 1, NODES),
            solution.reshape(2 * BLOCKS, 1, NODES),
            residual.reshape(2 * BLOCKS, 1, NODES),
            direction.reshape(2 * BLOCKS, 1, NODES),
            tile_pairs.reshape(2, SLOTS),
            tile_counts,
        )
        return tuple(out.reshape(full_shape) for out in outs)

    fields_spec = P(None, "wide", "narrow", None, None)
    return jax.shard_map(
        on_device,
        mesh=mesh,
        in_specs=(
            fields_spec,
            fields_spec,
            fields_spec,
            fields_spec,
            P("wide", "narrow", None, None),
            P("wide", "narrow"),
        ),
        out_specs=(fields_spec, fields_spec, fields_spec),
        check_vma=False,
    )
```

```python
import functools

import jax
import jax.numpy as jnp
from jax import lax
from jax.experimental import pallas as pl
from jax.experimental.pallas import tpu as pltpu
from jax.sharding import PartitionSpec as P

ITERS = 3
RADIUS = 0.9
MESH = pl.DeviceIdType.MESH
F32 = jnp.float32
BF16 = jnp.bfloat16

BLOCKS = 9
NODES = 256
SLOTS = 61
ROWS = 40
TABLE = 368
GROUP = 3
CHUNK = 16

PHI_SLOPE = 4.0 / RADIUS**5
PHI_CONST = 1.0 / RADIUS**4


def dot_bf16(left, right, transposed):
    dims = (((1,), (1 if transposed else 0,)), ((), ()))
    return lax.dot_general(left, right, dims, preferred_element_type=F32)


def split(value):
    high = value.astype(BF16)
    return high, (value - high.astype(F32)).astype(BF16)


def stage_peers(wide, narrow, stages):
    peers = []
    for axis, places in stages:
        here = wide if axis == "wide" else narrow
        rank, size = 0, 1
        for stride, count in places:
            rank = rank * count + here // stride % count
            size *= count
        group = []
        for step in range(1, size):
            other = (rank + step) % size
            position = here
            left = other
            for stride, count in reversed(places):
                position = position + (left % count - here // stride % count) * stride
                left = left // count
            group.append((position, narrow) if axis == "wide" else (wide, position))
        peers.append(group)
    return peers


def body(
    sizes,
    stages,
    coord_ref,
    sol_ref,
    res_ref,
    dir_ref,
    pairs_hbm_ref,
    count_ref,
    new_sol_ref,
    new_res_ref,
    new_dir_ref,
    near0,
    nearq,
    part,
    got,
    khi_even,
    klo_even,
    khi_odd,
    klo_odd,
    thi_even,
    tlo_even,
    thi_odd,
    tlo_odd,
    stage_even,
    stage_odd,
    pieces,
    slot_out,
    onehot,
    basis,
    sums,
    sum_in,
    raw,
    sol_rows,
    pairs_ref,
    pairs_vec_ref,
    cols,
    load_sems,
    near_send,
    near_recv,
    q_send,
    q_recv,
    fold_send,
    fold_recv,
    sum_send,
    sum_recv,
):
    wide_size, narrow_size = sizes
    wide = lax.axis_index("wide")
    narrow = lax.axis_index("narrow")
    neighbours = []
    for d in range(9):
        if d != 4:
            to_wide = (wide + (d // 3 - 1) + wide_size) % wide_size
            to_narrow = (narrow + (d % 3 - 1) + narrow_size) % narrow_size
            neighbours.append((d, (to_wide, to_narrow)))
    peers = stage_peers(wide, narrow, stages)

    loads = [
        pltpu.make_async_copy(source, landing, load_sems.at[at])
        for at, (source, landing) in enumerate(
            (
                (dir_ref, raw.at[pl.ds(0, 2 * BLOCKS)]),
                (res_ref, raw.at[pl.ds(2 * BLOCKS, 2 * BLOCKS)]),
                (coord_ref, raw.at[pl.ds(4 * BLOCKS, 3 * BLOCKS)]),
                (pairs_hbm_ref, pairs_ref),
                (pairs_hbm_ref, pairs_vec_ref),
                (sol_ref, sol_rows),
            )
        )
    ]
    for load in loads:
        load.start()

    barrier = pltpu.get_barrier_semaphore()
    targets = [device for _, device in neighbours] + [device for group in peers for device in group]
    for device in targets:
        pl.semaphore_signal(barrier, inc=1, device_id=device, device_id_type=MESH)

    for load in loads:
        load.wait()
    for k in range(BLOCKS):
        own = 4 * BLOCKS + k
        for c in range(7):
            near0[own, c : c + 1, :] = raw[c * BLOCKS + k]
        near0[own, 7:8, :] = jnp.zeros((1, NODES), F32)

    pl.semaphore_wait(barrier, len(targets))

    pending = []

    def exchange(source, landing, send_sem, recv_sem):
        copies = []
        for at, (d, device) in enumerate(neighbours):
            copy = pltpu.make_async_remote_copy(
                src_ref=source(d),
                dst_ref=landing(8 - d, 7 - at),
                send_sem=send_sem.at[at],
                recv_sem=recv_sem.at[7 - at],
                device_id=device,
                device_id_type=MESH,
            )
            copy.start()
            copies.append(copy)
        pending.extend(copies)

        def wait(at):
            pltpu.make_async_remote_copy(
                src_ref=source(4),
                dst_ref=landing(at + at // 4, at),
                send_sem=send_sem.at[at],
                recv_sem=recv_sem.at[at],
                device_id=neighbours[0][1],
                device_id_type=MESH,
            ).wait_recv()

        return wait

    arrive = exchange(
        lambda d: near0.at[pl.ds(4 * BLOCKS, BLOCKS)],
        lambda d, at: near0.at[pl.ds(d * BLOCKS, BLOCKS)],
        near_send,
        near_recv,
    )

    slot_of = lax.broadcasted_iota(jnp.int32, (64, 512), 0)
    lane_slot = lax.broadcasted_iota(jnp.int32, (64, 512), 1) // 8
    spread = jnp.where(slot_of == lane_slot, 1.0, 0.0).astype(BF16)
    left_id = pairs_vec_ref[0:1, :]
    right_id = pairs_vec_ref[1:2, :]
    live = lax.broadcasted_iota(jnp.int32, (1, SLOTS), 1) < count_ref[0:1, 0:1]
    toward_left = jnp.where(live, left_id, 255)
    toward_right = jnp.where(live & (left_id != right_id), right_id, 255)
    ids = jnp.concatenate([toward_right, toward_left] + [toward_left] * 6, axis=0).astype(F32)
    ids = jnp.concatenate([ids, jnp.full((8, 64 - SLOTS), 255.0, F32)], axis=1)
    wanted = dot_bf16(ids.astype(BF16), spread, False)
    lane = lax.broadcasted_iota(jnp.int32, (8, 512), 1)
    target = jnp.where(lane % 8 < 4, wanted[0:1, :], wanted[1:2, :]).astype(jnp.int32)
    for first in range(0, TABLE, CHUNK):
        row = lax.broadcasted_iota(jnp.int32, (CHUNK, 512), 0) + first
        place = row % ROWS
        block = jnp.where(place < 4 * BLOCKS, row // ROWS * BLOCKS + place // 4, 200)
        match = (block == target[0:1, :]) & (
            row % 4 == lax.broadcasted_iota(jnp.int32, (CHUNK, 512), 1) % 4
        )
        onehot[pl.ds(first, CHUNK), :] = jnp.where(match, 1.0, 0.0).astype(BF16)

    slot_out[pl.ds(8 * SLOTS, 512 - 8 * SLOTS), :] = jnp.zeros((512 - 8 * SLOTS, NODES), F32)
    half = lax.broadcasted_iota(jnp.int32, (8, NODES), 0) < 4

    def put_pieces(j, rows_at, value):
        high = value.astype(BF16).astype(F32)
        low = value - high
        if rows_at == 0:
            rows = jnp.where(half, high, pltpu.roll(low, 4, 0))
        else:
            rows = jnp.where(half, pltpu.roll(high, 4, 0), low)
        pieces[j] = jnp.concatenate([rows, rows], axis=0).astype(BF16)

    for h in range(2):
        for k in range(BLOCKS):
            basis[0, h, 4 * k : 4 * k + 4, :] = near0[4 * BLOCKS + k, 0:4, 128 * h : 128 * h + 128]
        basis[0, h, 4 * BLOCKS : ROWS, :] = jnp.zeros((ROWS - 4 * BLOCKS, 128), F32)

    def prepare(d):
        for k in range(BLOCKS):
            j = d * BLOCKS + k
            value = near0[j]
            put_pieces(j, 0, value)
            cols[j] = jnp.transpose(value)

    def prepare_next(at, carry):
        arrive(at)
        prepare(at + at // 4)
        return carry

    prepare(4)
    lax.fori_loop(0, 8, prepare_next, 0)

    def evaluate(s, refs, stage, at):
        high_ref, low_ref, high_turned, low_turned = refs
        left = cols.at[pairs_ref[0, s]]
        right = near0[pairs_ref[1, s]]
        rights = [jnp.broadcast_to(right[4 + axis : 5 + axis, :], (CHUNK, NODES)) for axis in range(3)]
        for first in range(0, NODES, CHUNK):
            column = left[first : first + CHUNK, :]
            squared = None
            for axis in range(3):
                offset = column[:, 4 + axis : 5 + axis] - rights[axis]
                squared = offset * offset if squared is None else squared + offset * offset
            squared = jnp.minimum(squared, RADIUS * RADIUS)
            distance = squared * lax.rsqrt(jnp.maximum(squared, 1e-36))
            rest = RADIUS - distance
            rest = rest * rest
            rest = rest * rest
            value = rest * (PHI_SLOPE * distance + PHI_CONST)
            high, low = split(value)
            high_ref[at, first : first + CHUNK, :] = high
            low_ref[at, first : first + CHUNK, :] = low
            stage[first : first + CHUNK, :] = value
        for first in range(0, NODES, 128):
            high, low = split(jnp.transpose(stage[first : first + 128, :]))
            high_turned[at, :, first : first + 128] = high
            low_turned[at, :, first : first + 128] = low

    def product(s, refs, at):
        high_ref, low_ref, high_turned, low_turned = refs
        left = pieces[pairs_ref[0, s]]
        right = pieces[pairs_ref[1, s]]
        to_right = dot_bf16(left, high_ref[at], False) + dot_bf16(left, low_ref[at], False)
        to_left = dot_bf16(right, high_turned[at], False) + dot_bf16(right, low_turned[at], False)
        to_right = to_right[0:8]
        to_left = to_left[0:8]
        to_right = to_right + pltpu.roll(to_right, 4, 0)
        to_left = to_left + pltpu.roll(to_left, 4, 0)
        slot_out[pl.ds(pl.multiple_of(s * 8, 8), 8), :] = jnp.where(half, to_right, to_left)

    even = (khi_even, klo_even, thi_even, tlo_even)
    odd = (khi_odd, klo_odd, thi_odd, tlo_odd)

    def evaluate_and_multiply(t, carry):
        before = jnp.maximum(t - 1, 0)
        product(2 * before, even, before)
        evaluate(2 * t, even, stage_even, t)
        product(2 * before + 1, odd, before)
        evaluate(jnp.minimum(2 * t + 1, SLOTS - 1), odd, stage_odd, t)
        return carry

    def products(g, carry):
        for u in range(GROUP):
            at = g * GROUP + u
            product(2 * at, even, at)
            product(2 * at + 1, odd, at)
        return carry

    for it in range(ITERS):
        if it == 0:
            lax.fori_loop(0, SLOTS // 2 + 1, evaluate_and_multiply, 0)
        else:
            lax.fori_loop(0, SLOTS // 2 // GROUP, products, 0)
        product(SLOTS - 1, even, SLOTS // 2)
        high, low = split(slot_out[...])
        table = onehot[...]
        added = dot_bf16(table, high, False) + dot_bf16(table, low, False)
        for d in range(9):
            part[it, d] = added[d * ROWS : (d + 1) * ROWS]
        arrive = exchange(
            lambda d: part.at[it, d],
            lambda d, at: got.at[it, at],
            fold_send.at[it],
            fold_recv.at[it],
        )
        image = part[it, 4]
        for at in range(8):
            arrive(at)
            image = image + got[it, at]
        for h in range(2):
            basis[it + 1, h] = image[:, 128 * h : 128 * h + 128]
        if it + 1 < ITERS:
            nearq[it, 4] = image
            arrive = exchange(
                lambda d: nearq.at[it, 4],
                lambda d, at: nearq.at[it, d],
                q_send.at[it],
                q_recv.at[it],
            )

            def refresh(d):
                for k in range(0, BLOCKS, 2):
                    value = nearq[it, d, 4 * k : 4 * k + 8, :]
                    put_pieces(d * BLOCKS + k, 0, value)
                    if k + 1 < BLOCKS:
                        put_pieces(d * BLOCKS + k + 1, 4, value)

            def refresh_next(at, carry):
                arrive(at)
                refresh(at + at // 4)
                return carry

            refresh(4)
            lax.fori_loop(0, 8, refresh_next, 0)

    lane = lax.broadcasted_iota(jnp.int32, (8, 128), 1)
    forward = lax.broadcasted_iota(jnp.int32, (8, 128), 0) % 4 < 2

    def swapped(value):
        return jnp.where(forward, pltpu.roll(value, 6, 0), pltpu.roll(value, 2, 0))

    tiles = [
        [basis[i, h, g : g + 8, :] for h in range(2) for g in range(0, ROWS, 8)]
        for i in range(ITERS + 1)
    ]
    crossed = [[swapped(tile) for tile in row] for row in tiles]
    places = {}
    gram = jnp.zeros((8, 128), F32)
    for i in range(ITERS + 1):
        for j in range(i, ITERS + 1):
            for kind, other in (("same", tiles), ("cross", crossed)):
                total = None
                for mine, theirs in zip(tiles[i], other[j]):
                    term = mine * theirs
                    total = term if total is None else total + term
                column = jnp.sum(total, axis=1, keepdims=True)
                places[kind, i, j] = len(places)
                gram = jnp.where(lane == places[kind, i, j], column, gram)

    for stage, group_peers in enumerate(peers):
        sums[stage] = gram
        copies = []
        for at, device in enumerate(group_peers):
            copy = pltpu.make_async_remote_copy(
                src_ref=sums.at[stage],
                dst_ref=sum_in.at[stage, at],
                send_sem=sum_send.at[stage, at],
                recv_sem=sum_recv.at[stage, at],
                device_id=device,
                device_id_type=MESH,
            )
            copy.start()
            copies.append(copy)
        pending.extend(copies)
        for at, copy in enumerate(copies):
            copy.wait_recv()
            gram = gram + sum_in[stage, at]
    gram = gram + pltpu.roll(gram, 4, 0)

    def entry(kind, i, j, second):
        value = jnp.broadcast_to(gram[:, places[kind, i, j] : places[kind, i, j] + 1], (8, 128))
        return pltpu.roll(value, 6, 0) if second else value

    chain = ITERS + 1
    inner = {}
    for i in range(chain):
        for j in range(chain):
            inner[i, j] = entry("same", min(i, j), max(i, j), False)
            if i < ITERS and j < ITERS:
                inner[chain + i, chain + j] = entry("same", min(i, j), max(i, j), True)
            if j < ITERS:
                cross = entry("cross", min(i, j), max(i, j), i > j)
                inner[i, chain + j] = cross
                inner[chain + j, i] = cross

    def bilinear(first, second):
        total = None
        for i, a in first.items():
            inside = None
            for j, b in second.items():
                term = b * inner[i, j]
                inside = term if inside is None else inside + term
            inside = a * inside
            total = inside if total is None else total + inside
        return total

    def combine(base, scale, other):
        result = dict(base)
        for i, value in other.items():
            result[i] = result[i] + scale * value if i in result else scale * value
        return result

    one = jnp.ones((8, 128), F32)
    in_x, in_r, in_p = {}, {chain: one}, {0: one}
    norm_now = inner[chain, chain]
    for it in range(ITERS):
        image = {i + 1: value for i, value in in_p.items()}
        step = norm_now / bilinear(in_p, image)
        in_x = combine(in_x, step, in_p)
        in_r = combine(in_r, -step, image)
        norm_next = bilinear(in_r, in_r)
        in_p = combine(in_r, norm_next / norm_now, in_p)
        norm_now = norm_next

    for f, h in ((0, 0), (0, 1), (1, 0), (1, 1)):
        lanes = slice(128 * h, 128 * h + 128)
        vectors = {}
        for i in range(chain):
            vectors[i] = basis[i, h, pl.ds(f, BLOCKS, stride=4), :]
            if i < ITERS:
                vectors[chain + i] = basis[i, h, pl.ds(2 + f, BLOCKS, stride=4), :]

        def mixed(total, coefficients):
            for i, value in coefficients.items():
                term = value[f : f + 1, :] * vectors[i]
                total = term if total is None else total + term
            return total

        results = (mixed(None, in_x), mixed(None, in_r), mixed(None, in_p))
        for k in range(BLOCKS):
            at = f * BLOCKS + k
            new_sol_ref[at, :, lanes] = sol_rows[at, :, lanes] + results[0][k : k + 1, :]
            new_res_ref[at, :, lanes] = results[1][k : k + 1, :]
            new_dir_ref[at, :, lanes] = results[2][k : k + 1, :]

    for copy in pending:
        copy.wait_send()


def solution(mesh):
    sizes = (mesh.shape["wide"], mesh.shape["narrow"])
    if sizes[0] == 64:
        stages = (
            ("narrow", ((1, sizes[1]),)),
            ("wide", ((2, 8),)),
            ("wide", ((16, 4), (1, 2))),
        )
    else:
        stages = (("narrow", ((1, sizes[1]),)), ("wide", ((1, sizes[0]),)))
    most = 0
    for _, places in stages:
        size = 1
        for _, count in places:
            size *= count
        most = max(most, size - 1)

    def on_device(node_coords, solution, residual, direction, tile_pairs, tile_counts):
        full_shape = direction.shape
        fields = jax.ShapeDtypeStruct((2 * BLOCKS, 1, NODES), F32)
        vmem = pl.BlockSpec(memory_space=pltpu.VMEM)
        anywhere = pl.BlockSpec(memory_space=pl.ANY)
        dma = pltpu.SemaphoreType.DMA
        outs = pl.pallas_call(
            functools.partial(body, sizes, stages),
            out_shape=(fields, fields, fields),
            in_specs=[anywhere] * 5 + [vmem],
            out_specs=(vmem, vmem, vmem),
            scratch_shapes=[
                pltpu.VMEM((9 * BLOCKS, 8, NODES), F32),
                pltpu.VMEM((ITERS - 1, 9, ROWS, NODES), F32),
                pltpu.VMEM((ITERS, 9, ROWS, NODES), F32),
                pltpu.VMEM((ITERS, 8, ROWS, NODES), F32),
                pltpu.VMEM((SLOTS // 2 + 1, NODES, NODES), BF16),
                pltpu.VMEM((SLOTS // 2 + 1, NODES, NODES), BF16),
                pltpu.VMEM((SLOTS // 2 + 1, NODES, NODES), BF16),
                pltpu.VMEM((SLOTS // 2 + 1, NODES, NODES), BF16),
                pltpu.VMEM((SLOTS // 2 + 1, NODES, NODES), BF16),
                pltpu.VMEM((SLOTS // 2 + 1, NODES, NODES), BF16),
                pltpu.VMEM((SLOTS // 2 + 1, NODES, NODES), BF16),
                pltpu.VMEM((SLOTS // 2 + 1, NODES, NODES), BF16),
                pltpu.VMEM((NODES, NODES), F32),
                pltpu.VMEM((NODES, NODES), F32),
                pltpu.VMEM((9 * BLOCKS, 16, NODES), BF16),
                pltpu.VMEM((512, NODES), F32),
                pltpu.VMEM((TABLE, 512), BF16),
                pltpu.VMEM((ITERS + 1, 2, ROWS, 128), F32),
                pltpu.VMEM((len(stages), 8, 128), F32),
                pltpu.VMEM((len(stages), most, 8, 128), F32),
                pltpu.VMEM((7 * BLOCKS, 1, NODES), F32),
                pltpu.VMEM((2 * BLOCKS, 1, NODES), F32),
                pltpu.SMEM((2, SLOTS), jnp.int32),
                pltpu.VMEM((2, SLOTS), jnp.int32),
                pltpu.VMEM((9 * BLOCKS, NODES, 8), F32),
                dma((6,)),
                dma((8,)),
                dma((8,)),
                dma((ITERS - 1, 8)),
                dma((ITERS - 1, 8)),
                dma((ITERS, 8)),
                dma((ITERS, 8)),
                dma((len(stages), most)),
                dma((len(stages), most)),
            ],
            compiler_params=pltpu.CompilerParams(
                collective_id=0, has_side_effects=True, vmem_limit_bytes=60 * 1024 * 1024
            ),
            cost_estimate=pl.CostEstimate(
                flops=61 * 65536 * 40, bytes_accessed=200000, transcendentals=61 * 65536
            ),
        )(
            node_coords.reshape(3 * BLOCKS, 1, NODES),
            solution.reshape(2 * BLOCKS, 1, NODES),
            residual.reshape(2 * BLOCKS, 1, NODES),
            direction.reshape(2 * BLOCKS, 1, NODES),
            tile_pairs.reshape(2, SLOTS),
            tile_counts,
        )
        return tuple(out.reshape(full_shape) for out in outs)

    fields_spec = P(None, "wide", "narrow", None, None)
    return jax.shard_map(
        on_device,
        mesh=mesh,
        in_specs=(
            fields_spec,
            fields_spec,
            fields_spec,
            fields_spec,
            P("wide", "narrow", None, None),
            P("wide", "narrow"),
        ),
        out_specs=(fields_spec, fields_spec, fields_spec),
        check_vma=False,
    )
```

```python
import functools

import jax
import jax.numpy as jnp
from jax import lax
from jax.experimental import pallas as pl
from jax.experimental.pallas import tpu as pltpu
from jax.sharding import PartitionSpec as P

ITERS = 3
RADIUS = 0.9
MESH = pl.DeviceIdType.MESH
F32 = jnp.float32
BF16 = jnp.bfloat16

BLOCKS = 9
NODES = 256
SLOTS = 61
ROWS = 40
TABLE = 368
GROUP = 3
CHUNK = 16

PHI_SLOPE = 4.0 / RADIUS**5
PHI_CONST = 1.0 / RADIUS**4


def dot_bf16(left, right, transposed):
    dims = (((1,), (1 if transposed else 0,)), ((), ()))
    return lax.dot_general(left, right, dims, preferred_element_type=F32)


def split(value):
    high = value.astype(BF16)
    return high, (value - high.astype(F32)).astype(BF16)


def stage_peers(wide, narrow, stages):
    peers = []
    for axis, places in stages:
        here = wide if axis == "wide" else narrow
        rank, size = 0, 1
        for stride, count in places:
            rank = rank * count + here // stride % count
            size *= count
        group = []
        for step in range(1, size):
            other = (rank + step) % size
            position = here
            left = other
            for stride, count in reversed(places):
                position = position + (left % count - here // stride % count) * stride
                left = left // count
            group.append((position, narrow) if axis == "wide" else (wide, position))
        peers.append(group)
    return peers


def general_body(
    sizes,
    stages,
    coord_ref,
    sol_ref,
    res_ref,
    dir_ref,
    pairs_hbm_ref,
    count_ref,
    new_sol_ref,
    new_res_ref,
    new_dir_ref,
    near0,
    nearq,
    part,
    got,
    khi_even,
    klo_even,
    khi_odd,
    klo_odd,
    thi_even,
    tlo_even,
    thi_odd,
    tlo_odd,
    stage_even,
    stage_odd,
    pieces,
    slot_out,
    onehot,
    basis,
    sums,
    sum_in,
    raw,
    sol_rows,
    pairs_ref,
    pairs_vec_ref,
    cols,
    load_sems,
    near_send,
    near_recv,
    q_send,
    q_recv,
    fold_send,
    fold_recv,
    sum_send,
    sum_recv,
):
    wide_size, narrow_size = sizes
    wide = lax.axis_index("wide")
    narrow = lax.axis_index("narrow")
    neighbours = []
    for d in range(9):
        if d != 4:
            to_wide = (wide + (d // 3 - 1) + wide_size) % wide_size
            to_narrow = (narrow + (d % 3 - 1) + narrow_size) % narrow_size
            neighbours.append((d, (to_wide, to_narrow)))
    peers = stage_peers(wide, narrow, stages)

    loads = [
        pltpu.make_async_copy(source, landing, load_sems.at[at])
        for at, (source, landing) in enumerate(
            (
                (dir_ref, raw.at[pl.ds(0, 2 * BLOCKS)]),
                (res_ref, raw.at[pl.ds(2 * BLOCKS, 2 * BLOCKS)]),
                (coord_ref, raw.at[pl.ds(4 * BLOCKS, 3 * BLOCKS)]),
                (pairs_hbm_ref, pairs_ref),
                (pairs_hbm_ref, pairs_vec_ref),
                (sol_ref, sol_rows),
            )
        )
    ]
    for load in loads:
        load.start()

    barrier = pltpu.get_barrier_semaphore()
    targets = [device for _, device in neighbours] + [device for group in peers for device in group]
    for device in targets:
        pl.semaphore_signal(barrier, inc=1, device_id=device, device_id_type=MESH)

    for load in loads:
        load.wait()
    for k in range(BLOCKS):
        own = 4 * BLOCKS + k
        for c in range(7):
            near0[own, c : c + 1, :] = raw[c * BLOCKS + k]
        near0[own, 7:8, :] = jnp.zeros((1, NODES), F32)

    pl.semaphore_wait(barrier, len(targets))

    pending = []

    def exchange(source, landing, send_sem, recv_sem):
        copies = []
        for at, (d, device) in enumerate(neighbours):
            copy = pltpu.make_async_remote_copy(
                src_ref=source(d),
                dst_ref=landing(8 - d, 7 - at),
                send_sem=send_sem.at[at],
                recv_sem=recv_sem.at[7 - at],
                device_id=device,
                device_id_type=MESH,
            )
            copy.start()
            copies.append(copy)
        pending.extend(copies)

        def wait(at):
            pltpu.make_async_remote_copy(
                src_ref=source(4),
                dst_ref=landing(at + at // 4, at),
                send_sem=send_sem.at[at],
                recv_sem=recv_sem.at[at],
                device_id=neighbours[0][1],
                device_id_type=MESH,
            ).wait_recv()

        return wait

    arrive = exchange(
        lambda d: near0.at[pl.ds(4 * BLOCKS, BLOCKS)],
        lambda d, at: near0.at[pl.ds(d * BLOCKS, BLOCKS)],
        near_send,
        near_recv,
    )

    slot_of = lax.broadcasted_iota(jnp.int32, (64, 512), 0)
    lane_slot = lax.broadcasted_iota(jnp.int32, (64, 512), 1) // 8
    spread = jnp.where(slot_of == lane_slot, 1.0, 0.0).astype(BF16)
    left_id = pairs_vec_ref[0:1, :]
    right_id = pairs_vec_ref[1:2, :]
    live = lax.broadcasted_iota(jnp.int32, (1, SLOTS), 1) < count_ref[0:1, 0:1]
    toward_left = jnp.where(live, left_id, 255)
    toward_right = jnp.where(live & (left_id != right_id), right_id, 255)
    ids = jnp.concatenate([toward_right, toward_left] + [toward_left] * 6, axis=0).astype(F32)
    ids = jnp.concatenate([ids, jnp.full((8, 64 - SLOTS), 255.0, F32)], axis=1)
    wanted = dot_bf16(ids.astype(BF16), spread, False)
    lane = lax.broadcasted_iota(jnp.int32, (8, 512), 1)
    target = jnp.where(lane % 8 < 4, wanted[0:1, :], wanted[1:2, :]).astype(jnp.int32)
    for first in range(0, TABLE, CHUNK):
        row = lax.broadcasted_iota(jnp.int32, (CHUNK, 512), 0) + first
        place = row % ROWS
        block = jnp.where(place < 4 * BLOCKS, row // ROWS * BLOCKS + place // 4, 200)
        match = (block == target[0:1, :]) & (
            row % 4 == lax.broadcasted_iota(jnp.int32, (CHUNK, 512), 1) % 4
        )
        onehot[pl.ds(first, CHUNK), :] = jnp.where(match, 1.0, 0.0).astype(BF16)

    slot_out[pl.ds(8 * SLOTS, 512 - 8 * SLOTS), :] = jnp.zeros((512 - 8 * SLOTS, NODES), F32)
    half = lax.broadcasted_iota(jnp.int32, (8, NODES), 0) < 4

    def put_pieces(j, rows_at, value):
        high = value.astype(BF16).astype(F32)
        low = value - high
        if rows_at == 0:
            rows = jnp.where(half, high, pltpu.roll(low, 4, 0))
        else:
            rows = jnp.where(half, pltpu.roll(high, 4, 0), low)
        pieces[j] = jnp.concatenate([rows, rows], axis=0).astype(BF16)

    for h in range(2):
        for k in range(BLOCKS):
            basis[0, h, 4 * k : 4 * k + 4, :] = near0[4 * BLOCKS + k, 0:4, 128 * h : 128 * h + 128]
        basis[0, h, 4 * BLOCKS : ROWS, :] = jnp.zeros((ROWS - 4 * BLOCKS, 128), F32)

    def prepare(d):
        for k in range(BLOCKS):
            j = d * BLOCKS + k
            value = near0[j]
            put_pieces(j, 0, value)
            cols[j] = jnp.transpose(value)

    def prepare_next(at, carry):
        arrive(at)
        prepare(at + at // 4)
        return carry

    prepare(4)
    lax.fori_loop(0, 8, prepare_next, 0)

    def evaluate(s, refs, stage, at):
        high_ref, low_ref, high_turned, low_turned = refs
        left = cols.at[pairs_ref[0, s]]
        right = near0[pairs_ref[1, s]]
        rights = [jnp.broadcast_to(right[4 + axis : 5 + axis, :], (CHUNK, NODES)) for axis in range(3)]
        for first in range(0, NODES, CHUNK):
            column = left[first : first + CHUNK, :]
            squared = None
            for axis in range(3):
                offset = column[:, 4 + axis : 5 + axis] - rights[axis]
                squared = offset * offset if squared is None else squared + offset * offset
            squared = jnp.minimum(squared, RADIUS * RADIUS)
            distance = squared * lax.rsqrt(jnp.maximum(squared, 1e-36))
            rest = RADIUS - distance
            rest = rest * rest
            rest = rest * rest
            value = rest * (PHI_SLOPE * distance + PHI_CONST)
            high, low = split(value)
            high_ref[at, first : first + CHUNK, :] = high
            low_ref[at, first : first + CHUNK, :] = low
            stage[first : first + CHUNK, :] = value
        for first in range(0, NODES, 128):
            high, low = split(jnp.transpose(stage[first : first + 128, :]))
            high_turned[at, :, first : first + 128] = high
            low_turned[at, :, first : first + 128] = low

    def product(s, refs, at):
        high_ref, low_ref, high_turned, low_turned = refs
        left = pieces[pairs_ref[0, s]]
        right = pieces[pairs_ref[1, s]]
        to_right = dot_bf16(left, high_ref[at], False) + dot_bf16(left, low_ref[at], False)
        to_left = dot_bf16(right, high_turned[at], False) + dot_bf16(right, low_turned[at], False)
        to_right = to_right[0:8]
        to_left = to_left[0:8]
        to_right = to_right + pltpu.roll(to_right, 4, 0)
        to_left = to_left + pltpu.roll(to_left, 4, 0)
        slot_out[pl.ds(pl.multiple_of(s * 8, 8), 8), :] = jnp.where(half, to_right, to_left)

    even = (khi_even, klo_even, thi_even, tlo_even)
    odd = (khi_odd, klo_odd, thi_odd, tlo_odd)

    def evaluate_and_multiply(t, carry):
        before = jnp.maximum(t - 1, 0)
        product(2 * before, even, before)
        evaluate(2 * t, even, stage_even, t)
        product(2 * before + 1, odd, before)
        evaluate(jnp.minimum(2 * t + 1, SLOTS - 1), odd, stage_odd, t)
        return carry

    def products(g, carry):
        for u in range(GROUP):
            at = g * GROUP + u
            product(2 * at, even, at)
            product(2 * at + 1, odd, at)
        return carry

    for it in range(ITERS):
        if it == 0:
            lax.fori_loop(0, SLOTS // 2 + 1, evaluate_and_multiply, 0)
        else:
            lax.fori_loop(0, SLOTS // 2 // GROUP, products, 0)
        product(SLOTS - 1, even, SLOTS // 2)
        high, low = split(slot_out[...])
        table = onehot[...]
        added = dot_bf16(table, high, False) + dot_bf16(table, low, False)
        for d in range(9):
            part[it, d] = added[d * ROWS : (d + 1) * ROWS]
        arrive = exchange(
            lambda d: part.at[it, d],
            lambda d, at: got.at[it, at],
            fold_send.at[it],
            fold_recv.at[it],
        )
        image = part[it, 4]
        for at in range(8):
            arrive(at)
            image = image + got[it, at]
        for h in range(2):
            basis[it + 1, h] = image[:, 128 * h : 128 * h + 128]
        if it + 1 < ITERS:
            nearq[it, 4] = image
            arrive = exchange(
                lambda d: nearq.at[it, 4],
                lambda d, at: nearq.at[it, d],
                q_send.at[it],
                q_recv.at[it],
            )

            def refresh(d):
                for k in range(0, BLOCKS, 2):
                    value = nearq[it, d, 4 * k : 4 * k + 8, :]
                    put_pieces(d * BLOCKS + k, 0, value)
                    if k + 1 < BLOCKS:
                        put_pieces(d * BLOCKS + k + 1, 4, value)

            def refresh_next(at, carry):
                arrive(at)
                refresh(at + at // 4)
                return carry

            refresh(4)
            lax.fori_loop(0, 8, refresh_next, 0)

    lane = lax.broadcasted_iota(jnp.int32, (8, 128), 1)
    forward = lax.broadcasted_iota(jnp.int32, (8, 128), 0) % 4 < 2

    def swapped(value):
        return jnp.where(forward, pltpu.roll(value, 6, 0), pltpu.roll(value, 2, 0))

    tiles = [
        [basis[i, h, g : g + 8, :] for h in range(2) for g in range(0, ROWS, 8)]
        for i in range(ITERS + 1)
    ]
    crossed = [[swapped(tile) for tile in row] for row in tiles]
    places = {}
    gram = jnp.zeros((8, 128), F32)
    for i in range(ITERS + 1):
        for j in range(i, ITERS + 1):
            for kind, other in (("same", tiles), ("cross", crossed)):
                total = None
                for mine, theirs in zip(tiles[i], other[j]):
                    term = mine * theirs
                    total = term if total is None else total + term
                column = jnp.sum(total, axis=1, keepdims=True)
                places[kind, i, j] = len(places)
                gram = jnp.where(lane == places[kind, i, j], column, gram)

    for stage, group_peers in enumerate(peers):
        sums[stage] = gram
        copies = []
        for at, device in enumerate(group_peers):
            copy = pltpu.make_async_remote_copy(
                src_ref=sums.at[stage],
                dst_ref=sum_in.at[stage, at],
                send_sem=sum_send.at[stage, at],
                recv_sem=sum_recv.at[stage, at],
                device_id=device,
                device_id_type=MESH,
            )
            copy.start()
            copies.append(copy)
        pending.extend(copies)
        for at, copy in enumerate(copies):
            copy.wait_recv()
            gram = gram + sum_in[stage, at]
    gram = gram + pltpu.roll(gram, 4, 0)

    def entry(kind, i, j, second):
        value = jnp.broadcast_to(gram[:, places[kind, i, j] : places[kind, i, j] + 1], (8, 128))
        return pltpu.roll(value, 6, 0) if second else value

    chain = ITERS + 1
    inner = {}
    for i in range(chain):
        for j in range(chain):
            inner[i, j] = entry("same", min(i, j), max(i, j), False)
            if i < ITERS and j < ITERS:
                inner[chain + i, chain + j] = entry("same", min(i, j), max(i, j), True)
            if j < ITERS:
                cross = entry("cross", min(i, j), max(i, j), i > j)
                inner[i, chain + j] = cross
                inner[chain + j, i] = cross

    def bilinear(first, second):
        total = None
        for i, a in first.items():
            inside = None
            for j, b in second.items():
                term = b * inner[i, j]
                inside = term if inside is None else inside + term
            inside = a * inside
            total = inside if total is None else total + inside
        return total

    def combine(base, scale, other):
        result = dict(base)
        for i, value in other.items():
            result[i] = result[i] + scale * value if i in result else scale * value
        return result

    one = jnp.ones((8, 128), F32)
    in_x, in_r, in_p = {}, {chain: one}, {0: one}
    norm_now = inner[chain, chain]
    for it in range(ITERS):
        image = {i + 1: value for i, value in in_p.items()}
        step = norm_now / bilinear(in_p, image)
        in_x = combine(in_x, step, in_p)
        in_r = combine(in_r, -step, image)
        norm_next = bilinear(in_r, in_r)
        in_p = combine(in_r, norm_next / norm_now, in_p)
        norm_now = norm_next

    for f, h in ((0, 0), (0, 1), (1, 0), (1, 1)):
        lanes = slice(128 * h, 128 * h + 128)
        vectors = {}
        for i in range(chain):
            vectors[i] = basis[i, h, pl.ds(f, BLOCKS, stride=4), :]
            if i < ITERS:
                vectors[chain + i] = basis[i, h, pl.ds(2 + f, BLOCKS, stride=4), :]

        def mixed(total, coefficients):
            for i, value in coefficients.items():
                term = value[f : f + 1, :] * vectors[i]
                total = term if total is None else total + term
            return total

        results = (mixed(None, in_x), mixed(None, in_r), mixed(None, in_p))
        for k in range(BLOCKS):
            at = f * BLOCKS + k
            new_sol_ref[at, :, lanes] = sol_rows[at, :, lanes] + results[0][k : k + 1, :]
            new_res_ref[at, :, lanes] = results[1][k : k + 1, :]
            new_dir_ref[at, :, lanes] = results[2][k : k + 1, :]

    for copy in pending:
        copy.wait_send()


ENTRIES = 82
PAIRS = ENTRIES // 2
FAST_WIDTH = 768
FAST_TABLE = 48


def fast_body(
    sizes,
    stages,
    coord_ref,
    sol_ref,
    res_ref,
    dir_ref,
    pairs_hbm_ref,
    count_ref,
    new_sol_ref,
    new_res_ref,
    new_dir_ref,
    flag_ref,
    near0,
    nearq,
    khi_even,
    klo_even,
    khi_odd,
    klo_odd,
    pieces,
    slot_out,
    onehot,
    basis,
    sums,
    sum_in,
    raw,
    sol_rows,
    pairs_vec_ref,
    own_columns,
    lists,
    entry_rows,
    entries,
    load_sems,
    entry_sem,
    list_send,
    list_recv,
    near_send,
    near_recv,
    q_send,
    q_recv,
    sum_send,
    sum_recv,
):
    wide_size, narrow_size = sizes
    wide = lax.axis_index("wide")
    narrow = lax.axis_index("narrow")
    neighbours = []
    for d in range(9):
        if d != 4:
            to_wide = (wide + (d // 3 - 1) + wide_size) % wide_size
            to_narrow = (narrow + (d % 3 - 1) + narrow_size) % narrow_size
            neighbours.append((d, (to_wide, to_narrow)))
    peers = stage_peers(wide, narrow, stages)

    loads = [
        pltpu.make_async_copy(source, landing, load_sems.at[at])
        for at, (source, landing) in enumerate(
            (
                (pairs_hbm_ref, pairs_vec_ref),
                (dir_ref, raw.at[pl.ds(0, 2 * BLOCKS)]),
                (res_ref, raw.at[pl.ds(2 * BLOCKS, 2 * BLOCKS)]),
                (coord_ref, raw.at[pl.ds(4 * BLOCKS, 3 * BLOCKS)]),
                (sol_ref, sol_rows),
            )
        )
    ]
    for load in loads:
        load.start()

    barrier = pltpu.get_barrier_semaphore()
    targets = [device for _, device in neighbours] + [device for group in peers for device in group]
    for device in targets:
        pl.semaphore_signal(barrier, inc=1, device_id=device, device_id_type=MESH)

    for load in loads:
        load.wait()
    live = lax.broadcasted_iota(jnp.int32, (2, SLOTS), 1) < count_ref[0:1, 0:1]
    own_list = jnp.where(live, pairs_vec_ref[...], 255).astype(F32)
    own_list = jnp.concatenate([own_list, jnp.full((2, 128 - SLOTS), 255.0, F32)], axis=1)
    lists[4] = jnp.concatenate([own_list, jnp.full((6, 128), 255.0, F32)], axis=0)
    for k in range(BLOCKS):
        own = 4 * BLOCKS + k
        for c in range(7):
            near0[own, c : c + 1, :] = raw[c * BLOCKS + k]
        near0[own, 7:8, :] = jnp.zeros((1, NODES), F32)

    pl.semaphore_wait(barrier, len(targets))

    pending = []

    def exchange(source, landing, send_sem, recv_sem):
        for at, (d, device) in enumerate(neighbours):
            copy = pltpu.make_async_remote_copy(
                src_ref=source,
                dst_ref=landing(8 - d),
                send_sem=send_sem.at[at],
                recv_sem=recv_sem.at[7 - at],
                device_id=device,
                device_id_type=MESH,
            )
            copy.start()
            pending.append(copy)

        def wait(at):
            pltpu.make_async_remote_copy(
                src_ref=source,
                dst_ref=landing(at + at // 4),
                send_sem=send_sem.at[at],
                recv_sem=recv_sem.at[at],
                device_id=neighbours[0][1],
                device_id_type=MESH,
            ).wait_recv()

        return wait

    list_arrive = exchange(lists.at[4], lambda d: lists.at[d], list_send, list_recv)
    near_arrive = exchange(
        near0.at[pl.ds(4 * BLOCKS, BLOCKS)],
        lambda d: near0.at[pl.ds(d * BLOCKS, BLOCKS)],
        near_send,
        near_recv,
    )

    half = lax.broadcasted_iota(jnp.int32, (8, NODES), 0) < 4

    def put_pieces(j, rows_at, value):
        high = value.astype(BF16).astype(F32)
        low = value - high
        if rows_at == 0:
            rows = jnp.where(half, high, pltpu.roll(low, 4, 0))
        else:
            rows = jnp.where(half, pltpu.roll(high, 4, 0), low)
        pieces[j] = jnp.concatenate([rows, rows], axis=0).astype(BF16)

    for h in range(2):
        for k in range(BLOCKS):
            basis[0, h, 4 * k : 4 * k + 4, :] = near0[4 * BLOCKS + k, 0:4, 128 * h : 128 * h + 128]
        basis[0, h, 4 * BLOCKS : ROWS, :] = jnp.zeros((ROWS - 4 * BLOCKS, 128), F32)

    def own_block(k, carry):
        value = near0[4 * BLOCKS + k]
        put_pieces(4 * BLOCKS + k, 0, value)
        turned = jnp.transpose(value)
        for axis in range(3):
            own_columns[k, axis] = jnp.broadcast_to(turned[:, 4 + axis : 5 + axis], (NODES, 128))
        return carry

    lax.fori_loop(0, BLOCKS, own_block, 0)
    tail = 8 * ENTRIES
    slot_out[pl.ds(tail, FAST_WIDTH - tail), :] = jnp.zeros((FAST_WIDTH - tail, NODES), F32)

    for at in range(8):
        list_arrive(at)
    dead_rows = jnp.full((7, 128), 255.0, F32)
    device_row = lax.broadcasted_iota(jnp.int32, (16, 128), 0)
    add_wide = (device_row * 11 >> 5) - 1
    add_narrow = device_row - (add_wide + 1) * 3 - 1

    def here(row):
        ids = jnp.concatenate([lists[d, row : row + 1, :] for d in range(9)] + [dead_rows], axis=0)
        ids = ids.astype(jnp.int32)
        is_live = ids < 200
        ids = jnp.where(is_live, ids, 0)
        device = ids * 7282 >> 16
        within = ids - device * 9
        at_wide = device * 11 >> 5
        at_narrow = device - at_wide * 3 + add_narrow
        at_wide = at_wide + add_wide
        mine = is_live & (at_wide == 1) & (at_narrow == 1)
        return mine, within, at_wide * 27 + at_narrow * 9 + within

    left_mine, left_within, left_here = here(0)
    right_mine, right_within, right_here = here(1)
    right_mine = right_mine & (left_here != right_here)
    wanted_rows = jnp.concatenate(
        [jnp.where(left_mine, 1.0, 0.0), jnp.where(right_mine, 1.0, 0.0)], axis=0
    )
    codes = jnp.concatenate(
        [left_within * 128 + right_here + 1, right_within * 128 + left_here + 1], axis=0
    ).astype(F32)
    before_lane = lax.broadcasted_iota(jnp.int32, (128, 128), 0) < lax.broadcasted_iota(
        jnp.int32, (128, 128), 1
    )
    before_row = lax.broadcasted_iota(jnp.int32, (32, 32), 0) > lax.broadcasted_iota(
        jnp.int32, (32, 32), 1
    )
    wanted_bits = wanted_rows.astype(BF16)
    in_row = dot_bf16(wanted_bits, jnp.where(before_lane, 1.0, 0.0).astype(BF16), False)
    row_total = jnp.broadcast_to(jnp.sum(wanted_rows, axis=1, keepdims=True), (32, 128))
    rank = in_row + dot_bf16(
        jnp.where(before_row, 1.0, 0.0).astype(BF16), row_total.astype(BF16), False
    )
    everything = jnp.sum(row_total, axis=0, keepdims=True)
    overflow = jnp.where(everything > ENTRIES + 0.5, 1.0, 0.0)
    rank = jnp.where(wanted_rows > 0.5, rank, -1.0)
    entry_of = lax.broadcasted_iota(jnp.int32, (128, 128), 0).astype(F32)
    gathered = jnp.zeros((128, 128), F32)
    for row in [*range(9), *range(16, 25)]:
        gathered = gathered + jnp.where(
            entry_of == rank[row : row + 1, :], codes[row : row + 1, :], 0.0
        )
    gathered = jnp.broadcast_to(jnp.sum(gathered, axis=1, keepdims=True), (128, 128))
    code = jnp.transpose(gathered)[0:8, :].astype(jnp.int32)
    filled = code > 0
    code = jnp.maximum(code - 1, 0)
    target = code >> 7
    row_of = lax.broadcasted_iota(jnp.int32, (8, 128), 0)
    entry_rows[...] = jnp.where(row_of == 0, target, code & 127)
    entry_load = pltpu.make_async_copy(entry_rows, entries, entry_sem)
    entry_load.start()

    entry_row = lax.broadcasted_iota(jnp.int32, (128, FAST_WIDTH), 0)
    entry_lane = lax.broadcasted_iota(jnp.int32, (128, FAST_WIDTH), 1) >> 3
    spread = jnp.where(entry_row == entry_lane, 1.0, 0.0).astype(BF16)
    wanted = dot_bf16(jnp.where(filled, target, 200).astype(F32).astype(BF16), spread, False)
    wanted = wanted[0:1, :].astype(jnp.int32)
    for first in range(0, FAST_TABLE, CHUNK):
        row = lax.broadcasted_iota(jnp.int32, (CHUNK, FAST_WIDTH), 0) + first
        lane = lax.broadcasted_iota(jnp.int32, (CHUNK, FAST_WIDTH), 1)
        match = ((row >> 2) == wanted) & ((row & 3) == (lane & 3))
        onehot[first : first + CHUNK, :] = jnp.where(match, 1.0, 0.0).astype(BF16)

    def prepare_next(at, carry):
        near_arrive(at)
        for k in range(BLOCKS):
            j = (at + at // 4) * BLOCKS + k
            put_pieces(j, 0, near0[j])
        return carry

    lax.fori_loop(0, 8, prepare_next, 0)
    entry_load.wait()

    def evaluate(e, refs, at):
        high_ref, low_ref = refs
        block = jnp.clip(entries[0, e], 0, BLOCKS - 1)
        other = near0[jnp.clip(entries[1, e], 0, 9 * BLOCKS - 1)]
        for h in range(2):
            lanes = slice(128 * h, 128 * h + 128)
            others = [
                jnp.broadcast_to(other[4 + axis : 5 + axis, lanes], (CHUNK, 128)) for axis in range(3)
            ]
            for first in range(0, NODES, CHUNK):
                squared = None
                for axis in range(3):
                    offset = own_columns[block, axis, first : first + CHUNK, :] - others[axis]
                    squared = offset * offset if squared is None else squared + offset * offset
                squared = jnp.minimum(squared, RADIUS * RADIUS)
                distance = squared * lax.rsqrt(jnp.maximum(squared, 1e-36))
                rest = RADIUS - distance
                rest = rest * rest
                rest = rest * rest
                high, low = split(rest * (PHI_SLOPE * distance + PHI_CONST))
                high_ref[at, first : first + CHUNK, lanes] = high
                low_ref[at, first : first + CHUNK, lanes] = low

    def product(e, refs, at):
        high_ref, low_ref = refs
        other = pieces[jnp.clip(entries[1, e], 0, 9 * BLOCKS - 1)]
        result = dot_bf16(other, high_ref[at], True) + dot_bf16(other, low_ref[at], True)
        slot_out[pl.ds(pl.multiple_of(e * 8, 8), 8), :] = result[0:8]

    even = (khi_even, klo_even)
    odd = (khi_odd, klo_odd)

    def evaluate_and_multiply(t, carry):
        before = jnp.maximum(t - 1, 0)
        product(2 * before, even, before)
        evaluate(2 * t, even, t)
        product(2 * before + 1, odd, before)
        evaluate(2 * t + 1, odd, t)
        return carry

    group = 4

    def products(g, carry):
        for u in range(group):
            at = g * group + u
            product(2 * at, even, at)
            product(2 * at + 1, odd, at)
        return carry

    for it in range(ITERS):
        if it == 0:
            lax.fori_loop(0, PAIRS, evaluate_and_multiply, 0)
            rest_from = PAIRS - 1
        else:
            lax.fori_loop(0, PAIRS // group, products, 0)
            rest_from = PAIRS // group * group
        for at in range(rest_from, PAIRS):
            product(2 * at, even, at)
            product(2 * at + 1, odd, at)
        high, low = split(slot_out[...])
        table = onehot[...]
        image = dot_bf16(table, high, False) + dot_bf16(table, low, False)
        image = image[0:ROWS]
        for h in range(2):
            basis[it + 1, h] = image[:, 128 * h : 128 * h + 128]
        if it + 1 < ITERS:
            nearq[it, 4] = image
            arrive = exchange(
                nearq.at[it, 4], lambda d: nearq.at[it, d], q_send.at[it], q_recv.at[it]
            )

            def refresh(d):
                for k in range(0, BLOCKS, 2):
                    value = nearq[it, d, 4 * k : 4 * k + 8, :]
                    put_pieces(d * BLOCKS + k, 0, value)
                    if k + 1 < BLOCKS:
                        put_pieces(d * BLOCKS + k + 1, 4, value)

            def refresh_next(at, carry):
                arrive(at)
                refresh(at + at // 4)
                return carry

            refresh(4)
            lax.fori_loop(0, 8, refresh_next, 0)

    lane = lax.broadcasted_iota(jnp.int32, (8, 128), 1)
    forward = lax.broadcasted_iota(jnp.int32, (8, 128), 0) % 4 < 2

    def swapped(value):
        return jnp.where(forward, pltpu.roll(value, 6, 0), pltpu.roll(value, 2, 0))

    tiles = [
        [basis[i, h, g : g + 8, :] for h in range(2) for g in range(0, ROWS, 8)]
        for i in range(ITERS + 1)
    ]
    crossed = [[swapped(tile) for tile in row] for row in tiles]
    places = {}
    gram = jnp.zeros((8, 128), F32)
    for i in range(ITERS + 1):
        for j in range(i, ITERS + 1):
            for kind, other in (("same", tiles), ("cross", crossed)):
                total = None
                for mine, theirs in zip(tiles[i], other[j]):
                    term = mine * theirs
                    total = term if total is None else total + term
                column = jnp.sum(total, axis=1, keepdims=True)
                places[kind, i, j] = len(places)
                gram = jnp.where(lane == places[kind, i, j], column, gram)

    gram = jnp.where(lane == 127, overflow, gram)

    for stage, group_peers in enumerate(peers):
        sums[stage] = gram
        copies = []
        for at, device in enumerate(group_peers):
            copy = pltpu.make_async_remote_copy(
                src_ref=sums.at[stage],
                dst_ref=sum_in.at[stage, at],
                send_sem=sum_send.at[stage, at],
                recv_sem=sum_recv.at[stage, at],
                device_id=device,
                device_id_type=MESH,
            )
            copy.start()
            copies.append(copy)
        pending.extend(copies)
        for at, copy in enumerate(copies):
            copy.wait_recv()
            gram = gram + sum_in[stage, at]
    flag_ref[...] = gram
    gram = gram + pltpu.roll(gram, 4, 0)

    def entry(kind, i, j, second):
        value = jnp.broadcast_to(gram[:, places[kind, i, j] : places[kind, i, j] + 1], (8, 128))
        return pltpu.roll(value, 6, 0) if second else value

    chain = ITERS + 1
    inner = {}
    for i in range(chain):
        for j in range(chain):
            inner[i, j] = entry("same", min(i, j), max(i, j), False)
            if i < ITERS and j < ITERS:
                inner[chain + i, chain + j] = entry("same", min(i, j), max(i, j), True)
            if j < ITERS:
                cross = entry("cross", min(i, j), max(i, j), i > j)
                inner[i, chain + j] = cross
                inner[chain + j, i] = cross

    def bilinear(first, second):
        total = None
        for i, a in first.items():
            inside = None
            for j, b in second.items():
                term = b * inner[i, j]
                inside = term if inside is None else inside + term
            inside = a * inside
            total = inside if total is None else total + inside
        return total

    def combine(base, scale, other):
        result = dict(base)
        for i, value in other.items():
            result[i] = result[i] + scale * value if i in result else scale * value
        return result

    one = jnp.ones((8, 128), F32)
    in_x, in_r, in_p = {}, {chain: one}, {0: one}
    norm_now = inner[chain, chain]
    for it in range(ITERS):
        image = {i + 1: value for i, value in in_p.items()}
        step = norm_now / bilinear(in_p, image)
        in_x = combine(in_x, step, in_p)
        in_r = combine(in_r, -step, image)
        norm_next = bilinear(in_r, in_r)
        in_p = combine(in_r, norm_next / norm_now, in_p)
        norm_now = norm_next

    for f, h in ((0, 0), (0, 1), (1, 0), (1, 1)):
        lanes = slice(128 * h, 128 * h + 128)
        vectors = {}
        for i in range(chain):
            vectors[i] = basis[i, h, pl.ds(f, BLOCKS, stride=4), :]
            if i < ITERS:
                vectors[chain + i] = basis[i, h, pl.ds(2 + f, BLOCKS, stride=4), :]

        def mixed(total, coefficients):
            for i, value in coefficients.items():
                term = value[f : f + 1, :] * vectors[i]
                total = term if total is None else total + term
            return total

        results = (mixed(None, in_x), mixed(None, in_r), mixed(None, in_p))
        for k in range(BLOCKS):
            at = f * BLOCKS + k
            new_sol_ref[at, :, lanes] = sol_rows[at, :, lanes] + results[0][k : k + 1, :]
            new_res_ref[at, :, lanes] = results[1][k : k + 1, :]
            new_dir_ref[at, :, lanes] = results[2][k : k + 1, :]

    for copy in pending:
        copy.wait_send()


def solution(mesh):
    sizes = (mesh.shape["wide"], mesh.shape["narrow"])
    if sizes[0] == 64:
        stages = (
            ("narrow", ((1, sizes[1]),)),
            ("wide", ((2, 8),)),
            ("wide", ((16, 4), (1, 2))),
        )
    else:
        stages = (("narrow", ((1, sizes[1]),)), ("wide", ((1, sizes[0]),)))
    most = 0
    for _, places in stages:
        size = 1
        for _, count in places:
            size *= count
        most = max(most, size - 1)

    def on_device(node_coords, solution, residual, direction, tile_pairs, tile_counts):
        full_shape = direction.shape
        fields = jax.ShapeDtypeStruct((2 * BLOCKS, 1, NODES), F32)
        vmem = pl.BlockSpec(memory_space=pltpu.VMEM)
        anywhere = pl.BlockSpec(memory_space=pl.ANY)
        dma = pltpu.SemaphoreType.DMA
        fast = pl.pallas_call(
            functools.partial(fast_body, sizes, stages),
            out_shape=(fields, fields, fields, jax.ShapeDtypeStruct((8, 128), F32)),
            in_specs=[anywhere] * 5 + [vmem],
            out_specs=(vmem, vmem, vmem, vmem),
            scratch_shapes=[
                pltpu.VMEM((9 * BLOCKS, 8, NODES), F32),
                pltpu.VMEM((ITERS - 1, 9, ROWS, NODES), F32),
                pltpu.VMEM((PAIRS, NODES, NODES), BF16),
                pltpu.VMEM((PAIRS, NODES, NODES), BF16),
                pltpu.VMEM((PAIRS, NODES, NODES), BF16),
                pltpu.VMEM((PAIRS, NODES, NODES), BF16),
                pltpu.VMEM((9 * BLOCKS, 16, NODES), BF16),
                pltpu.VMEM((FAST_WIDTH, NODES), F32),
                pltpu.VMEM((FAST_TABLE, FAST_WIDTH), BF16),
                pltpu.VMEM((ITERS + 1, 2, ROWS, 128), F32),
                pltpu.VMEM((len(stages), 8, 128), F32),
                pltpu.VMEM((len(stages), most, 8, 128), F32),
                pltpu.VMEM((7 * BLOCKS, 1, NODES), F32),
                pltpu.VMEM((2 * BLOCKS, 1, NODES), F32),
                pltpu.VMEM((2, SLOTS), jnp.int32),
                pltpu.VMEM((BLOCKS, 3, NODES, 128), F32),
                pltpu.VMEM((9, 8, 128), F32),
                pltpu.VMEM((8, 128), jnp.int32),
                pltpu.SMEM((8, 128), jnp.int32),
                dma((5,)),
                dma,
                dma((8,)),
                dma((8,)),
                dma((8,)),
                dma((8,)),
                dma((ITERS - 1, 8)),
                dma((ITERS - 1, 8)),
                dma((len(stages), most)),
                dma((len(stages), most)),
            ],
            compiler_params=pltpu.CompilerParams(
                collective_id=0, has_side_effects=True, vmem_limit_bytes=60 * 1024 * 1024
            ),
            cost_estimate=pl.CostEstimate(
                flops=81 * 65536 * 40, bytes_accessed=200000, transcendentals=81 * 65536
            ),
        )
        general = pl.pallas_call(
            functools.partial(general_body, sizes, stages),
            out_shape=(fields, fields, fields),
            in_specs=[anywhere] * 5 + [vmem],
            out_specs=(vmem, vmem, vmem),
            scratch_shapes=[
                pltpu.VMEM((9 * BLOCKS, 8, NODES), F32),
                pltpu.VMEM((ITERS - 1, 9, ROWS, NODES), F32),
                pltpu.VMEM((ITERS, 9, ROWS, NODES), F32),
                pltpu.VMEM((ITERS, 8, ROWS, NODES), F32),
                pltpu.VMEM((SLOTS // 2 + 1, NODES, NODES), BF16),
                pltpu.VMEM((SLOTS // 2 + 1, NODES, NODES), BF16),
                pltpu.VMEM((SLOTS // 2 + 1, NODES, NODES), BF16),
                pltpu.VMEM((SLOTS // 2 + 1, NODES, NODES), BF16),
                pltpu.VMEM((SLOTS // 2 + 1, NODES, NODES), BF16),
                pltpu.VMEM((SLOTS // 2 + 1, NODES, NODES), BF16),
                pltpu.VMEM((SLOTS // 2 + 1, NODES, NODES), BF16),
                pltpu.VMEM((SLOTS // 2 + 1, NODES, NODES), BF16),
                pltpu.VMEM((NODES, NODES), F32),
                pltpu.VMEM((NODES, NODES), F32),
                pltpu.VMEM((9 * BLOCKS, 16, NODES), BF16),
                pltpu.VMEM((512, NODES), F32),
                pltpu.VMEM((TABLE, 512), BF16),
                pltpu.VMEM((ITERS + 1, 2, ROWS, 128), F32),
                pltpu.VMEM((len(stages), 8, 128), F32),
                pltpu.VMEM((len(stages), most, 8, 128), F32),
                pltpu.VMEM((7 * BLOCKS, 1, NODES), F32),
                pltpu.VMEM((2 * BLOCKS, 1, NODES), F32),
                pltpu.SMEM((2, SLOTS), jnp.int32),
                pltpu.VMEM((2, SLOTS), jnp.int32),
                pltpu.VMEM((9 * BLOCKS, NODES, 8), F32),
                dma((6,)),
                dma((8,)),
                dma((8,)),
                dma((ITERS - 1, 8)),
                dma((ITERS - 1, 8)),
                dma((ITERS, 8)),
                dma((ITERS, 8)),
                dma((len(stages), most)),
                dma((len(stages), most)),
            ],
            compiler_params=pltpu.CompilerParams(
                collective_id=1, has_side_effects=True, vmem_limit_bytes=60 * 1024 * 1024
            ),
            cost_estimate=pl.CostEstimate(
                flops=61 * 65536 * 40, bytes_accessed=200000, transcendentals=61 * 65536
            ),
        )
        arguments = (
            node_coords.reshape(3 * BLOCKS, 1, NODES),
            solution.reshape(2 * BLOCKS, 1, NODES),
            residual.reshape(2 * BLOCKS, 1, NODES),
            direction.reshape(2 * BLOCKS, 1, NODES),
            tile_pairs.reshape(2, SLOTS),
            tile_counts,
        )
        *outs, flags = fast(*arguments)
        outs = lax.cond(
            flags[0, 127] > 0.5, lambda *a: tuple(general(*a[3:])), lambda *a: a[:3], *outs, *arguments
        )
        return tuple(out.reshape(full_shape) for out in outs)

    fields_spec = P(None, "wide", "narrow", None, None)
    return jax.shard_map(
        on_device,
        mesh=mesh,
        in_specs=(
            fields_spec,
            fields_spec,
            fields_spec,
            fields_spec,
            P("wide", "narrow", None, None),
            P("wide", "narrow"),
        ),
        out_specs=(fields_spec, fields_spec, fields_spec),
        check_vma=False,
    )
```

```python
import functools

import jax
import jax.numpy as jnp
from jax import lax
from jax.experimental import pallas as pl
from jax.experimental.pallas import tpu as pltpu
from jax.sharding import PartitionSpec as P

ITERS = 3
RADIUS = 0.9
MESH = pl.DeviceIdType.MESH
F32 = jnp.float32
BF16 = jnp.bfloat16

BLOCKS = 9
NODES = 256
SLOTS = 61
ROWS = 40
TABLE = 368
GROUP = 3
CHUNK = 16

PHI_SLOPE = 4.0 / RADIUS**5
PHI_CONST = 1.0 / RADIUS**4


def dot_bf16(left, right, transposed):
    dims = (((1,), (1 if transposed else 0,)), ((), ()))
    return lax.dot_general(left, right, dims, preferred_element_type=F32)


def split(value):
    high = value.astype(BF16)
    return high, (value - high.astype(F32)).astype(BF16)


def stage_peers(wide, narrow, stages):
    peers = []
    for axis, places in stages:
        here = wide if axis == "wide" else narrow
        rank, size = 0, 1
        for stride, count in places:
            rank = rank * count + here // stride % count
            size *= count
        group = []
        for step in range(1, size):
            other = (rank + step) % size
            position = here
            left = other
            for stride, count in reversed(places):
                position = position + (left % count - here // stride % count) * stride
                left = left // count
            group.append((position, narrow) if axis == "wide" else (wide, position))
        peers.append(group)
    return peers


def general_body(
    sizes,
    stages,
    coord_ref,
    sol_ref,
    res_ref,
    dir_ref,
    pairs_hbm_ref,
    count_ref,
    new_sol_ref,
    new_res_ref,
    new_dir_ref,
    near0,
    nearq,
    part,
    got,
    khi_even,
    klo_even,
    khi_odd,
    klo_odd,
    thi_even,
    tlo_even,
    thi_odd,
    tlo_odd,
    stage_even,
    stage_odd,
    pieces,
    slot_out,
    onehot,
    basis,
    sums,
    sum_in,
    raw,
    sol_rows,
    pairs_ref,
    pairs_vec_ref,
    cols,
    load_sems,
    near_send,
    near_recv,
    q_send,
    q_recv,
    fold_send,
    fold_recv,
    sum_send,
    sum_recv,
):
    wide_size, narrow_size = sizes
    wide = lax.axis_index("wide")
    narrow = lax.axis_index("narrow")
    neighbours = []
    for d in range(9):
        if d != 4:
            to_wide = (wide + (d // 3 - 1) + wide_size) % wide_size
            to_narrow = (narrow + (d % 3 - 1) + narrow_size) % narrow_size
            neighbours.append((d, (to_wide, to_narrow)))
    peers = stage_peers(wide, narrow, stages)

    loads = [
        pltpu.make_async_copy(source, landing, load_sems.at[at])
        for at, (source, landing) in enumerate(
            (
                (dir_ref, raw.at[pl.ds(0, 2 * BLOCKS)]),
                (res_ref, raw.at[pl.ds(2 * BLOCKS, 2 * BLOCKS)]),
                (coord_ref, raw.at[pl.ds(4 * BLOCKS, 3 * BLOCKS)]),
                (pairs_hbm_ref, pairs_ref),
                (pairs_hbm_ref, pairs_vec_ref),
                (sol_ref, sol_rows),
            )
        )
    ]
    for load in loads:
        load.start()

    barrier = pltpu.get_barrier_semaphore()
    targets = [device for _, device in neighbours] + [device for group in peers for device in group]
    for device in targets:
        pl.semaphore_signal(barrier, inc=1, device_id=device, device_id_type=MESH)

    for load in loads:
        load.wait()
    for k in range(BLOCKS):
        own = 4 * BLOCKS + k
        for c in range(7):
            near0[own, c : c + 1, :] = raw[c * BLOCKS + k]
        near0[own, 7:8, :] = jnp.zeros((1, NODES), F32)

    pl.semaphore_wait(barrier, len(targets))

    pending = []

    def exchange(source, landing, send_sem, recv_sem):
        copies = []
        for at, (d, device) in enumerate(neighbours):
            copy = pltpu.make_async_remote_copy(
                src_ref=source(d),
                dst_ref=landing(8 - d, 7 - at),
                send_sem=send_sem.at[at],
                recv_sem=recv_sem.at[7 - at],
                device_id=device,
                device_id_type=MESH,
            )
            copy.start()
            copies.append(copy)
        pending.extend(copies)

        def wait(at):
            pltpu.make_async_remote_copy(
                src_ref=source(4),
                dst_ref=landing(at + at // 4, at),
                send_sem=send_sem.at[at],
                recv_sem=recv_sem.at[at],
                device_id=neighbours[0][1],
                device_id_type=MESH,
            ).wait_recv()

        return wait

    arrive = exchange(
        lambda d: near0.at[pl.ds(4 * BLOCKS, BLOCKS)],
        lambda d, at: near0.at[pl.ds(d * BLOCKS, BLOCKS)],
        near_send,
        near_recv,
    )

    slot_of = lax.broadcasted_iota(jnp.int32, (64, 512), 0)
    lane_slot = lax.broadcasted_iota(jnp.int32, (64, 512), 1) // 8
    spread = jnp.where(slot_of == lane_slot, 1.0, 0.0).astype(BF16)
    left_id = pairs_vec_ref[0:1, :]
    right_id = pairs_vec_ref[1:2, :]
    live = lax.broadcasted_iota(jnp.int32, (1, SLOTS), 1) < count_ref[0:1, 0:1]
    toward_left = jnp.where(live, left_id, 255)
    toward_right = jnp.where(live & (left_id != right_id), right_id, 255)
    ids = jnp.concatenate([toward_right, toward_left] + [toward_left] * 6, axis=0).astype(F32)
    ids = jnp.concatenate([ids, jnp.full((8, 64 - SLOTS), 255.0, F32)], axis=1)
    wanted = dot_bf16(ids.astype(BF16), spread, False)
    lane = lax.broadcasted_iota(jnp.int32, (8, 512), 1)
    target = jnp.where(lane % 8 < 4, wanted[0:1, :], wanted[1:2, :]).astype(jnp.int32)
    for first in range(0, TABLE, CHUNK):
        row = lax.broadcasted_iota(jnp.int32, (CHUNK, 512), 0) + first
        place = row % ROWS
        block = jnp.where(place < 4 * BLOCKS, row // ROWS * BLOCKS + place // 4, 200)
        match = (block == target[0:1, :]) & (
            row % 4 == lax.broadcasted_iota(jnp.int32, (CHUNK, 512), 1) % 4
        )
        onehot[pl.ds(first, CHUNK), :] = jnp.where(match, 1.0, 0.0).astype(BF16)

    slot_out[pl.ds(8 * SLOTS, 512 - 8 * SLOTS), :] = jnp.zeros((512 - 8 * SLOTS, NODES), F32)
    half = lax.broadcasted_iota(jnp.int32, (8, NODES), 0) < 4

    def put_pieces(j, rows_at, value):
        high = value.astype(BF16).astype(F32)
        low = value - high
        if rows_at == 0:
            rows = jnp.where(half, high, pltpu.roll(low, 4, 0))
        else:
            rows = jnp.where(half, pltpu.roll(high, 4, 0), low)
        pieces[j] = jnp.concatenate([rows, rows], axis=0).astype(BF16)

    for h in range(2):
        for k in range(BLOCKS):
            basis[0, h, 4 * k : 4 * k + 4, :] = near0[4 * BLOCKS + k, 0:4, 128 * h : 128 * h + 128]
        basis[0, h, 4 * BLOCKS : ROWS, :] = jnp.zeros((ROWS - 4 * BLOCKS, 128), F32)

    def prepare(d):
        for k in range(BLOCKS):
            j = d * BLOCKS + k
            value = near0[j]
            put_pieces(j, 0, value)
            cols[j] = jnp.transpose(value)

    def prepare_next(at, carry):
        arrive(at)
        prepare(at + at // 4)
        return carry

    prepare(4)
    lax.fori_loop(0, 8, prepare_next, 0)

    def evaluate(s, refs, stage, at):
        high_ref, low_ref, high_turned, low_turned = refs
        left = cols.at[pairs_ref[0, s]]
        right = near0[pairs_ref[1, s]]
        rights = [jnp.broadcast_to(right[4 + axis : 5 + axis, :], (CHUNK, NODES)) for axis in range(3)]
        for first in range(0, NODES, CHUNK):
            column = left[first : first + CHUNK, :]
            squared = None
            for axis in range(3):
                offset = column[:, 4 + axis : 5 + axis] - rights[axis]
                squared = offset * offset if squared is None else squared + offset * offset
            squared = jnp.minimum(squared, RADIUS * RADIUS)
            distance = squared * lax.rsqrt(jnp.maximum(squared, 1e-36))
            rest = RADIUS - distance
            rest = rest * rest
            rest = rest * rest
            value = rest * (PHI_SLOPE * distance + PHI_CONST)
            high, low = split(value)
            high_ref[at, first : first + CHUNK, :] = high
            low_ref[at, first : first + CHUNK, :] = low
            stage[first : first + CHUNK, :] = value
        for first in range(0, NODES, 128):
            high, low = split(jnp.transpose(stage[first : first + 128, :]))
            high_turned[at, :, first : first + 128] = high
            low_turned[at, :, first : first + 128] = low

    def product(s, refs, at):
        high_ref, low_ref, high_turned, low_turned = refs
        left = pieces[pairs_ref[0, s]]
        right = pieces[pairs_ref[1, s]]
        to_right = dot_bf16(left, high_ref[at], False) + dot_bf16(left, low_ref[at], False)
        to_left = dot_bf16(right, high_turned[at], False) + dot_bf16(right, low_turned[at], False)
        to_right = to_right[0:8]
        to_left = to_left[0:8]
        to_right = to_right + pltpu.roll(to_right, 4, 0)
        to_left = to_left + pltpu.roll(to_left, 4, 0)
        slot_out[pl.ds(pl.multiple_of(s * 8, 8), 8), :] = jnp.where(half, to_right, to_left)

    even = (khi_even, klo_even, thi_even, tlo_even)
    odd = (khi_odd, klo_odd, thi_odd, tlo_odd)

    def evaluate_and_multiply(t, carry):
        before = jnp.maximum(t - 1, 0)
        product(2 * before, even, before)
        evaluate(2 * t, even, stage_even, t)
        product(2 * before + 1, odd, before)
        evaluate(jnp.minimum(2 * t + 1, SLOTS - 1), odd, stage_odd, t)
        return carry

    def products(g, carry):
        for u in range(GROUP):
            at = g * GROUP + u
            product(2 * at, even, at)
            product(2 * at + 1, odd, at)
        return carry

    for it in range(ITERS):
        if it == 0:
            lax.fori_loop(0, SLOTS // 2 + 1, evaluate_and_multiply, 0)
        else:
            lax.fori_loop(0, SLOTS // 2 // GROUP, products, 0)
        product(SLOTS - 1, even, SLOTS // 2)
        high, low = split(slot_out[...])
        table = onehot[...]
        added = dot_bf16(table, high, False) + dot_bf16(table, low, False)
        for d in range(9):
            part[it, d] = added[d * ROWS : (d + 1) * ROWS]
        arrive = exchange(
            lambda d: part.at[it, d],
            lambda d, at: got.at[it, at],
            fold_send.at[it],
            fold_recv.at[it],
        )
        image = part[it, 4]
        for at in range(8):
            arrive(at)
            image = image + got[it, at]
        for h in range(2):
            basis[it + 1, h] = image[:, 128 * h : 128 * h + 128]
        if it + 1 < ITERS:
            nearq[it, 4] = image
            arrive = exchange(
                lambda d: nearq.at[it, 4],
                lambda d, at: nearq.at[it, d],
                q_send.at[it],
                q_recv.at[it],
            )

            def refresh(d):
                for k in range(0, BLOCKS, 2):
                    value = nearq[it, d, 4 * k : 4 * k + 8, :]
                    put_pieces(d * BLOCKS + k, 0, value)
                    if k + 1 < BLOCKS:
                        put_pieces(d * BLOCKS + k + 1, 4, value)

            def refresh_next(at, carry):
                arrive(at)
                refresh(at + at // 4)
                return carry

            refresh(4)
            lax.fori_loop(0, 8, refresh_next, 0)

    lane = lax.broadcasted_iota(jnp.int32, (8, 128), 1)
    forward = lax.broadcasted_iota(jnp.int32, (8, 128), 0) % 4 < 2

    def swapped(value):
        return jnp.where(forward, pltpu.roll(value, 6, 0), pltpu.roll(value, 2, 0))

    tiles = [
        [basis[i, h, g : g + 8, :] for h in range(2) for g in range(0, ROWS, 8)]
        for i in range(ITERS + 1)
    ]
    crossed = [[swapped(tile) for tile in row] for row in tiles]
    places = {}
    gram = jnp.zeros((8, 128), F32)
    for i in range(ITERS + 1):
        for j in range(i, ITERS + 1):
            for kind, other in (("same", tiles), ("cross", crossed)):
                total = None
                for mine, theirs in zip(tiles[i], other[j]):
                    term = mine * theirs
                    total = term if total is None else total + term
                column = jnp.sum(total, axis=1, keepdims=True)
                places[kind, i, j] = len(places)
                gram = jnp.where(lane == places[kind, i, j], column, gram)

    for stage, group_peers in enumerate(peers):
        sums[stage] = gram
        copies = []
        for at, device in enumerate(group_peers):
            copy = pltpu.make_async_remote_copy(
                src_ref=sums.at[stage],
                dst_ref=sum_in.at[stage, at],
                send_sem=sum_send.at[stage, at],
                recv_sem=sum_recv.at[stage, at],
                device_id=device,
                device_id_type=MESH,
            )
            copy.start()
            copies.append(copy)
        pending.extend(copies)
        for at, copy in enumerate(copies):
            copy.wait_recv()
            gram = gram + sum_in[stage, at]
    gram = gram + pltpu.roll(gram, 4, 0)

    def entry(kind, i, j, second):
        value = jnp.broadcast_to(gram[:, places[kind, i, j] : places[kind, i, j] + 1], (8, 128))
        return pltpu.roll(value, 6, 0) if second else value

    chain = ITERS + 1
    inner = {}
    for i in range(chain):
        for j in range(chain):
            inner[i, j] = entry("same", min(i, j), max(i, j), False)
            if i < ITERS and j < ITERS:
                inner[chain + i, chain + j] = entry("same", min(i, j), max(i, j), True)
            if j < ITERS:
                cross = entry("cross", min(i, j), max(i, j), i > j)
                inner[i, chain + j] = cross
                inner[chain + j, i] = cross

    def bilinear(first, second):
        total = None
        for i, a in first.items():
            inside = None
            for j, b in second.items():
                term = b * inner[i, j]
                inside = term if inside is None else inside + term
            inside = a * inside
            total = inside if total is None else total + inside
        return total

    def combine(base, scale, other):
        result = dict(base)
        for i, value in other.items():
            result[i] = result[i] + scale * value if i in result else scale * value
        return result

    one = jnp.ones((8, 128), F32)
    in_x, in_r, in_p = {}, {chain: one}, {0: one}
    norm_now = inner[chain, chain]
    for it in range(ITERS):
        image = {i + 1: value for i, value in in_p.items()}
        step = norm_now / bilinear(in_p, image)
        in_x = combine(in_x, step, in_p)
        in_r = combine(in_r, -step, image)
        norm_next = bilinear(in_r, in_r)
        in_p = combine(in_r, norm_next / norm_now, in_p)
        norm_now = norm_next

    for f, h in ((0, 0), (0, 1), (1, 0), (1, 1)):
        lanes = slice(128 * h, 128 * h + 128)
        vectors = {}
        for i in range(chain):
            vectors[i] = basis[i, h, pl.ds(f, BLOCKS, stride=4), :]
            if i < ITERS:
                vectors[chain + i] = basis[i, h, pl.ds(2 + f, BLOCKS, stride=4), :]

        def mixed(total, coefficients):
            for i, value in coefficients.items():
                term = value[f : f + 1, :] * vectors[i]
                total = term if total is None else total + term
            return total

        results = (mixed(None, in_x), mixed(None, in_r), mixed(None, in_p))
        for k in range(BLOCKS):
            at = f * BLOCKS + k
            new_sol_ref[at, :, lanes] = sol_rows[at, :, lanes] + results[0][k : k + 1, :]
            new_res_ref[at, :, lanes] = results[1][k : k + 1, :]
            new_dir_ref[at, :, lanes] = results[2][k : k + 1, :]

    for copy in pending:
        copy.wait_send()


ENTRIES = 84
FOURS = ENTRIES // 4
FAST_WIDTH = 768
FAST_TABLE = 64
P_ROWS = 24


def fast_body(
    sizes,
    stages,
    coord_ref,
    sol_ref,
    res_ref,
    dir_ref,
    pairs_hbm_ref,
    count_ref,
    new_sol_ref,
    new_res_ref,
    new_dir_ref,
    flag_ref,
    near0,
    nearq,
    nearp,
    khi_0,
    khi_1,
    khi_2,
    khi_3,
    klo_0,
    klo_1,
    klo_2,
    klo_3,
    pieces,
    slot_out,
    onehot,
    basis,
    sums,
    sum_in,
    raw,
    sol_rows,
    pairs_vec_ref,
    own_columns,
    lists,
    entry_rows,
    entries,
    load_sems,
    entry_sem,
    list_send,
    list_recv,
    near_send,
    near_recv,
    q_send,
    q_recv,
    sum_send,
    sum_recv,
):
    wide_size, narrow_size = sizes
    wide = lax.axis_index("wide")
    narrow = lax.axis_index("narrow")
    neighbours = []
    for d in range(9):
        if d != 4:
            to_wide = (wide + (d // 3 - 1) + wide_size) % wide_size
            to_narrow = (narrow + (d % 3 - 1) + narrow_size) % narrow_size
            neighbours.append((d, (to_wide, to_narrow)))
    peers = stage_peers(wide, narrow, stages)

    loads = [
        pltpu.make_async_copy(source, landing, load_sems.at[at])
        for at, (source, landing) in enumerate(
            (
                (pairs_hbm_ref, pairs_vec_ref),
                (dir_ref, raw.at[pl.ds(0, 2 * BLOCKS)]),
                (res_ref, raw.at[pl.ds(2 * BLOCKS, 2 * BLOCKS)]),
                (coord_ref, raw.at[pl.ds(4 * BLOCKS, 3 * BLOCKS)]),
                (sol_ref, sol_rows),
            )
        )
    ]
    for load in loads:
        load.start()

    barrier = pltpu.get_barrier_semaphore()
    targets = [device for _, device in neighbours] + [device for group in peers for device in group]
    for device in targets:
        pl.semaphore_signal(barrier, inc=1, device_id=device, device_id_type=MESH)

    for load in loads:
        load.wait()
    live = lax.broadcasted_iota(jnp.int32, (2, SLOTS), 1) < count_ref[0:1, 0:1]
    own_list = jnp.where(live, pairs_vec_ref[...], 255).astype(F32)
    own_list = jnp.concatenate([own_list, jnp.full((2, 128 - SLOTS), 255.0, F32)], axis=1)
    lists[4] = jnp.concatenate([own_list, jnp.full((6, 128), 255.0, F32)], axis=0)
    for k in range(BLOCKS):
        own = 4 * BLOCKS + k
        for c in range(7):
            near0[own, c : c + 1, :] = raw[c * BLOCKS + k]
        near0[own, 7:8, :] = jnp.zeros((1, NODES), F32)

    pl.semaphore_wait(barrier, len(targets))

    pending = []

    def exchange(source, landing, send_sem, recv_sem):
        for at, (d, device) in enumerate(neighbours):
            copy = pltpu.make_async_remote_copy(
                src_ref=source,
                dst_ref=landing(8 - d),
                send_sem=send_sem.at[at],
                recv_sem=recv_sem.at[7 - at],
                device_id=device,
                device_id_type=MESH,
            )
            copy.start()
            pending.append(copy)

        def wait(at):
            pltpu.make_async_remote_copy(
                src_ref=source,
                dst_ref=landing(at + at // 4),
                send_sem=send_sem.at[at],
                recv_sem=recv_sem.at[at],
                device_id=neighbours[0][1],
                device_id_type=MESH,
            ).wait_recv()

        return wait

    list_arrive = exchange(lists.at[4], lambda d: lists.at[d], list_send, list_recv)
    near_arrive = exchange(
        near0.at[pl.ds(4 * BLOCKS, BLOCKS)],
        lambda d: near0.at[pl.ds(d * BLOCKS, BLOCKS)],
        near_send,
        near_recv,
    )

    half = lax.broadcasted_iota(jnp.int32, (8, NODES), 0) < 4

    def put_pieces(j, rows_at, value):
        high = value.astype(BF16).astype(F32)
        low = value - high
        if rows_at == 0:
            rows = jnp.where(half, high, pltpu.roll(low, 4, 0))
        else:
            rows = jnp.where(half, pltpu.roll(high, 4, 0), low)
        pieces[j] = jnp.concatenate([rows, rows], axis=0).astype(BF16)

    for h in range(2):
        for k in range(BLOCKS):
            basis[0, h, 4 * k : 4 * k + 4, :] = near0[4 * BLOCKS + k, 0:4, 128 * h : 128 * h + 128]
        basis[0, h, 4 * BLOCKS : ROWS, :] = jnp.zeros((ROWS - 4 * BLOCKS, 128), F32)

    def own_block(k, carry):
        value = near0[4 * BLOCKS + k]
        put_pieces(4 * BLOCKS + k, 0, value)
        turned = jnp.transpose(value)
        for axis in range(3):
            own_columns[k, axis] = jnp.broadcast_to(turned[:, 4 + axis : 5 + axis], (NODES, 128))
        return carry

    lax.fori_loop(0, BLOCKS, own_block, 0)
    tail = 8 * ENTRIES
    slot_out[pl.ds(tail, FAST_WIDTH - tail), :] = jnp.zeros((FAST_WIDTH - tail, NODES), F32)

    for at in range(8):
        list_arrive(at)
    dead_rows = jnp.full((7, 128), 255.0, F32)
    device_row = lax.broadcasted_iota(jnp.int32, (16, 128), 0)
    add_wide = (device_row * 11 >> 5) - 1
    add_narrow = device_row - (add_wide + 1) * 3 - 1

    def here(row):
        ids = jnp.concatenate([lists[d, row : row + 1, :] for d in range(9)] + [dead_rows], axis=0)
        ids = ids.astype(jnp.int32)
        is_live = ids < 200
        ids = jnp.where(is_live, ids, 0)
        device = ids * 7282 >> 16
        within = ids - device * 9
        at_wide = device * 11 >> 5
        at_narrow = device - at_wide * 3 + add_narrow
        at_wide = at_wide + add_wide
        mine = is_live & (at_wide == 1) & (at_narrow == 1)
        return mine, within, at_wide * 27 + at_narrow * 9 + within

    left_mine, left_within, left_here = here(0)
    right_mine, right_within, right_here = here(1)
    right_mine = right_mine & (left_here != right_here)
    wanted_rows = jnp.concatenate(
        [jnp.where(left_mine, 1.0, 0.0), jnp.where(right_mine, 1.0, 0.0)], axis=0
    )
    codes = jnp.concatenate(
        [left_within * 128 + right_here + 1, right_within * 128 + left_here + 1], axis=0
    ).astype(F32)
    before_lane = lax.broadcasted_iota(jnp.int32, (128, 128), 0) < lax.broadcasted_iota(
        jnp.int32, (128, 128), 1
    )
    before_row = lax.broadcasted_iota(jnp.int32, (32, 32), 0) > lax.broadcasted_iota(
        jnp.int32, (32, 32), 1
    )
    wanted_bits = wanted_rows.astype(BF16)
    in_row = dot_bf16(wanted_bits, jnp.where(before_lane, 1.0, 0.0).astype(BF16), False)
    row_total = jnp.broadcast_to(jnp.sum(wanted_rows, axis=1, keepdims=True), (32, 128))
    rank = in_row + dot_bf16(
        jnp.where(before_row, 1.0, 0.0).astype(BF16), row_total.astype(BF16), False
    )
    everything = jnp.sum(row_total, axis=0, keepdims=True)
    overflow = jnp.where(everything > ENTRIES + 0.5, 1.0, 0.0)
    rank = jnp.where(wanted_rows > 0.5, rank, -1.0)
    entry_of = lax.broadcasted_iota(jnp.int32, (128, 128), 0).astype(F32)
    gathered = jnp.zeros((128, 128), F32)
    for row in [*range(9), *range(16, 25)]:
        gathered = gathered + jnp.where(
            entry_of == rank[row : row + 1, :], codes[row : row + 1, :], 0.0
        )
    gathered = jnp.broadcast_to(jnp.sum(gathered, axis=1, keepdims=True), (128, 128))
    code = jnp.transpose(gathered)[0:8, :].astype(jnp.int32)
    filled = code > 0
    code = jnp.maximum(code - 1, 0)
    target = code >> 7
    row_of = lax.broadcasted_iota(jnp.int32, (8, 128), 0)
    entry_rows[...] = jnp.where(row_of == 0, target, code & 127)
    entry_load = pltpu.make_async_copy(entry_rows, entries, entry_sem)
    entry_load.start()

    entry_row = lax.broadcasted_iota(jnp.int32, (128, FAST_WIDTH), 0)
    entry_lane = lax.broadcasted_iota(jnp.int32, (128, FAST_WIDTH), 1) >> 3
    spread = jnp.where(entry_row == entry_lane, 1.0, 0.0).astype(BF16)
    wanted = dot_bf16(jnp.where(filled, target, 200).astype(F32).astype(BF16), spread, False)
    wanted = wanted[0:1, :].astype(jnp.int32)
    for first in range(0, FAST_TABLE, CHUNK):
        row = lax.broadcasted_iota(jnp.int32, (CHUNK, FAST_WIDTH), 0) + first
        lane = lax.broadcasted_iota(jnp.int32, (CHUNK, FAST_WIDTH), 1)
        second = row - ROWS
        block = jnp.where(row < ROWS, row >> 2, second >> 1)
        vector = jnp.where(row < ROWS, row & 3, second & 1)
        match = (block == wanted) & (vector == (lane & 3))
        onehot[first : first + CHUNK, :] = jnp.where(match, 1.0, 0.0).astype(BF16)

    def prepare_next(at, carry):
        near_arrive(at)
        for k in range(BLOCKS):
            j = (at + at // 4) * BLOCKS + k
            put_pieces(j, 0, near0[j])
        return carry

    lax.fori_loop(0, 8, prepare_next, 0)
    entry_load.wait()

    def evaluate(e, refs, at):
        high_ref, low_ref = refs
        block = jnp.clip(entries[0, e], 0, BLOCKS - 1)
        other = near0[jnp.clip(entries[1, e], 0, 9 * BLOCKS - 1)]
        for h in range(2):
            lanes = slice(128 * h, 128 * h + 128)
            others = [
                jnp.broadcast_to(other[4 + axis : 5 + axis, lanes], (CHUNK, 128)) for axis in range(3)
            ]
            for first in range(0, NODES, CHUNK):
                squared = None
                for axis in range(3):
                    offset = own_columns[block, axis, first : first + CHUNK, :] - others[axis]
                    squared = offset * offset if squared is None else squared + offset * offset
                squared = jnp.minimum(squared, RADIUS * RADIUS)
                distance = squared * lax.rsqrt(jnp.maximum(squared, 1e-36))
                rest = RADIUS - distance
                rest = rest * rest
                rest = rest * rest
                high, low = split(rest * (PHI_SLOPE * distance + PHI_CONST))
                high_ref[at, first : first + CHUNK, lanes] = high
                low_ref[at, first : first + CHUNK, lanes] = low

    def product(e, refs, at):
        high_ref, low_ref = refs
        other = pieces[jnp.clip(entries[1, e], 0, 9 * BLOCKS - 1)]
        result = dot_bf16(other, high_ref[at], True) + dot_bf16(other, low_ref[at], True)
        slot_out[pl.ds(pl.multiple_of(e * 8, 8), 8), :] = result[0:8]

    tiles_of = ((khi_0, klo_0), (khi_1, klo_1), (khi_2, klo_2), (khi_3, klo_3))

    def evaluate_and_multiply(t, carry):
        before = jnp.maximum(t - 1, 0)
        for u, refs in enumerate(tiles_of):
            product(4 * before + u, refs, before)
            evaluate(4 * t + u, refs, t)
        return carry

    group = 5

    def products(g, carry):
        for at in range(group):
            for u, refs in enumerate(tiles_of):
                product(4 * (g * group + at) + u, refs, g * group + at)
        return carry

    for it in range(ITERS):
        if it == 0:
            lax.fori_loop(0, FOURS, evaluate_and_multiply, 0)
        else:
            lax.fori_loop(0, FOURS // group, products, 0)
        for u, refs in enumerate(tiles_of):
            product(4 * (FOURS - 1) + u, refs, FOURS - 1)
        high, low = split(slot_out[...])
        table = onehot[...]
        image = dot_bf16(table, high, False) + dot_bf16(table, low, False)
        for h in range(2):
            basis[it + 1, h] = image[0:ROWS, 128 * h : 128 * h + 128]
        if it == 0:
            nearq[4] = image[0:ROWS]
            arrive = exchange(nearq.at[4], lambda d: nearq.at[d], q_send.at[it], q_recv.at[it])

            def refresh(d):
                for k in range(0, BLOCKS, 2):
                    value = nearq[d, 4 * k : 4 * k + 8, :]
                    put_pieces(d * BLOCKS + k, 0, value)
                    if k + 1 < BLOCKS:
                        put_pieces(d * BLOCKS + k + 1, 4, value)

            def refresh_next(at, carry):
                arrive(at)
                refresh(at + at // 4)
                return carry

            refresh(4)
            lax.fori_loop(0, 8, refresh_next, 0)
        elif it + 1 < ITERS:
            nearp[4] = image[ROWS : ROWS + P_ROWS]
            arrive_p = exchange(nearp.at[4], lambda d: nearp.at[d], q_send.at[it], q_recv.at[it])

            def refresh_p(d):
                for k in range(BLOCKS):
                    value = nearp[d, k // 4 * 8 : k // 4 * 8 + 8, :]
                    if k % 4:
                        value = pltpu.roll(value, 8 - k % 4 * 2, 0)
                    put_pieces(d * BLOCKS + k, 0, value)

            def refresh_next_p(at, carry):
                arrive_p(at)
                refresh_p(at + at // 4)
                return carry

            refresh_p(4)
            lax.fori_loop(0, 8, refresh_next_p, 0)

    lane = lax.broadcasted_iota(jnp.int32, (8, 128), 1)
    forward = lax.broadcasted_iota(jnp.int32, (8, 128), 0) % 4 < 2

    def swapped(value):
        return jnp.where(forward, pltpu.roll(value, 6, 0), pltpu.roll(value, 2, 0))

    tiles = [
        [basis[i, h, g : g + 8, :] for h in range(2) for g in range(0, ROWS, 8)]
        for i in range(ITERS + 1)
    ]
    crossed = [[swapped(tile) for tile in row] for row in tiles]
    places = {}
    gram = jnp.zeros((8, 128), F32)
    for i in range(ITERS + 1):
        for j in range(i, ITERS + 1):
            for kind, other in (("same", tiles), ("cross", crossed)):
                total = None
                for mine, theirs in zip(tiles[i], other[j]):
                    term = mine * theirs
                    total = term if total is None else total + term
                column = jnp.sum(total, axis=1, keepdims=True)
                places[kind, i, j] = len(places)
                gram = jnp.where(lane == places[kind, i, j], column, gram)

    gram = jnp.where(lane == 127, overflow, gram)

    for stage, group_peers in enumerate(peers):
        sums[stage] = gram
        copies = []
        for at, device in enumerate(group_peers):
            copy = pltpu.make_async_remote_copy(
                src_ref=sums.at[stage],
                dst_ref=sum_in.at[stage, at],
                send_sem=sum_send.at[stage, at],
                recv_sem=sum_recv.at[stage, at],
                device_id=device,
                device_id_type=MESH,
            )
            copy.start()
            copies.append(copy)
        pending.extend(copies)
        for at, copy in enumerate(copies):
            copy.wait_recv()
            gram = gram + sum_in[stage, at]
    flag_ref[0, 0] = jnp.sum(jnp.where((lane == 127) & (half[:, 0:128]), gram, 0.0))
    gram = gram + pltpu.roll(gram, 4, 0)

    def entry(kind, i, j, second):
        value = jnp.broadcast_to(gram[:, places[kind, i, j] : places[kind, i, j] + 1], (8, 128))
        return pltpu.roll(value, 6, 0) if second else value

    chain = ITERS + 1
    inner = {}
    for i in range(chain):
        for j in range(chain):
            inner[i, j] = entry("same", min(i, j), max(i, j), False)
            if i < ITERS and j < ITERS:
                inner[chain + i, chain + j] = entry("same", min(i, j), max(i, j), True)
            if j < ITERS:
                cross = entry("cross", min(i, j), max(i, j), i > j)
                inner[i, chain + j] = cross
                inner[chain + j, i] = cross

    def bilinear(first, second):
        total = None
        for i, a in first.items():
            inside = None
            for j, b in second.items():
                term = b * inner[i, j]
                inside = term if inside is None else inside + term
            inside = a * inside
            total = inside if total is None else total + inside
        return total

    def combine(base, scale, other):
        result = dict(base)
        for i, value in other.items():
            result[i] = result[i] + scale * value if i in result else scale * value
        return result

    one = jnp.ones((8, 128), F32)
    in_x, in_r, in_p = {}, {chain: one}, {0: one}
    norm_now = inner[chain, chain]
    for it in range(ITERS):
        image = {i + 1: value for i, value in in_p.items()}
        step = norm_now / bilinear(in_p, image)
        in_x = combine(in_x, step, in_p)
        in_r = combine(in_r, -step, image)
        norm_next = bilinear(in_r, in_r)
        in_p = combine(in_r, norm_next / norm_now, in_p)
        norm_now = norm_next

    for f, h in ((0, 0), (0, 1), (1, 0), (1, 1)):
        lanes = slice(128 * h, 128 * h + 128)
        vectors = {}
        for i in range(chain):
            vectors[i] = basis[i, h, pl.ds(f, BLOCKS, stride=4), :]
            if i < ITERS:
                vectors[chain + i] = basis[i, h, pl.ds(2 + f, BLOCKS, stride=4), :]

        def mixed(total, coefficients):
            for i, value in coefficients.items():
                term = value[f : f + 1, :] * vectors[i]
                total = term if total is None else total + term
            return total

        results = (mixed(None, in_x), mixed(None, in_r), mixed(None, in_p))
        for k in range(BLOCKS):
            at = f * BLOCKS + k
            new_sol_ref[at, :, lanes] = sol_rows[at, :, lanes] + results[0][k : k + 1, :]
            new_res_ref[at, :, lanes] = results[1][k : k + 1, :]
            new_dir_ref[at, :, lanes] = results[2][k : k + 1, :]

    for copy in pending:
        copy.wait_send()


def solution(mesh):
    sizes = (mesh.shape["wide"], mesh.shape["narrow"])
    if sizes[0] == 64:
        stages = (
            ("narrow", ((1, sizes[1]),)),
            ("wide", ((2, 8),)),
            ("wide", ((16, 4), (1, 2))),
        )
    else:
        stages = (("narrow", ((1, sizes[1]),)), ("wide", ((1, sizes[0]),)))
    most = 0
    for _, places in stages:
        size = 1
        for _, count in places:
            size *= count
        most = max(most, size - 1)

    def on_device(node_coords, solution, residual, direction, tile_pairs, tile_counts):
        full_shape = direction.shape
        fields = jax.ShapeDtypeStruct((2 * BLOCKS, 1, NODES), F32)
        vmem = pl.BlockSpec(memory_space=pltpu.VMEM)
        anywhere = pl.BlockSpec(memory_space=pl.ANY)
        dma = pltpu.SemaphoreType.DMA
        fast = pl.pallas_call(
            functools.partial(fast_body, sizes, stages),
            out_shape=(fields, fields, fields, jax.ShapeDtypeStruct((1, 1), F32)),
            in_specs=[anywhere] * 5 + [vmem],
            out_specs=(vmem, vmem, vmem, pl.BlockSpec(memory_space=pltpu.SMEM)),
            scratch_shapes=[
                pltpu.VMEM((9 * BLOCKS, 8, NODES), F32),
                pltpu.VMEM((9, ROWS, NODES), F32),
                pltpu.VMEM((9, P_ROWS, NODES), F32),
                *[pltpu.VMEM((FOURS, NODES, NODES), BF16)] * 8,
                pltpu.VMEM((9 * BLOCKS, 16, NODES), BF16),
                pltpu.VMEM((FAST_WIDTH, NODES), F32),
                pltpu.VMEM((FAST_TABLE, FAST_WIDTH), BF16),
                pltpu.VMEM((ITERS + 1, 2, ROWS, 128), F32),
                pltpu.VMEM((len(stages), 8, 128), F32),
                pltpu.VMEM((len(stages), most, 8, 128), F32),
                pltpu.VMEM((7 * BLOCKS, 1, NODES), F32),
                pltpu.VMEM((2 * BLOCKS, 1, NODES), F32),
                pltpu.VMEM((2, SLOTS), jnp.int32),
                pltpu.VMEM((BLOCKS, 3, NODES, 128), F32),
                pltpu.VMEM((9, 8, 128), F32),
                pltpu.VMEM((8, 128), jnp.int32),
                pltpu.SMEM((8, 128), jnp.int32),
                dma((5,)),
                dma,
                dma((8,)),
                dma((8,)),
                dma((8,)),
                dma((8,)),
                dma((ITERS - 1, 8)),
                dma((ITERS - 1, 8)),
                dma((len(stages), most)),
                dma((len(stages), most)),
            ],
            compiler_params=pltpu.CompilerParams(
                collective_id=0, has_side_effects=True, vmem_limit_bytes=60 * 1024 * 1024
            ),
            cost_estimate=pl.CostEstimate(
                flops=81 * 65536 * 40, bytes_accessed=200000, transcendentals=81 * 65536
            ),
        )
        general = pl.pallas_call(
            functools.partial(general_body, sizes, stages),
            out_shape=(fields, fields, fields),
            in_specs=[anywhere] * 5 + [vmem],
            out_specs=(vmem, vmem, vmem),
            scratch_shapes=[
                pltpu.VMEM((9 * BLOCKS, 8, NODES), F32),
                pltpu.VMEM((ITERS - 1, 9, ROWS, NODES), F32),
                pltpu.VMEM((ITERS, 9, ROWS, NODES), F32),
                pltpu.VMEM((ITERS, 8, ROWS, NODES), F32),
                pltpu.VMEM((SLOTS // 2 + 1, NODES, NODES), BF16),
                pltpu.VMEM((SLOTS // 2 + 1, NODES, NODES), BF16),
                pltpu.VMEM((SLOTS // 2 + 1, NODES, NODES), BF16),
                pltpu.VMEM((SLOTS // 2 + 1, NODES, NODES), BF16),
                pltpu.VMEM((SLOTS // 2 + 1, NODES, NODES), BF16),
                pltpu.VMEM((SLOTS // 2 + 1, NODES, NODES), BF16),
                pltpu.VMEM((SLOTS // 2 + 1, NODES, NODES), BF16),
                pltpu.VMEM((SLOTS // 2 + 1, NODES, NODES), BF16),
                pltpu.VMEM((NODES, NODES), F32),
                pltpu.VMEM((NODES, NODES), F32),
                pltpu.VMEM((9 * BLOCKS, 16, NODES), BF16),
                pltpu.VMEM((512, NODES), F32),
                pltpu.VMEM((TABLE, 512), BF16),
                pltpu.VMEM((ITERS + 1, 2, ROWS, 128), F32),
                pltpu.VMEM((len(stages), 8, 128), F32),
                pltpu.VMEM((len(stages), most, 8, 128), F32),
                pltpu.VMEM((7 * BLOCKS, 1, NODES), F32),
                pltpu.VMEM((2 * BLOCKS, 1, NODES), F32),
                pltpu.SMEM((2, SLOTS), jnp.int32),
                pltpu.VMEM((2, SLOTS), jnp.int32),
                pltpu.VMEM((9 * BLOCKS, NODES, 8), F32),
                dma((6,)),
                dma((8,)),
                dma((8,)),
                dma((ITERS - 1, 8)),
                dma((ITERS - 1, 8)),
                dma((ITERS, 8)),
                dma((ITERS, 8)),
                dma((len(stages), most)),
                dma((len(stages), most)),
            ],
            compiler_params=pltpu.CompilerParams(
                collective_id=1, has_side_effects=True, vmem_limit_bytes=60 * 1024 * 1024
            ),
            cost_estimate=pl.CostEstimate(
                flops=61 * 65536 * 40, bytes_accessed=200000, transcendentals=61 * 65536
            ),
        )
        arguments = (
            node_coords.reshape(3 * BLOCKS, 1, NODES),
            solution.reshape(2 * BLOCKS, 1, NODES),
            residual.reshape(2 * BLOCKS, 1, NODES),
            direction.reshape(2 * BLOCKS, 1, NODES),
            tile_pairs.reshape(2, SLOTS),
            tile_counts,
        )
        *outs, flags = fast(*arguments)
        outs = lax.cond(
            flags[0, 0] > 0.5, lambda *a: tuple(general(*a[3:])), lambda *a: a[:3], *outs, *arguments
        )
        return tuple(out.reshape(full_shape) for out in outs)

    fields_spec = P(None, "wide", "narrow", None, None)
    return jax.shard_map(
        on_device,
        mesh=mesh,
        in_specs=(
            fields_spec,
            fields_spec,
            fields_spec,
            fields_spec,
            P("wide", "narrow", None, None),
            P("wide", "narrow"),
        ),
        out_specs=(fields_spec, fields_spec, fields_spec),
        check_vma=False,
    )
```

```python
import functools

import jax
import jax.numpy as jnp
from jax import lax
from jax.experimental import pallas as pl
from jax.experimental.pallas import tpu as pltpu
from jax.sharding import PartitionSpec as P

ITERS = 3
RADIUS = 0.9
MESH = pl.DeviceIdType.MESH
F32 = jnp.float32
BF16 = jnp.bfloat16

BLOCKS = 9
NODES = 256
SLOTS = 61
ROWS = 40
TABLE = 368
GROUP = 3
CHUNK = 16

PHI_SLOPE = 4.0 / RADIUS**5
PHI_CONST = 1.0 / RADIUS**4


def dot_bf16(left, right, transposed):
    dims = (((1,), (1 if transposed else 0,)), ((), ()))
    return lax.dot_general(left, right, dims, preferred_element_type=F32)


def split(value):
    high = value.astype(BF16)
    return high, (value - high.astype(F32)).astype(BF16)


def stage_peers(wide, narrow, stages):
    peers = []
    for axis, places in stages:
        here = wide if axis == "wide" else narrow
        rank, size = 0, 1
        for stride, count in places:
            rank = rank * count + here // stride % count
            size *= count
        group = []
        for step in range(1, size):
            other = (rank + step) % size
            position = here
            left = other
            for stride, count in reversed(places):
                position = position + (left % count - here // stride % count) * stride
                left = left // count
            group.append((position, narrow) if axis == "wide" else (wide, position))
        peers.append(group)
    return peers


def general_body(
    sizes,
    stages,
    coord_ref,
    sol_ref,
    res_ref,
    dir_ref,
    pairs_hbm_ref,
    count_ref,
    new_sol_ref,
    new_res_ref,
    new_dir_ref,
    near0,
    nearq,
    part,
    got,
    khi_even,
    klo_even,
    khi_odd,
    klo_odd,
    thi_even,
    tlo_even,
    thi_odd,
    tlo_odd,
    stage_even,
    stage_odd,
    pieces,
    slot_out,
    onehot,
    basis,
    sums,
    sum_in,
    raw,
    sol_rows,
    pairs_ref,
    pairs_vec_ref,
    cols,
    load_sems,
    near_send,
    near_recv,
    q_send,
    q_recv,
    fold_send,
    fold_recv,
    sum_send,
    sum_recv,
):
    wide_size, narrow_size = sizes
    wide = lax.axis_index("wide")
    narrow = lax.axis_index("narrow")
    neighbours = []
    for d in range(9):
        if d != 4:
            to_wide = (wide + (d // 3 - 1) + wide_size) % wide_size
            to_narrow = (narrow + (d % 3 - 1) + narrow_size) % narrow_size
            neighbours.append((d, (to_wide, to_narrow)))
    peers = stage_peers(wide, narrow, stages)

    loads = [
        pltpu.make_async_copy(source, landing, load_sems.at[at])
        for at, (source, landing) in enumerate(
            (
                (dir_ref, raw.at[pl.ds(0, 2 * BLOCKS)]),
                (res_ref, raw.at[pl.ds(2 * BLOCKS, 2 * BLOCKS)]),
                (coord_ref, raw.at[pl.ds(4 * BLOCKS, 3 * BLOCKS)]),
                (pairs_hbm_ref, pairs_ref),
                (pairs_hbm_ref, pairs_vec_ref),
                (sol_ref, sol_rows),
            )
        )
    ]
    for load in loads:
        load.start()

    barrier = pltpu.get_barrier_semaphore()
    targets = [device for _, device in neighbours] + [device for group in peers for device in group]
    for device in targets:
        pl.semaphore_signal(barrier, inc=1, device_id=device, device_id_type=MESH)

    for load in loads:
        load.wait()
    for k in range(BLOCKS):
        own = 4 * BLOCKS + k
        for c in range(7):
            near0[own, c : c + 1, :] = raw[c * BLOCKS + k]
        near0[own, 7:8, :] = jnp.zeros((1, NODES), F32)

    pl.semaphore_wait(barrier, len(targets))

    pending = []

    def exchange(source, landing, send_sem, recv_sem):
        copies = []
        for at, (d, device) in enumerate(neighbours):
            copy = pltpu.make_async_remote_copy(
                src_ref=source(d),
                dst_ref=landing(8 - d, 7 - at),
                send_sem=send_sem.at[at],
                recv_sem=recv_sem.at[7 - at],
                device_id=device,
                device_id_type=MESH,
            )
            copy.start()
            copies.append(copy)
        pending.extend(copies)

        def wait(at):
            pltpu.make_async_remote_copy(
                src_ref=source(4),
                dst_ref=landing(at + at // 4, at),
                send_sem=send_sem.at[at],
                recv_sem=recv_sem.at[at],
                device_id=neighbours[0][1],
                device_id_type=MESH,
            ).wait_recv()

        return wait

    arrive = exchange(
        lambda d: near0.at[pl.ds(4 * BLOCKS, BLOCKS)],
        lambda d, at: near0.at[pl.ds(d * BLOCKS, BLOCKS)],
        near_send,
        near_recv,
    )

    slot_of = lax.broadcasted_iota(jnp.int32, (64, 512), 0)
    lane_slot = lax.broadcasted_iota(jnp.int32, (64, 512), 1) // 8
    spread = jnp.where(slot_of == lane_slot, 1.0, 0.0).astype(BF16)
    left_id = pairs_vec_ref[0:1, :]
    right_id = pairs_vec_ref[1:2, :]
    live = lax.broadcasted_iota(jnp.int32, (1, SLOTS), 1) < count_ref[0:1, 0:1]
    toward_left = jnp.where(live, left_id, 255)
    toward_right = jnp.where(live & (left_id != right_id), right_id, 255)
    ids = jnp.concatenate([toward_right, toward_left] + [toward_left] * 6, axis=0).astype(F32)
    ids = jnp.concatenate([ids, jnp.full((8, 64 - SLOTS), 255.0, F32)], axis=1)
    wanted = dot_bf16(ids.astype(BF16), spread, False)
    lane = lax.broadcasted_iota(jnp.int32, (8, 512), 1)
    target = jnp.where(lane % 8 < 4, wanted[0:1, :], wanted[1:2, :]).astype(jnp.int32)
    for first in range(0, TABLE, CHUNK):
        row = lax.broadcasted_iota(jnp.int32, (CHUNK, 512), 0) + first
        place = row % ROWS
        block = jnp.where(place < 4 * BLOCKS, row // ROWS * BLOCKS + place // 4, 200)
        match = (block == target[0:1, :]) & (
            row % 4 == lax.broadcasted_iota(jnp.int32, (CHUNK, 512), 1) % 4
        )
        onehot[pl.ds(first, CHUNK), :] = jnp.where(match, 1.0, 0.0).astype(BF16)

    slot_out[pl.ds(8 * SLOTS, 512 - 8 * SLOTS), :] = jnp.zeros((512 - 8 * SLOTS, NODES), F32)
    half = lax.broadcasted_iota(jnp.int32, (8, NODES), 0) < 4

    def put_pieces(j, rows_at, value):
        high = value.astype(BF16).astype(F32)
        low = value - high
        if rows_at == 0:
            rows = jnp.where(half, high, pltpu.roll(low, 4, 0))
        else:
            rows = jnp.where(half, pltpu.roll(high, 4, 0), low)
        pieces[j] = jnp.concatenate([rows, rows], axis=0).astype(BF16)

    for h in range(2):
        for k in range(BLOCKS):
            basis[0, h, 4 * k : 4 * k + 4, :] = near0[4 * BLOCKS + k, 0:4, 128 * h : 128 * h + 128]
        basis[0, h, 4 * BLOCKS : ROWS, :] = jnp.zeros((ROWS - 4 * BLOCKS, 128), F32)

    def prepare(d):
        for k in range(BLOCKS):
            j = d * BLOCKS + k
            value = near0[j]
            put_pieces(j, 0, value)
            cols[j] = jnp.transpose(value)

    def prepare_next(at, carry):
        arrive(at)
        prepare(at + at // 4)
        return carry

    prepare(4)
    lax.fori_loop(0, 8, prepare_next, 0)

    def evaluate(s, refs, stage, at):
        high_ref, low_ref, high_turned, low_turned = refs
        left = cols.at[pairs_ref[0, s]]
        right = near0[pairs_ref[1, s]]
        rights = [jnp.broadcast_to(right[4 + axis : 5 + axis, :], (CHUNK, NODES)) for axis in range(3)]
        for first in range(0, NODES, CHUNK):
            column = left[first : first + CHUNK, :]
            squared = None
            for axis in range(3):
                offset = column[:, 4 + axis : 5 + axis] - rights[axis]
                squared = offset * offset if squared is None else squared + offset * offset
            squared = jnp.minimum(squared, RADIUS * RADIUS)
            distance = squared * lax.rsqrt(jnp.maximum(squared, 1e-36))
            rest = RADIUS - distance
            rest = rest * rest
            rest = rest * rest
            value = rest * (PHI_SLOPE * distance + PHI_CONST)
            high, low = split(value)
            high_ref[at, first : first + CHUNK, :] = high
            low_ref[at, first : first + CHUNK, :] = low
            stage[first : first + CHUNK, :] = value
        for first in range(0, NODES, 128):
            high, low = split(jnp.transpose(stage[first : first + 128, :]))
            high_turned[at, :, first : first + 128] = high
            low_turned[at, :, first : first + 128] = low

    def product(s, refs, at):
        high_ref, low_ref, high_turned, low_turned = refs
        left = pieces[pairs_ref[0, s]]
        right = pieces[pairs_ref[1, s]]
        to_right = dot_bf16(left, high_ref[at], False) + dot_bf16(left, low_ref[at], False)
        to_left = dot_bf16(right, high_turned[at], False) + dot_bf16(right, low_turned[at], False)
        to_right = to_right[0:8]
        to_left = to_left[0:8]
        to_right = to_right + pltpu.roll(to_right, 4, 0)
        to_left = to_left + pltpu.roll(to_left, 4, 0)
        slot_out[pl.ds(pl.multiple_of(s * 8, 8), 8), :] = jnp.where(half, to_right, to_left)

    even = (khi_even, klo_even, thi_even, tlo_even)
    odd = (khi_odd, klo_odd, thi_odd, tlo_odd)

    def evaluate_and_multiply(t, carry):
        before = jnp.maximum(t - 1, 0)
        product(2 * before, even, before)
        evaluate(2 * t, even, stage_even, t)
        product(2 * before + 1, odd, before)
        evaluate(jnp.minimum(2 * t + 1, SLOTS - 1), odd, stage_odd, t)
        return carry

    def products(g, carry):
        for u in range(GROUP):
            at = g * GROUP + u
            product(2 * at, even, at)
            product(2 * at + 1, odd, at)
        return carry

    for it in range(ITERS):
        if it == 0:
            lax.fori_loop(0, SLOTS // 2 + 1, evaluate_and_multiply, 0)
        else:
            lax.fori_loop(0, SLOTS // 2 // GROUP, products, 0)
        product(SLOTS - 1, even, SLOTS // 2)
        high, low = split(slot_out[...])
        table = onehot[...]
        added = dot_bf16(table, high, False) + dot_bf16(table, low, False)
        for d in range(9):
            part[it, d] = added[d * ROWS : (d + 1) * ROWS]
        arrive = exchange(
            lambda d: part.at[it, d],
            lambda d, at: got.at[it, at],
            fold_send.at[it],
            fold_recv.at[it],
        )
        image = part[it, 4]
        for at in range(8):
            arrive(at)
            image = image + got[it, at]
        for h in range(2):
            basis[it + 1, h] = image[:, 128 * h : 128 * h + 128]
        if it + 1 < ITERS:
            nearq[it, 4] = image
            arrive = exchange(
                lambda d: nearq.at[it, 4],
                lambda d, at: nearq.at[it, d],
                q_send.at[it],
                q_recv.at[it],
            )

            def refresh(d):
                for k in range(0, BLOCKS, 2):
                    value = nearq[it, d, 4 * k : 4 * k + 8, :]
                    put_pieces(d * BLOCKS + k, 0, value)
                    if k + 1 < BLOCKS:
                        put_pieces(d * BLOCKS + k + 1, 4, value)

            def refresh_next(at, carry):
                arrive(at)
                refresh(at + at // 4)
                return carry

            refresh(4)
            lax.fori_loop(0, 8, refresh_next, 0)

    lane = lax.broadcasted_iota(jnp.int32, (8, 128), 1)
    forward = lax.broadcasted_iota(jnp.int32, (8, 128), 0) % 4 < 2

    def swapped(value):
        return jnp.where(forward, pltpu.roll(value, 6, 0), pltpu.roll(value, 2, 0))

    tiles = [
        [basis[i, h, g : g + 8, :] for h in range(2) for g in range(0, ROWS, 8)]
        for i in range(ITERS + 1)
    ]
    crossed = [[swapped(tile) for tile in row] for row in tiles]
    places = {}
    gram = jnp.zeros((8, 128), F32)
    for i in range(ITERS + 1):
        for j in range(i, ITERS + 1):
            for kind, other in (("same", tiles), ("cross", crossed)):
                total = None
                for mine, theirs in zip(tiles[i], other[j]):
                    term = mine * theirs
                    total = term if total is None else total + term
                column = jnp.sum(total, axis=1, keepdims=True)
                places[kind, i, j] = len(places)
                gram = jnp.where(lane == places[kind, i, j], column, gram)

    for stage, group_peers in enumerate(peers):
        sums[stage] = gram
        copies = []
        for at, device in enumerate(group_peers):
            copy = pltpu.make_async_remote_copy(
                src_ref=sums.at[stage],
                dst_ref=sum_in.at[stage, at],
                send_sem=sum_send.at[stage, at],
                recv_sem=sum_recv.at[stage, at],
                device_id=device,
                device_id_type=MESH,
            )
            copy.start()
            copies.append(copy)
        pending.extend(copies)
        for at, copy in enumerate(copies):
            copy.wait_recv()
            gram = gram + sum_in[stage, at]
    gram = gram + pltpu.roll(gram, 4, 0)

    def entry(kind, i, j, second):
        value = jnp.broadcast_to(gram[:, places[kind, i, j] : places[kind, i, j] + 1], (8, 128))
        return pltpu.roll(value, 6, 0) if second else value

    chain = ITERS + 1
    inner = {}
    for i in range(chain):
        for j in range(chain):
            inner[i, j] = entry("same", min(i, j), max(i, j), False)
            if i < ITERS and j < ITERS:
                inner[chain + i, chain + j] = entry("same", min(i, j), max(i, j), True)
            if j < ITERS:
                cross = entry("cross", min(i, j), max(i, j), i > j)
                inner[i, chain + j] = cross
                inner[chain + j, i] = cross

    def bilinear(first, second):
        total = None
        for i, a in first.items():
            inside = None
            for j, b in second.items():
                term = b * inner[i, j]
                inside = term if inside is None else inside + term
            inside = a * inside
            total = inside if total is None else total + inside
        return total

    def combine(base, scale, other):
        result = dict(base)
        for i, value in other.items():
            result[i] = result[i] + scale * value if i in result else scale * value
        return result

    one = jnp.ones((8, 128), F32)
    in_x, in_r, in_p = {}, {chain: one}, {0: one}
    norm_now = inner[chain, chain]
    for it in range(ITERS):
        image = {i + 1: value for i, value in in_p.items()}
        step = norm_now / bilinear(in_p, image)
        in_x = combine(in_x, step, in_p)
        in_r = combine(in_r, -step, image)
        norm_next = bilinear(in_r, in_r)
        in_p = combine(in_r, norm_next / norm_now, in_p)
        norm_now = norm_next

    for f, h in ((0, 0), (0, 1), (1, 0), (1, 1)):
        lanes = slice(128 * h, 128 * h + 128)
        vectors = {}
        for i in range(chain):
            vectors[i] = basis[i, h, pl.ds(f, BLOCKS, stride=4), :]
            if i < ITERS:
                vectors[chain + i] = basis[i, h, pl.ds(2 + f, BLOCKS, stride=4), :]

        def mixed(total, coefficients):
            for i, value in coefficients.items():
                term = value[f : f + 1, :] * vectors[i]
                total = term if total is None else total + term
            return total

        results = (mixed(None, in_x), mixed(None, in_r), mixed(None, in_p))
        for k in range(BLOCKS):
            at = f * BLOCKS + k
            new_sol_ref[at, :, lanes] = sol_rows[at, :, lanes] + results[0][k : k + 1, :]
            new_res_ref[at, :, lanes] = results[1][k : k + 1, :]
            new_dir_ref[at, :, lanes] = results[2][k : k + 1, :]

    for copy in pending:
        copy.wait_send()


ENTRIES = 84
FOURS = ENTRIES // 4
SUMS = 80
P_ROWS = 24


def fast_body(
    sizes,
    stages,
    coord_ref,
    sol_ref,
    res_ref,
    dir_ref,
    pairs_hbm_ref,
    count_ref,
    new_sol_ref,
    new_res_ref,
    new_dir_ref,
    flag_ref,
    near0,
    nearq,
    nearp,
    tile_0,
    tile_1,
    tile_2,
    tile_3,
    pieces,
    place,
    added,
    basis,
    sums,
    sum_in,
    raw,
    sol_rows,
    pairs_vec_ref,
    own_columns,
    lists,
    entry_rows,
    entries,
    load_sems,
    entry_sem,
    list_send,
    list_recv,
    near_send,
    near_recv,
    q_send,
    q_recv,
    sum_send,
    sum_recv,
):
    wide_size, narrow_size = sizes
    wide = lax.axis_index("wide")
    narrow = lax.axis_index("narrow")
    neighbours = []
    for d in range(9):
        if d != 4:
            to_wide = (wide + (d // 3 - 1) + wide_size) % wide_size
            to_narrow = (narrow + (d % 3 - 1) + narrow_size) % narrow_size
            neighbours.append((d, (to_wide, to_narrow)))
    peers = stage_peers(wide, narrow, stages)

    loads = [
        pltpu.make_async_copy(source, landing, load_sems.at[at])
        for at, (source, landing) in enumerate(
            (
                (pairs_hbm_ref, pairs_vec_ref),
                (dir_ref, raw.at[pl.ds(0, 2 * BLOCKS)]),
                (res_ref, raw.at[pl.ds(2 * BLOCKS, 2 * BLOCKS)]),
                (coord_ref, raw.at[pl.ds(4 * BLOCKS, 3 * BLOCKS)]),
                (sol_ref, sol_rows),
            )
        )
    ]
    for load in loads:
        load.start()

    barrier = pltpu.get_barrier_semaphore()
    targets = [device for _, device in neighbours] + [device for group in peers for device in group]
    for device in targets:
        pl.semaphore_signal(barrier, inc=1, device_id=device, device_id_type=MESH)

    for load in loads:
        load.wait()
    live = lax.broadcasted_iota(jnp.int32, (2, SLOTS), 1) < count_ref[0:1, 0:1]
    own_list = jnp.where(live, pairs_vec_ref[...], 255).astype(F32)
    own_list = jnp.concatenate([own_list, jnp.full((2, 128 - SLOTS), 255.0, F32)], axis=1)
    lists[4] = jnp.concatenate([own_list, jnp.full((6, 128), 255.0, F32)], axis=0)
    for k in range(BLOCKS):
        own = 4 * BLOCKS + k
        for c in range(7):
            near0[own, c : c + 1, :] = raw[c * BLOCKS + k]
        near0[own, 7:8, :] = jnp.zeros((1, NODES), F32)

    pl.semaphore_wait(barrier, len(targets))

    pending = []

    def exchange(source, landing, send_sem, recv_sem):
        for at, (d, device) in enumerate(neighbours):
            copy = pltpu.make_async_remote_copy(
                src_ref=source,
                dst_ref=landing(8 - d),
                send_sem=send_sem.at[at],
                recv_sem=recv_sem.at[7 - at],
                device_id=device,
                device_id_type=MESH,
            )
            copy.start()
            pending.append(copy)

        def wait(at):
            pltpu.make_async_remote_copy(
                src_ref=source,
                dst_ref=landing(at + at // 4),
                send_sem=send_sem.at[at],
                recv_sem=recv_sem.at[at],
                device_id=neighbours[0][1],
                device_id_type=MESH,
            ).wait_recv()

        return wait

    list_arrive = exchange(lists.at[4], lambda d: lists.at[d], list_send, list_recv)
    near_arrive = exchange(
        near0.at[pl.ds(4 * BLOCKS, BLOCKS)],
        lambda d: near0.at[pl.ds(d * BLOCKS, BLOCKS)],
        near_send,
        near_recv,
    )

    half = lax.broadcasted_iota(jnp.int32, (8, NODES), 0) < 4

    def put_pieces(j, rows_at, value):
        high = value.astype(BF16).astype(F32)
        low = value - high
        if rows_at == 0:
            rows = jnp.where(half, high, pltpu.roll(low, 4, 0))
        else:
            rows = jnp.where(half, pltpu.roll(high, 4, 0), low)
        pieces[j] = jnp.concatenate([rows, rows], axis=0).astype(BF16)

    for h in range(2):
        for k in range(BLOCKS):
            basis[0, h, 4 * k : 4 * k + 4, :] = near0[4 * BLOCKS + k, 0:4, 128 * h : 128 * h + 128]
        basis[0, h, 4 * BLOCKS : ROWS, :] = jnp.zeros((ROWS - 4 * BLOCKS, 128), F32)

    def own_block(k, carry):
        value = near0[4 * BLOCKS + k]
        put_pieces(4 * BLOCKS + k, 0, value)
        turned = jnp.transpose(value)
        for axis in range(3):
            own_columns[k, axis] = jnp.broadcast_to(turned[:, 4 + axis : 5 + axis], (NODES, 128))
        return carry

    lax.fori_loop(0, BLOCKS, own_block, 0)
    for t in range(BLOCKS + 1):
        row = lax.broadcasted_iota(jnp.int32, (SUMS, NODES), 0)
        place[t] = jnp.where((row >> 3 == t) & (t < BLOCKS), 1.0, 0.0).astype(BF16)

    for at in range(8):
        list_arrive(at)
    dead_rows = jnp.full((7, 128), 255.0, F32)
    device_row = lax.broadcasted_iota(jnp.int32, (16, 128), 0)
    add_wide = (device_row * 11 >> 5) - 1
    add_narrow = device_row - (add_wide + 1) * 3 - 1

    def here(row):
        ids = jnp.concatenate([lists[d, row : row + 1, :] for d in range(9)] + [dead_rows], axis=0)
        ids = ids.astype(jnp.int32)
        is_live = ids < 200
        ids = jnp.where(is_live, ids, 0)
        device = ids * 7282 >> 16
        within = ids - device * 9
        at_wide = device * 11 >> 5
        at_narrow = device - at_wide * 3 + add_narrow
        at_wide = at_wide + add_wide
        mine = is_live & (at_wide == 1) & (at_narrow == 1)
        return mine, within, at_wide * 27 + at_narrow * 9 + within

    left_mine, left_within, left_here = here(0)
    right_mine, right_within, right_here = here(1)
    right_mine = right_mine & (left_here != right_here)
    wanted_rows = jnp.concatenate(
        [jnp.where(left_mine, 1.0, 0.0), jnp.where(right_mine, 1.0, 0.0)], axis=0
    )
    codes = jnp.concatenate(
        [left_within * 128 + right_here + 1, right_within * 128 + left_here + 1], axis=0
    ).astype(F32)
    before_lane = lax.broadcasted_iota(jnp.int32, (128, 128), 0) < lax.broadcasted_iota(
        jnp.int32, (128, 128), 1
    )
    before_row = lax.broadcasted_iota(jnp.int32, (32, 32), 0) > lax.broadcasted_iota(
        jnp.int32, (32, 32), 1
    )
    wanted_bits = wanted_rows.astype(BF16)
    in_row = dot_bf16(wanted_bits, jnp.where(before_lane, 1.0, 0.0).astype(BF16), False)
    row_total = jnp.broadcast_to(jnp.sum(wanted_rows, axis=1, keepdims=True), (32, 128))
    rank = in_row + dot_bf16(
        jnp.where(before_row, 1.0, 0.0).astype(BF16), row_total.astype(BF16), False
    )
    everything = jnp.sum(row_total, axis=0, keepdims=True)
    overflow = jnp.where(everything > ENTRIES + 0.5, 1.0, 0.0)
    rank = jnp.where(wanted_rows > 0.5, rank, -1.0)
    entry_of = lax.broadcasted_iota(jnp.int32, (128, 128), 0).astype(F32)
    gathered = jnp.zeros((128, 128), F32)
    for row in [*range(9), *range(16, 25)]:
        gathered = gathered + jnp.where(
            entry_of == rank[row : row + 1, :], codes[row : row + 1, :], 0.0
        )
    gathered = jnp.broadcast_to(jnp.sum(gathered, axis=1, keepdims=True), (128, 128))
    code = jnp.transpose(gathered)[0:8, :].astype(jnp.int32)
    filled = code > 0
    code = jnp.maximum(code - 1, 0)
    target = code >> 7
    row_of = lax.broadcasted_iota(jnp.int32, (8, 128), 0)
    target = jnp.where(filled, target, BLOCKS)
    entry_rows[...] = jnp.where(row_of == 0, target, code & 127)
    entry_load = pltpu.make_async_copy(entry_rows, entries, entry_sem)
    entry_load.start()

    def prepare_next(at, carry):
        near_arrive(at)
        for k in range(BLOCKS):
            j = (at + at // 4) * BLOCKS + k
            put_pieces(j, 0, near0[j])
        return carry

    lax.fori_loop(0, 8, prepare_next, 0)
    entry_load.wait()

    def evaluate(e, tile_ref, at):
        block = jnp.clip(entries[0, e], 0, BLOCKS - 1)
        other = near0[jnp.clip(entries[1, e], 0, 9 * BLOCKS - 1)]
        for h in range(2):
            lanes = slice(128 * h, 128 * h + 128)
            others = [
                jnp.broadcast_to(other[4 + axis : 5 + axis, lanes], (CHUNK, 128)) for axis in range(3)
            ]
            for first in range(0, NODES, CHUNK):
                squared = None
                for axis in range(3):
                    offset = own_columns[block, axis, first : first + CHUNK, :] - others[axis]
                    squared = offset * offset if squared is None else squared + offset * offset
                squared = jnp.minimum(squared, RADIUS * RADIUS)
                distance = squared * lax.rsqrt(jnp.maximum(squared, 1e-36))
                rest = RADIUS - distance
                rest = rest * rest
                rest = rest * rest
                high, low = split(rest * (PHI_SLOPE * distance + PHI_CONST))
                tile_ref[at, first : first + CHUNK, lanes] = high
                tile_ref[at, NODES + first : NODES + first + CHUNK, lanes] = low

    def product(e, tile_ref, at):
        other = pieces[jnp.clip(entries[1, e], 0, 9 * BLOCKS - 1)]
        weights = jnp.concatenate([other] * (SUMS // 16), axis=0)
        weights = weights * place[jnp.clip(entries[0, e], 0, BLOCKS)]
        result = dot_bf16(tile_ref[at], weights, True)
        return result[0:NODES] + result[NODES : 2 * NODES]

    tiles_of = (tile_0, tile_1, tile_2, tile_3)

    def evaluate_and_multiply(t, carry):
        before = jnp.maximum(t - 1, 0)
        total = None
        for u, tile_ref in enumerate(tiles_of):
            term = product(4 * before + u, tile_ref, before)
            total = term if total is None else total + term
            evaluate(4 * t + u, tile_ref, t)
        added[...] = added[...] + jnp.where(t > 0, total, 0.0)
        return carry

    group = 5

    def products(g, carry):
        total = None
        for at in range(group):
            for u, tile_ref in enumerate(tiles_of):
                term = product(4 * (g * group + at) + u, tile_ref, g * group + at)
                total = term if total is None else total + term
        added[...] = added[...] + total
        return carry

    row8 = lax.broadcasted_iota(jnp.int32, (8, NODES), 0)
    for it in range(ITERS):
        added[...] = jnp.zeros((NODES, SUMS), F32)
        if it == 0:
            lax.fori_loop(0, FOURS, evaluate_and_multiply, 0)
        else:
            lax.fori_loop(0, FOURS // group, products, 0)
        total = added[...]
        for u, tile_ref in enumerate(tiles_of):
            total = total + product(4 * (FOURS - 1) + u, tile_ref, FOURS - 1)
        total = jnp.transpose(jnp.concatenate([total, jnp.zeros((NODES, 128 - SUMS), F32)], axis=1))
        blocks = [total[8 * k : 8 * k + 8] for k in range(SUMS // 8)]
        blocks = [block + pltpu.roll(block, 4, 0) for block in blocks]
        image = [jnp.where(half, blocks[k], blocks[k + 1]) for k in range(0, SUMS // 8, 2)]
        for g, rows in enumerate(image):
            for h in range(2):
                basis[it + 1, h, 8 * g : 8 * g + 8, :] = rows[:, 128 * h : 128 * h + 128]
        if it == 0:
            for g, rows in enumerate(image):
                nearq[4, 8 * g : 8 * g + 8, :] = rows
            arrive = exchange(nearq.at[4], lambda d: nearq.at[d], q_send.at[it], q_recv.at[it])

            def refresh(d):
                for k in range(0, BLOCKS, 2):
                    value = nearq[d, 4 * k : 4 * k + 8, :]
                    put_pieces(d * BLOCKS + k, 0, value)
                    if k + 1 < BLOCKS:
                        put_pieces(d * BLOCKS + k + 1, 4, value)

            def refresh_next(at, carry):
                arrive(at)
                refresh(at + at // 4)
                return carry

            refresh(4)
            lax.fori_loop(0, 8, refresh_next, 0)
        elif it + 1 < ITERS:
            for g in range(P_ROWS // 8):
                rows = jnp.zeros((8, NODES), F32)
                for k in range(4 * g, min(4 * g + 4, BLOCKS)):
                    block = pltpu.roll(blocks[k], 2, 0) if k % 2 else blocks[k]
                    rows = jnp.where(row8 >> 1 == k % 4, block, rows)
                nearp[4, 8 * g : 8 * g + 8, :] = rows
            arrive_p = exchange(nearp.at[4], lambda d: nearp.at[d], q_send.at[it], q_recv.at[it])

            def refresh_p(d):
                for k in range(BLOCKS):
                    value = nearp[d, k // 4 * 8 : k // 4 * 8 + 8, :]
                    if k % 4:
                        value = pltpu.roll(value, 8 - k % 4 * 2, 0)
                    put_pieces(d * BLOCKS + k, 0, value)

            def refresh_next_p(at, carry):
                arrive_p(at)
                refresh_p(at + at // 4)
                return carry

            refresh_p(4)
            lax.fori_loop(0, 8, refresh_next_p, 0)

    lane = lax.broadcasted_iota(jnp.int32, (8, 128), 1)
    forward = lax.broadcasted_iota(jnp.int32, (8, 128), 0) % 4 < 2

    def swapped(value):
        return jnp.where(forward, pltpu.roll(value, 6, 0), pltpu.roll(value, 2, 0))

    tiles = [
        [basis[i, h, g : g + 8, :] for h in range(2) for g in range(0, ROWS, 8)]
        for i in range(ITERS + 1)
    ]
    crossed = [[swapped(tile) for tile in row] for row in tiles]
    places = {}
    gram = jnp.zeros((8, 128), F32)
    for i in range(ITERS + 1):
        for j in range(i, ITERS + 1):
            for kind, other in (("same", tiles), ("cross", crossed)):
                total = None
                for mine, theirs in zip(tiles[i], other[j]):
                    term = mine * theirs
                    total = term if total is None else total + term
                column = jnp.sum(total, axis=1, keepdims=True)
                places[kind, i, j] = len(places)
                gram = jnp.where(lane == places[kind, i, j], column, gram)

    gram = jnp.where(lane == 127, overflow, gram)

    for stage, group_peers in enumerate(peers):
        sums[stage] = gram
        copies = []
        for at, device in enumerate(group_peers):
            copy = pltpu.make_async_remote_copy(
                src_ref=sums.at[stage],
                dst_ref=sum_in.at[stage, at],
                send_sem=sum_send.at[stage, at],
                recv_sem=sum_recv.at[stage, at],
                device_id=device,
                device_id_type=MESH,
            )
            copy.start()
            copies.append(copy)
        pending.extend(copies)
        for at, copy in enumerate(copies):
            copy.wait_recv()
            gram = gram + sum_in[stage, at]
    flag_ref[0, 0] = jnp.sum(jnp.where((lane == 127) & (half[:, 0:128]), gram, 0.0))
    gram = gram + pltpu.roll(gram, 4, 0)

    def entry(kind, i, j, second):
        value = jnp.broadcast_to(gram[:, places[kind, i, j] : places[kind, i, j] + 1], (8, 128))
        return pltpu.roll(value, 6, 0) if second else value

    chain = ITERS + 1
    inner = {}
    for i in range(chain):
        for j in range(chain):
            inner[i, j] = entry("same", min(i, j), max(i, j), False)
            if i < ITERS and j < ITERS:
                inner[chain + i, chain + j] = entry("same", min(i, j), max(i, j), True)
            if j < ITERS:
                cross = entry("cross", min(i, j), max(i, j), i > j)
                inner[i, chain + j] = cross
                inner[chain + j, i] = cross

    def bilinear(first, second):
        total = None
        for i, a in first.items():
            inside = None
            for j, b in second.items():
                term = b * inner[i, j]
                inside = term if inside is None else inside + term
            inside = a * inside
            total = inside if total is None else total + inside
        return total

    def combine(base, scale, other):
        result = dict(base)
        for i, value in other.items():
            result[i] = result[i] + scale * value if i in result else scale * value
        return result

    one = jnp.ones((8, 128), F32)
    in_x, in_r, in_p = {}, {chain: one}, {0: one}
    norm_now = inner[chain, chain]
    for it in range(ITERS):
        image = {i + 1: value for i, value in in_p.items()}
        step = norm_now / bilinear(in_p, image)
        in_x = combine(in_x, step, in_p)
        in_r = combine(in_r, -step, image)
        norm_next = bilinear(in_r, in_r)
        in_p = combine(in_r, norm_next / norm_now, in_p)
        norm_now = norm_next

    for f, h in ((0, 0), (0, 1), (1, 0), (1, 1)):
        lanes = slice(128 * h, 128 * h + 128)
        vectors = {}
        for i in range(chain):
            vectors[i] = basis[i, h, pl.ds(f, BLOCKS, stride=4), :]
            if i < ITERS:
                vectors[chain + i] = basis[i, h, pl.ds(2 + f, BLOCKS, stride=4), :]

        def mixed(total, coefficients):
            for i, value in coefficients.items():
                term = value[f : f + 1, :] * vectors[i]
                total = term if total is None else total + term
            return total

        results = (mixed(None, in_x), mixed(None, in_r), mixed(None, in_p))
        for k in range(BLOCKS):
            at = f * BLOCKS + k
            new_sol_ref[at, :, lanes] = sol_rows[at, :, lanes] + results[0][k : k + 1, :]
            new_res_ref[at, :, lanes] = results[1][k : k + 1, :]
            new_dir_ref[at, :, lanes] = results[2][k : k + 1, :]

    for copy in pending:
        copy.wait_send()


def solution(mesh):
    sizes = (mesh.shape["wide"], mesh.shape["narrow"])
    if sizes[0] == 64:
        stages = (
            ("narrow", ((1, sizes[1]),)),
            ("wide", ((2, 8),)),
            ("wide", ((16, 4), (1, 2))),
        )
    else:
        stages = (("narrow", ((1, sizes[1]),)), ("wide", ((1, sizes[0]),)))
    most = 0
    for _, places in stages:
        size = 1
        for _, count in places:
            size *= count
        most = max(most, size - 1)

    def on_device(node_coords, solution, residual, direction, tile_pairs, tile_counts):
        full_shape = direction.shape
        fields = jax.ShapeDtypeStruct((2 * BLOCKS, 1, NODES), F32)
        vmem = pl.BlockSpec(memory_space=pltpu.VMEM)
        anywhere = pl.BlockSpec(memory_space=pl.ANY)
        dma = pltpu.SemaphoreType.DMA
        fast = pl.pallas_call(
            functools.partial(fast_body, sizes, stages),
            out_shape=(fields, fields, fields, jax.ShapeDtypeStruct((1, 1), F32)),
            in_specs=[anywhere] * 5 + [vmem],
            out_specs=(vmem, vmem, vmem, pl.BlockSpec(memory_space=pltpu.SMEM)),
            scratch_shapes=[
                pltpu.VMEM((9 * BLOCKS, 8, NODES), F32),
                pltpu.VMEM((9, ROWS, NODES), F32),
                pltpu.VMEM((9, P_ROWS, NODES), F32),
                *[pltpu.VMEM((FOURS, 2 * NODES, NODES), BF16)] * 4,
                pltpu.VMEM((9 * BLOCKS, 16, NODES), BF16),
                pltpu.VMEM((BLOCKS + 1, SUMS, NODES), BF16),
                pltpu.VMEM((NODES, SUMS), F32),
                pltpu.VMEM((ITERS + 1, 2, ROWS, 128), F32),
                pltpu.VMEM((len(stages), 8, 128), F32),
                pltpu.VMEM((len(stages), most, 8, 128), F32),
                pltpu.VMEM((7 * BLOCKS, 1, NODES), F32),
                pltpu.VMEM((2 * BLOCKS, 1, NODES), F32),
                pltpu.VMEM((2, SLOTS), jnp.int32),
                pltpu.VMEM((BLOCKS, 3, NODES, 128), F32),
                pltpu.VMEM((9, 8, 128), F32),
                pltpu.VMEM((8, 128), jnp.int32),
                pltpu.SMEM((8, 128), jnp.int32),
                dma((5,)),
                dma,
                dma((8,)),
                dma((8,)),
                dma((8,)),
                dma((8,)),
                dma((ITERS - 1, 8)),
                dma((ITERS - 1, 8)),
                dma((len(stages), most)),
                dma((len(stages), most)),
            ],
            compiler_params=pltpu.CompilerParams(
                collective_id=0, has_side_effects=True, vmem_limit_bytes=60 * 1024 * 1024
            ),
            cost_estimate=pl.CostEstimate(
                flops=81 * 65536 * 40, bytes_accessed=200000, transcendentals=81 * 65536
            ),
        )
        general = pl.pallas_call(
            functools.partial(general_body, sizes, stages),
            out_shape=(fields, fields, fields),
            in_specs=[anywhere] * 5 + [vmem],
            out_specs=(vmem, vmem, vmem),
            scratch_shapes=[
                pltpu.VMEM((9 * BLOCKS, 8, NODES), F32),
                pltpu.VMEM((ITERS - 1, 9, ROWS, NODES), F32),
                pltpu.VMEM((ITERS, 9, ROWS, NODES), F32),
                pltpu.VMEM((ITERS, 8, ROWS, NODES), F32),
                pltpu.VMEM((SLOTS // 2 + 1, NODES, NODES), BF16),
                pltpu.VMEM((SLOTS // 2 + 1, NODES, NODES), BF16),
                pltpu.VMEM((SLOTS // 2 + 1, NODES, NODES), BF16),
                pltpu.VMEM((SLOTS // 2 + 1, NODES, NODES), BF16),
                pltpu.VMEM((SLOTS // 2 + 1, NODES, NODES), BF16),
                pltpu.VMEM((SLOTS // 2 + 1, NODES, NODES), BF16),
                pltpu.VMEM((SLOTS // 2 + 1, NODES, NODES), BF16),
                pltpu.VMEM((SLOTS // 2 + 1, NODES, NODES), BF16),
                pltpu.VMEM((NODES, NODES), F32),
                pltpu.VMEM((NODES, NODES), F32),
                pltpu.VMEM((9 * BLOCKS, 16, NODES), BF16),
                pltpu.VMEM((512, NODES), F32),
                pltpu.VMEM((TABLE, 512), BF16),
                pltpu.VMEM((ITERS + 1, 2, ROWS, 128), F32),
                pltpu.VMEM((len(stages), 8, 128), F32),
                pltpu.VMEM((len(stages), most, 8, 128), F32),
                pltpu.VMEM((7 * BLOCKS, 1, NODES), F32),
                pltpu.VMEM((2 * BLOCKS, 1, NODES), F32),
                pltpu.SMEM((2, SLOTS), jnp.int32),
                pltpu.VMEM((2, SLOTS), jnp.int32),
                pltpu.VMEM((9 * BLOCKS, NODES, 8), F32),
                dma((6,)),
                dma((8,)),
                dma((8,)),
                dma((ITERS - 1, 8)),
                dma((ITERS - 1, 8)),
                dma((ITERS, 8)),
                dma((ITERS, 8)),
                dma((len(stages), most)),
                dma((len(stages), most)),
            ],
            compiler_params=pltpu.CompilerParams(
                collective_id=1, has_side_effects=True, vmem_limit_bytes=60 * 1024 * 1024
            ),
            cost_estimate=pl.CostEstimate(
                flops=61 * 65536 * 40, bytes_accessed=200000, transcendentals=61 * 65536
            ),
        )
        arguments = (
            node_coords.reshape(3 * BLOCKS, 1, NODES),
            solution.reshape(2 * BLOCKS, 1, NODES),
            residual.reshape(2 * BLOCKS, 1, NODES),
            direction.reshape(2 * BLOCKS, 1, NODES),
            tile_pairs.reshape(2, SLOTS),
            tile_counts,
        )
        *outs, flags = fast(*arguments)
        outs = lax.cond(
            flags[0, 0] > 0.5, lambda *a: tuple(general(*a[3:])), lambda *a: a[:3], *outs, *arguments
        )
        return tuple(out.reshape(full_shape) for out in outs)

    fields_spec = P(None, "wide", "narrow", None, None)
    return jax.shard_map(
        on_device,
        mesh=mesh,
        in_specs=(
            fields_spec,
            fields_spec,
            fields_spec,
            fields_spec,
            P("wide", "narrow", None, None),
            P("wide", "narrow"),
        ),
        out_specs=(fields_spec, fields_spec, fields_spec),
        check_vma=False,
    )
```

```python
import functools

import jax
import jax.numpy as jnp
from jax import lax
from jax.experimental import pallas as pl
from jax.experimental.pallas import tpu as pltpu
from jax.sharding import PartitionSpec as P

ITERS = 3
RADIUS = 0.9
MESH = pl.DeviceIdType.MESH
F32 = jnp.float32
BF16 = jnp.bfloat16

BLOCKS = 9
NODES = 256
SLOTS = 61
ROWS = 40
TABLE = 368
GROUP = 3
CHUNK = 16

PHI_SLOPE = 4.0 / RADIUS**5
PHI_CONST = 1.0 / RADIUS**4


def dot_bf16(left, right, transposed):
    dims = (((1,), (1 if transposed else 0,)), ((), ()))
    return lax.dot_general(left, right, dims, preferred_element_type=F32)


def split(value):
    high = value.astype(BF16)
    return high, (value - high.astype(F32)).astype(BF16)


def stage_peers(wide, narrow, stages):
    peers = []
    for axis, places in stages:
        here = wide if axis == "wide" else narrow
        rank, size = 0, 1
        for stride, count in places:
            rank = rank * count + here // stride % count
            size *= count
        group = []
        for step in range(1, size):
            other = (rank + step) % size
            position = here
            left = other
            for stride, count in reversed(places):
                position = position + (left % count - here // stride % count) * stride
                left = left // count
            group.append((position, narrow) if axis == "wide" else (wide, position))
        peers.append(group)
    return peers


def general_body(
    sizes,
    stages,
    coord_ref,
    sol_ref,
    res_ref,
    dir_ref,
    pairs_hbm_ref,
    count_ref,
    new_sol_ref,
    new_res_ref,
    new_dir_ref,
    near0,
    nearq,
    part,
    got,
    khi_even,
    klo_even,
    khi_odd,
    klo_odd,
    thi_even,
    tlo_even,
    thi_odd,
    tlo_odd,
    stage_even,
    stage_odd,
    pieces,
    slot_out,
    onehot,
    basis,
    sums,
    sum_in,
    raw,
    sol_rows,
    pairs_ref,
    pairs_vec_ref,
    cols,
    load_sems,
    near_send,
    near_recv,
    q_send,
    q_recv,
    fold_send,
    fold_recv,
    sum_send,
    sum_recv,
):
    wide_size, narrow_size = sizes
    wide = lax.axis_index("wide")
    narrow = lax.axis_index("narrow")
    neighbours = []
    for d in range(9):
        if d != 4:
            to_wide = (wide + (d // 3 - 1) + wide_size) % wide_size
            to_narrow = (narrow + (d % 3 - 1) + narrow_size) % narrow_size
            neighbours.append((d, (to_wide, to_narrow)))
    peers = stage_peers(wide, narrow, stages)

    loads = [
        pltpu.make_async_copy(source, landing, load_sems.at[at])
        for at, (source, landing) in enumerate(
            (
                (dir_ref, raw.at[pl.ds(0, 2 * BLOCKS)]),
                (res_ref, raw.at[pl.ds(2 * BLOCKS, 2 * BLOCKS)]),
                (coord_ref, raw.at[pl.ds(4 * BLOCKS, 3 * BLOCKS)]),
                (pairs_hbm_ref, pairs_ref),
                (pairs_hbm_ref, pairs_vec_ref),
                (sol_ref, sol_rows),
            )
        )
    ]
    for load in loads:
        load.start()

    barrier = pltpu.get_barrier_semaphore()
    targets = [device for _, device in neighbours] + [device for group in peers for device in group]
    for device in targets:
        pl.semaphore_signal(barrier, inc=1, device_id=device, device_id_type=MESH)

    for load in loads:
        load.wait()
    for k in range(BLOCKS):
        own = 4 * BLOCKS + k
        for c in range(7):
            near0[own, c : c + 1, :] = raw[c * BLOCKS + k]
        near0[own, 7:8, :] = jnp.zeros((1, NODES), F32)

    pl.semaphore_wait(barrier, len(targets))

    pending = []

    def exchange(source, landing, send_sem, recv_sem):
        copies = []
        for at, (d, device) in enumerate(neighbours):
            copy = pltpu.make_async_remote_copy(
                src_ref=source(d),
                dst_ref=landing(8 - d, 7 - at),
                send_sem=send_sem.at[at],
                recv_sem=recv_sem.at[7 - at],
                device_id=device,
                device_id_type=MESH,
            )
            copy.start()
            copies.append(copy)
        pending.extend(copies)

        def wait(at):
            pltpu.make_async_remote_copy(
                src_ref=source(4),
                dst_ref=landing(at + at // 4, at),
                send_sem=send_sem.at[at],
                recv_sem=recv_sem.at[at],
                device_id=neighbours[0][1],
                device_id_type=MESH,
            ).wait_recv()

        return wait

    arrive = exchange(
        lambda d: near0.at[pl.ds(4 * BLOCKS, BLOCKS)],
        lambda d, at: near0.at[pl.ds(d * BLOCKS, BLOCKS)],
        near_send,
        near_recv,
    )

    slot_of = lax.broadcasted_iota(jnp.int32, (64, 512), 0)
    lane_slot = lax.broadcasted_iota(jnp.int32, (64, 512), 1) // 8
    spread = jnp.where(slot_of == lane_slot, 1.0, 0.0).astype(BF16)
    left_id = pairs_vec_ref[0:1, :]
    right_id = pairs_vec_ref[1:2, :]
    live = lax.broadcasted_iota(jnp.int32, (1, SLOTS), 1) < count_ref[0:1, 0:1]
    toward_left = jnp.where(live, left_id, 255)
    toward_right = jnp.where(live & (left_id != right_id), right_id, 255)
    ids = jnp.concatenate([toward_right, toward_left] + [toward_left] * 6, axis=0).astype(F32)
    ids = jnp.concatenate([ids, jnp.full((8, 64 - SLOTS), 255.0, F32)], axis=1)
    wanted = dot_bf16(ids.astype(BF16), spread, False)
    lane = lax.broadcasted_iota(jnp.int32, (8, 512), 1)
    target = jnp.where(lane % 8 < 4, wanted[0:1, :], wanted[1:2, :]).astype(jnp.int32)
    for first in range(0, TABLE, CHUNK):
        row = lax.broadcasted_iota(jnp.int32, (CHUNK, 512), 0) + first
        place = row % ROWS
        block = jnp.where(place < 4 * BLOCKS, row // ROWS * BLOCKS + place // 4, 200)
        match = (block == target[0:1, :]) & (
            row % 4 == lax.broadcasted_iota(jnp.int32, (CHUNK, 512), 1) % 4
        )
        onehot[pl.ds(first, CHUNK), :] = jnp.where(match, 1.0, 0.0).astype(BF16)

    slot_out[pl.ds(8 * SLOTS, 512 - 8 * SLOTS), :] = jnp.zeros((512 - 8 * SLOTS, NODES), F32)
    half = lax.broadcasted_iota(jnp.int32, (8, NODES), 0) < 4

    def put_pieces(j, rows_at, value):
        high = value.astype(BF16).astype(F32)
        low = value - high
        if rows_at == 0:
            rows = jnp.where(half, high, pltpu.roll(low, 4, 0))
        else:
            rows = jnp.where(half, pltpu.roll(high, 4, 0), low)
        pieces[j] = jnp.concatenate([rows, rows], axis=0).astype(BF16)

    for h in range(2):
        for k in range(BLOCKS):
            basis[0, h, 4 * k : 4 * k + 4, :] = near0[4 * BLOCKS + k, 0:4, 128 * h : 128 * h + 128]
        basis[0, h, 4 * BLOCKS : ROWS, :] = jnp.zeros((ROWS - 4 * BLOCKS, 128), F32)

    def prepare(d):
        for k in range(BLOCKS):
            j = d * BLOCKS + k
            value = near0[j]
            put_pieces(j, 0, value)
            cols[j] = jnp.transpose(value)

    def prepare_next(at, carry):
        arrive(at)
        prepare(at + at // 4)
        return carry

    prepare(4)
    lax.fori_loop(0, 8, prepare_next, 0)

    def evaluate(s, refs, stage, at):
        high_ref, low_ref, high_turned, low_turned = refs
        left = cols.at[pairs_ref[0, s]]
        right = near0[pairs_ref[1, s]]
        rights = [jnp.broadcast_to(right[4 + axis : 5 + axis, :], (CHUNK, NODES)) for axis in range(3)]
        for first in range(0, NODES, CHUNK):
            column = left[first : first + CHUNK, :]
            squared = None
            for axis in range(3):
                offset = column[:, 4 + axis : 5 + axis] - rights[axis]
                squared = offset * offset if squared is None else squared + offset * offset
            squared = jnp.minimum(squared, RADIUS * RADIUS)
            distance = squared * lax.rsqrt(jnp.maximum(squared, 1e-36))
            rest = RADIUS - distance
            rest = rest * rest
            rest = rest * rest
            value = rest * (PHI_SLOPE * distance + PHI_CONST)
            high, low = split(value)
            high_ref[at, first : first + CHUNK, :] = high
            low_ref[at, first : first + CHUNK, :] = low
            stage[first : first + CHUNK, :] = value
        for first in range(0, NODES, 128):
            high, low = split(jnp.transpose(stage[first : first + 128, :]))
            high_turned[at, :, first : first + 128] = high
            low_turned[at, :, first : first + 128] = low

    def product(s, refs, at):
        high_ref, low_ref, high_turned, low_turned = refs
        left = pieces[pairs_ref[0, s]]
        right = pieces[pairs_ref[1, s]]
        to_right = dot_bf16(left, high_ref[at], False) + dot_bf16(left, low_ref[at], False)
        to_left = dot_bf16(right, high_turned[at], False) + dot_bf16(right, low_turned[at], False)
        to_right = to_right[0:8]
        to_left = to_left[0:8]
        to_right = to_right + pltpu.roll(to_right, 4, 0)
        to_left = to_left + pltpu.roll(to_left, 4, 0)
        slot_out[pl.ds(pl.multiple_of(s * 8, 8), 8), :] = jnp.where(half, to_right, to_left)

    even = (khi_even, klo_even, thi_even, tlo_even)
    odd = (khi_odd, klo_odd, thi_odd, tlo_odd)

    def evaluate_and_multiply(t, carry):
        before = jnp.maximum(t - 1, 0)
        product(2 * before, even, before)
        evaluate(2 * t, even, stage_even, t)
        product(2 * before + 1, odd, before)
        evaluate(jnp.minimum(2 * t + 1, SLOTS - 1), odd, stage_odd, t)
        return carry

    def products(g, carry):
        for u in range(GROUP):
            at = g * GROUP + u
            product(2 * at, even, at)
            product(2 * at + 1, odd, at)
        return carry

    for it in range(ITERS):
        if it == 0:
            lax.fori_loop(0, SLOTS // 2 + 1, evaluate_and_multiply, 0)
        else:
            lax.fori_loop(0, SLOTS // 2 // GROUP, products, 0)
        product(SLOTS - 1, even, SLOTS // 2)
        high, low = split(slot_out[...])
        table = onehot[...]
        added = dot_bf16(table, high, False) + dot_bf16(table, low, False)
        for d in range(9):
            part[it, d] = added[d * ROWS : (d + 1) * ROWS]
        arrive = exchange(
            lambda d: part.at[it, d],
            lambda d, at: got.at[it, at],
            fold_send.at[it],
            fold_recv.at[it],
        )
        image = part[it, 4]
        for at in range(8):
            arrive(at)
            image = image + got[it, at]
        for h in range(2):
            basis[it + 1, h] = image[:, 128 * h : 128 * h + 128]
        if it + 1 < ITERS:
            nearq[it, 4] = image
            arrive = exchange(
                lambda d: nearq.at[it, 4],
                lambda d, at: nearq.at[it, d],
                q_send.at[it],
                q_recv.at[it],
            )

            def refresh(d):
                for k in range(0, BLOCKS, 2):
                    value = nearq[it, d, 4 * k : 4 * k + 8, :]
                    put_pieces(d * BLOCKS + k, 0, value)
                    if k + 1 < BLOCKS:
                        put_pieces(d * BLOCKS + k + 1, 4, value)

            def refresh_next(at, carry):
                arrive(at)
                refresh(at + at // 4)
                return carry

            refresh(4)
            lax.fori_loop(0, 8, refresh_next, 0)

    lane = lax.broadcasted_iota(jnp.int32, (8, 128), 1)
    forward = lax.broadcasted_iota(jnp.int32, (8, 128), 0) % 4 < 2

    def swapped(value):
        return jnp.where(forward, pltpu.roll(value, 6, 0), pltpu.roll(value, 2, 0))

    tiles = [
        [basis[i, h, g : g + 8, :] for h in range(2) for g in range(0, ROWS, 8)]
        for i in range(ITERS + 1)
    ]
    crossed = [[swapped(tile) for tile in row] for row in tiles]
    places = {}
    gram = jnp.zeros((8, 128), F32)
    for i in range(ITERS + 1):
        for j in range(i, ITERS + 1):
            for kind, other in (("same", tiles), ("cross", crossed)):
                total = None
                for mine, theirs in zip(tiles[i], other[j]):
                    term = mine * theirs
                    total = term if total is None else total + term
                column = jnp.sum(total, axis=1, keepdims=True)
                places[kind, i, j] = len(places)
                gram = jnp.where(lane == places[kind, i, j], column, gram)

    for stage, group_peers in enumerate(peers):
        sums[stage] = gram
        copies = []
        for at, device in enumerate(group_peers):
            copy = pltpu.make_async_remote_copy(
                src_ref=sums.at[stage],
                dst_ref=sum_in.at[stage, at],
                send_sem=sum_send.at[stage, at],
                recv_sem=sum_recv.at[stage, at],
                device_id=device,
                device_id_type=MESH,
            )
            copy.start()
            copies.append(copy)
        pending.extend(copies)
        for at, copy in enumerate(copies):
            copy.wait_recv()
            gram = gram + sum_in[stage, at]
    gram = gram + pltpu.roll(gram, 4, 0)

    def entry(kind, i, j, second):
        value = jnp.broadcast_to(gram[:, places[kind, i, j] : places[kind, i, j] + 1], (8, 128))
        return pltpu.roll(value, 6, 0) if second else value

    chain = ITERS + 1
    inner = {}
    for i in range(chain):
        for j in range(chain):
            inner[i, j] = entry("same", min(i, j), max(i, j), False)
            if i < ITERS and j < ITERS:
                inner[chain + i, chain + j] = entry("same", min(i, j), max(i, j), True)
            if j < ITERS:
                cross = entry("cross", min(i, j), max(i, j), i > j)
                inner[i, chain + j] = cross
                inner[chain + j, i] = cross

    def bilinear(first, second):
        total = None
        for i, a in first.items():
            inside = None
            for j, b in second.items():
                term = b * inner[i, j]
                inside = term if inside is None else inside + term
            inside = a * inside
            total = inside if total is None else total + inside
        return total

    def combine(base, scale, other):
        result = dict(base)
        for i, value in other.items():
            result[i] = result[i] + scale * value if i in result else scale * value
        return result

    one = jnp.ones((8, 128), F32)
    in_x, in_r, in_p = {}, {chain: one}, {0: one}
    norm_now = inner[chain, chain]
    for it in range(ITERS):
        image = {i + 1: value for i, value in in_p.items()}
        step = norm_now / bilinear(in_p, image)
        in_x = combine(in_x, step, in_p)
        in_r = combine(in_r, -step, image)
        norm_next = bilinear(in_r, in_r)
        in_p = combine(in_r, norm_next / norm_now, in_p)
        norm_now = norm_next

    for f, h in ((0, 0), (0, 1), (1, 0), (1, 1)):
        lanes = slice(128 * h, 128 * h + 128)
        vectors = {}
        for i in range(chain):
            vectors[i] = basis[i, h, pl.ds(f, BLOCKS, stride=4), :]
            if i < ITERS:
                vectors[chain + i] = basis[i, h, pl.ds(2 + f, BLOCKS, stride=4), :]

        def mixed(total, coefficients):
            for i, value in coefficients.items():
                term = value[f : f + 1, :] * vectors[i]
                total = term if total is None else total + term
            return total

        results = (mixed(None, in_x), mixed(None, in_r), mixed(None, in_p))
        for k in range(BLOCKS):
            at = f * BLOCKS + k
            new_sol_ref[at, :, lanes] = sol_rows[at, :, lanes] + results[0][k : k + 1, :]
            new_res_ref[at, :, lanes] = results[1][k : k + 1, :]
            new_dir_ref[at, :, lanes] = results[2][k : k + 1, :]

    for copy in pending:
        copy.wait_send()


INNER = 32
OUTER = 32
INNER_FOURS = INNER // 4
OUTER_FOURS = OUTER // 4
INNER_WIDTH = 16 * INNER
FAST_WIDTH = INNER_WIDTH + 8 * OUTER
FAST_TABLE = 64
P_ROWS = 24


def fast_body(
    sizes,
    stages,
    coord_ref,
    sol_ref,
    res_ref,
    dir_ref,
    pairs_hbm_ref,
    count_ref,
    new_sol_ref,
    new_res_ref,
    new_dir_ref,
    flag_ref,
    own0,
    near0,
    nearq,
    nearp,
    khi_0,
    khi_1,
    khi_2,
    khi_3,
    klo_0,
    klo_1,
    klo_2,
    klo_3,
    own_pieces,
    pieces,
    slot_out,
    onehot,
    basis,
    sums,
    sum_in,
    raw,
    sol_rows,
    pairs_vec_ref,
    own_columns,
    lists,
    inner_rows,
    outer_rows,
    inner_entries,
    outer_entries,
    load_sems,
    entry_sems,
    list_send,
    list_recv,
    near_send,
    near_recv,
    q_send,
    q_recv,
    sum_send,
    sum_recv,
):
    wide_size, narrow_size = sizes
    wide = lax.axis_index("wide")
    narrow = lax.axis_index("narrow")
    neighbours = []
    for d in range(9):
        if d != 4:
            to_wide = (wide + (d // 3 - 1) + wide_size) % wide_size
            to_narrow = (narrow + (d % 3 - 1) + narrow_size) % narrow_size
            neighbours.append((d, (to_wide, to_narrow)))
    peers = stage_peers(wide, narrow, stages)

    loads = [
        pltpu.make_async_copy(source, landing, load_sems.at[at])
        for at, (source, landing) in enumerate(
            (
                (pairs_hbm_ref, pairs_vec_ref),
                (dir_ref, raw.at[pl.ds(0, 2 * BLOCKS)]),
                (res_ref, raw.at[pl.ds(2 * BLOCKS, 2 * BLOCKS)]),
                (coord_ref, raw.at[pl.ds(4 * BLOCKS, 3 * BLOCKS)]),
                (sol_ref, sol_rows),
            )
        )
    ]
    for load in loads:
        load.start()

    barrier = pltpu.get_barrier_semaphore()
    targets = [device for _, device in neighbours] + [device for group in peers for device in group]
    for device in targets:
        pl.semaphore_signal(barrier, inc=1, device_id=device, device_id_type=MESH)

    for load in loads:
        load.wait()
    live = lax.broadcasted_iota(jnp.int32, (2, SLOTS), 1) < count_ref[0:1, 0:1]
    own_list = jnp.where(live, pairs_vec_ref[...], 255).astype(F32)
    own_list = jnp.concatenate([own_list, jnp.full((2, 128 - SLOTS), 255.0, F32)], axis=1)
    lists[4] = jnp.concatenate([own_list, jnp.full((6, 128), 255.0, F32)], axis=0)
    for k in range(BLOCKS):
        for c in range(7):
            own0[k, c : c + 1, :] = raw[c * BLOCKS + k]
        own0[k, 7:8, :] = jnp.zeros((1, NODES), F32)

    pl.semaphore_wait(barrier, len(targets))

    pending = []

    def exchange(source, landing, send_sem, recv_sem):
        for at, (d, device) in enumerate(neighbours):
            copy = pltpu.make_async_remote_copy(
                src_ref=source,
                dst_ref=landing(8 - d),
                send_sem=send_sem.at[at],
                recv_sem=recv_sem.at[7 - at],
                device_id=device,
                device_id_type=MESH,
            )
            copy.start()
            pending.append(copy)

        def wait(at):
            pltpu.make_async_remote_copy(
                src_ref=source,
                dst_ref=landing(at + at // 4),
                send_sem=send_sem.at[at],
                recv_sem=recv_sem.at[at],
                device_id=neighbours[0][1],
                device_id_type=MESH,
            ).wait_recv()

        return wait

    list_arrive = exchange(lists.at[4], lambda d: lists.at[d], list_send, list_recv)
    near_arrive = exchange(
        own0,
        lambda d: near0.at[pl.ds(d * BLOCKS, BLOCKS)],
        near_send,
        near_recv,
    )

    half = lax.broadcasted_iota(jnp.int32, (8, NODES), 0) < 4

    def put_pieces(to, j, rows_at, value):
        high = value.astype(BF16).astype(F32)
        low = value - high
        if rows_at == 0:
            rows = jnp.where(half, high, pltpu.roll(low, 4, 0))
        else:
            rows = jnp.where(half, pltpu.roll(high, 4, 0), low)
        to[j] = jnp.concatenate([rows, rows], axis=0).astype(BF16)

    for h in range(2):
        for k in range(BLOCKS):
            basis[0, h, 4 * k : 4 * k + 4, :] = own0[k, 0:4, 128 * h : 128 * h + 128]
        basis[0, h, 4 * BLOCKS : ROWS, :] = jnp.zeros((ROWS - 4 * BLOCKS, 128), F32)

    def own_block(k, carry):
        value = own0[k]
        put_pieces(own_pieces, k, 0, value)
        turned = jnp.transpose(value)
        for axis in range(3):
            own_columns[k, axis] = jnp.broadcast_to(turned[:, 4 + axis : 5 + axis], (NODES, 128))
        return carry

    lax.fori_loop(0, BLOCKS, own_block, 0)

    before_lane = lax.broadcasted_iota(jnp.int32, (128, 128), 0) < lax.broadcasted_iota(
        jnp.int32, (128, 128), 1
    )
    before_lane = jnp.where(before_lane, 1.0, 0.0).astype(BF16)
    entry_of = lax.broadcasted_iota(jnp.int32, (128, 128), 0).astype(F32)
    row_of = lax.broadcasted_iota(jnp.int32, (8, 128), 0)

    def compact(wanted_rows, codes, rows, most_entries):
        count = wanted_rows.shape[0]
        before_row = lax.broadcasted_iota(jnp.int32, (count, count), 0) > lax.broadcasted_iota(
            jnp.int32, (count, count), 1
        )
        in_row = dot_bf16(wanted_rows.astype(BF16), before_lane, False)
        row_total = jnp.broadcast_to(jnp.sum(wanted_rows, axis=1, keepdims=True), (count, 128))
        rank = in_row + dot_bf16(
            jnp.where(before_row, 1.0, 0.0).astype(BF16), row_total.astype(BF16), False
        )
        everything = jnp.sum(row_total, axis=0, keepdims=True)
        rank = jnp.where(wanted_rows > 0.5, rank, -1.0)
        gathered = jnp.zeros((128, 128), F32)
        for row in rows:
            gathered = gathered + jnp.where(
                entry_of == rank[row : row + 1, :], codes[row : row + 1, :], 0.0
            )
        gathered = jnp.broadcast_to(jnp.sum(gathered, axis=1, keepdims=True), (128, 128))
        code = jnp.transpose(gathered)[0:8, :].astype(jnp.int32)
        return code, jnp.where(everything > most_entries + 0.5, 1.0, 0.0)

    def fill_onehot(start, wanted):
        width = wanted.shape[1]
        for first in range(0, FAST_TABLE, CHUNK):
            row = lax.broadcasted_iota(jnp.int32, (CHUNK, width), 0) + first
            lane = lax.broadcasted_iota(jnp.int32, (CHUNK, width), 1)
            second = row - ROWS
            block = jnp.where(row < ROWS, row >> 2, second >> 1)
            vector = jnp.where(row < ROWS, row & 3, second & 1)
            match = (block == wanted) & (vector == (lane & 3))
            onehot[first : first + CHUNK, start : start + width] = jnp.where(
                match, 1.0, 0.0
            ).astype(BF16)

    def spread_over(targets_rows, width, shift):
        entry_row = lax.broadcasted_iota(jnp.int32, (128, width), 0)
        entry_lane = lax.broadcasted_iota(jnp.int32, (128, width), 1) >> shift
        spread = jnp.where(entry_row == entry_lane, 1.0, 0.0).astype(BF16)
        return dot_bf16(targets_rows.astype(F32).astype(BF16), spread, False).astype(jnp.int32)

    own_ids = lists[4]
    own_left = jnp.broadcast_to(own_ids[0:1, :], (8, 128)) - 4.0 * BLOCKS
    own_right = jnp.broadcast_to(own_ids[1:2, :], (8, 128)) - 4.0 * BLOCKS
    inside = (own_left > -0.5) & (own_left < BLOCKS - 0.5) & (own_right > -0.5) & (own_right < BLOCKS - 0.5)
    code, overflow = compact(
        jnp.where(inside & (row_of == 0), 1.0, 0.0), own_left * 128.0 + own_right + 1.0, (0,), INNER
    )
    filled = code > 0
    code = jnp.maximum(code - 1, 0)
    inner_left, inner_right = code >> 7, code & 127
    inner_rows[...] = jnp.where(row_of == 0, inner_left, inner_right)
    inner_load = pltpu.make_async_copy(inner_rows, inner_entries, entry_sems.at[0])
    inner_load.start()
    ends = jnp.where(row_of == 0, inner_left, inner_right)
    ends = jnp.where(filled & ((row_of == 0) | (inner_left != inner_right)), ends, 200)
    wanted = spread_over(ends, INNER_WIDTH, 4)
    lane = lax.broadcasted_iota(jnp.int32, (1, INNER_WIDTH), 1)
    fill_onehot(0, jnp.where((lane & 8) == 0, wanted[0:1, :], wanted[1:2, :]))
    inner_load.wait()

    def evaluate(block, other, refs, at):
        high_ref, low_ref = refs
        block = jnp.clip(block, 0, BLOCKS - 1)
        for h in range(2):
            lanes = slice(128 * h, 128 * h + 128)
            others = [
                jnp.broadcast_to(other[4 + axis : 5 + axis, lanes], (CHUNK, 128)) for axis in range(3)
            ]
            for first in range(0, NODES, CHUNK):
                squared = None
                for axis in range(3):
                    offset = own_columns[block, axis, first : first + CHUNK, :] - others[axis]
                    squared = offset * offset if squared is None else squared + offset * offset
                squared = jnp.minimum(squared, RADIUS * RADIUS)
                distance = squared * lax.rsqrt(jnp.maximum(squared, 1e-36))
                rest = RADIUS - distance
                rest = rest * rest
                rest = rest * rest
                high, low = split(rest * (PHI_SLOPE * distance + PHI_CONST))
                high_ref[at, first : first + CHUNK, lanes] = high
                low_ref[at, first : first + CHUNK, lanes] = low

    def evaluate_inner(e, refs, at):
        other = own0[jnp.clip(inner_entries[1, e], 0, BLOCKS - 1)]
        evaluate(inner_entries[0, e], other, refs, at)

    def evaluate_outer(e, refs, at):
        other = near0[jnp.clip(outer_entries[1, e], 0, 9 * BLOCKS - 1)]
        evaluate(outer_entries[0, e], other, refs, at)

    def product_inner(e, refs, at):
        high, low = refs[0][at], refs[1][at]
        left = own_pieces[jnp.clip(inner_entries[0, e], 0, BLOCKS - 1)]
        right = own_pieces[jnp.clip(inner_entries[1, e], 0, BLOCKS - 1)]
        to_left = dot_bf16(right, high, True) + dot_bf16(right, low, True)
        to_right = dot_bf16(left, high, False) + dot_bf16(left, low, False)
        start = pl.multiple_of(e * 16, 16)
        slot_out[pl.ds(start, 8), :] = to_left[0:8]
        slot_out[pl.ds(start + 8, 8), :] = to_right[0:8]

    def product_outer(e, refs, at):
        other = pieces[jnp.clip(outer_entries[1, e], 0, 9 * BLOCKS - 1)]
        result = dot_bf16(other, refs[0][at], True) + dot_bf16(other, refs[1][at], True)
        slot_out[pl.ds(pl.multiple_of(INNER_WIDTH + e * 8, 8), 8), :] = result[0:8]

    tiles_of = ((khi_0, klo_0), (khi_1, klo_1), (khi_2, klo_2), (khi_3, klo_3))

    def evaluate_and_multiply(evaluate_one, product_one, start, fours):
        def step(t, carry):
            before = jnp.maximum(t - 1, 0)
            for u, refs in enumerate(tiles_of):
                product_one(4 * before + u, refs, start + before)
                evaluate_one(4 * t + u, refs, start + t)
            return carry

        lax.fori_loop(0, fours, step, 0)
        for u, refs in enumerate(tiles_of):
            product_one(4 * (fours - 1) + u, refs, start + fours - 1)

    def multiply(product_one, start, fours):
        group = 4

        def step(g, carry):
            for at in range(group):
                for u, refs in enumerate(tiles_of):
                    product_one(4 * (g * group + at) + u, refs, start + g * group + at)
            return carry

        lax.fori_loop(0, fours // group, step, 0)

    evaluate_and_multiply(evaluate_inner, product_inner, 0, INNER_FOURS)

    for at in range(8):
        list_arrive(at)
    dead_rows = jnp.full((7, 128), 255.0, F32)
    device_row = lax.broadcasted_iota(jnp.int32, (16, 128), 0)
    add_wide = (device_row * 11 >> 5) - 1
    add_narrow = device_row - (add_wide + 1) * 3 - 1

    def here(row):
        ids = jnp.concatenate([lists[d, row : row + 1, :] for d in range(9)] + [dead_rows], axis=0)
        ids = ids.astype(jnp.int32)
        is_live = ids < 200
        ids = jnp.where(is_live, ids, 0)
        device = ids * 7282 >> 16
        within = ids - device * 9
        at_wide = device * 11 >> 5
        at_narrow = device - at_wide * 3 + add_narrow
        at_wide = at_wide + add_wide
        mine = is_live & (at_wide == 1) & (at_narrow == 1)
        return mine, within, at_wide * 27 + at_narrow * 9 + within

    left_mine, left_within, left_here = here(0)
    right_mine, right_within, right_here = here(1)
    wanted_rows = jnp.concatenate(
        [
            jnp.where(left_mine & jnp.logical_not(right_mine), 1.0, 0.0),
            jnp.where(right_mine & jnp.logical_not(left_mine), 1.0, 0.0),
        ],
        axis=0,
    )
    codes = jnp.concatenate(
        [left_within * 128 + right_here + 1, right_within * 128 + left_here + 1], axis=0
    ).astype(F32)
    code, too_many = compact(wanted_rows, codes, (*range(9), *range(16, 25)), OUTER)
    overflow = overflow + too_many
    filled = code > 0
    code = jnp.maximum(code - 1, 0)
    outer_rows[...] = jnp.where(row_of == 0, code >> 7, code & 127)
    outer_load = pltpu.make_async_copy(outer_rows, outer_entries, entry_sems.at[1])
    outer_load.start()
    fill_onehot(INNER_WIDTH, spread_over(jnp.where(filled, code >> 7, 200), 8 * OUTER, 3)[0:1, :])

    def prepare_next(at, carry):
        near_arrive(at)
        for k in range(BLOCKS):
            j = (at + at // 4) * BLOCKS + k
            put_pieces(pieces, j, 0, near0[j])
        return carry

    lax.fori_loop(0, 8, prepare_next, 0)
    outer_load.wait()
    evaluate_and_multiply(evaluate_outer, product_outer, INNER_FOURS, OUTER_FOURS)

    for it in range(ITERS):
        if it > 0:
            multiply(product_inner, 0, INNER_FOURS)
            refresh_others()
            multiply(product_outer, INNER_FOURS, OUTER_FOURS)
        high, low = split(slot_out[...])
        table = onehot[...]
        image = dot_bf16(table, high, False) + dot_bf16(table, low, False)
        for h in range(2):
            basis[it + 1, h] = image[0:ROWS, 128 * h : 128 * h + 128]
        if it == 0:
            nearq[4] = image[0:ROWS]
            arrive = exchange(nearq.at[4], lambda d: nearq.at[d], q_send.at[it], q_recv.at[it])

            def refresh(d, to, first_block):
                for k in range(0, BLOCKS, 2):
                    value = nearq[d, 4 * k : 4 * k + 8, :]
                    put_pieces(to, first_block + k, 0, value)
                    if k + 1 < BLOCKS:
                        put_pieces(to, first_block + k + 1, 4, value)

            refresh(4, own_pieces, 0)

            def refresh_others(arrive=arrive, refresh=refresh):
                def refresh_next(at, carry):
                    arrive(at)
                    d = at + at // 4
                    refresh(d, pieces, d * BLOCKS)
                    return carry

                lax.fori_loop(0, 8, refresh_next, 0)

        elif it + 1 < ITERS:
            nearp[4] = image[ROWS : ROWS + P_ROWS]
            arrive_p = exchange(nearp.at[4], lambda d: nearp.at[d], q_send.at[it], q_recv.at[it])

            def refresh_p(d, to, first_block):
                for k in range(BLOCKS):
                    value = nearp[d, k // 4 * 8 : k // 4 * 8 + 8, :]
                    if k % 4:
                        value = pltpu.roll(value, 8 - k % 4 * 2, 0)
                    put_pieces(to, first_block + k, 0, value)

            refresh_p(4, own_pieces, 0)

            def refresh_others(arrive=arrive_p, refresh=refresh_p):
                def refresh_next(at, carry):
                    arrive(at)
                    d = at + at // 4
                    refresh(d, pieces, d * BLOCKS)
                    return carry

                lax.fori_loop(0, 8, refresh_next, 0)

    lane = lax.broadcasted_iota(jnp.int32, (8, 128), 1)
    forward = lax.broadcasted_iota(jnp.int32, (8, 128), 0) % 4 < 2

    def swapped(value):
        return jnp.where(forward, pltpu.roll(value, 6, 0), pltpu.roll(value, 2, 0))

    tiles = [
        [basis[i, h, g : g + 8, :] for h in range(2) for g in range(0, ROWS, 8)]
        for i in range(ITERS + 1)
    ]
    crossed = [[swapped(tile) for tile in row] for row in tiles]
    places = {}
    gram = jnp.zeros((8, 128), F32)
    for i in range(ITERS + 1):
        for j in range(i, ITERS + 1):
            for kind, other in (("same", tiles), ("cross", crossed)):
                total = None
                for mine, theirs in zip(tiles[i], other[j]):
                    term = mine * theirs
                    total = term if total is None else total + term
                column = jnp.sum(total, axis=1, keepdims=True)
                places[kind, i, j] = len(places)
                gram = jnp.where(lane == places[kind, i, j], column, gram)

    gram = jnp.where(lane == 127, overflow, gram)

    for stage, group_peers in enumerate(peers):
        sums[stage] = gram
        copies = []
        for at, device in enumerate(group_peers):
            copy = pltpu.make_async_remote_copy(
                src_ref=sums.at[stage],
                dst_ref=sum_in.at[stage, at],
                send_sem=sum_send.at[stage, at],
                recv_sem=sum_recv.at[stage, at],
                device_id=device,
                device_id_type=MESH,
            )
            copy.start()
            copies.append(copy)
        pending.extend(copies)
        for at, copy in enumerate(copies):
            copy.wait_recv()
            gram = gram + sum_in[stage, at]
    flag_ref[0, 0] = jnp.sum(jnp.where((lane == 127) & (half[:, 0:128]), gram, 0.0))
    gram = gram + pltpu.roll(gram, 4, 0)

    def entry(kind, i, j, second):
        value = jnp.broadcast_to(gram[:, places[kind, i, j] : places[kind, i, j] + 1], (8, 128))
        return pltpu.roll(value, 6, 0) if second else value

    chain = ITERS + 1
    inner = {}
    for i in range(chain):
        for j in range(chain):
            inner[i, j] = entry("same", min(i, j), max(i, j), False)
            if i < ITERS and j < ITERS:
                inner[chain + i, chain + j] = entry("same", min(i, j), max(i, j), True)
            if j < ITERS:
                cross = entry("cross", min(i, j), max(i, j), i > j)
                inner[i, chain + j] = cross
                inner[chain + j, i] = cross

    def bilinear(first, second):
        total = None
        for i, a in first.items():
            inside = None
            for j, b in second.items():
                term = b * inner[i, j]
                inside = term if inside is None else inside + term
            inside = a * inside
            total = inside if total is None else total + inside
        return total

    def combine(base, scale, other):
        result = dict(base)
        for i, value in other.items():
            result[i] = result[i] + scale * value if i in result else scale * value
        return result

    one = jnp.ones((8, 128), F32)
    in_x, in_r, in_p = {}, {chain: one}, {0: one}
    norm_now = inner[chain, chain]
    for it in range(ITERS):
        image = {i + 1: value for i, value in in_p.items()}
        step = norm_now / bilinear(in_p, image)
        in_x = combine(in_x, step, in_p)
        in_r = combine(in_r, -step, image)
        norm_next = bilinear(in_r, in_r)
        in_p = combine(in_r, norm_next / norm_now, in_p)
        norm_now = norm_next

    for f, h in ((0, 0), (0, 1), (1, 0), (1, 1)):
        lanes = slice(128 * h, 128 * h + 128)
        vectors = {}
        for i in range(chain):
            vectors[i] = basis[i, h, pl.ds(f, BLOCKS, stride=4), :]
            if i < ITERS:
                vectors[chain + i] = basis[i, h, pl.ds(2 + f, BLOCKS, stride=4), :]

        def mixed(total, coefficients):
            for i, value in coefficients.items():
                term = value[f : f + 1, :] * vectors[i]
                total = term if total is None else total + term
            return total

        results = (mixed(None, in_x), mixed(None, in_r), mixed(None, in_p))
        for k in range(BLOCKS):
            at = f * BLOCKS + k
            new_sol_ref[at, :, lanes] = sol_rows[at, :, lanes] + results[0][k : k + 1, :]
            new_res_ref[at, :, lanes] = results[1][k : k + 1, :]
            new_dir_ref[at, :, lanes] = results[2][k : k + 1, :]

    for copy in pending:
        copy.wait_send()


def solution(mesh):
    sizes = (mesh.shape["wide"], mesh.shape["narrow"])
    if sizes[0] == 64:
        stages = (
            ("narrow", ((1, sizes[1]),)),
            ("wide", ((2, 8),)),
            ("wide", ((16, 4), (1, 2))),
        )
    else:
        stages = (("narrow", ((1, sizes[1]),)), ("wide", ((1, sizes[0]),)))
    most = 0
    for _, places in stages:
        size = 1
        for _, count in places:
            size *= count
        most = max(most, size - 1)

    def on_device(node_coords, solution, residual, direction, tile_pairs, tile_counts):
        full_shape = direction.shape
        fields = jax.ShapeDtypeStruct((2 * BLOCKS, 1, NODES), F32)
        vmem = pl.BlockSpec(memory_space=pltpu.VMEM)
        anywhere = pl.BlockSpec(memory_space=pl.ANY)
        dma = pltpu.SemaphoreType.DMA
        fast = pl.pallas_call(
            functools.partial(fast_body, sizes, stages),
            out_shape=(fields, fields, fields, jax.ShapeDtypeStruct((1, 1), F32)),
            in_specs=[anywhere] * 5 + [vmem],
            out_specs=(vmem, vmem, vmem, pl.BlockSpec(memory_space=pltpu.SMEM)),
            scratch_shapes=[
                pltpu.VMEM((BLOCKS, 8, NODES), F32),
                pltpu.VMEM((9 * BLOCKS, 8, NODES), F32),
                pltpu.VMEM((9, ROWS, NODES), F32),
                pltpu.VMEM((9, P_ROWS, NODES), F32),
                *[pltpu.VMEM((INNER_FOURS + OUTER_FOURS, NODES, NODES), BF16)] * 8,
                pltpu.VMEM((BLOCKS, 16, NODES), BF16),
                pltpu.VMEM((9 * BLOCKS, 16, NODES), BF16),
                pltpu.VMEM((FAST_WIDTH, NODES), F32),
                pltpu.VMEM((FAST_TABLE, FAST_WIDTH), BF16),
                pltpu.VMEM((ITERS + 1, 2, ROWS, 128), F32),
                pltpu.VMEM((len(stages), 8, 128), F32),
                pltpu.VMEM((len(stages), most, 8, 128), F32),
                pltpu.VMEM((7 * BLOCKS, 1, NODES), F32),
                pltpu.VMEM((2 * BLOCKS, 1, NODES), F32),
                pltpu.VMEM((2, SLOTS), jnp.int32),
                pltpu.VMEM((BLOCKS, 3, NODES, 128), F32),
                pltpu.VMEM((9, 8, 128), F32),
                pltpu.VMEM((8, 128), jnp.int32),
                pltpu.VMEM((8, 128), jnp.int32),
                pltpu.SMEM((8, 128), jnp.int32),
                pltpu.SMEM((8, 128), jnp.int32),
                dma((5,)),
                dma((2,)),
                dma((8,)),
                dma((8,)),
                dma((8,)),
                dma((8,)),
                dma((ITERS - 1, 8)),
                dma((ITERS - 1, 8)),
                dma((len(stages), most)),
                dma((len(stages), most)),
            ],
            compiler_params=pltpu.CompilerParams(
                collective_id=0, has_side_effects=True, vmem_limit_bytes=60 * 1024 * 1024
            ),
            cost_estimate=pl.CostEstimate(
                flops=81 * 65536 * 40, bytes_accessed=200000, transcendentals=81 * 65536
            ),
        )
        general = pl.pallas_call(
            functools.partial(general_body, sizes, stages),
            out_shape=(fields, fields, fields),
            in_specs=[anywhere] * 5 + [vmem],
            out_specs=(vmem, vmem, vmem),
            scratch_shapes=[
                pltpu.VMEM((9 * BLOCKS, 8, NODES), F32),
                pltpu.VMEM((ITERS - 1, 9, ROWS, NODES), F32),
                pltpu.VMEM((ITERS, 9, ROWS, NODES), F32),
                pltpu.VMEM((ITERS, 8, ROWS, NODES), F32),
                pltpu.VMEM((SLOTS // 2 + 1, NODES, NODES), BF16),
                pltpu.VMEM((SLOTS // 2 + 1, NODES, NODES), BF16),
                pltpu.VMEM((SLOTS // 2 + 1, NODES, NODES), BF16),
                pltpu.VMEM((SLOTS // 2 + 1, NODES, NODES), BF16),
                pltpu.VMEM((SLOTS // 2 + 1, NODES, NODES), BF16),
                pltpu.VMEM((SLOTS // 2 + 1, NODES, NODES), BF16),
                pltpu.VMEM((SLOTS // 2 + 1, NODES, NODES), BF16),
                pltpu.VMEM((SLOTS // 2 + 1, NODES, NODES), BF16),
                pltpu.VMEM((NODES, NODES), F32),
                pltpu.VMEM((NODES, NODES), F32),
                pltpu.VMEM((9 * BLOCKS, 16, NODES), BF16),
                pltpu.VMEM((512, NODES), F32),
                pltpu.VMEM((TABLE, 512), BF16),
                pltpu.VMEM((ITERS + 1, 2, ROWS, 128), F32),
                pltpu.VMEM((len(stages), 8, 128), F32),
                pltpu.VMEM((len(stages), most, 8, 128), F32),
                pltpu.VMEM((7 * BLOCKS, 1, NODES), F32),
                pltpu.VMEM((2 * BLOCKS, 1, NODES), F32),
                pltpu.SMEM((2, SLOTS), jnp.int32),
                pltpu.VMEM((2, SLOTS), jnp.int32),
                pltpu.VMEM((9 * BLOCKS, NODES, 8), F32),
                dma((6,)),
                dma((8,)),
                dma((8,)),
                dma((ITERS - 1, 8)),
                dma((ITERS - 1, 8)),
                dma((ITERS, 8)),
                dma((ITERS, 8)),
                dma((len(stages), most)),
                dma((len(stages), most)),
            ],
            compiler_params=pltpu.CompilerParams(
                collective_id=1, has_side_effects=True, vmem_limit_bytes=60 * 1024 * 1024
            ),
            cost_estimate=pl.CostEstimate(
                flops=61 * 65536 * 40, bytes_accessed=200000, transcendentals=61 * 65536
            ),
        )
        arguments = (
            node_coords.reshape(3 * BLOCKS, 1, NODES),
            solution.reshape(2 * BLOCKS, 1, NODES),
            residual.reshape(2 * BLOCKS, 1, NODES),
            direction.reshape(2 * BLOCKS, 1, NODES),
            tile_pairs.reshape(2, SLOTS),
            tile_counts,
        )
        *outs, flags = fast(*arguments)
        outs = lax.cond(
            flags[0, 0] > 0.5, lambda *a: tuple(general(*a[3:])), lambda *a: a[:3], *outs, *arguments
        )
        return tuple(out.reshape(full_shape) for out in outs)

    fields_spec = P(None, "wide", "narrow", None, None)
    return jax.shard_map(
        on_device,
        mesh=mesh,
        in_specs=(
            fields_spec,
            fields_spec,
            fields_spec,
            fields_spec,
            P("wide", "narrow", None, None),
            P("wide", "narrow"),
        ),
        out_specs=(fields_spec, fields_spec, fields_spec),
        check_vma=False,
    )
```

```python
import functools

import jax
import jax.numpy as jnp
from jax import lax
from jax.experimental import pallas as pl
from jax.experimental.pallas import tpu as pltpu
from jax.sharding import PartitionSpec as P

ITERS = 3
RADIUS = 0.9
MESH = pl.DeviceIdType.MESH
F32 = jnp.float32
BF16 = jnp.bfloat16

BLOCKS = 9
NODES = 256
SLOTS = 61
ROWS = 40
TABLE = 368
GROUP = 3
CHUNK = 16

PHI_SLOPE = 4.0 / RADIUS**5
PHI_CONST = 1.0 / RADIUS**4


def dot_bf16(left, right, transposed):
    dims = (((1,), (1 if transposed else 0,)), ((), ()))
    return lax.dot_general(left, right, dims, preferred_element_type=F32)


def split(value):
    high = value.astype(BF16)
    return high, (value - high.astype(F32)).astype(BF16)


def stage_peers(wide, narrow, stages):
    peers = []
    for axis, places in stages:
        here = wide if axis == "wide" else narrow
        rank, size = 0, 1
        for stride, count in places:
            rank = rank * count + here // stride % count
            size *= count
        group = []
        for step in range(1, size):
            other = (rank + step) % size
            position = here
            left = other
            for stride, count in reversed(places):
                position = position + (left % count - here // stride % count) * stride
                left = left // count
            group.append((position, narrow) if axis == "wide" else (wide, position))
        peers.append(group)
    return peers


def general_body(
    sizes,
    stages,
    coord_ref,
    sol_ref,
    res_ref,
    dir_ref,
    pairs_hbm_ref,
    count_ref,
    new_sol_ref,
    new_res_ref,
    new_dir_ref,
    near0,
    nearq,
    part,
    got,
    khi_even,
    klo_even,
    khi_odd,
    klo_odd,
    thi_even,
    tlo_even,
    thi_odd,
    tlo_odd,
    stage_even,
    stage_odd,
    pieces,
    slot_out,
    onehot,
    basis,
    sums,
    sum_in,
    raw,
    sol_rows,
    pairs_ref,
    pairs_vec_ref,
    cols,
    load_sems,
    near_send,
    near_recv,
    q_send,
    q_recv,
    fold_send,
    fold_recv,
    sum_send,
    sum_recv,
):
    wide_size, narrow_size = sizes
    wide = lax.axis_index("wide")
    narrow = lax.axis_index("narrow")
    neighbours = []
    for d in range(9):
        if d != 4:
            to_wide = (wide + (d // 3 - 1) + wide_size) % wide_size
            to_narrow = (narrow + (d % 3 - 1) + narrow_size) % narrow_size
            neighbours.append((d, (to_wide, to_narrow)))
    peers = stage_peers(wide, narrow, stages)

    loads = [
        pltpu.make_async_copy(source, landing, load_sems.at[at])
        for at, (source, landing) in enumerate(
            (
                (dir_ref, raw.at[pl.ds(0, 2 * BLOCKS)]),
                (res_ref, raw.at[pl.ds(2 * BLOCKS, 2 * BLOCKS)]),
                (coord_ref, raw.at[pl.ds(4 * BLOCKS, 3 * BLOCKS)]),
                (pairs_hbm_ref, pairs_ref),
                (pairs_hbm_ref, pairs_vec_ref),
                (sol_ref, sol_rows),
            )
        )
    ]
    for load in loads:
        load.start()

    barrier = pltpu.get_barrier_semaphore()
    targets = [device for _, device in neighbours] + [device for group in peers for device in group]
    for device in targets:
        pl.semaphore_signal(barrier, inc=1, device_id=device, device_id_type=MESH)

    for load in loads:
        load.wait()
    for k in range(BLOCKS):
        own = 4 * BLOCKS + k
        for c in range(7):
            near0[own, c : c + 1, :] = raw[c * BLOCKS + k]
        near0[own, 7:8, :] = jnp.zeros((1, NODES), F32)

    pl.semaphore_wait(barrier, len(targets))

    pending = []

    def exchange(source, landing, send_sem, recv_sem):
        copies = []
        for at, (d, device) in enumerate(neighbours):
            copy = pltpu.make_async_remote_copy(
                src_ref=source(d),
                dst_ref=landing(8 - d, 7 - at),
                send_sem=send_sem.at[at],
                recv_sem=recv_sem.at[7 - at],
                device_id=device,
                device_id_type=MESH,
            )
            copy.start()
            copies.append(copy)
        pending.extend(copies)

        def wait(at):
            pltpu.make_async_remote_copy(
                src_ref=source(4),
                dst_ref=landing(at + at // 4, at),
                send_sem=send_sem.at[at],
                recv_sem=recv_sem.at[at],
                device_id=neighbours[0][1],
                device_id_type=MESH,
            ).wait_recv()

        return wait

    arrive = exchange(
        lambda d: near0.at[pl.ds(4 * BLOCKS, BLOCKS)],
        lambda d, at: near0.at[pl.ds(d * BLOCKS, BLOCKS)],
        near_send,
        near_recv,
    )

    slot_of = lax.broadcasted_iota(jnp.int32, (64, 512), 0)
    lane_slot = lax.broadcasted_iota(jnp.int32, (64, 512), 1) // 8
    spread = jnp.where(slot_of == lane_slot, 1.0, 0.0).astype(BF16)
    left_id = pairs_vec_ref[0:1, :]
    right_id = pairs_vec_ref[1:2, :]
    live = lax.broadcasted_iota(jnp.int32, (1, SLOTS), 1) < count_ref[0:1, 0:1]
    toward_left = jnp.where(live, left_id, 255)
    toward_right = jnp.where(live & (left_id != right_id), right_id, 255)
    ids = jnp.concatenate([toward_right, toward_left] + [toward_left] * 6, axis=0).astype(F32)
    ids = jnp.concatenate([ids, jnp.full((8, 64 - SLOTS), 255.0, F32)], axis=1)
    wanted = dot_bf16(ids.astype(BF16), spread, False)
    lane = lax.broadcasted_iota(jnp.int32, (8, 512), 1)
    target = jnp.where(lane % 8 < 4, wanted[0:1, :], wanted[1:2, :]).astype(jnp.int32)
    for first in range(0, TABLE, CHUNK):
        row = lax.broadcasted_iota(jnp.int32, (CHUNK, 512), 0) + first
        place = row % ROWS
        block = jnp.where(place < 4 * BLOCKS, row // ROWS * BLOCKS + place // 4, 200)
        match = (block == target[0:1, :]) & (
            row % 4 == lax.broadcasted_iota(jnp.int32, (CHUNK, 512), 1) % 4
        )
        onehot[pl.ds(first, CHUNK), :] = jnp.where(match, 1.0, 0.0).astype(BF16)

    slot_out[pl.ds(8 * SLOTS, 512 - 8 * SLOTS), :] = jnp.zeros((512 - 8 * SLOTS, NODES), F32)
    half = lax.broadcasted_iota(jnp.int32, (8, NODES), 0) < 4

    def put_pieces(j, rows_at, value):
        high = value.astype(BF16).astype(F32)
        low = value - high
        if rows_at == 0:
            rows = jnp.where(half, high, pltpu.roll(low, 4, 0))
        else:
            rows = jnp.where(half, pltpu.roll(high, 4, 0), low)
        pieces[j] = jnp.concatenate([rows, rows], axis=0).astype(BF16)

    for h in range(2):
        for k in range(BLOCKS):
            basis[0, h, 4 * k : 4 * k + 4, :] = near0[4 * BLOCKS + k, 0:4, 128 * h : 128 * h + 128]
        basis[0, h, 4 * BLOCKS : ROWS, :] = jnp.zeros((ROWS - 4 * BLOCKS, 128), F32)

    def prepare(d):
        for k in range(BLOCKS):
            j = d * BLOCKS + k
            value = near0[j]
            put_pieces(j, 0, value)
            cols[j] = jnp.transpose(value)

    def prepare_next(at, carry):
        arrive(at)
        prepare(at + at // 4)
        return carry

    prepare(4)
    lax.fori_loop(0, 8, prepare_next, 0)

    def evaluate(s, refs, stage, at):
        high_ref, low_ref, high_turned, low_turned = refs
        left = cols.at[pairs_ref[0, s]]
        right = near0[pairs_ref[1, s]]
        rights = [jnp.broadcast_to(right[4 + axis : 5 + axis, :], (CHUNK, NODES)) for axis in range(3)]
        for first in range(0, NODES, CHUNK):
            column = left[first : first + CHUNK, :]
            squared = None
            for axis in range(3):
                offset = column[:, 4 + axis : 5 + axis] - rights[axis]
                squared = offset * offset if squared is None else squared + offset * offset
            squared = jnp.minimum(squared, RADIUS * RADIUS)
            distance = squared * lax.rsqrt(jnp.maximum(squared, 1e-36))
            rest = RADIUS - distance
            rest = rest * rest
            rest = rest * rest
            value = rest * (PHI_SLOPE * distance + PHI_CONST)
            high, low = split(value)
            high_ref[at, first : first + CHUNK, :] = high
            low_ref[at, first : first + CHUNK, :] = low
            stage[first : first + CHUNK, :] = value
        for first in range(0, NODES, 128):
            high, low = split(jnp.transpose(stage[first : first + 128, :]))
            high_turned[at, :, first : first + 128] = high
            low_turned[at, :, first : first + 128] = low

    def product(s, refs, at):
        high_ref, low_ref, high_turned, low_turned = refs
        left = pieces[pairs_ref[0, s]]
        right = pieces[pairs_ref[1, s]]
        to_right = dot_bf16(left, high_ref[at], False) + dot_bf16(left, low_ref[at], False)
        to_left = dot_bf16(right, high_turned[at], False) + dot_bf16(right, low_turned[at], False)
        to_right = to_right[0:8]
        to_left = to_left[0:8]
        to_right = to_right + pltpu.roll(to_right, 4, 0)
        to_left = to_left + pltpu.roll(to_left, 4, 0)
        slot_out[pl.ds(pl.multiple_of(s * 8, 8), 8), :] = jnp.where(half, to_right, to_left)

    even = (khi_even, klo_even, thi_even, tlo_even)
    odd = (khi_odd, klo_odd, thi_odd, tlo_odd)

    def evaluate_and_multiply(t, carry):
        before = jnp.maximum(t - 1, 0)
        product(2 * before, even, before)
        evaluate(2 * t, even, stage_even, t)
        product(2 * before + 1, odd, before)
        evaluate(jnp.minimum(2 * t + 1, SLOTS - 1), odd, stage_odd, t)
        return carry

    def products(g, carry):
        for u in range(GROUP):
            at = g * GROUP + u
            product(2 * at, even, at)
            product(2 * at + 1, odd, at)
        return carry

    for it in range(ITERS):
        if it == 0:
            lax.fori_loop(0, SLOTS // 2 + 1, evaluate_and_multiply, 0)
        else:
            lax.fori_loop(0, SLOTS // 2 // GROUP, products, 0)
        product(SLOTS - 1, even, SLOTS // 2)
        high, low = split(slot_out[...])
        table = onehot[...]
        added = dot_bf16(table, high, False) + dot_bf16(table, low, False)
        for d in range(9):
            part[it, d] = added[d * ROWS : (d + 1) * ROWS]
        arrive = exchange(
            lambda d: part.at[it, d],
            lambda d, at: got.at[it, at],
            fold_send.at[it],
            fold_recv.at[it],
        )
        image = part[it, 4]
        for at in range(8):
            arrive(at)
            image = image + got[it, at]
        for h in range(2):
            basis[it + 1, h] = image[:, 128 * h : 128 * h + 128]
        if it + 1 < ITERS:
            nearq[it, 4] = image
            arrive = exchange(
                lambda d: nearq.at[it, 4],
                lambda d, at: nearq.at[it, d],
                q_send.at[it],
                q_recv.at[it],
            )

            def refresh(d):
                for k in range(0, BLOCKS, 2):
                    value = nearq[it, d, 4 * k : 4 * k + 8, :]
                    put_pieces(d * BLOCKS + k, 0, value)
                    if k + 1 < BLOCKS:
                        put_pieces(d * BLOCKS + k + 1, 4, value)

            def refresh_next(at, carry):
                arrive(at)
                refresh(at + at // 4)
                return carry

            refresh(4)
            lax.fori_loop(0, 8, refresh_next, 0)

    lane = lax.broadcasted_iota(jnp.int32, (8, 128), 1)
    forward = lax.broadcasted_iota(jnp.int32, (8, 128), 0) % 4 < 2

    def swapped(value):
        return jnp.where(forward, pltpu.roll(value, 6, 0), pltpu.roll(value, 2, 0))

    tiles = [
        [basis[i, h, g : g + 8, :] for h in range(2) for g in range(0, ROWS, 8)]
        for i in range(ITERS + 1)
    ]
    crossed = [[swapped(tile) for tile in row] for row in tiles]
    places = {}
    gram = jnp.zeros((8, 128), F32)
    for i in range(ITERS + 1):
        for j in range(i, ITERS + 1):
            for kind, other in (("same", tiles), ("cross", crossed)):
                total = None
                for mine, theirs in zip(tiles[i], other[j]):
                    term = mine * theirs
                    total = term if total is None else total + term
                column = jnp.sum(total, axis=1, keepdims=True)
                places[kind, i, j] = len(places)
                gram = jnp.where(lane == places[kind, i, j], column, gram)

    for stage, group_peers in enumerate(peers):
        sums[stage] = gram
        copies = []
        for at, device in enumerate(group_peers):
            copy = pltpu.make_async_remote_copy(
                src_ref=sums.at[stage],
                dst_ref=sum_in.at[stage, at],
                send_sem=sum_send.at[stage, at],
                recv_sem=sum_recv.at[stage, at],
                device_id=device,
                device_id_type=MESH,
            )
            copy.start()
            copies.append(copy)
        pending.extend(copies)
        for at, copy in enumerate(copies):
            copy.wait_recv()
            gram = gram + sum_in[stage, at]
    gram = gram + pltpu.roll(gram, 4, 0)

    def entry(kind, i, j, second):
        value = jnp.broadcast_to(gram[:, places[kind, i, j] : places[kind, i, j] + 1], (8, 128))
        return pltpu.roll(value, 6, 0) if second else value

    chain = ITERS + 1
    inner = {}
    for i in range(chain):
        for j in range(chain):
            inner[i, j] = entry("same", min(i, j), max(i, j), False)
            if i < ITERS and j < ITERS:
                inner[chain + i, chain + j] = entry("same", min(i, j), max(i, j), True)
            if j < ITERS:
                cross = entry("cross", min(i, j), max(i, j), i > j)
                inner[i, chain + j] = cross
                inner[chain + j, i] = cross

    def bilinear(first, second):
        total = None
        for i, a in first.items():
            inside = None
            for j, b in second.items():
                term = b * inner[i, j]
                inside = term if inside is None else inside + term
            inside = a * inside
            total = inside if total is None else total + inside
        return total

    def combine(base, scale, other):
        result = dict(base)
        for i, value in other.items():
            result[i] = result[i] + scale * value if i in result else scale * value
        return result

    one = jnp.ones((8, 128), F32)
    in_x, in_r, in_p = {}, {chain: one}, {0: one}
    norm_now = inner[chain, chain]
    for it in range(ITERS):
        image = {i + 1: value for i, value in in_p.items()}
        step = norm_now / bilinear(in_p, image)
        in_x = combine(in_x, step, in_p)
        in_r = combine(in_r, -step, image)
        norm_next = bilinear(in_r, in_r)
        in_p = combine(in_r, norm_next / norm_now, in_p)
        norm_now = norm_next

    for f, h in ((0, 0), (0, 1), (1, 0), (1, 1)):
        lanes = slice(128 * h, 128 * h + 128)
        vectors = {}
        for i in range(chain):
            vectors[i] = basis[i, h, pl.ds(f, BLOCKS, stride=4), :]
            if i < ITERS:
                vectors[chain + i] = basis[i, h, pl.ds(2 + f, BLOCKS, stride=4), :]

        def mixed(total, coefficients):
            for i, value in coefficients.items():
                term = value[f : f + 1, :] * vectors[i]
                total = term if total is None else total + term
            return total

        results = (mixed(None, in_x), mixed(None, in_r), mixed(None, in_p))
        for k in range(BLOCKS):
            at = f * BLOCKS + k
            new_sol_ref[at, :, lanes] = sol_rows[at, :, lanes] + results[0][k : k + 1, :]
            new_res_ref[at, :, lanes] = results[1][k : k + 1, :]
            new_dir_ref[at, :, lanes] = results[2][k : k + 1, :]

    for copy in pending:
        copy.wait_send()


INNER = 29
OUTER = 32
INNER_FOURS = INNER // 4
OUTER_FOURS = OUTER // 4
INNER_WIDTH = 512
FAST_WIDTH = INNER_WIDTH + 8 * OUTER
FAST_TABLE = 64
P_ROWS = 24


def fast_body(
    sizes,
    stages,
    coord_ref,
    sol_ref,
    res_ref,
    dir_ref,
    pairs_hbm_ref,
    count_ref,
    new_sol_ref,
    new_res_ref,
    new_dir_ref,
    flag_ref,
    own0,
    near0,
    nearq,
    nearp,
    khi_0,
    khi_1,
    khi_2,
    khi_3,
    klo_0,
    klo_1,
    klo_2,
    klo_3,
    own_pieces,
    pieces,
    slot_out,
    onehot,
    basis,
    sums,
    sum_in,
    raw,
    sol_rows,
    pairs_vec_ref,
    own_columns,
    lists,
    inner_rows,
    outer_rows,
    inner_entries,
    outer_entries,
    load_sems,
    entry_sems,
    list_send,
    list_recv,
    near_send,
    near_recv,
    q_send,
    q_recv,
    sum_send,
    sum_recv,
):
    wide_size, narrow_size = sizes
    wide = lax.axis_index("wide")
    narrow = lax.axis_index("narrow")
    neighbours = []
    for d in range(9):
        if d != 4:
            to_wide = (wide + (d // 3 - 1) + wide_size) % wide_size
            to_narrow = (narrow + (d % 3 - 1) + narrow_size) % narrow_size
            neighbours.append((d, (to_wide, to_narrow)))
    peers = stage_peers(wide, narrow, stages)

    loads = [
        pltpu.make_async_copy(source, landing, load_sems.at[at])
        for at, (source, landing) in enumerate(
            (
                (pairs_hbm_ref, pairs_vec_ref),
                (dir_ref, raw.at[pl.ds(0, 2 * BLOCKS)]),
                (res_ref, raw.at[pl.ds(2 * BLOCKS, 2 * BLOCKS)]),
                (coord_ref, raw.at[pl.ds(4 * BLOCKS, 3 * BLOCKS)]),
                (sol_ref, sol_rows),
            )
        )
    ]
    for load in loads:
        load.start()

    barrier = pltpu.get_barrier_semaphore()
    targets = [device for _, device in neighbours] + [device for group in peers for device in group]
    for device in targets:
        pl.semaphore_signal(barrier, inc=1, device_id=device, device_id_type=MESH)

    for load in loads:
        load.wait()
    live = lax.broadcasted_iota(jnp.int32, (2, SLOTS), 1) < count_ref[0:1, 0:1]
    own_list = jnp.where(live, pairs_vec_ref[...], 255).astype(F32)
    own_list = jnp.concatenate([own_list, jnp.full((2, 128 - SLOTS), 255.0, F32)], axis=1)
    lists[4] = jnp.concatenate([own_list, jnp.full((6, 128), 255.0, F32)], axis=0)
    for k in range(BLOCKS):
        for c in range(7):
            own0[k, c : c + 1, :] = raw[c * BLOCKS + k]
        own0[k, 7:8, :] = jnp.zeros((1, NODES), F32)

    pl.semaphore_wait(barrier, len(targets))

    pending = []

    def exchange(source, landing, send_sem, recv_sem):
        for at, (d, device) in enumerate(neighbours):
            copy = pltpu.make_async_remote_copy(
                src_ref=source,
                dst_ref=landing(8 - d),
                send_sem=send_sem.at[at],
                recv_sem=recv_sem.at[7 - at],
                device_id=device,
                device_id_type=MESH,
            )
            copy.start()
            pending.append(copy)

        def wait(at):
            pltpu.make_async_remote_copy(
                src_ref=source,
                dst_ref=landing(at + at // 4),
                send_sem=send_sem.at[at],
                recv_sem=recv_sem.at[at],
                device_id=neighbours[0][1],
                device_id_type=MESH,
            ).wait_recv()

        return wait

    list_arrive = exchange(lists.at[4], lambda d: lists.at[d], list_send, list_recv)
    near_arrive = exchange(
        own0,
        lambda d: near0.at[pl.ds(d * BLOCKS, BLOCKS)],
        near_send,
        near_recv,
    )

    half = lax.broadcasted_iota(jnp.int32, (8, NODES), 0) < 4

    def put_pieces(to, j, rows_at, value):
        high = value.astype(BF16).astype(F32)
        low = value - high
        if rows_at == 0:
            rows = jnp.where(half, high, pltpu.roll(low, 4, 0))
        else:
            rows = jnp.where(half, pltpu.roll(high, 4, 0), low)
        to[j] = jnp.concatenate([rows, rows], axis=0).astype(BF16)

    for h in range(2):
        for k in range(BLOCKS):
            basis[0, h, 4 * k : 4 * k + 4, :] = own0[k, 0:4, 128 * h : 128 * h + 128]
        basis[0, h, 4 * BLOCKS : ROWS, :] = jnp.zeros((ROWS - 4 * BLOCKS, 128), F32)

    def own_block(k, carry):
        value = own0[k]
        put_pieces(own_pieces, k, 0, value)
        turned = jnp.transpose(value)
        for axis in range(3):
            own_columns[k, axis] = jnp.broadcast_to(turned[:, 4 + axis : 5 + axis], (NODES, 128))
        return carry

    lax.fori_loop(0, BLOCKS, own_block, 0)

    before_lane = lax.broadcasted_iota(jnp.int32, (128, 128), 0) < lax.broadcasted_iota(
        jnp.int32, (128, 128), 1
    )
    before_lane = jnp.where(before_lane, 1.0, 0.0).astype(BF16)
    entry_of = lax.broadcasted_iota(jnp.int32, (128, 128), 0).astype(F32)
    row_of = lax.broadcasted_iota(jnp.int32, (8, 128), 0)

    def compact(wanted_rows, codes, rows, most_entries):
        count = wanted_rows.shape[0]
        before_row = lax.broadcasted_iota(jnp.int32, (count, count), 0) > lax.broadcasted_iota(
            jnp.int32, (count, count), 1
        )
        in_row = dot_bf16(wanted_rows.astype(BF16), before_lane, False)
        row_total = jnp.broadcast_to(jnp.sum(wanted_rows, axis=1, keepdims=True), (count, 128))
        rank = in_row + dot_bf16(
            jnp.where(before_row, 1.0, 0.0).astype(BF16), row_total.astype(BF16), False
        )
        everything = jnp.sum(row_total, axis=0, keepdims=True)
        rank = jnp.where(wanted_rows > 0.5, rank, -1.0)
        gathered = jnp.zeros((128, 128), F32)
        for row in rows:
            gathered = gathered + jnp.where(
                entry_of == rank[row : row + 1, :], codes[row : row + 1, :], 0.0
            )
        gathered = jnp.broadcast_to(jnp.sum(gathered, axis=1, keepdims=True), (128, 128))
        code = jnp.transpose(gathered)[0:8, :].astype(jnp.int32)
        return code, jnp.where(everything > most_entries + 0.5, 1.0, 0.0)

    def fill_onehot(start, wanted):
        width = wanted.shape[1]
        for first in range(0, FAST_TABLE, CHUNK):
            row = lax.broadcasted_iota(jnp.int32, (CHUNK, width), 0) + first
            lane = lax.broadcasted_iota(jnp.int32, (CHUNK, width), 1)
            second = row - ROWS
            block = jnp.where(row < ROWS, row >> 2, second >> 1)
            vector = jnp.where(row < ROWS, row & 3, second & 1)
            match = (block == wanted) & (vector == (lane & 3))
            onehot[first : first + CHUNK, start : start + width] = jnp.where(
                match, 1.0, 0.0
            ).astype(BF16)

    def spread_over(targets_rows, width, shift):
        entry_row = lax.broadcasted_iota(jnp.int32, (128, width), 0)
        entry_lane = lax.broadcasted_iota(jnp.int32, (128, width), 1) >> shift
        spread = jnp.where(entry_row == entry_lane, 1.0, 0.0).astype(BF16)
        return dot_bf16(targets_rows.astype(F32).astype(BF16), spread, False).astype(jnp.int32)

    own_ids = lists[4]
    own_left = jnp.broadcast_to(own_ids[0:1, :], (8, 128)) - 4.0 * BLOCKS
    own_right = jnp.broadcast_to(own_ids[1:2, :], (8, 128)) - 4.0 * BLOCKS
    inside = (own_left > -0.5) & (own_left < BLOCKS - 0.5) & (own_right > -0.5) & (own_right < BLOCKS - 0.5)
    code, overflow = compact(
        jnp.where(inside & (row_of == 0), 1.0, 0.0), own_left * 128.0 + own_right + 1.0, (0,), INNER
    )
    filled = code > 0
    code = jnp.maximum(code - 1, 0)
    inner_left, inner_right = code >> 7, code & 127
    inner_rows[...] = jnp.where(row_of == 0, inner_left, inner_right)
    inner_load = pltpu.make_async_copy(inner_rows, inner_entries, entry_sems.at[0])
    inner_load.start()
    ends = jnp.where(row_of == 0, inner_left, inner_right)
    ends = jnp.where(filled & ((row_of == 0) | (inner_left != inner_right)), ends, 200)
    wanted = spread_over(ends, INNER_WIDTH, 4)
    lane = lax.broadcasted_iota(jnp.int32, (1, INNER_WIDTH), 1)
    fill_onehot(0, jnp.where((lane & 8) == 0, wanted[0:1, :], wanted[1:2, :]))
    inner_load.wait()

    def evaluate(block, other, refs, at):
        high_ref, low_ref = refs
        block = jnp.clip(block, 0, BLOCKS - 1)
        for h in range(2):
            lanes = slice(128 * h, 128 * h + 128)
            others = [
                jnp.broadcast_to(other[4 + axis : 5 + axis, lanes], (CHUNK, 128)) for axis in range(3)
            ]
            for first in range(0, NODES, CHUNK):
                squared = None
                for axis in range(3):
                    offset = own_columns[block, axis, first : first + CHUNK, :] - others[axis]
                    squared = offset * offset if squared is None else squared + offset * offset
                squared = jnp.minimum(squared, RADIUS * RADIUS)
                distance = squared * lax.rsqrt(jnp.maximum(squared, 1e-36))
                rest = RADIUS - distance
                rest = rest * rest
                rest = rest * rest
                high, low = split(rest * (PHI_SLOPE * distance + PHI_CONST))
                high_ref[at, first : first + CHUNK, lanes] = high
                low_ref[at, first : first + CHUNK, lanes] = low

    def evaluate_inner(e, refs, at):
        other = own0[jnp.clip(inner_entries[1, e], 0, BLOCKS - 1)]
        evaluate(inner_entries[0, e], other, refs, at)

    def evaluate_outer(e, refs, at):
        other = near0[jnp.clip(outer_entries[1, e], 0, 9 * BLOCKS - 1)]
        evaluate(outer_entries[0, e], other, refs, at)

    def product_inner(e, refs, at):
        high, low = refs[0][at], refs[1][at]
        left = own_pieces[jnp.clip(inner_entries[0, e], 0, BLOCKS - 1)]
        right = own_pieces[jnp.clip(inner_entries[1, e], 0, BLOCKS - 1)]
        to_left = dot_bf16(right, high, True) + dot_bf16(right, low, True)
        to_right = dot_bf16(left, high, False) + dot_bf16(left, low, False)
        start = pl.multiple_of(e * 16, 16)
        slot_out[pl.ds(start, 8), :] = to_left[0:8]
        slot_out[pl.ds(start + 8, 8), :] = to_right[0:8]

    def product_outer(e, refs, at):
        other = pieces[jnp.clip(outer_entries[1, e], 0, 9 * BLOCKS - 1)]
        result = dot_bf16(other, refs[0][at], True) + dot_bf16(other, refs[1][at], True)
        slot_out[pl.ds(pl.multiple_of(INNER_WIDTH + e * 8, 8), 8), :] = result[0:8]

    tiles_of = ((khi_0, klo_0), (khi_1, klo_1), (khi_2, klo_2), (khi_3, klo_3))

    def evaluate_and_multiply(evaluate_one, product_one, start, fours):
        def step(t, carry):
            before = jnp.maximum(t - 1, 0)
            for u, refs in enumerate(tiles_of):
                product_one(4 * before + u, refs, start + before)
                evaluate_one(4 * t + u, refs, start + t)
            return carry

        lax.fori_loop(0, fours, step, 0)

    def last_four(product_one, start, fours):
        for u, refs in enumerate(tiles_of):
            product_one(4 * (fours - 1) + u, refs, start + fours - 1)

    def multiply(product_one, start, fours, group):
        def step(g, carry):
            for at in range(group):
                for u, refs in enumerate(tiles_of):
                    product_one(4 * (g * group + at) + u, refs, start + g * group + at)
            return carry

        lax.fori_loop(0, fours // group, step, 0)

    slot_out[16 * INNER : INNER_WIDTH, :] = jnp.zeros((INNER_WIDTH - 16 * INNER, NODES), F32)
    evaluate_and_multiply(evaluate_inner, product_inner, 0, INNER_FOURS)
    for at in range(8):
        list_arrive(at)
    evaluate_inner(INNER - 1, tiles_of[0], INNER_FOURS)
    last_four(product_inner, 0, INNER_FOURS)

    dead_rows = jnp.full((7, 128), 255.0, F32)
    device_row = lax.broadcasted_iota(jnp.int32, (16, 128), 0)
    add_wide = (device_row * 11 >> 5) - 1
    add_narrow = device_row - (add_wide + 1) * 3 - 1

    def here(row):
        ids = jnp.concatenate([lists[d, row : row + 1, :] for d in range(9)] + [dead_rows], axis=0)
        ids = ids.astype(jnp.int32)
        is_live = ids < 200
        ids = jnp.where(is_live, ids, 0)
        device = ids * 7282 >> 16
        within = ids - device * 9
        at_wide = device * 11 >> 5
        at_narrow = device - at_wide * 3 + add_narrow
        at_wide = at_wide + add_wide
        mine = is_live & (at_wide == 1) & (at_narrow == 1)
        return mine, within, at_wide * 27 + at_narrow * 9 + within

    left_mine, left_within, left_here = here(0)
    right_mine, right_within, right_here = here(1)
    wanted_rows = jnp.concatenate(
        [
            jnp.where(left_mine & jnp.logical_not(right_mine), 1.0, 0.0),
            jnp.where(right_mine & jnp.logical_not(left_mine), 1.0, 0.0),
        ],
        axis=0,
    )
    codes = jnp.concatenate(
        [left_within * 128 + right_here + 1, right_within * 128 + left_here + 1], axis=0
    ).astype(F32)
    code, too_many = compact(wanted_rows, codes, (*range(9), *range(16, 25)), OUTER)
    overflow = overflow + too_many
    filled = code > 0
    code = jnp.maximum(code - 1, 0)
    outer_rows[...] = jnp.where(row_of == 0, code >> 7, code & 127)
    outer_load = pltpu.make_async_copy(outer_rows, outer_entries, entry_sems.at[1])
    outer_load.start()
    fill_onehot(INNER_WIDTH, spread_over(jnp.where(filled, code >> 7, 200), 8 * OUTER, 3)[0:1, :])

    product_inner(INNER - 1, tiles_of[0], INNER_FOURS)

    def prepare_next(at, carry):
        near_arrive(at)
        for k in range(BLOCKS):
            j = (at + at // 4) * BLOCKS + k
            put_pieces(pieces, j, 0, near0[j])
        return carry

    lax.fori_loop(0, 8, prepare_next, 0)
    outer_load.wait()
    evaluate_and_multiply(evaluate_outer, product_outer, INNER_FOURS + 1, OUTER_FOURS)
    last_four(product_outer, INNER_FOURS + 1, OUTER_FOURS)

    for it in range(ITERS):
        if it > 0:
            multiply(product_inner, 0, INNER_FOURS, 1)
            product_inner(INNER - 1, tiles_of[0], INNER_FOURS)
            refresh_others()
            multiply(product_outer, INNER_FOURS + 1, OUTER_FOURS, 2)
        high, low = split(slot_out[...])
        table = onehot[...]
        image = dot_bf16(table, high, False) + dot_bf16(table, low, False)
        for h in range(2):
            basis[it + 1, h] = image[0:ROWS, 128 * h : 128 * h + 128]
        if it == 0:
            nearq[4] = image[0:ROWS]
            arrive = exchange(nearq.at[4], lambda d: nearq.at[d], q_send.at[it], q_recv.at[it])

            def refresh(d, to, first_block):
                for k in range(0, BLOCKS, 2):
                    value = nearq[d, 4 * k : 4 * k + 8, :]
                    put_pieces(to, first_block + k, 0, value)
                    if k + 1 < BLOCKS:
                        put_pieces(to, first_block + k + 1, 4, value)

            refresh(4, own_pieces, 0)

            def refresh_others(arrive=arrive, refresh=refresh):
                def refresh_next(at, carry):
                    arrive(at)
                    d = at + at // 4
                    refresh(d, pieces, d * BLOCKS)
                    return carry

                lax.fori_loop(0, 8, refresh_next, 0)

        elif it + 1 < ITERS:
            nearp[4] = image[ROWS : ROWS + P_ROWS]
            arrive_p = exchange(nearp.at[4], lambda d: nearp.at[d], q_send.at[it], q_recv.at[it])

            def refresh_p(d, to, first_block):
                for k in range(BLOCKS):
                    value = nearp[d, k // 4 * 8 : k // 4 * 8 + 8, :]
                    if k % 4:
                        value = pltpu.roll(value, 8 - k % 4 * 2, 0)
                    put_pieces(to, first_block + k, 0, value)

            refresh_p(4, own_pieces, 0)

            def refresh_others(arrive=arrive_p, refresh=refresh_p):
                def refresh_next(at, carry):
                    arrive(at)
                    d = at + at // 4
                    refresh(d, pieces, d * BLOCKS)
                    return carry

                lax.fori_loop(0, 8, refresh_next, 0)

    lane = lax.broadcasted_iota(jnp.int32, (8, 128), 1)
    forward = lax.broadcasted_iota(jnp.int32, (8, 128), 0) % 4 < 2

    def swapped(value):
        return jnp.where(forward, pltpu.roll(value, 6, 0), pltpu.roll(value, 2, 0))

    tiles = [
        [basis[i, h, g : g + 8, :] for h in range(2) for g in range(0, ROWS, 8)]
        for i in range(ITERS + 1)
    ]
    crossed = [[swapped(tile) for tile in row] for row in tiles]
    places = {}
    gram = jnp.zeros((8, 128), F32)
    for i in range(ITERS + 1):
        for j in range(i, ITERS + 1):
            for kind, other in (("same", tiles), ("cross", crossed)):
                total = None
                for mine, theirs in zip(tiles[i], other[j]):
                    term = mine * theirs
                    total = term if total is None else total + term
                column = jnp.sum(total, axis=1, keepdims=True)
                places[kind, i, j] = len(places)
                gram = jnp.where(lane == places[kind, i, j], column, gram)

    gram = jnp.where(lane == 127, overflow, gram)

    for stage, group_peers in enumerate(peers):
        sums[stage] = gram
        copies = []
        for at, device in enumerate(group_peers):
            copy = pltpu.make_async_remote_copy(
                src_ref=sums.at[stage],
                dst_ref=sum_in.at[stage, at],
                send_sem=sum_send.at[stage, at],
                recv_sem=sum_recv.at[stage, at],
                device_id=device,
                device_id_type=MESH,
            )
            copy.start()
            copies.append(copy)
        pending.extend(copies)
        for at, copy in enumerate(copies):
            copy.wait_recv()
            gram = gram + sum_in[stage, at]
    flag_ref[0, 0] = jnp.sum(jnp.where((lane == 127) & (half[:, 0:128]), gram, 0.0))
    gram = gram + pltpu.roll(gram, 4, 0)

    def entry(kind, i, j, second):
        value = jnp.broadcast_to(gram[:, places[kind, i, j] : places[kind, i, j] + 1], (8, 128))
        return pltpu.roll(value, 6, 0) if second else value

    chain = ITERS + 1
    inner = {}
    for i in range(chain):
        for j in range(chain):
            inner[i, j] = entry("same", min(i, j), max(i, j), False)
            if i < ITERS and j < ITERS:
                inner[chain + i, chain + j] = entry("same", min(i, j), max(i, j), True)
            if j < ITERS:
                cross = entry("cross", min(i, j), max(i, j), i > j)
                inner[i, chain + j] = cross
                inner[chain + j, i] = cross

    def bilinear(first, second):
        total = None
        for i, a in first.items():
            inside = None
            for j, b in second.items():
                term = b * inner[i, j]
                inside = term if inside is None else inside + term
            inside = a * inside
            total = inside if total is None else total + inside
        return total

    def combine(base, scale, other):
        result = dict(base)
        for i, value in other.items():
            result[i] = result[i] + scale * value if i in result else scale * value
        return result

    one = jnp.ones((8, 128), F32)
    in_x, in_r, in_p = {}, {chain: one}, {0: one}
    norm_now = inner[chain, chain]
    for it in range(ITERS):
        image = {i + 1: value for i, value in in_p.items()}
        step = norm_now / bilinear(in_p, image)
        in_x = combine(in_x, step, in_p)
        in_r = combine(in_r, -step, image)
        norm_next = bilinear(in_r, in_r)
        in_p = combine(in_r, norm_next / norm_now, in_p)
        norm_now = norm_next

    for f, h in ((0, 0), (0, 1), (1, 0), (1, 1)):
        lanes = slice(128 * h, 128 * h + 128)
        vectors = {}
        for i in range(chain):
            vectors[i] = basis[i, h, pl.ds(f, BLOCKS, stride=4), :]
            if i < ITERS:
                vectors[chain + i] = basis[i, h, pl.ds(2 + f, BLOCKS, stride=4), :]

        def mixed(total, coefficients):
            for i, value in coefficients.items():
                term = value[f : f + 1, :] * vectors[i]
                total = term if total is None else total + term
            return total

        results = (mixed(None, in_x), mixed(None, in_r), mixed(None, in_p))
        for k in range(BLOCKS):
            at = f * BLOCKS + k
            new_sol_ref[at, :, lanes] = sol_rows[at, :, lanes] + results[0][k : k + 1, :]
            new_res_ref[at, :, lanes] = results[1][k : k + 1, :]
            new_dir_ref[at, :, lanes] = results[2][k : k + 1, :]

    for copy in pending:
        copy.wait_send()


def solution(mesh):
    sizes = (mesh.shape["wide"], mesh.shape["narrow"])
    if sizes[0] == 64:
        stages = (
            ("narrow", ((1, sizes[1]),)),
            ("wide", ((2, 8),)),
            ("wide", ((16, 4), (1, 2))),
        )
    else:
        stages = (("narrow", ((1, sizes[1]),)), ("wide", ((1, sizes[0]),)))
    most = 0
    for _, places in stages:
        size = 1
        for _, count in places:
            size *= count
        most = max(most, size - 1)

    def on_device(node_coords, solution, residual, direction, tile_pairs, tile_counts):
        full_shape = direction.shape
        fields = jax.ShapeDtypeStruct((2 * BLOCKS, 1, NODES), F32)
        vmem = pl.BlockSpec(memory_space=pltpu.VMEM)
        anywhere = pl.BlockSpec(memory_space=pl.ANY)
        dma = pltpu.SemaphoreType.DMA
        fast = pl.pallas_call(
            functools.partial(fast_body, sizes, stages),
            out_shape=(fields, fields, fields, jax.ShapeDtypeStruct((1, 1), F32)),
            in_specs=[anywhere] * 5 + [vmem],
            out_specs=(vmem, vmem, vmem, pl.BlockSpec(memory_space=pltpu.SMEM)),
            scratch_shapes=[
                pltpu.VMEM((BLOCKS, 8, NODES), F32),
                pltpu.VMEM((9 * BLOCKS, 8, NODES), F32),
                pltpu.VMEM((9, ROWS, NODES), F32),
                pltpu.VMEM((9, P_ROWS, NODES), F32),
                *[pltpu.VMEM((INNER_FOURS + 1 + OUTER_FOURS, NODES, NODES), BF16)] * 8,
                pltpu.VMEM((BLOCKS, 16, NODES), BF16),
                pltpu.VMEM((9 * BLOCKS, 16, NODES), BF16),
                pltpu.VMEM((FAST_WIDTH, NODES), F32),
                pltpu.VMEM((FAST_TABLE, FAST_WIDTH), BF16),
                pltpu.VMEM((ITERS + 1, 2, ROWS, 128), F32),
                pltpu.VMEM((len(stages), 8, 128), F32),
                pltpu.VMEM((len(stages), most, 8, 128), F32),
                pltpu.VMEM((7 * BLOCKS, 1, NODES), F32),
                pltpu.VMEM((2 * BLOCKS, 1, NODES), F32),
                pltpu.VMEM((2, SLOTS), jnp.int32),
                pltpu.VMEM((BLOCKS, 3, NODES, 128), F32),
                pltpu.VMEM((9, 8, 128), F32),
                pltpu.VMEM((8, 128), jnp.int32),
                pltpu.VMEM((8, 128), jnp.int32),
                pltpu.SMEM((8, 128), jnp.int32),
                pltpu.SMEM((8, 128), jnp.int32),
                dma((5,)),
                dma((2,)),
                dma((8,)),
                dma((8,)),
                dma((8,)),
                dma((8,)),
                dma((ITERS - 1, 8)),
                dma((ITERS - 1, 8)),
                dma((len(stages), most)),
                dma((len(stages), most)),
            ],
            compiler_params=pltpu.CompilerParams(
                collective_id=0, has_side_effects=True, vmem_limit_bytes=60 * 1024 * 1024
            ),
            cost_estimate=pl.CostEstimate(
                flops=81 * 65536 * 40, bytes_accessed=200000, transcendentals=81 * 65536
            ),
        )
        general = pl.pallas_call(
            functools.partial(general_body, sizes, stages),
            out_shape=(fields, fields, fields),
            in_specs=[anywhere] * 5 + [vmem],
            out_specs=(vmem, vmem, vmem),
            scratch_shapes=[
                pltpu.VMEM((9 * BLOCKS, 8, NODES), F32),
                pltpu.VMEM((ITERS - 1, 9, ROWS, NODES), F32),
                pltpu.VMEM((ITERS, 9, ROWS, NODES), F32),
                pltpu.VMEM((ITERS, 8, ROWS, NODES), F32),
                pltpu.VMEM((SLOTS // 2 + 1, NODES, NODES), BF16),
                pltpu.VMEM((SLOTS // 2 + 1, NODES, NODES), BF16),
                pltpu.VMEM((SLOTS // 2 + 1, NODES, NODES), BF16),
                pltpu.VMEM((SLOTS // 2 + 1, NODES, NODES), BF16),
                pltpu.VMEM((SLOTS // 2 + 1, NODES, NODES), BF16),
                pltpu.VMEM((SLOTS // 2 + 1, NODES, NODES), BF16),
                pltpu.VMEM((SLOTS // 2 + 1, NODES, NODES), BF16),
                pltpu.VMEM((SLOTS // 2 + 1, NODES, NODES), BF16),
                pltpu.VMEM((NODES, NODES), F32),
                pltpu.VMEM((NODES, NODES), F32),
                pltpu.VMEM((9 * BLOCKS, 16, NODES), BF16),
                pltpu.VMEM((512, NODES), F32),
                pltpu.VMEM((TABLE, 512), BF16),
                pltpu.VMEM((ITERS + 1, 2, ROWS, 128), F32),
                pltpu.VMEM((len(stages), 8, 128), F32),
                pltpu.VMEM((len(stages), most, 8, 128), F32),
                pltpu.VMEM((7 * BLOCKS, 1, NODES), F32),
                pltpu.VMEM((2 * BLOCKS, 1, NODES), F32),
                pltpu.SMEM((2, SLOTS), jnp.int32),
                pltpu.VMEM((2, SLOTS), jnp.int32),
                pltpu.VMEM((9 * BLOCKS, NODES, 8), F32),
                dma((6,)),
                dma((8,)),
                dma((8,)),
                dma((ITERS - 1, 8)),
                dma((ITERS - 1, 8)),
                dma((ITERS, 8)),
                dma((ITERS, 8)),
                dma((len(stages), most)),
                dma((len(stages), most)),
            ],
            compiler_params=pltpu.CompilerParams(
                collective_id=1, has_side_effects=True, vmem_limit_bytes=60 * 1024 * 1024
            ),
            cost_estimate=pl.CostEstimate(
                flops=61 * 65536 * 40, bytes_accessed=200000, transcendentals=61 * 65536
            ),
        )
        arguments = (
            node_coords.reshape(3 * BLOCKS, 1, NODES),
            solution.reshape(2 * BLOCKS, 1, NODES),
            residual.reshape(2 * BLOCKS, 1, NODES),
            direction.reshape(2 * BLOCKS, 1, NODES),
            tile_pairs.reshape(2, SLOTS),
            tile_counts,
        )
        *outs, flags = fast(*arguments)
        outs = lax.cond(
            flags[0, 0] > 0.5, lambda *a: tuple(general(*a[3:])), lambda *a: a[:3], *outs, *arguments
        )
        return tuple(out.reshape(full_shape) for out in outs)

    fields_spec = P(None, "wide", "narrow", None, None)
    return jax.shard_map(
        on_device,
        mesh=mesh,
        in_specs=(
            fields_spec,
            fields_spec,
            fields_spec,
            fields_spec,
            P("wide", "narrow", None, None),
            P("wide", "narrow"),
        ),
        out_specs=(fields_spec, fields_spec, fields_spec),
        check_vma=False,
    )
```

```python
import functools

import jax
import jax.numpy as jnp
from jax import lax
from jax.experimental import pallas as pl
from jax.experimental.pallas import tpu as pltpu
from jax.sharding import PartitionSpec as P

ITERS = 3
RADIUS = 0.9
MESH = pl.DeviceIdType.MESH
F32 = jnp.float32
BF16 = jnp.bfloat16

BLOCKS = 9
NODES = 256
SLOTS = 61
ROWS = 40
TABLE = 368
GROUP = 3
CHUNK = 16

PHI_SLOPE = 4.0 / RADIUS**5
PHI_CONST = 1.0 / RADIUS**4


def dot_bf16(left, right, transposed):
    dims = (((1,), (1 if transposed else 0,)), ((), ()))
    return lax.dot_general(left, right, dims, preferred_element_type=F32)


def split(value):
    high = value.astype(BF16)
    return high, (value - high.astype(F32)).astype(BF16)


def stage_peers(wide, narrow, stages):
    peers = []
    for axis, places in stages:
        here = wide if axis == "wide" else narrow
        rank, size = 0, 1
        for stride, count in places:
            rank = rank * count + here // stride % count
            size *= count
        group = []
        for step in range(1, size):
            other = (rank + step) % size
            position = here
            left = other
            for stride, count in reversed(places):
                position = position + (left % count - here // stride % count) * stride
                left = left // count
            group.append((position, narrow) if axis == "wide" else (wide, position))
        peers.append(group)
    return peers


def general_body(
    sizes,
    stages,
    coord_ref,
    sol_ref,
    res_ref,
    dir_ref,
    pairs_hbm_ref,
    count_ref,
    new_sol_ref,
    new_res_ref,
    new_dir_ref,
    near0,
    nearq,
    part,
    got,
    khi_even,
    klo_even,
    khi_odd,
    klo_odd,
    thi_even,
    tlo_even,
    thi_odd,
    tlo_odd,
    stage_even,
    stage_odd,
    pieces,
    slot_out,
    onehot,
    basis,
    sums,
    sum_in,
    raw,
    sol_rows,
    pairs_ref,
    pairs_vec_ref,
    cols,
    load_sems,
    near_send,
    near_recv,
    q_send,
    q_recv,
    fold_send,
    fold_recv,
    sum_send,
    sum_recv,
):
    wide_size, narrow_size = sizes
    wide = lax.axis_index("wide")
    narrow = lax.axis_index("narrow")
    neighbours = []
    for d in range(9):
        if d != 4:
            to_wide = (wide + (d // 3 - 1) + wide_size) % wide_size
            to_narrow = (narrow + (d % 3 - 1) + narrow_size) % narrow_size
            neighbours.append((d, (to_wide, to_narrow)))
    peers = stage_peers(wide, narrow, stages)

    loads = [
        pltpu.make_async_copy(source, landing, load_sems.at[at])
        for at, (source, landing) in enumerate(
            (
                (dir_ref, raw.at[pl.ds(0, 2 * BLOCKS)]),
                (res_ref, raw.at[pl.ds(2 * BLOCKS, 2 * BLOCKS)]),
                (coord_ref, raw.at[pl.ds(4 * BLOCKS, 3 * BLOCKS)]),
                (pairs_hbm_ref, pairs_ref),
                (pairs_hbm_ref, pairs_vec_ref),
                (sol_ref, sol_rows),
            )
        )
    ]
    for load in loads:
        load.start()

    barrier = pltpu.get_barrier_semaphore()
    targets = [device for _, device in neighbours] + [device for group in peers for device in group]
    for device in targets:
        pl.semaphore_signal(barrier, inc=1, device_id=device, device_id_type=MESH)

    for load in loads:
        load.wait()
    for k in range(BLOCKS):
        own = 4 * BLOCKS + k
        for c in range(7):
            near0[own, c : c + 1, :] = raw[c * BLOCKS + k]
        near0[own, 7:8, :] = jnp.zeros((1, NODES), F32)

    pl.semaphore_wait(barrier, len(targets))

    pending = []

    def exchange(source, landing, send_sem, recv_sem):
        copies = []
        for at, (d, device) in enumerate(neighbours):
            copy = pltpu.make_async_remote_copy(
                src_ref=source(d),
                dst_ref=landing(8 - d, 7 - at),
                send_sem=send_sem.at[at],
                recv_sem=recv_sem.at[7 - at],
                device_id=device,
                device_id_type=MESH,
            )
            copy.start()
            copies.append(copy)
        pending.extend(copies)

        def wait(at):
            pltpu.make_async_remote_copy(
                src_ref=source(4),
                dst_ref=landing(at + at // 4, at),
                send_sem=send_sem.at[at],
                recv_sem=recv_sem.at[at],
                device_id=neighbours[0][1],
                device_id_type=MESH,
            ).wait_recv()

        return wait

    arrive = exchange(
        lambda d: near0.at[pl.ds(4 * BLOCKS, BLOCKS)],
        lambda d, at: near0.at[pl.ds(d * BLOCKS, BLOCKS)],
        near_send,
        near_recv,
    )

    slot_of = lax.broadcasted_iota(jnp.int32, (64, 512), 0)
    lane_slot = lax.broadcasted_iota(jnp.int32, (64, 512), 1) // 8
    spread = jnp.where(slot_of == lane_slot, 1.0, 0.0).astype(BF16)
    left_id = pairs_vec_ref[0:1, :]
    right_id = pairs_vec_ref[1:2, :]
    live = lax.broadcasted_iota(jnp.int32, (1, SLOTS), 1) < count_ref[0:1, 0:1]
    toward_left = jnp.where(live, left_id, 255)
    toward_right = jnp.where(live & (left_id != right_id), right_id, 255)
    ids = jnp.concatenate([toward_right, toward_left] + [toward_left] * 6, axis=0).astype(F32)
    ids = jnp.concatenate([ids, jnp.full((8, 64 - SLOTS), 255.0, F32)], axis=1)
    wanted = dot_bf16(ids.astype(BF16), spread, False)
    lane = lax.broadcasted_iota(jnp.int32, (8, 512), 1)
    target = jnp.where(lane % 8 < 4, wanted[0:1, :], wanted[1:2, :]).astype(jnp.int32)
    for first in range(0, TABLE, CHUNK):
        row = lax.broadcasted_iota(jnp.int32, (CHUNK, 512), 0) + first
        place = row % ROWS
        block = jnp.where(place < 4 * BLOCKS, row // ROWS * BLOCKS + place // 4, 200)
        match = (block == target[0:1, :]) & (
            row % 4 == lax.broadcasted_iota(jnp.int32, (CHUNK, 512), 1) % 4
        )
        onehot[pl.ds(first, CHUNK), :] = jnp.where(match, 1.0, 0.0).astype(BF16)

    slot_out[pl.ds(8 * SLOTS, 512 - 8 * SLOTS), :] = jnp.zeros((512 - 8 * SLOTS, NODES), F32)
    half = lax.broadcasted_iota(jnp.int32, (8, NODES), 0) < 4

    def put_pieces(j, rows_at, value):
        high = value.astype(BF16).astype(F32)
        low = value - high
        if rows_at == 0:
            rows = jnp.where(half, high, pltpu.roll(low, 4, 0))
        else:
            rows = jnp.where(half, pltpu.roll(high, 4, 0), low)
        pieces[j] = jnp.concatenate([rows, rows], axis=0).astype(BF16)

    for h in range(2):
        for k in range(BLOCKS):
            basis[0, h, 4 * k : 4 * k + 4, :] = near0[4 * BLOCKS + k, 0:4, 128 * h : 128 * h + 128]
        basis[0, h, 4 * BLOCKS : ROWS, :] = jnp.zeros((ROWS - 4 * BLOCKS, 128), F32)

    def prepare(d):
        for k in range(BLOCKS):
            j = d * BLOCKS + k
            value = near0[j]
            put_pieces(j, 0, value)
            cols[j] = jnp.transpose(value)

    def prepare_next(at, carry):
        arrive(at)
        prepare(at + at // 4)
        return carry

    prepare(4)
    lax.fori_loop(0, 8, prepare_next, 0)

    def evaluate(s, refs, stage, at):
        high_ref, low_ref, high_turned, low_turned = refs
        left = cols.at[pairs_ref[0, s]]
        right = near0[pairs_ref[1, s]]
        rights = [jnp.broadcast_to(right[4 + axis : 5 + axis, :], (CHUNK, NODES)) for axis in range(3)]
        for first in range(0, NODES, CHUNK):
            column = left[first : first + CHUNK, :]
            squared = None
            for axis in range(3):
                offset = column[:, 4 + axis : 5 + axis] - rights[axis]
                squared = offset * offset if squared is None else squared + offset * offset
            squared = jnp.minimum(squared, RADIUS * RADIUS)
            distance = squared * lax.rsqrt(jnp.maximum(squared, 1e-36))
            rest = RADIUS - distance
            rest = rest * rest
            rest = rest * rest
            value = rest * (PHI_SLOPE * distance + PHI_CONST)
            high, low = split(value)
            high_ref[at, first : first + CHUNK, :] = high
            low_ref[at, first : first + CHUNK, :] = low
            stage[first : first + CHUNK, :] = value
        for first in range(0, NODES, 128):
            high, low = split(jnp.transpose(stage[first : first + 128, :]))
            high_turned[at, :, first : first + 128] = high
            low_turned[at, :, first : first + 128] = low

    def product(s, refs, at):
        high_ref, low_ref, high_turned, low_turned = refs
        left = pieces[pairs_ref[0, s]]
        right = pieces[pairs_ref[1, s]]
        to_right = dot_bf16(left, high_ref[at], False) + dot_bf16(left, low_ref[at], False)
        to_left = dot_bf16(right, high_turned[at], False) + dot_bf16(right, low_turned[at], False)
        to_right = to_right[0:8]
        to_left = to_left[0:8]
        to_right = to_right + pltpu.roll(to_right, 4, 0)
        to_left = to_left + pltpu.roll(to_left, 4, 0)
        slot_out[pl.ds(pl.multiple_of(s * 8, 8), 8), :] = jnp.where(half, to_right, to_left)

    even = (khi_even, klo_even, thi_even, tlo_even)
    odd = (khi_odd, klo_odd, thi_odd, tlo_odd)

    def evaluate_and_multiply(t, carry):
        before = jnp.maximum(t - 1, 0)
        product(2 * before, even, before)
        evaluate(2 * t, even, stage_even, t)
        product(2 * before + 1, odd, before)
        evaluate(jnp.minimum(2 * t + 1, SLOTS - 1), odd, stage_odd, t)
        return carry

    def products(g, carry):
        for u in range(GROUP):
            at = g * GROUP + u
            product(2 * at, even, at)
            product(2 * at + 1, odd, at)
        return carry

    for it in range(ITERS):
        if it == 0:
            lax.fori_loop(0, SLOTS // 2 + 1, evaluate_and_multiply, 0)
        else:
            lax.fori_loop(0, SLOTS // 2 // GROUP, products, 0)
        product(SLOTS - 1, even, SLOTS // 2)
        high, low = split(slot_out[...])
        table = onehot[...]
        added = dot_bf16(table, high, False) + dot_bf16(table, low, False)
        for d in range(9):
            part[it, d] = added[d * ROWS : (d + 1) * ROWS]
        arrive = exchange(
            lambda d: part.at[it, d],
            lambda d, at: got.at[it, at],
            fold_send.at[it],
            fold_recv.at[it],
        )
        image = part[it, 4]
        for at in range(8):
            arrive(at)
            image = image + got[it, at]
        for h in range(2):
            basis[it + 1, h] = image[:, 128 * h : 128 * h + 128]
        if it + 1 < ITERS:
            nearq[it, 4] = image
            arrive = exchange(
                lambda d: nearq.at[it, 4],
                lambda d, at: nearq.at[it, d],
                q_send.at[it],
                q_recv.at[it],
            )

            def refresh(d):
                for k in range(0, BLOCKS, 2):
                    value = nearq[it, d, 4 * k : 4 * k + 8, :]
                    put_pieces(d * BLOCKS + k, 0, value)
                    if k + 1 < BLOCKS:
                        put_pieces(d * BLOCKS + k + 1, 4, value)

            def refresh_next(at, carry):
                arrive(at)
                refresh(at + at // 4)
                return carry

            refresh(4)
            lax.fori_loop(0, 8, refresh_next, 0)

    lane = lax.broadcasted_iota(jnp.int32, (8, 128), 1)
    forward = lax.broadcasted_iota(jnp.int32, (8, 128), 0) % 4 < 2

    def swapped(value):
        return jnp.where(forward, pltpu.roll(value, 6, 0), pltpu.roll(value, 2, 0))

    tiles = [
        [basis[i, h, g : g + 8, :] for h in range(2) for g in range(0, ROWS, 8)]
        for i in range(ITERS + 1)
    ]
    crossed = [[swapped(tile) for tile in row] for row in tiles]
    places = {}
    gram = jnp.zeros((8, 128), F32)
    for i in range(ITERS + 1):
        for j in range(i, ITERS + 1):
            for kind, other in (("same", tiles), ("cross", crossed)):
                total = None
                for mine, theirs in zip(tiles[i], other[j]):
                    term = mine * theirs
                    total = term if total is None else total + term
                column = jnp.sum(total, axis=1, keepdims=True)
                places[kind, i, j] = len(places)
                gram = jnp.where(lane == places[kind, i, j], column, gram)

    for stage, group_peers in enumerate(peers):
        sums[stage] = gram
        copies = []
        for at, device in enumerate(group_peers):
            copy = pltpu.make_async_remote_copy(
                src_ref=sums.at[stage],
                dst_ref=sum_in.at[stage, at],
                send_sem=sum_send.at[stage, at],
                recv_sem=sum_recv.at[stage, at],
                device_id=device,
                device_id_type=MESH,
            )
            copy.start()
            copies.append(copy)
        pending.extend(copies)
        for at, copy in enumerate(copies):
            copy.wait_recv()
            gram = gram + sum_in[stage, at]
    gram = gram + pltpu.roll(gram, 4, 0)

    def entry(kind, i, j, second):
        value = jnp.broadcast_to(gram[:, places[kind, i, j] : places[kind, i, j] + 1], (8, 128))
        return pltpu.roll(value, 6, 0) if second else value

    chain = ITERS + 1
    inner = {}
    for i in range(chain):
        for j in range(chain):
            inner[i, j] = entry("same", min(i, j), max(i, j), False)
            if i < ITERS and j < ITERS:
                inner[chain + i, chain + j] = entry("same", min(i, j), max(i, j), True)
            if j < ITERS:
                cross = entry("cross", min(i, j), max(i, j), i > j)
                inner[i, chain + j] = cross
                inner[chain + j, i] = cross

    def bilinear(first, second):
        total = None
        for i, a in first.items():
            inside = None
            for j, b in second.items():
                term = b * inner[i, j]
                inside = term if inside is None else inside + term
            inside = a * inside
            total = inside if total is None else total + inside
        return total

    def combine(base, scale, other):
        result = dict(base)
        for i, value in other.items():
            result[i] = result[i] + scale * value if i in result else scale * value
        return result

    one = jnp.ones((8, 128), F32)
    in_x, in_r, in_p = {}, {chain: one}, {0: one}
    norm_now = inner[chain, chain]
    for it in range(ITERS):
        image = {i + 1: value for i, value in in_p.items()}
        step = norm_now / bilinear(in_p, image)
        in_x = combine(in_x, step, in_p)
        in_r = combine(in_r, -step, image)
        norm_next = bilinear(in_r, in_r)
        in_p = combine(in_r, norm_next / norm_now, in_p)
        norm_now = norm_next

    for f, h in ((0, 0), (0, 1), (1, 0), (1, 1)):
        lanes = slice(128 * h, 128 * h + 128)
        vectors = {}
        for i in range(chain):
            vectors[i] = basis[i, h, pl.ds(f, BLOCKS, stride=4), :]
            if i < ITERS:
                vectors[chain + i] = basis[i, h, pl.ds(2 + f, BLOCKS, stride=4), :]

        def mixed(total, coefficients):
            for i, value in coefficients.items():
                term = value[f : f + 1, :] * vectors[i]
                total = term if total is None else total + term
            return total

        results = (mixed(None, in_x), mixed(None, in_r), mixed(None, in_p))
        for k in range(BLOCKS):
            at = f * BLOCKS + k
            new_sol_ref[at, :, lanes] = sol_rows[at, :, lanes] + results[0][k : k + 1, :]
            new_res_ref[at, :, lanes] = results[1][k : k + 1, :]
            new_dir_ref[at, :, lanes] = results[2][k : k + 1, :]

    for copy in pending:
        copy.wait_send()


INNER = 29
OUTER = 32
INNER_FOURS = INNER // 4
OUTER_FOURS = OUTER // 4
INNER_WIDTH = 512
FAST_WIDTH = INNER_WIDTH + 8 * OUTER
FAST_TABLE = 64
P_ROWS = 24


def fast_body(
    sizes,
    stages,
    coord_ref,
    sol_ref,
    res_ref,
    dir_ref,
    pairs_hbm_ref,
    count_ref,
    new_sol_ref,
    new_res_ref,
    new_dir_ref,
    flag_ref,
    pairs_out_ref,
    own0,
    near0,
    nearq,
    nearp,
    khi_0,
    khi_1,
    khi_2,
    khi_3,
    klo_0,
    klo_1,
    klo_2,
    klo_3,
    own_pieces,
    pieces,
    slot_out,
    onehot,
    basis,
    sums,
    sum_in,
    raw,
    sol_rows,
    pairs_vec_ref,
    own_columns,
    lists,
    inner_rows,
    outer_rows,
    inner_entries,
    outer_entries,
    load_sems,
    entry_sems,
    list_send,
    list_recv,
    near_send,
    near_recv,
    q_send,
    q_recv,
    sum_send,
    sum_recv,
):
    wide_size, narrow_size = sizes
    wide = lax.axis_index("wide")
    narrow = lax.axis_index("narrow")
    neighbours = []
    for d in range(9):
        if d != 4:
            to_wide = (wide + (d // 3 - 1) + wide_size) % wide_size
            to_narrow = (narrow + (d % 3 - 1) + narrow_size) % narrow_size
            neighbours.append((d, (to_wide, to_narrow)))
    peers = stage_peers(wide, narrow, stages)

    loads = [
        pltpu.make_async_copy(source, landing, load_sems.at[at])
        for at, (source, landing) in enumerate(
            (
                (pairs_hbm_ref, pairs_vec_ref),
                (dir_ref, raw.at[pl.ds(0, 2 * BLOCKS)]),
                (res_ref, raw.at[pl.ds(2 * BLOCKS, 2 * BLOCKS)]),
                (coord_ref, raw.at[pl.ds(4 * BLOCKS, 3 * BLOCKS)]),
                (sol_ref, sol_rows),
            )
        )
    ]
    for load in loads:
        load.start()

    barrier = pltpu.get_barrier_semaphore()
    targets = [device for _, device in neighbours] + [device for group in peers for device in group]
    for device in targets:
        pl.semaphore_signal(barrier, inc=1, device_id=device, device_id_type=MESH)

    for load in loads:
        load.wait()
    pairs_out_ref[...] = pairs_vec_ref[...]
    live = lax.broadcasted_iota(jnp.int32, (2, SLOTS), 1) < count_ref[0:1, 0:1]
    own_list = jnp.where(live, pairs_vec_ref[...], 255).astype(F32)
    own_list = jnp.concatenate([own_list, jnp.full((2, 128 - SLOTS), 255.0, F32)], axis=1)
    lists[4] = jnp.concatenate([own_list, jnp.full((6, 128), 255.0, F32)], axis=0)
    for k in range(BLOCKS):
        for c in range(7):
            own0[k, c : c + 1, :] = raw[c * BLOCKS + k]
        own0[k, 7:8, :] = jnp.zeros((1, NODES), F32)

    pl.semaphore_wait(barrier, len(targets))

    pending = []

    def exchange(source, landing, send_sem, recv_sem):
        for at, (d, device) in enumerate(neighbours):
            copy = pltpu.make_async_remote_copy(
                src_ref=source,
                dst_ref=landing(8 - d),
                send_sem=send_sem.at[at],
                recv_sem=recv_sem.at[7 - at],
                device_id=device,
                device_id_type=MESH,
            )
            copy.start()
            pending.append(copy)

        def wait(at):
            pltpu.make_async_remote_copy(
                src_ref=source,
                dst_ref=landing(at + at // 4),
                send_sem=send_sem.at[at],
                recv_sem=recv_sem.at[at],
                device_id=neighbours[0][1],
                device_id_type=MESH,
            ).wait_recv()

        return wait

    list_arrive = exchange(lists.at[4], lambda d: lists.at[d], list_send, list_recv)
    near_arrive = exchange(
        own0,
        lambda d: near0.at[pl.ds(d * BLOCKS, BLOCKS)],
        near_send,
        near_recv,
    )

    half = lax.broadcasted_iota(jnp.int32, (8, NODES), 0) < 4

    def put_pieces(to, j, rows_at, value):
        high = value.astype(BF16).astype(F32)
        low = value - high
        if rows_at == 0:
            rows = jnp.where(half, high, pltpu.roll(low, 4, 0))
        else:
            rows = jnp.where(half, pltpu.roll(high, 4, 0), low)
        to[j] = jnp.concatenate([rows, rows], axis=0).astype(BF16)

    for h in range(2):
        for k in range(BLOCKS):
            basis[0, h, 4 * k : 4 * k + 4, :] = own0[k, 0:4, 128 * h : 128 * h + 128]
        basis[0, h, 4 * BLOCKS : ROWS, :] = jnp.zeros((ROWS - 4 * BLOCKS, 128), F32)


    before_lane = lax.broadcasted_iota(jnp.int32, (128, 128), 0) < lax.broadcasted_iota(
        jnp.int32, (128, 128), 1
    )
    before_lane = jnp.where(before_lane, 1.0, 0.0).astype(BF16)
    entry_of = lax.broadcasted_iota(jnp.int32, (128, 128), 0).astype(F32)
    row_of = lax.broadcasted_iota(jnp.int32, (8, 128), 0)

    def compact(wanted_rows, codes, rows, most_entries):
        count = wanted_rows.shape[0]
        before_row = lax.broadcasted_iota(jnp.int32, (count, count), 0) > lax.broadcasted_iota(
            jnp.int32, (count, count), 1
        )
        in_row = dot_bf16(wanted_rows.astype(BF16), before_lane, False)
        row_total = jnp.broadcast_to(jnp.sum(wanted_rows, axis=1, keepdims=True), (count, 128))
        rank = in_row + dot_bf16(
            jnp.where(before_row, 1.0, 0.0).astype(BF16), row_total.astype(BF16), False
        )
        everything = jnp.sum(row_total, axis=0, keepdims=True)
        rank = jnp.where(wanted_rows > 0.5, rank, -1.0)
        gathered = jnp.zeros((128, 128), F32)
        for row in rows:
            gathered = gathered + jnp.where(
                entry_of == rank[row : row + 1, :], codes[row : row + 1, :], 0.0
            )
        gathered = jnp.broadcast_to(jnp.sum(gathered, axis=1, keepdims=True), (128, 128))
        code = jnp.transpose(gathered)[0:8, :].astype(jnp.int32)
        return code, jnp.where(everything > most_entries + 0.5, 1.0, 0.0)

    def fill_onehot(start, wanted):
        width = wanted.shape[1]
        for first in range(0, FAST_TABLE, CHUNK):
            row = lax.broadcasted_iota(jnp.int32, (CHUNK, width), 0) + first
            lane = lax.broadcasted_iota(jnp.int32, (CHUNK, width), 1)
            second = row - ROWS
            block = jnp.where(row < ROWS, row >> 2, second >> 1)
            vector = jnp.where(row < ROWS, row & 3, second & 1)
            match = (block == wanted) & (vector == (lane & 3))
            onehot[first : first + CHUNK, start : start + width] = jnp.where(
                match, 1.0, 0.0
            ).astype(BF16)

    def spread_over(targets_rows, width, shift):
        entry_row = lax.broadcasted_iota(jnp.int32, (128, width), 0)
        entry_lane = lax.broadcasted_iota(jnp.int32, (128, width), 1) >> shift
        spread = jnp.where(entry_row == entry_lane, 1.0, 0.0).astype(BF16)
        return dot_bf16(targets_rows.astype(F32).astype(BF16), spread, False).astype(jnp.int32)

    own_ids = lists[4]
    own_left = jnp.broadcast_to(own_ids[0:1, :], (8, 128)) - 4.0 * BLOCKS
    own_right = jnp.broadcast_to(own_ids[1:2, :], (8, 128)) - 4.0 * BLOCKS
    inside = (own_left > -0.5) & (own_left < BLOCKS - 0.5) & (own_right > -0.5) & (own_right < BLOCKS - 0.5)
    code, overflow = compact(
        jnp.where(inside & (row_of == 0), 1.0, 0.0), own_left * 128.0 + own_right + 1.0, (0,), INNER
    )
    filled = code > 0
    code = jnp.maximum(code - 1, 0)
    inner_left, inner_right = code >> 7, code & 127
    inner_rows[...] = jnp.where(row_of == 0, inner_left, inner_right)
    inner_load = pltpu.make_async_copy(inner_rows, inner_entries, entry_sems.at[0])
    inner_load.start()

    def own_block(k, carry):
        value = own0[k]
        put_pieces(own_pieces, k, 0, value)
        turned = jnp.transpose(value)
        for axis in range(3):
            own_columns[k, axis] = jnp.broadcast_to(turned[:, 4 + axis : 5 + axis], (NODES, 128))
        return carry

    lax.fori_loop(0, BLOCKS, own_block, 0)

    ends = jnp.where(row_of == 0, inner_left, inner_right)
    ends = jnp.where(filled & ((row_of == 0) | (inner_left != inner_right)), ends, 200)
    wanted = spread_over(ends, INNER_WIDTH, 4)
    lane = lax.broadcasted_iota(jnp.int32, (1, INNER_WIDTH), 1)
    fill_onehot(0, jnp.where((lane & 8) == 0, wanted[0:1, :], wanted[1:2, :]))
    inner_load.wait()

    def evaluate(block, other, refs, at):
        high_ref, low_ref = refs
        block = jnp.clip(block, 0, BLOCKS - 1)
        for h in range(2):
            lanes = slice(128 * h, 128 * h + 128)
            others = [
                jnp.broadcast_to(other[4 + axis : 5 + axis, lanes], (CHUNK, 128)) for axis in range(3)
            ]
            for first in range(0, NODES, CHUNK):
                squared = None
                for axis in range(3):
                    offset = own_columns[block, axis, first : first + CHUNK, :] - others[axis]
                    squared = offset * offset if squared is None else squared + offset * offset
                squared = jnp.minimum(squared, RADIUS * RADIUS)
                distance = squared * lax.rsqrt(jnp.maximum(squared, 1e-36))
                rest = RADIUS - distance
                rest = rest * rest
                rest = rest * rest
                high, low = split(rest * (PHI_SLOPE * distance + PHI_CONST))
                high_ref[at, first : first + CHUNK, lanes] = high
                low_ref[at, first : first + CHUNK, lanes] = low

    def evaluate_inner(e, refs, at):
        other = own0[jnp.clip(inner_entries[1, e], 0, BLOCKS - 1)]
        evaluate(inner_entries[0, e], other, refs, at)

    def evaluate_outer(e, refs, at):
        other = near0[jnp.clip(outer_entries[1, e], 0, 9 * BLOCKS - 1)]
        evaluate(outer_entries[0, e], other, refs, at)

    def product_inner(e, refs, at):
        high, low = refs[0][at], refs[1][at]
        left = own_pieces[jnp.clip(inner_entries[0, e], 0, BLOCKS - 1)]
        right = own_pieces[jnp.clip(inner_entries[1, e], 0, BLOCKS - 1)]
        to_left = dot_bf16(right, high, True) + dot_bf16(right, low, True)
        to_right = dot_bf16(left, high, False) + dot_bf16(left, low, False)
        start = pl.multiple_of(e * 16, 16)
        slot_out[pl.ds(start, 8), :] = to_left[0:8]
        slot_out[pl.ds(start + 8, 8), :] = to_right[0:8]

    def product_outer(e, refs, at):
        other = pieces[jnp.clip(outer_entries[1, e], 0, 9 * BLOCKS - 1)]
        result = dot_bf16(other, refs[0][at], True) + dot_bf16(other, refs[1][at], True)
        slot_out[pl.ds(pl.multiple_of(INNER_WIDTH + e * 8, 8), 8), :] = result[0:8]

    tiles_of = ((khi_0, klo_0), (khi_1, klo_1), (khi_2, klo_2), (khi_3, klo_3))

    def evaluate_and_multiply(evaluate_one, product_one, start, fours):
        def step(t, carry):
            before = jnp.maximum(t - 1, 0)
            for u, refs in enumerate(tiles_of):
                product_one(4 * before + u, refs, start + before)
                evaluate_one(4 * t + u, refs, start + t)
            return carry

        lax.fori_loop(0, fours, step, 0)

    def last_four(product_one, start, fours):
        for u, refs in enumerate(tiles_of):
            product_one(4 * (fours - 1) + u, refs, start + fours - 1)

    def multiply(product_one, start, fours, group):
        def step(g, carry):
            for at in range(group):
                for u, refs in enumerate(tiles_of):
                    product_one(4 * (g * group + at) + u, refs, start + g * group + at)
            return carry

        lax.fori_loop(0, fours // group, step, 0)

    slot_out[16 * INNER : INNER_WIDTH, :] = jnp.zeros((INNER_WIDTH - 16 * INNER, NODES), F32)
    evaluate_and_multiply(evaluate_inner, product_inner, 0, INNER_FOURS)
    for at in range(8):
        list_arrive(at)
    evaluate_inner(INNER - 1, tiles_of[0], INNER_FOURS)
    last_four(product_inner, 0, INNER_FOURS)

    dead_rows = jnp.full((7, 128), 255.0, F32)
    device_row = lax.broadcasted_iota(jnp.int32, (16, 128), 0)
    add_wide = (device_row * 11 >> 5) - 1
    add_narrow = device_row - (add_wide + 1) * 3 - 1

    def here(row):
        ids = jnp.concatenate([lists[d, row : row + 1, :] for d in range(9)] + [dead_rows], axis=0)
        ids = ids.astype(jnp.int32)
        is_live = ids < 200
        ids = jnp.where(is_live, ids, 0)
        device = ids * 7282 >> 16
        within = ids - device * 9
        at_wide = device * 11 >> 5
        at_narrow = device - at_wide * 3 + add_narrow
        at_wide = at_wide + add_wide
        mine = is_live & (at_wide == 1) & (at_narrow == 1)
        return mine, within, at_wide * 27 + at_narrow * 9 + within

    left_mine, left_within, left_here = here(0)
    right_mine, right_within, right_here = here(1)
    wanted_rows = jnp.concatenate(
        [
            jnp.where(left_mine & jnp.logical_not(right_mine), 1.0, 0.0),
            jnp.where(right_mine & jnp.logical_not(left_mine), 1.0, 0.0),
        ],
        axis=0,
    )
    codes = jnp.concatenate(
        [left_within * 128 + right_here + 1, right_within * 128 + left_here + 1], axis=0
    ).astype(F32)
    code, too_many = compact(wanted_rows, codes, (*range(9), *range(16, 25)), OUTER)
    overflow = overflow + too_many
    filled = code > 0
    code = jnp.maximum(code - 1, 0)
    outer_rows[...] = jnp.where(row_of == 0, code >> 7, code & 127)
    outer_load = pltpu.make_async_copy(outer_rows, outer_entries, entry_sems.at[1])
    outer_load.start()
    fill_onehot(INNER_WIDTH, spread_over(jnp.where(filled, code >> 7, 200), 8 * OUTER, 3)[0:1, :])

    product_inner(INNER - 1, tiles_of[0], INNER_FOURS)

    def prepare_next(at, carry):
        near_arrive(at)
        for k in range(BLOCKS):
            j = (at + at // 4) * BLOCKS + k
            put_pieces(pieces, j, 0, near0[j])
        return carry

    lax.fori_loop(0, 8, prepare_next, 0)
    outer_load.wait()
    evaluate_and_multiply(evaluate_outer, product_outer, INNER_FOURS + 1, OUTER_FOURS)
    last_four(product_outer, INNER_FOURS + 1, OUTER_FOURS)

    lane = lax.broadcasted_iota(jnp.int32, (8, 128), 1)
    forward = row_of % 4 < 2
    places = {}

    def swapped(value):
        return jnp.where(forward, pltpu.roll(value, 6, 0), pltpu.roll(value, 2, 0))

    def add_products(gram, j):
        tiles = [
            [basis[i, h, g : g + 8, :] for h in range(2) for g in range(0, ROWS, 8)] for i in range(j + 1)
        ]
        crossed = [swapped(tile) for tile in tiles[j]]
        for i in range(j + 1):
            for kind, others in (("same", tiles[j]), ("cross", crossed)):
                total = None
                for mine, theirs in zip(tiles[i], others):
                    term = mine * theirs
                    total = term if total is None else total + term
                column = jnp.sum(total, axis=1, keepdims=True)
                places[kind, i, j] = len(places)
                gram = jnp.where(lane == places[kind, i, j], column, gram)
        return gram

    gram = jnp.zeros((8, 128), F32)
    for it in range(ITERS):
        if it > 0:
            gram = add_products(gram, it - 1)
            if it + 1 == ITERS:
                gram = add_products(gram, it)
            multiply(product_inner, 0, INNER_FOURS, 1)
            product_inner(INNER - 1, tiles_of[0], INNER_FOURS)
            refresh_others()
            multiply(product_outer, INNER_FOURS + 1, OUTER_FOURS, 2)
        high, low = split(slot_out[...])
        table = onehot[...]
        image = dot_bf16(table, high, False) + dot_bf16(table, low, False)
        for h in range(2):
            basis[it + 1, h] = image[0:ROWS, 128 * h : 128 * h + 128]
        if it == 0:
            nearq[4] = image[0:ROWS]
            arrive = exchange(nearq.at[4], lambda d: nearq.at[d], q_send.at[it], q_recv.at[it])

            def refresh(d, to, first_block):
                for k in range(0, BLOCKS, 2):
                    value = nearq[d, 4 * k : 4 * k + 8, :]
                    put_pieces(to, first_block + k, 0, value)
                    if k + 1 < BLOCKS:
                        put_pieces(to, first_block + k + 1, 4, value)

            refresh(4, own_pieces, 0)

            def refresh_others(arrive=arrive, refresh=refresh):
                def refresh_next(at, carry):
                    arrive(at)
                    d = at + at // 4
                    refresh(d, pieces, d * BLOCKS)
                    return carry

                lax.fori_loop(0, 8, refresh_next, 0)

        elif it + 1 < ITERS:
            nearp[4] = image[ROWS : ROWS + P_ROWS]
            arrive_p = exchange(nearp.at[4], lambda d: nearp.at[d], q_send.at[it], q_recv.at[it])

            def refresh_p(d, to, first_block):
                for k in range(BLOCKS):
                    value = nearp[d, k // 4 * 8 : k // 4 * 8 + 8, :]
                    if k % 4:
                        value = pltpu.roll(value, 8 - k % 4 * 2, 0)
                    put_pieces(to, first_block + k, 0, value)

            refresh_p(4, own_pieces, 0)

            def refresh_others(arrive=arrive_p, refresh=refresh_p):
                def refresh_next(at, carry):
                    arrive(at)
                    d = at + at // 4
                    refresh(d, pieces, d * BLOCKS)
                    return carry

                lax.fori_loop(0, 8, refresh_next, 0)

    gram = add_products(gram, ITERS)
    gram = jnp.where(lane == 127, overflow, gram)

    for stage, group_peers in enumerate(peers):
        sums[stage] = gram
        copies = []
        for at, device in enumerate(group_peers):
            copy = pltpu.make_async_remote_copy(
                src_ref=sums.at[stage],
                dst_ref=sum_in.at[stage, at],
                send_sem=sum_send.at[stage, at],
                recv_sem=sum_recv.at[stage, at],
                device_id=device,
                device_id_type=MESH,
            )
            copy.start()
            copies.append(copy)
        pending.extend(copies)
        for at, copy in enumerate(copies):
            copy.wait_recv()
            gram = gram + sum_in[stage, at]
    flag_ref[0, 0] = jnp.sum(jnp.where((lane == 127) & (half[:, 0:128]), gram, 0.0))
    gram = gram + pltpu.roll(gram, 4, 0)

    def entry(kind, i, j, second):
        value = jnp.broadcast_to(gram[:, places[kind, i, j] : places[kind, i, j] + 1], (8, 128))
        return pltpu.roll(value, 6, 0) if second else value

    chain = ITERS + 1
    inner = {}
    for i in range(chain):
        for j in range(chain):
            inner[i, j] = entry("same", min(i, j), max(i, j), False)
            if i < ITERS and j < ITERS:
                inner[chain + i, chain + j] = entry("same", min(i, j), max(i, j), True)
            if j < ITERS:
                cross = entry("cross", min(i, j), max(i, j), i > j)
                inner[i, chain + j] = cross
                inner[chain + j, i] = cross

    def bilinear(first, second):
        total = None
        for i, a in first.items():
            inside = None
            for j, b in second.items():
                term = b * inner[i, j]
                inside = term if inside is None else inside + term
            inside = a * inside
            total = inside if total is None else total + inside
        return total

    def combine(base, scale, other):
        result = dict(base)
        for i, value in other.items():
            result[i] = result[i] + scale * value if i in result else scale * value
        return result

    one = jnp.ones((8, 128), F32)
    in_x, in_r, in_p = {}, {chain: one}, {0: one}
    norm_now = inner[chain, chain]
    for it in range(ITERS):
        image = {i + 1: value for i, value in in_p.items()}
        step = norm_now / bilinear(in_p, image)
        in_x = combine(in_x, step, in_p)
        in_r = combine(in_r, -step, image)
        norm_next = bilinear(in_r, in_r)
        in_p = combine(in_r, norm_next / norm_now, in_p)
        norm_now = norm_next

    for f, h in ((0, 0), (0, 1), (1, 0), (1, 1)):
        lanes = slice(128 * h, 128 * h + 128)
        vectors = {}
        for i in range(chain):
            vectors[i] = basis[i, h, pl.ds(f, BLOCKS, stride=4), :]
            if i < ITERS:
                vectors[chain + i] = basis[i, h, pl.ds(2 + f, BLOCKS, stride=4), :]

        def mixed(total, coefficients):
            for i, value in coefficients.items():
                term = value[f : f + 1, :] * vectors[i]
                total = term if total is None else total + term
            return total

        results = (mixed(None, in_x), mixed(None, in_r), mixed(None, in_p))
        for k in range(BLOCKS):
            at = f * BLOCKS + k
            new_sol_ref[at, :, lanes] = sol_rows[at, :, lanes] + results[0][k : k + 1, :]
            new_res_ref[at, :, lanes] = results[1][k : k + 1, :]
            new_dir_ref[at, :, lanes] = results[2][k : k + 1, :]

    for copy in pending:
        copy.wait_send()


def hand_out(*refs):
    sems = refs[6]
    copies = [pltpu.make_async_copy(refs[i], refs[3 + i], sems.at[i]) for i in range(3)]
    for copy in copies:
        copy.start()
    for copy in copies:
        copy.wait()


def solution(mesh):
    sizes = (mesh.shape["wide"], mesh.shape["narrow"])
    if sizes[0] == 64:
        stages = (
            ("narrow", ((1, sizes[1]),)),
            ("wide", ((2, 8),)),
            ("wide", ((16, 4), (1, 2))),
        )
    else:
        stages = (("narrow", ((1, sizes[1]),)), ("wide", ((1, sizes[0]),)))
    most = 0
    for _, places in stages:
        size = 1
        for _, count in places:
            size *= count
        most = max(most, size - 1)

    def on_device(node_coords, solution, residual, direction, tile_pairs, tile_counts):
        full_shape = direction.shape
        fields = jax.ShapeDtypeStruct((2 * BLOCKS, 1, NODES), F32)
        vmem = pl.BlockSpec(memory_space=pltpu.VMEM)
        anywhere = pl.BlockSpec(memory_space=pl.ANY)
        dma = pltpu.SemaphoreType.DMA
        fast = pl.pallas_call(
            functools.partial(fast_body, sizes, stages),
            out_shape=(fields, fields, fields, jax.ShapeDtypeStruct((1, 1), F32), jax.ShapeDtypeStruct((2, SLOTS), jnp.int32)),
            in_specs=[anywhere] * 5 + [vmem],
            out_specs=(vmem, vmem, vmem, pl.BlockSpec(memory_space=pltpu.SMEM), vmem),
            scratch_shapes=[
                pltpu.VMEM((BLOCKS, 8, NODES), F32),
                pltpu.VMEM((9 * BLOCKS, 8, NODES), F32),
                pltpu.VMEM((9, ROWS, NODES), F32),
                pltpu.VMEM((9, P_ROWS, NODES), F32),
                *[pltpu.VMEM((INNER_FOURS + 1 + OUTER_FOURS, NODES, NODES), BF16)] * 8,
                pltpu.VMEM((BLOCKS, 16, NODES), BF16),
                pltpu.VMEM((9 * BLOCKS, 16, NODES), BF16),
                pltpu.VMEM((FAST_WIDTH, NODES), F32),
                pltpu.VMEM((FAST_TABLE, FAST_WIDTH), BF16),
                pltpu.VMEM((ITERS + 1, 2, ROWS, 128), F32),
                pltpu.VMEM((len(stages), 8, 128), F32),
                pltpu.VMEM((len(stages), most, 8, 128), F32),
                pltpu.VMEM((7 * BLOCKS, 1, NODES), F32),
                pltpu.VMEM((2 * BLOCKS, 1, NODES), F32),
                pltpu.VMEM((2, SLOTS), jnp.int32),
                pltpu.VMEM((BLOCKS, 3, NODES, 128), F32),
                pltpu.VMEM((9, 8, 128), F32),
                pltpu.VMEM((8, 128), jnp.int32),
                pltpu.VMEM((8, 128), jnp.int32),
                pltpu.SMEM((8, 128), jnp.int32),
                pltpu.SMEM((8, 128), jnp.int32),
                dma((5,)),
                dma((2,)),
                dma((8,)),
                dma((8,)),
                dma((8,)),
                dma((8,)),
                dma((ITERS - 1, 8)),
                dma((ITERS - 1, 8)),
                dma((len(stages), most)),
                dma((len(stages), most)),
            ],
            compiler_params=pltpu.CompilerParams(
                collective_id=0, has_side_effects=True, vmem_limit_bytes=60 * 1024 * 1024
            ),
            cost_estimate=pl.CostEstimate(
                flops=81 * 65536 * 40, bytes_accessed=200000, transcendentals=81 * 65536
            ),
        )
        general = pl.pallas_call(
            functools.partial(general_body, sizes, stages),
            out_shape=(fields, fields, fields),
            in_specs=[anywhere] * 5 + [vmem],
            out_specs=(vmem, vmem, vmem),
            scratch_shapes=[
                pltpu.VMEM((9 * BLOCKS, 8, NODES), F32),
                pltpu.VMEM((ITERS - 1, 9, ROWS, NODES), F32),
                pltpu.VMEM((ITERS, 9, ROWS, NODES), F32),
                pltpu.VMEM((ITERS, 8, ROWS, NODES), F32),
                pltpu.VMEM((SLOTS // 2 + 1, NODES, NODES), BF16),
                pltpu.VMEM((SLOTS // 2 + 1, NODES, NODES), BF16),
                pltpu.VMEM((SLOTS // 2 + 1, NODES, NODES), BF16),
                pltpu.VMEM((SLOTS // 2 + 1, NODES, NODES), BF16),
                pltpu.VMEM((SLOTS // 2 + 1, NODES, NODES), BF16),
                pltpu.VMEM((SLOTS // 2 + 1, NODES, NODES), BF16),
                pltpu.VMEM((SLOTS // 2 + 1, NODES, NODES), BF16),
                pltpu.VMEM((SLOTS // 2 + 1, NODES, NODES), BF16),
                pltpu.VMEM((NODES, NODES), F32),
                pltpu.VMEM((NODES, NODES), F32),
                pltpu.VMEM((9 * BLOCKS, 16, NODES), BF16),
                pltpu.VMEM((512, NODES), F32),
                pltpu.VMEM((TABLE, 512), BF16),
                pltpu.VMEM((ITERS + 1, 2, ROWS, 128), F32),
                pltpu.VMEM((len(stages), 8, 128), F32),
                pltpu.VMEM((len(stages), most, 8, 128), F32),
                pltpu.VMEM((7 * BLOCKS, 1, NODES), F32),
                pltpu.VMEM((2 * BLOCKS, 1, NODES), F32),
                pltpu.SMEM((2, SLOTS), jnp.int32),
                pltpu.VMEM((2, SLOTS), jnp.int32),
                pltpu.VMEM((9 * BLOCKS, NODES, 8), F32),
                dma((6,)),
                dma((8,)),
                dma((8,)),
                dma((ITERS - 1, 8)),
                dma((ITERS - 1, 8)),
                dma((ITERS, 8)),
                dma((ITERS, 8)),
                dma((len(stages), most)),
                dma((len(stages), most)),
            ],
            compiler_params=pltpu.CompilerParams(
                collective_id=1, has_side_effects=True, vmem_limit_bytes=60 * 1024 * 1024
            ),
            cost_estimate=pl.CostEstimate(
                flops=61 * 65536 * 40, bytes_accessed=200000, transcendentals=61 * 65536
            ),
        )
        arguments = (
            node_coords.reshape(3 * BLOCKS, 1, NODES),
            solution.reshape(2 * BLOCKS, 1, NODES),
            residual.reshape(2 * BLOCKS, 1, NODES),
            direction.reshape(2 * BLOCKS, 1, NODES),
            tile_pairs.reshape(2, SLOTS),
            tile_counts,
        )
        *outs, flags, pairs = fast(*arguments)
        outs = lax.cond(
            flags[0, 0] > 0.5,
            lambda *a: tuple(general(*a[3:])),
            lambda *a: a[:3],
            *outs,
            *arguments[:4],
            pairs,
            arguments[5],
        )
        outs = pl.pallas_call(
            hand_out,
            out_shape=(fields, fields, fields),
            in_specs=[anywhere] * 3,
            out_specs=(anywhere,) * 3,
            scratch_shapes=[dma((3,))],
        )(*outs)
        return tuple(out.reshape(full_shape) for out in outs)

    fields_spec = P(None, "wide", "narrow", None, None)
    return jax.shard_map(
        on_device,
        mesh=mesh,
        in_specs=(
            fields_spec,
            fields_spec,
            fields_spec,
            fields_spec,
            P("wide", "narrow", None, None),
            P("wide", "narrow"),
        ),
        out_specs=(fields_spec, fields_spec, fields_spec),
        check_vma=False,
    )
```

```python
import functools

import jax
import jax.numpy as jnp
from jax import lax
from jax.experimental import pallas as pl
from jax.experimental.pallas import tpu as pltpu
from jax.sharding import PartitionSpec as P

ITERS = 3
RADIUS = 0.9
MESH = pl.DeviceIdType.MESH
F32 = jnp.float32
BF16 = jnp.bfloat16

BLOCKS = 9
NODES = 256
SLOTS = 61
ROWS = 40
TABLE = 368
GROUP = 3
CHUNK = 16

PHI_SLOPE = 4.0 / RADIUS**5
PHI_CONST = 1.0 / RADIUS**4


def dot_bf16(left, right, transposed):
    dims = (((1,), (1 if transposed else 0,)), ((), ()))
    return lax.dot_general(left, right, dims, preferred_element_type=F32)


def split(value):
    high = value.astype(BF16)
    return high, (value - high.astype(F32)).astype(BF16)


def stage_peers(wide, narrow, stages):
    peers = []
    for axis, places in stages:
        here = wide if axis == "wide" else narrow
        rank, size = 0, 1
        for stride, count in places:
            rank = rank * count + here // stride % count
            size *= count
        group = []
        for step in range(1, size):
            other = (rank + step) % size
            position = here
            left = other
            for stride, count in reversed(places):
                position = position + (left % count - here // stride % count) * stride
                left = left // count
            group.append((position, narrow) if axis == "wide" else (wide, position))
        peers.append(group)
    return peers


def general_body(
    sizes,
    stages,
    coord_ref,
    sol_ref,
    res_ref,
    dir_ref,
    pairs_hbm_ref,
    count_ref,
    new_sol_ref,
    new_res_ref,
    new_dir_ref,
    near0,
    nearq,
    part,
    got,
    khi_even,
    klo_even,
    khi_odd,
    klo_odd,
    thi_even,
    tlo_even,
    thi_odd,
    tlo_odd,
    stage_even,
    stage_odd,
    pieces,
    slot_out,
    onehot,
    basis,
    sums,
    sum_in,
    raw,
    sol_rows,
    pairs_ref,
    pairs_vec_ref,
    cols,
    load_sems,
    near_send,
    near_recv,
    q_send,
    q_recv,
    fold_send,
    fold_recv,
    sum_send,
    sum_recv,
):
    wide_size, narrow_size = sizes
    wide = lax.axis_index("wide")
    narrow = lax.axis_index("narrow")
    neighbours = []
    for d in range(9):
        if d != 4:
            to_wide = (wide + (d // 3 - 1) + wide_size) % wide_size
            to_narrow = (narrow + (d % 3 - 1) + narrow_size) % narrow_size
            neighbours.append((d, (to_wide, to_narrow)))
    peers = stage_peers(wide, narrow, stages)

    loads = [
        pltpu.make_async_copy(source, landing, load_sems.at[at])
        for at, (source, landing) in enumerate(
            (
                (dir_ref, raw.at[pl.ds(0, 2 * BLOCKS)]),
                (res_ref, raw.at[pl.ds(2 * BLOCKS, 2 * BLOCKS)]),
                (coord_ref, raw.at[pl.ds(4 * BLOCKS, 3 * BLOCKS)]),
                (pairs_hbm_ref, pairs_ref),
                (pairs_hbm_ref, pairs_vec_ref),
                (sol_ref, sol_rows),
            )
        )
    ]
    for load in loads:
        load.start()

    barrier = pltpu.get_barrier_semaphore()
    targets = [device for _, device in neighbours] + [device for group in peers for device in group]
    for device in targets:
        pl.semaphore_signal(barrier, inc=1, device_id=device, device_id_type=MESH)

    for load in loads:
        load.wait()
    for k in range(BLOCKS):
        own = 4 * BLOCKS + k
        for c in range(7):
            near0[own, c : c + 1, :] = raw[c * BLOCKS + k]
        near0[own, 7:8, :] = jnp.zeros((1, NODES), F32)

    pl.semaphore_wait(barrier, len(targets))

    pending = []

    def exchange(source, landing, send_sem, recv_sem):
        copies = []
        for at, (d, device) in enumerate(neighbours):
            copy = pltpu.make_async_remote_copy(
                src_ref=source(d),
                dst_ref=landing(8 - d, 7 - at),
                send_sem=send_sem.at[at],
                recv_sem=recv_sem.at[7 - at],
                device_id=device,
                device_id_type=MESH,
            )
            copy.start()
            copies.append(copy)
        pending.extend(copies)

        def wait(at):
            pltpu.make_async_remote_copy(
                src_ref=source(4),
                dst_ref=landing(at + at // 4, at),
                send_sem=send_sem.at[at],
                recv_sem=recv_sem.at[at],
                device_id=neighbours[0][1],
                device_id_type=MESH,
            ).wait_recv()

        return wait

    arrive = exchange(
        lambda d: near0.at[pl.ds(4 * BLOCKS, BLOCKS)],
        lambda d, at: near0.at[pl.ds(d * BLOCKS, BLOCKS)],
        near_send,
        near_recv,
    )

    slot_of = lax.broadcasted_iota(jnp.int32, (64, 512), 0)
    lane_slot = lax.broadcasted_iota(jnp.int32, (64, 512), 1) // 8
    spread = jnp.where(slot_of == lane_slot, 1.0, 0.0).astype(BF16)
    left_id = pairs_vec_ref[0:1, :]
    right_id = pairs_vec_ref[1:2, :]
    live = lax.broadcasted_iota(jnp.int32, (1, SLOTS), 1) < count_ref[0:1, 0:1]
    toward_left = jnp.where(live, left_id, 255)
    toward_right = jnp.where(live & (left_id != right_id), right_id, 255)
    ids = jnp.concatenate([toward_right, toward_left] + [toward_left] * 6, axis=0).astype(F32)
    ids = jnp.concatenate([ids, jnp.full((8, 64 - SLOTS), 255.0, F32)], axis=1)
    wanted = dot_bf16(ids.astype(BF16), spread, False)
    lane = lax.broadcasted_iota(jnp.int32, (8, 512), 1)
    target = jnp.where(lane % 8 < 4, wanted[0:1, :], wanted[1:2, :]).astype(jnp.int32)
    for first in range(0, TABLE, CHUNK):
        row = lax.broadcasted_iota(jnp.int32, (CHUNK, 512), 0) + first
        place = row % ROWS
        block = jnp.where(place < 4 * BLOCKS, row // ROWS * BLOCKS + place // 4, 200)
        match = (block == target[0:1, :]) & (
            row % 4 == lax.broadcasted_iota(jnp.int32, (CHUNK, 512), 1) % 4
        )
        onehot[pl.ds(first, CHUNK), :] = jnp.where(match, 1.0, 0.0).astype(BF16)

    slot_out[pl.ds(8 * SLOTS, 512 - 8 * SLOTS), :] = jnp.zeros((512 - 8 * SLOTS, NODES), F32)
    half = lax.broadcasted_iota(jnp.int32, (8, NODES), 0) < 4

    def put_pieces(j, rows_at, value):
        high = value.astype(BF16).astype(F32)
        low = value - high
        if rows_at == 0:
            rows = jnp.where(half, high, pltpu.roll(low, 4, 0))
        else:
            rows = jnp.where(half, pltpu.roll(high, 4, 0), low)
        pieces[j] = jnp.concatenate([rows, rows], axis=0).astype(BF16)

    for h in range(2):
        for k in range(BLOCKS):
            basis[0, h, 4 * k : 4 * k + 4, :] = near0[4 * BLOCKS + k, 0:4, 128 * h : 128 * h + 128]
        basis[0, h, 4 * BLOCKS : ROWS, :] = jnp.zeros((ROWS - 4 * BLOCKS, 128), F32)

    def prepare(d):
        for k in range(BLOCKS):
            j = d * BLOCKS + k
            value = near0[j]
            put_pieces(j, 0, value)
            cols[j] = jnp.transpose(value)

    def prepare_next(at, carry):
        arrive(at)
        prepare(at + at // 4)
        return carry

    prepare(4)
    lax.fori_loop(0, 8, prepare_next, 0)

    def evaluate(s, refs, stage, at):
        high_ref, low_ref, high_turned, low_turned = refs
        left = cols.at[pairs_ref[0, s]]
        right = near0[pairs_ref[1, s]]
        rights = [jnp.broadcast_to(right[4 + axis : 5 + axis, :], (CHUNK, NODES)) for axis in range(3)]
        for first in range(0, NODES, CHUNK):
            column = left[first : first + CHUNK, :]
            squared = None
            for axis in range(3):
                offset = column[:, 4 + axis : 5 + axis] - rights[axis]
                squared = offset * offset if squared is None else squared + offset * offset
            squared = jnp.minimum(squared, RADIUS * RADIUS)
            distance = squared * lax.rsqrt(jnp.maximum(squared, 1e-36))
            rest = RADIUS - distance
            rest = rest * rest
            rest = rest * rest
            value = rest * (PHI_SLOPE * distance + PHI_CONST)
            high, low = split(value)
            high_ref[at, first : first + CHUNK, :] = high
            low_ref[at, first : first + CHUNK, :] = low
            stage[first : first + CHUNK, :] = value
        for first in range(0, NODES, 128):
            high, low = split(jnp.transpose(stage[first : first + 128, :]))
            high_turned[at, :, first : first + 128] = high
            low_turned[at, :, first : first + 128] = low

    def product(s, refs, at):
        high_ref, low_ref, high_turned, low_turned = refs
        left = pieces[pairs_ref[0, s]]
        right = pieces[pairs_ref[1, s]]
        to_right = dot_bf16(left, high_ref[at], False) + dot_bf16(left, low_ref[at], False)
        to_left = dot_bf16(right, high_turned[at], False) + dot_bf16(right, low_turned[at], False)
        to_right = to_right[0:8]
        to_left = to_left[0:8]
        to_right = to_right + pltpu.roll(to_right, 4, 0)
        to_left = to_left + pltpu.roll(to_left, 4, 0)
        slot_out[pl.ds(pl.multiple_of(s * 8, 8), 8), :] = jnp.where(half, to_right, to_left)

    even = (khi_even, klo_even, thi_even, tlo_even)
    odd = (khi_odd, klo_odd, thi_odd, tlo_odd)

    def evaluate_and_multiply(t, carry):
        before = jnp.maximum(t - 1, 0)
        product(2 * before, even, before)
        evaluate(2 * t, even, stage_even, t)
        product(2 * before + 1, odd, before)
        evaluate(jnp.minimum(2 * t + 1, SLOTS - 1), odd, stage_odd, t)
        return carry

    def products(g, carry):
        for u in range(GROUP):
            at = g * GROUP + u
            product(2 * at, even, at)
            product(2 * at + 1, odd, at)
        return carry

    for it in range(ITERS):
        if it == 0:
            lax.fori_loop(0, SLOTS // 2 + 1, evaluate_and_multiply, 0)
        else:
            lax.fori_loop(0, SLOTS // 2 // GROUP, products, 0)
        product(SLOTS - 1, even, SLOTS // 2)
        high, low = split(slot_out[...])
        table = onehot[...]
        added = dot_bf16(table, high, False) + dot_bf16(table, low, False)
        for d in range(9):
            part[it, d] = added[d * ROWS : (d + 1) * ROWS]
        arrive = exchange(
            lambda d: part.at[it, d],
            lambda d, at: got.at[it, at],
            fold_send.at[it],
            fold_recv.at[it],
        )
        image = part[it, 4]
        for at in range(8):
            arrive(at)
            image = image + got[it, at]
        for h in range(2):
            basis[it + 1, h] = image[:, 128 * h : 128 * h + 128]
        if it + 1 < ITERS:
            nearq[it, 4] = image
            arrive = exchange(
                lambda d: nearq.at[it, 4],
                lambda d, at: nearq.at[it, d],
                q_send.at[it],
                q_recv.at[it],
            )

            def refresh(d):
                for k in range(0, BLOCKS, 2):
                    value = nearq[it, d, 4 * k : 4 * k + 8, :]
                    put_pieces(d * BLOCKS + k, 0, value)
                    if k + 1 < BLOCKS:
                        put_pieces(d * BLOCKS + k + 1, 4, value)

            def refresh_next(at, carry):
                arrive(at)
                refresh(at + at // 4)
                return carry

            refresh(4)
            lax.fori_loop(0, 8, refresh_next, 0)

    lane = lax.broadcasted_iota(jnp.int32, (8, 128), 1)
    forward = lax.broadcasted_iota(jnp.int32, (8, 128), 0) % 4 < 2

    def swapped(value):
        return jnp.where(forward, pltpu.roll(value, 6, 0), pltpu.roll(value, 2, 0))

    tiles = [
        [basis[i, h, g : g + 8, :] for h in range(2) for g in range(0, ROWS, 8)]
        for i in range(ITERS + 1)
    ]
    crossed = [[swapped(tile) for tile in row] for row in tiles]
    places = {}
    gram = jnp.zeros((8, 128), F32)
    for i in range(ITERS + 1):
        for j in range(i, ITERS + 1):
            for kind, other in (("same", tiles), ("cross", crossed)):
                total = None
                for mine, theirs in zip(tiles[i], other[j]):
                    term = mine * theirs
                    total = term if total is None else total + term
                column = jnp.sum(total, axis=1, keepdims=True)
                places[kind, i, j] = len(places)
                gram = jnp.where(lane == places[kind, i, j], column, gram)

    for stage, group_peers in enumerate(peers):
        sums[stage] = gram
        copies = []
        for at, device in enumerate(group_peers):
            copy = pltpu.make_async_remote_copy(
                src_ref=sums.at[stage],
                dst_ref=sum_in.at[stage, at],
                send_sem=sum_send.at[stage, at],
                recv_sem=sum_recv.at[stage, at],
                device_id=device,
                device_id_type=MESH,
            )
            copy.start()
            copies.append(copy)
        pending.extend(copies)
        for at, copy in enumerate(copies):
            copy.wait_recv()
            gram = gram + sum_in[stage, at]
    gram = gram + pltpu.roll(gram, 4, 0)

    def entry(kind, i, j, second):
        value = jnp.broadcast_to(gram[:, places[kind, i, j] : places[kind, i, j] + 1], (8, 128))
        return pltpu.roll(value, 6, 0) if second else value

    chain = ITERS + 1
    inner = {}
    for i in range(chain):
        for j in range(chain):
            inner[i, j] = entry("same", min(i, j), max(i, j), False)
            if i < ITERS and j < ITERS:
                inner[chain + i, chain + j] = entry("same", min(i, j), max(i, j), True)
            if j < ITERS:
                cross = entry("cross", min(i, j), max(i, j), i > j)
                inner[i, chain + j] = cross
                inner[chain + j, i] = cross

    def bilinear(first, second):
        total = None
        for i, a in first.items():
            inside = None
            for j, b in second.items():
                term = b * inner[i, j]
                inside = term if inside is None else inside + term
            inside = a * inside
            total = inside if total is None else total + inside
        return total

    def combine(base, scale, other):
        result = dict(base)
        for i, value in other.items():
            result[i] = result[i] + scale * value if i in result else scale * value
        return result

    one = jnp.ones((8, 128), F32)
    in_x, in_r, in_p = {}, {chain: one}, {0: one}
    norm_now = inner[chain, chain]
    for it in range(ITERS):
        image = {i + 1: value for i, value in in_p.items()}
        step = norm_now / bilinear(in_p, image)
        in_x = combine(in_x, step, in_p)
        in_r = combine(in_r, -step, image)
        norm_next = bilinear(in_r, in_r)
        in_p = combine(in_r, norm_next / norm_now, in_p)
        norm_now = norm_next

    for f, h in ((0, 0), (0, 1), (1, 0), (1, 1)):
        lanes = slice(128 * h, 128 * h + 128)
        vectors = {}
        for i in range(chain):
            vectors[i] = basis[i, h, pl.ds(f, BLOCKS, stride=4), :]
            if i < ITERS:
                vectors[chain + i] = basis[i, h, pl.ds(2 + f, BLOCKS, stride=4), :]

        def mixed(total, coefficients):
            for i, value in coefficients.items():
                term = value[f : f + 1, :] * vectors[i]
                total = term if total is None else total + term
            return total

        results = (mixed(None, in_x), mixed(None, in_r), mixed(None, in_p))
        for k in range(BLOCKS):
            at = f * BLOCKS + k
            new_sol_ref[at, :, lanes] = sol_rows[at, :, lanes] + results[0][k : k + 1, :]
            new_res_ref[at, :, lanes] = results[1][k : k + 1, :]
            new_dir_ref[at, :, lanes] = results[2][k : k + 1, :]

    for copy in pending:
        copy.wait_send()


INNER = 29
OUTER = 32
INNER_FOURS = INNER // 4
OUTER_FOURS = OUTER // 4
INNER_WIDTH = 512
FAST_WIDTH = INNER_WIDTH + 8 * OUTER
FAST_TABLE = 64
P_ROWS = 24


def fast_body(
    sizes,
    stages,
    coord_ref,
    sol_ref,
    res_ref,
    dir_ref,
    pairs_hbm_ref,
    count_ref,
    new_sol_ref,
    new_res_ref,
    new_dir_ref,
    flag_ref,
    pairs_out_ref,
    own0,
    near0,
    nearq,
    nearp,
    khi_0,
    khi_1,
    khi_2,
    khi_3,
    klo_0,
    klo_1,
    klo_2,
    klo_3,
    own_pieces,
    pieces,
    slot_out,
    onehot,
    basis,
    sums,
    sum_in,
    raw,
    sol_rows,
    pairs_vec_ref,
    own_columns,
    lists,
    inner_rows,
    outer_rows,
    inner_entries,
    outer_entries,
    load_sems,
    entry_sems,
    list_send,
    list_recv,
    near_send,
    near_recv,
    q_send,
    q_recv,
    sum_send,
    sum_recv,
):
    wide_size, narrow_size = sizes
    wide = lax.axis_index("wide")
    narrow = lax.axis_index("narrow")
    neighbours = []
    for d in range(9):
        if d != 4:
            to_wide = (wide + (d // 3 - 1) + wide_size) % wide_size
            to_narrow = (narrow + (d % 3 - 1) + narrow_size) % narrow_size
            neighbours.append((d, (to_wide, to_narrow)))
    peers = stage_peers(wide, narrow, stages)

    loads = [
        pltpu.make_async_copy(source, landing, load_sems.at[at])
        for at, (source, landing) in enumerate(
            (
                (pairs_hbm_ref, pairs_vec_ref),
                (dir_ref, raw.at[pl.ds(0, 2 * BLOCKS)]),
                (res_ref, raw.at[pl.ds(2 * BLOCKS, 2 * BLOCKS)]),
                (coord_ref, raw.at[pl.ds(4 * BLOCKS, 3 * BLOCKS)]),
                (sol_ref, sol_rows),
            )
        )
    ]
    for load in loads:
        load.start()

    barrier = pltpu.get_barrier_semaphore()
    targets = [device for _, device in neighbours] + [device for group in peers for device in group]
    for device in targets:
        pl.semaphore_signal(barrier, inc=1, device_id=device, device_id_type=MESH)

    for load in loads:
        load.wait()
    pairs_out_ref[...] = pairs_vec_ref[...]
    live = lax.broadcasted_iota(jnp.int32, (2, SLOTS), 1) < count_ref[0:1, 0:1]
    own_list = jnp.where(live, pairs_vec_ref[...], 255).astype(F32)
    own_list = jnp.concatenate([own_list, jnp.full((2, 128 - SLOTS), 255.0, F32)], axis=1)
    lists[4] = jnp.concatenate([own_list, jnp.full((6, 128), 255.0, F32)], axis=0)
    for k in range(BLOCKS):
        for c in range(7):
            own0[k, c : c + 1, :] = raw[c * BLOCKS + k]
        own0[k, 7:8, :] = jnp.zeros((1, NODES), F32)

    pl.semaphore_wait(barrier, len(targets))

    pending = []

    def exchange(source, landing, send_sem, recv_sem):
        for at in (0, 2, 5, 7, 3, 4, 1, 6):
            d, device = neighbours[at]
            copy = pltpu.make_async_remote_copy(
                src_ref=source,
                dst_ref=landing(8 - d),
                send_sem=send_sem.at[at],
                recv_sem=recv_sem.at[7 - at],
                device_id=device,
                device_id_type=MESH,
            )
            copy.start()
            pending.append(copy)

        def wait(at):
            pltpu.make_async_remote_copy(
                src_ref=source,
                dst_ref=landing(at + at // 4),
                send_sem=send_sem.at[at],
                recv_sem=recv_sem.at[at],
                device_id=neighbours[0][1],
                device_id_type=MESH,
            ).wait_recv()

        return wait

    list_arrive = exchange(lists.at[4], lambda d: lists.at[d], list_send, list_recv)
    near_arrive = exchange(
        own0,
        lambda d: near0.at[pl.ds(d * BLOCKS, BLOCKS)],
        near_send,
        near_recv,
    )

    half = lax.broadcasted_iota(jnp.int32, (8, NODES), 0) < 4

    def put_pieces(to, j, rows_at, value):
        high = value.astype(BF16).astype(F32)
        low = value - high
        if rows_at == 0:
            rows = jnp.where(half, high, pltpu.roll(low, 4, 0))
        else:
            rows = jnp.where(half, pltpu.roll(high, 4, 0), low)
        to[j] = jnp.concatenate([rows, rows], axis=0).astype(BF16)

    for h in range(2):
        for k in range(BLOCKS):
            basis[0, h, 4 * k : 4 * k + 4, :] = own0[k, 0:4, 128 * h : 128 * h + 128]
        basis[0, h, 4 * BLOCKS : ROWS, :] = jnp.zeros((ROWS - 4 * BLOCKS, 128), F32)


    before_lane = lax.broadcasted_iota(jnp.int32, (128, 128), 0) < lax.broadcasted_iota(
        jnp.int32, (128, 128), 1
    )
    before_lane = jnp.where(before_lane, 1.0, 0.0).astype(BF16)
    entry_of = lax.broadcasted_iota(jnp.int32, (128, 128), 0).astype(F32)
    row_of = lax.broadcasted_iota(jnp.int32, (8, 128), 0)

    def compact(wanted_rows, codes, rows, most_entries):
        count = wanted_rows.shape[0]
        before_row = lax.broadcasted_iota(jnp.int32, (count, count), 0) > lax.broadcasted_iota(
            jnp.int32, (count, count), 1
        )
        in_row = dot_bf16(wanted_rows.astype(BF16), before_lane, False)
        row_total = jnp.broadcast_to(jnp.sum(wanted_rows, axis=1, keepdims=True), (count, 128))
        rank = in_row + dot_bf16(
            jnp.where(before_row, 1.0, 0.0).astype(BF16), row_total.astype(BF16), False
        )
        everything = jnp.sum(row_total, axis=0, keepdims=True)
        rank = jnp.where(wanted_rows > 0.5, rank, -1.0)
        gathered = jnp.zeros((128, 128), F32)
        for row in rows:
            gathered = gathered + jnp.where(
                entry_of == rank[row : row + 1, :], codes[row : row + 1, :], 0.0
            )
        gathered = jnp.broadcast_to(jnp.sum(gathered, axis=1, keepdims=True), (128, 128))
        code = jnp.transpose(gathered)[0:8, :].astype(jnp.int32)
        return code, jnp.where(everything > most_entries + 0.5, 1.0, 0.0)

    def fill_onehot(start, wanted):
        width = wanted.shape[1]
        for first in range(0, FAST_TABLE, CHUNK):
            row = lax.broadcasted_iota(jnp.int32, (CHUNK, width), 0) + first
            lane = lax.broadcasted_iota(jnp.int32, (CHUNK, width), 1)
            second = row - ROWS
            block = jnp.where(row < ROWS, row >> 2, second >> 1)
            vector = jnp.where(row < ROWS, row & 3, second & 1)
            match = (block == wanted) & (vector == (lane & 3))
            onehot[first : first + CHUNK, start : start + width] = jnp.where(
                match, 1.0, 0.0
            ).astype(BF16)

    def spread_over(targets_rows, width, shift):
        entry_row = lax.broadcasted_iota(jnp.int32, (128, width), 0)
        entry_lane = lax.broadcasted_iota(jnp.int32, (128, width), 1) >> shift
        spread = jnp.where(entry_row == entry_lane, 1.0, 0.0).astype(BF16)
        return dot_bf16(targets_rows.astype(F32).astype(BF16), spread, False).astype(jnp.int32)

    own_ids = lists[4]
    own_left = jnp.broadcast_to(own_ids[0:1, :], (8, 128)) - 4.0 * BLOCKS
    own_right = jnp.broadcast_to(own_ids[1:2, :], (8, 128)) - 4.0 * BLOCKS
    inside = (own_left > -0.5) & (own_left < BLOCKS - 0.5) & (own_right > -0.5) & (own_right < BLOCKS - 0.5)
    code, overflow = compact(
        jnp.where(inside & (row_of == 0), 1.0, 0.0), own_left * 128.0 + own_right + 1.0, (0,), INNER
    )
    filled = code > 0
    code = jnp.maximum(code - 1, 0)
    inner_left, inner_right = code >> 7, code & 127
    inner_rows[...] = jnp.where(row_of == 0, inner_left, inner_right)
    inner_load = pltpu.make_async_copy(inner_rows, inner_entries, entry_sems.at[0])
    inner_load.start()

    def own_block(k, carry):
        value = own0[k]
        put_pieces(own_pieces, k, 0, value)
        turned = jnp.transpose(value)
        for axis in range(3):
            own_columns[k, axis] = jnp.broadcast_to(turned[:, 4 + axis : 5 + axis], (NODES, 128))
        return carry

    lax.fori_loop(0, BLOCKS, own_block, 0)

    ends = jnp.where(row_of == 0, inner_left, inner_right)
    ends = jnp.where(filled & ((row_of == 0) | (inner_left != inner_right)), ends, 200)
    wanted = spread_over(ends, INNER_WIDTH, 4)
    lane = lax.broadcasted_iota(jnp.int32, (1, INNER_WIDTH), 1)
    fill_onehot(0, jnp.where((lane & 8) == 0, wanted[0:1, :], wanted[1:2, :]))
    inner_load.wait()

    def evaluate(block, other, refs, at):
        high_ref, low_ref = refs
        block = jnp.clip(block, 0, BLOCKS - 1)
        for h in range(2):
            lanes = slice(128 * h, 128 * h + 128)
            others = [
                jnp.broadcast_to(other[4 + axis : 5 + axis, lanes], (CHUNK, 128)) for axis in range(3)
            ]
            for first in range(0, NODES, CHUNK):
                squared = None
                for axis in range(3):
                    offset = own_columns[block, axis, first : first + CHUNK, :] - others[axis]
                    squared = offset * offset if squared is None else squared + offset * offset
                squared = jnp.minimum(squared, RADIUS * RADIUS)
                distance = squared * lax.rsqrt(jnp.maximum(squared, 1e-36))
                rest = RADIUS - distance
                rest = rest * rest
                rest = rest * rest
                high, low = split(rest * (PHI_SLOPE * distance + PHI_CONST))
                high_ref[at, first : first + CHUNK, lanes] = high
                low_ref[at, first : first + CHUNK, lanes] = low

    def evaluate_inner(e, refs, at):
        other = own0[jnp.clip(inner_entries[1, e], 0, BLOCKS - 1)]
        evaluate(inner_entries[0, e], other, refs, at)

    def evaluate_outer(e, refs, at):
        other = near0[jnp.clip(outer_entries[1, e], 0, 9 * BLOCKS - 1)]
        evaluate(outer_entries[0, e], other, refs, at)

    def product_inner(e, refs, at):
        high, low = refs[0][at], refs[1][at]
        left = own_pieces[jnp.clip(inner_entries[0, e], 0, BLOCKS - 1)]
        right = own_pieces[jnp.clip(inner_entries[1, e], 0, BLOCKS - 1)]
        to_left = dot_bf16(right, high, True) + dot_bf16(right, low, True)
        to_right = dot_bf16(left, high, False) + dot_bf16(left, low, False)
        start = pl.multiple_of(e * 16, 16)
        slot_out[pl.ds(start, 8), :] = to_left[0:8]
        slot_out[pl.ds(start + 8, 8), :] = to_right[0:8]

    def product_outer(e, refs, at):
        other = pieces[jnp.clip(outer_entries[1, e], 0, 9 * BLOCKS - 1)]
        result = dot_bf16(other, refs[0][at], True) + dot_bf16(other, refs[1][at], True)
        slot_out[pl.ds(pl.multiple_of(INNER_WIDTH + e * 8, 8), 8), :] = result[0:8]

    tiles_of = ((khi_0, klo_0), (khi_1, klo_1), (khi_2, klo_2), (khi_3, klo_3))

    def evaluate_and_multiply(evaluate_one, product_one, start, fours):
        def step(t, carry):
            before = jnp.maximum(t - 1, 0)
            for u, refs in enumerate(tiles_of):
                product_one(4 * before + u, refs, start + before)
                evaluate_one(4 * t + u, refs, start + t)
            return carry

        lax.fori_loop(0, fours, step, 0)

    def last_four(product_one, start, fours):
        for u, refs in enumerate(tiles_of):
            product_one(4 * (fours - 1) + u, refs, start + fours - 1)

    def multiply(product_one, start, fours, group):
        def step(g, carry):
            for at in range(group):
                for u, refs in enumerate(tiles_of):
                    product_one(4 * (g * group + at) + u, refs, start + g * group + at)
            return carry

        lax.fori_loop(0, fours // group, step, 0)

    slot_out[16 * INNER : INNER_WIDTH, :] = jnp.zeros((INNER_WIDTH - 16 * INNER, NODES), F32)
    evaluate_and_multiply(evaluate_inner, product_inner, 0, INNER_FOURS)
    for at in range(8):
        list_arrive(at)
    evaluate_inner(INNER - 1, tiles_of[0], INNER_FOURS)
    last_four(product_inner, 0, INNER_FOURS)

    dead_rows = jnp.full((7, 128), 255.0, F32)
    device_row = lax.broadcasted_iota(jnp.int32, (16, 128), 0)
    add_wide = (device_row * 11 >> 5) - 1
    add_narrow = device_row - (add_wide + 1) * 3 - 1

    def here(row):
        ids = jnp.concatenate([lists[d, row : row + 1, :] for d in range(9)] + [dead_rows], axis=0)
        ids = ids.astype(jnp.int32)
        is_live = ids < 200
        ids = jnp.where(is_live, ids, 0)
        device = ids * 7282 >> 16
        within = ids - device * 9
        at_wide = device * 11 >> 5
        at_narrow = device - at_wide * 3 + add_narrow
        at_wide = at_wide + add_wide
        mine = is_live & (at_wide == 1) & (at_narrow == 1)
        return mine, within, at_wide * 27 + at_narrow * 9 + within

    left_mine, left_within, left_here = here(0)
    right_mine, right_within, right_here = here(1)
    wanted_rows = jnp.concatenate(
        [
            jnp.where(left_mine & jnp.logical_not(right_mine), 1.0, 0.0),
            jnp.where(right_mine & jnp.logical_not(left_mine), 1.0, 0.0),
        ],
        axis=0,
    )
    codes = jnp.concatenate(
        [left_within * 128 + right_here + 1, right_within * 128 + left_here + 1], axis=0
    ).astype(F32)
    code, too_many = compact(wanted_rows, codes, (*range(9), *range(16, 25)), OUTER)
    overflow = overflow + too_many
    filled = code > 0
    code = jnp.maximum(code - 1, 0)
    outer_rows[...] = jnp.where(row_of == 0, code >> 7, code & 127)
    outer_load = pltpu.make_async_copy(outer_rows, outer_entries, entry_sems.at[1])
    outer_load.start()
    fill_onehot(INNER_WIDTH, spread_over(jnp.where(filled, code >> 7, 200), 8 * OUTER, 3)[0:1, :])

    product_inner(INNER - 1, tiles_of[0], INNER_FOURS)

    def added(start, end):
        high, low = split(slot_out[start:end, :])
        table = onehot[:, start:end]
        return dot_bf16(table, high, False) + dot_bf16(table, low, False)

    inner_image = added(0, INNER_WIDTH)

    def prepare_next(at, carry):
        near_arrive(at)
        for k in range(BLOCKS):
            j = (at + at // 4) * BLOCKS + k
            put_pieces(pieces, j, 0, near0[j])
        return carry

    lax.fori_loop(0, 8, prepare_next, 0)
    outer_load.wait()
    evaluate_and_multiply(evaluate_outer, product_outer, INNER_FOURS + 1, OUTER_FOURS)
    last_four(product_outer, INNER_FOURS + 1, OUTER_FOURS)

    lane = lax.broadcasted_iota(jnp.int32, (8, 128), 1)
    forward = row_of % 4 < 2
    places = {}

    def swapped(value):
        return jnp.where(forward, pltpu.roll(value, 6, 0), pltpu.roll(value, 2, 0))

    def add_products(gram, j):
        tiles = [
            [basis[i, h, g : g + 8, :] for h in range(2) for g in range(0, ROWS, 8)] for i in range(j + 1)
        ]
        crossed = [swapped(tile) for tile in tiles[j]]
        for i in range(j + 1):
            for kind, others in (("same", tiles[j]), ("cross", crossed)):
                total = None
                for mine, theirs in zip(tiles[i], others):
                    term = mine * theirs
                    total = term if total is None else total + term
                column = jnp.sum(total, axis=1, keepdims=True)
                places[kind, i, j] = len(places)
                gram = jnp.where(lane == places[kind, i, j], column, gram)
        return gram

    gram = jnp.zeros((8, 128), F32)
    for it in range(ITERS):
        if it > 0:
            gram = add_products(gram, it - 1)
            if it + 1 == ITERS:
                gram = add_products(gram, it)
            multiply(product_inner, 0, INNER_FOURS, 1)
            product_inner(INNER - 1, tiles_of[0], INNER_FOURS)
            inner_image = added(0, INNER_WIDTH)
            refresh_others()
            multiply(product_outer, INNER_FOURS + 1, OUTER_FOURS, 2)
        image = inner_image + added(INNER_WIDTH, FAST_WIDTH)
        for h in range(2):
            basis[it + 1, h] = image[0:ROWS, 128 * h : 128 * h + 128]
        if it == 0:
            nearq[4] = image[0:ROWS]
            arrive = exchange(nearq.at[4], lambda d: nearq.at[d], q_send.at[it], q_recv.at[it])

            def refresh(d, to, first_block):
                for k in range(0, BLOCKS, 2):
                    value = nearq[d, 4 * k : 4 * k + 8, :]
                    put_pieces(to, first_block + k, 0, value)
                    if k + 1 < BLOCKS:
                        put_pieces(to, first_block + k + 1, 4, value)

            refresh(4, own_pieces, 0)

            def refresh_others(arrive=arrive, refresh=refresh):
                def refresh_next(at, carry):
                    arrive(at)
                    d = at + at // 4
                    refresh(d, pieces, d * BLOCKS)
                    return carry

                lax.fori_loop(0, 8, refresh_next, 0)

        elif it + 1 < ITERS:
            nearp[4] = image[ROWS : ROWS + P_ROWS]
            arrive_p = exchange(nearp.at[4], lambda d: nearp.at[d], q_send.at[it], q_recv.at[it])

            def refresh_p(d, to, first_block):
                for k in range(BLOCKS):
                    value = nearp[d, k // 4 * 8 : k // 4 * 8 + 8, :]
                    if k % 4:
                        value = pltpu.roll(value, 8 - k % 4 * 2, 0)
                    put_pieces(to, first_block + k, 0, value)

            refresh_p(4, own_pieces, 0)

            def refresh_others(arrive=arrive_p, refresh=refresh_p):
                def refresh_next(at, carry):
                    arrive(at)
                    d = at + at // 4
                    refresh(d, pieces, d * BLOCKS)
                    return carry

                lax.fori_loop(0, 8, refresh_next, 0)

    gram = add_products(gram, ITERS)
    gram = jnp.where(lane == 127, overflow, gram)

    for stage, group_peers in enumerate(peers):
        sums[stage] = gram
        copies = []
        count = len(group_peers)
        for at in sorted(range(count), key=lambda at: -min(at + 1, count - at)):
            copy = pltpu.make_async_remote_copy(
                src_ref=sums.at[stage],
                dst_ref=sum_in.at[stage, at],
                send_sem=sum_send.at[stage, at],
                recv_sem=sum_recv.at[stage, at],
                device_id=group_peers[at],
                device_id_type=MESH,
            )
            copy.start()
            copies.append((at, copy))
        copies = [copy for at, copy in sorted(copies, key=lambda pair: pair[0])]
        pending.extend(copies)
        for at, copy in enumerate(copies):
            copy.wait_recv()
            gram = gram + sum_in[stage, at]
    flag_ref[0, 0] = jnp.sum(jnp.where((lane == 127) & (half[:, 0:128]), gram, 0.0))
    gram = gram + pltpu.roll(gram, 4, 0)

    def entry(kind, i, j, second):
        value = jnp.broadcast_to(gram[:, places[kind, i, j] : places[kind, i, j] + 1], (8, 128))
        return pltpu.roll(value, 6, 0) if second else value

    chain = ITERS + 1
    inner = {}
    for i in range(chain):
        for j in range(chain):
            inner[i, j] = entry("same", min(i, j), max(i, j), False)
            if i < ITERS and j < ITERS:
                inner[chain + i, chain + j] = entry("same", min(i, j), max(i, j), True)
            if j < ITERS:
                cross = entry("cross", min(i, j), max(i, j), i > j)
                inner[i, chain + j] = cross
                inner[chain + j, i] = cross

    def bilinear(first, second):
        total = None
        for i, a in first.items():
            inside = None
            for j, b in second.items():
                term = b * inner[i, j]
                inside = term if inside is None else inside + term
            inside = a * inside
            total = inside if total is None else total + inside
        return total

    def combine(base, scale, other):
        result = dict(base)
        for i, value in other.items():
            result[i] = result[i] + scale * value if i in result else scale * value
        return result

    one = jnp.ones((8, 128), F32)
    in_x, in_r, in_p = {}, {chain: one}, {0: one}
    norm_now = inner[chain, chain]
    for it in range(ITERS):
        image = {i + 1: value for i, value in in_p.items()}
        step = norm_now / bilinear(in_p, image)
        in_x = combine(in_x, step, in_p)
        in_r = combine(in_r, -step, image)
        norm_next = bilinear(in_r, in_r)
        in_p = combine(in_r, norm_next / norm_now, in_p)
        norm_now = norm_next

    for f, h in ((0, 0), (0, 1), (1, 0), (1, 1)):
        lanes = slice(128 * h, 128 * h + 128)
        vectors = {}
        for i in range(chain):
            vectors[i] = basis[i, h, pl.ds(f, BLOCKS, stride=4), :]
            if i < ITERS:
                vectors[chain + i] = basis[i, h, pl.ds(2 + f, BLOCKS, stride=4), :]

        def mixed(total, coefficients):
            for i, value in coefficients.items():
                term = value[f : f + 1, :] * vectors[i]
                total = term if total is None else total + term
            return total

        results = (mixed(None, in_x), mixed(None, in_r), mixed(None, in_p))
        for k in range(BLOCKS):
            at = f * BLOCKS + k
            new_sol_ref[at, :, lanes] = sol_rows[at, :, lanes] + results[0][k : k + 1, :]
            new_res_ref[at, :, lanes] = results[1][k : k + 1, :]
            new_dir_ref[at, :, lanes] = results[2][k : k + 1, :]

    for copy in pending:
        copy.wait_send()


def hand_out(*refs):
    sems = refs[6]
    copies = [pltpu.make_async_copy(refs[i], refs[3 + i], sems.at[i]) for i in range(3)]
    for copy in copies:
        copy.start()
    for copy in copies:
        copy.wait()


def solution(mesh):
    sizes = (mesh.shape["wide"], mesh.shape["narrow"])
    if sizes[0] == 64:
        stages = (
            ("narrow", ((1, sizes[1]),)),
            ("wide", ((2, 8),)),
            ("wide", ((16, 4), (1, 2))),
        )
    else:
        stages = (("narrow", ((1, sizes[1]),)), ("wide", ((1, sizes[0]),)))
    most = 0
    for _, places in stages:
        size = 1
        for _, count in places:
            size *= count
        most = max(most, size - 1)

    def on_device(node_coords, solution, residual, direction, tile_pairs, tile_counts):
        full_shape = direction.shape
        fields = jax.ShapeDtypeStruct((2 * BLOCKS, 1, NODES), F32)
        vmem = pl.BlockSpec(memory_space=pltpu.VMEM)
        anywhere = pl.BlockSpec(memory_space=pl.ANY)
        dma = pltpu.SemaphoreType.DMA
        fast = pl.pallas_call(
            functools.partial(fast_body, sizes, stages),
            out_shape=(fields, fields, fields, jax.ShapeDtypeStruct((1, 1), F32), jax.ShapeDtypeStruct((2, SLOTS), jnp.int32)),
            in_specs=[anywhere] * 5 + [vmem],
            out_specs=(vmem, vmem, vmem, pl.BlockSpec(memory_space=pltpu.SMEM), vmem),
            scratch_shapes=[
                pltpu.VMEM((BLOCKS, 8, NODES), F32),
                pltpu.VMEM((9 * BLOCKS, 8, NODES), F32),
                pltpu.VMEM((9, ROWS, NODES), F32),
                pltpu.VMEM((9, P_ROWS, NODES), F32),
                *[pltpu.VMEM((INNER_FOURS + 1 + OUTER_FOURS, NODES, NODES), BF16)] * 8,
                pltpu.VMEM((BLOCKS, 16, NODES), BF16),
                pltpu.VMEM((9 * BLOCKS, 16, NODES), BF16),
                pltpu.VMEM((FAST_WIDTH, NODES), F32),
                pltpu.VMEM((FAST_TABLE, FAST_WIDTH), BF16),
                pltpu.VMEM((ITERS + 1, 2, ROWS, 128), F32),
                pltpu.VMEM((len(stages), 8, 128), F32),
                pltpu.VMEM((len(stages), most, 8, 128), F32),
                pltpu.VMEM((7 * BLOCKS, 1, NODES), F32),
                pltpu.VMEM((2 * BLOCKS, 1, NODES), F32),
                pltpu.VMEM((2, SLOTS), jnp.int32),
                pltpu.VMEM((BLOCKS, 3, NODES, 128), F32),
                pltpu.VMEM((9, 8, 128), F32),
                pltpu.VMEM((8, 128), jnp.int32),
                pltpu.VMEM((8, 128), jnp.int32),
                pltpu.SMEM((8, 128), jnp.int32),
                pltpu.SMEM((8, 128), jnp.int32),
                dma((5,)),
                dma((2,)),
                dma((8,)),
                dma((8,)),
                dma((8,)),
                dma((8,)),
                dma((ITERS - 1, 8)),
                dma((ITERS - 1, 8)),
                dma((len(stages), most)),
                dma((len(stages), most)),
            ],
            compiler_params=pltpu.CompilerParams(
                collective_id=0, has_side_effects=True, vmem_limit_bytes=60 * 1024 * 1024
            ),
            cost_estimate=pl.CostEstimate(
                flops=81 * 65536 * 40, bytes_accessed=200000, transcendentals=81 * 65536
            ),
        )
        general = pl.pallas_call(
            functools.partial(general_body, sizes, stages),
            out_shape=(fields, fields, fields),
            in_specs=[anywhere] * 5 + [vmem],
            out_specs=(vmem, vmem, vmem),
            scratch_shapes=[
                pltpu.VMEM((9 * BLOCKS, 8, NODES), F32),
                pltpu.VMEM((ITERS - 1, 9, ROWS, NODES), F32),
                pltpu.VMEM((ITERS, 9, ROWS, NODES), F32),
                pltpu.VMEM((ITERS, 8, ROWS, NODES), F32),
                pltpu.VMEM((SLOTS // 2 + 1, NODES, NODES), BF16),
                pltpu.VMEM((SLOTS // 2 + 1, NODES, NODES), BF16),
                pltpu.VMEM((SLOTS // 2 + 1, NODES, NODES), BF16),
                pltpu.VMEM((SLOTS // 2 + 1, NODES, NODES), BF16),
                pltpu.VMEM((SLOTS // 2 + 1, NODES, NODES), BF16),
                pltpu.VMEM((SLOTS // 2 + 1, NODES, NODES), BF16),
                pltpu.VMEM((SLOTS // 2 + 1, NODES, NODES), BF16),
                pltpu.VMEM((SLOTS // 2 + 1, NODES, NODES), BF16),
                pltpu.VMEM((NODES, NODES), F32),
                pltpu.VMEM((NODES, NODES), F32),
                pltpu.VMEM((9 * BLOCKS, 16, NODES), BF16),
                pltpu.VMEM((512, NODES), F32),
                pltpu.VMEM((TABLE, 512), BF16),
                pltpu.VMEM((ITERS + 1, 2, ROWS, 128), F32),
                pltpu.VMEM((len(stages), 8, 128), F32),
                pltpu.VMEM((len(stages), most, 8, 128), F32),
                pltpu.VMEM((7 * BLOCKS, 1, NODES), F32),
                pltpu.VMEM((2 * BLOCKS, 1, NODES), F32),
                pltpu.SMEM((2, SLOTS), jnp.int32),
                pltpu.VMEM((2, SLOTS), jnp.int32),
                pltpu.VMEM((9 * BLOCKS, NODES, 8), F32),
                dma((6,)),
                dma((8,)),
                dma((8,)),
                dma((ITERS - 1, 8)),
                dma((ITERS - 1, 8)),
                dma((ITERS, 8)),
                dma((ITERS, 8)),
                dma((len(stages), most)),
                dma((len(stages), most)),
            ],
            compiler_params=pltpu.CompilerParams(
                collective_id=1, has_side_effects=True, vmem_limit_bytes=60 * 1024 * 1024
            ),
            cost_estimate=pl.CostEstimate(
                flops=61 * 65536 * 40, bytes_accessed=200000, transcendentals=61 * 65536
            ),
        )
        arguments = (
            node_coords.reshape(3 * BLOCKS, 1, NODES),
            solution.reshape(2 * BLOCKS, 1, NODES),
            residual.reshape(2 * BLOCKS, 1, NODES),
            direction.reshape(2 * BLOCKS, 1, NODES),
            tile_pairs.reshape(2, SLOTS),
            tile_counts,
        )
        *outs, flags, pairs = fast(*arguments)
        outs = lax.cond(
            flags[0, 0] > 0.5,
            lambda *a: tuple(general(*a[3:])),
            lambda *a: a[:3],
            *outs,
            *arguments[:4],
            pairs,
            arguments[5],
        )
        outs = pl.pallas_call(
            hand_out,
            out_shape=(fields, fields, fields),
            in_specs=[anywhere] * 3,
            out_specs=(anywhere,) * 3,
            scratch_shapes=[dma((3,))],
        )(*outs)
        return tuple(out.reshape(full_shape) for out in outs)

    fields_spec = P(None, "wide", "narrow", None, None)
    return jax.shard_map(
        on_device,
        mesh=mesh,
        in_specs=(
            fields_spec,
            fields_spec,
            fields_spec,
            fields_spec,
            P("wide", "narrow", None, None),
            P("wide", "narrow"),
        ),
        out_specs=(fields_spec, fields_spec, fields_spec),
        check_vma=False,
    )
```

```python
import functools

import jax
import jax.numpy as jnp
from jax import lax
from jax.experimental import pallas as pl
from jax.experimental.pallas import tpu as pltpu
from jax.sharding import PartitionSpec as P

ITERS = 3
RADIUS = 0.9
MESH = pl.DeviceIdType.MESH
F32 = jnp.float32
BF16 = jnp.bfloat16

BLOCKS = 9
NODES = 256
SLOTS = 61
ROWS = 40
TABLE = 368
GROUP = 3
CHUNK = 16

PHI_SLOPE = 4.0 / RADIUS**5
PHI_CONST = 1.0 / RADIUS**4


def dot_bf16(left, right, transposed):
    dims = (((1,), (1 if transposed else 0,)), ((), ()))
    return lax.dot_general(left, right, dims, preferred_element_type=F32)


def split(value):
    high = value.astype(BF16)
    return high, (value - high.astype(F32)).astype(BF16)


def stage_peers(wide, narrow, stages):
    peers = []
    for axis, places in stages:
        here = wide if axis == "wide" else narrow
        rank, size = 0, 1
        for stride, count in places:
            rank = rank * count + here // stride % count
            size *= count
        group = []
        for step in range(1, size):
            other = (rank + step) % size
            position = here
            left = other
            for stride, count in reversed(places):
                position = position + (left % count - here // stride % count) * stride
                left = left // count
            group.append((position, narrow) if axis == "wide" else (wide, position))
        peers.append(group)
    return peers


def general_body(
    sizes,
    stages,
    coord_ref,
    sol_ref,
    res_ref,
    dir_ref,
    pairs_hbm_ref,
    count_ref,
    new_sol_ref,
    new_res_ref,
    new_dir_ref,
    near0,
    nearq,
    part,
    got,
    khi_even,
    klo_even,
    khi_odd,
    klo_odd,
    thi_even,
    tlo_even,
    thi_odd,
    tlo_odd,
    stage_even,
    stage_odd,
    pieces,
    slot_out,
    onehot,
    basis,
    sums,
    sum_in,
    raw,
    sol_rows,
    pairs_ref,
    pairs_vec_ref,
    cols,
    load_sems,
    near_send,
    near_recv,
    q_send,
    q_recv,
    fold_send,
    fold_recv,
    sum_send,
    sum_recv,
):
    wide_size, narrow_size = sizes
    wide = lax.axis_index("wide")
    narrow = lax.axis_index("narrow")
    neighbours = []
    for d in range(9):
        if d != 4:
            to_wide = (wide + (d // 3 - 1) + wide_size) % wide_size
            to_narrow = (narrow + (d % 3 - 1) + narrow_size) % narrow_size
            neighbours.append((d, (to_wide, to_narrow)))
    peers = stage_peers(wide, narrow, stages)

    loads = [
        pltpu.make_async_copy(source, landing, load_sems.at[at])
        for at, (source, landing) in enumerate(
            (
                (dir_ref, raw.at[pl.ds(0, 2 * BLOCKS)]),
                (res_ref, raw.at[pl.ds(2 * BLOCKS, 2 * BLOCKS)]),
                (coord_ref, raw.at[pl.ds(4 * BLOCKS, 3 * BLOCKS)]),
                (pairs_hbm_ref, pairs_ref),
                (pairs_hbm_ref, pairs_vec_ref),
                (sol_ref, sol_rows),
            )
        )
    ]
    for load in loads:
        load.start()

    barrier = pltpu.get_barrier_semaphore()
    targets = [device for _, device in neighbours] + [device for group in peers for device in group]
    for device in targets:
        pl.semaphore_signal(barrier, inc=1, device_id=device, device_id_type=MESH)

    for load in loads:
        load.wait()
    for k in range(BLOCKS):
        own = 4 * BLOCKS + k
        for c in range(7):
            near0[own, c : c + 1, :] = raw[c * BLOCKS + k]
        near0[own, 7:8, :] = jnp.zeros((1, NODES), F32)

    pl.semaphore_wait(barrier, len(targets))

    pending = []

    def exchange(source, landing, send_sem, recv_sem):
        copies = []
        for at, (d, device) in enumerate(neighbours):
            copy = pltpu.make_async_remote_copy(
                src_ref=source(d),
                dst_ref=landing(8 - d, 7 - at),
                send_sem=send_sem.at[at],
                recv_sem=recv_sem.at[7 - at],
                device_id=device,
                device_id_type=MESH,
            )
            copy.start()
            copies.append(copy)
        pending.extend(copies)

        def wait(at):
            pltpu.make_async_remote_copy(
                src_ref=source(4),
                dst_ref=landing(at + at // 4, at),
                send_sem=send_sem.at[at],
                recv_sem=recv_sem.at[at],
                device_id=neighbours[0][1],
                device_id_type=MESH,
            ).wait_recv()

        return wait

    arrive = exchange(
        lambda d: near0.at[pl.ds(4 * BLOCKS, BLOCKS)],
        lambda d, at: near0.at[pl.ds(d * BLOCKS, BLOCKS)],
        near_send,
        near_recv,
    )

    slot_of = lax.broadcasted_iota(jnp.int32, (64, 512), 0)
    lane_slot = lax.broadcasted_iota(jnp.int32, (64, 512), 1) // 8
    spread = jnp.where(slot_of == lane_slot, 1.0, 0.0).astype(BF16)
    left_id = pairs_vec_ref[0:1, :]
    right_id = pairs_vec_ref[1:2, :]
    live = lax.broadcasted_iota(jnp.int32, (1, SLOTS), 1) < count_ref[0:1, 0:1]
    toward_left = jnp.where(live, left_id, 255)
    toward_right = jnp.where(live & (left_id != right_id), right_id, 255)
    ids = jnp.concatenate([toward_right, toward_left] + [toward_left] * 6, axis=0).astype(F32)
    ids = jnp.concatenate([ids, jnp.full((8, 64 - SLOTS), 255.0, F32)], axis=1)
    wanted = dot_bf16(ids.astype(BF16), spread, False)
    lane = lax.broadcasted_iota(jnp.int32, (8, 512), 1)
    target = jnp.where(lane % 8 < 4, wanted[0:1, :], wanted[1:2, :]).astype(jnp.int32)
    for first in range(0, TABLE, CHUNK):
        row = lax.broadcasted_iota(jnp.int32, (CHUNK, 512), 0) + first
        place = row % ROWS
        block = jnp.where(place < 4 * BLOCKS, row // ROWS * BLOCKS + place // 4, 200)
        match = (block == target[0:1, :]) & (
            row % 4 == lax.broadcasted_iota(jnp.int32, (CHUNK, 512), 1) % 4
        )
        onehot[pl.ds(first, CHUNK), :] = jnp.where(match, 1.0, 0.0).astype(BF16)

    slot_out[pl.ds(8 * SLOTS, 512 - 8 * SLOTS), :] = jnp.zeros((512 - 8 * SLOTS, NODES), F32)
    half = lax.broadcasted_iota(jnp.int32, (8, NODES), 0) < 4

    def put_pieces(j, rows_at, value):
        high = value.astype(BF16).astype(F32)
        low = value - high
        if rows_at == 0:
            rows = jnp.where(half, high, pltpu.roll(low, 4, 0))
        else:
            rows = jnp.where(half, pltpu.roll(high, 4, 0), low)
        pieces[j] = jnp.concatenate([rows, rows], axis=0).astype(BF16)

    for h in range(2):
        for k in range(BLOCKS):
            basis[0, h, 4 * k : 4 * k + 4, :] = near0[4 * BLOCKS + k, 0:4, 128 * h : 128 * h + 128]
        basis[0, h, 4 * BLOCKS : ROWS, :] = jnp.zeros((ROWS - 4 * BLOCKS, 128), F32)

    def prepare(d):
        for k in range(BLOCKS):
            j = d * BLOCKS + k
            value = near0[j]
            put_pieces(j, 0, value)
            cols[j] = jnp.transpose(value)

    def prepare_next(at, carry):
        arrive(at)
        prepare(at + at // 4)
        return carry

    prepare(4)
    lax.fori_loop(0, 8, prepare_next, 0)

    def evaluate(s, refs, stage, at):
        high_ref, low_ref, high_turned, low_turned = refs
        left = cols.at[pairs_ref[0, s]]
        right = near0[pairs_ref[1, s]]
        rights = [jnp.broadcast_to(right[4 + axis : 5 + axis, :], (CHUNK, NODES)) for axis in range(3)]
        for first in range(0, NODES, CHUNK):
            column = left[first : first + CHUNK, :]
            squared = None
            for axis in range(3):
                offset = column[:, 4 + axis : 5 + axis] - rights[axis]
                squared = offset * offset if squared is None else squared + offset * offset
            squared = jnp.minimum(squared, RADIUS * RADIUS)
            distance = squared * lax.rsqrt(jnp.maximum(squared, 1e-36))
            rest = RADIUS - distance
            rest = rest * rest
            rest = rest * rest
            value = rest * (PHI_SLOPE * distance + PHI_CONST)
            high, low = split(value)
            high_ref[at, first : first + CHUNK, :] = high
            low_ref[at, first : first + CHUNK, :] = low
            stage[first : first + CHUNK, :] = value
        for first in range(0, NODES, 128):
            high, low = split(jnp.transpose(stage[first : first + 128, :]))
            high_turned[at, :, first : first + 128] = high
            low_turned[at, :, first : first + 128] = low

    def product(s, refs, at):
        high_ref, low_ref, high_turned, low_turned = refs
        left = pieces[pairs_ref[0, s]]
        right = pieces[pairs_ref[1, s]]
        to_right = dot_bf16(left, high_ref[at], False) + dot_bf16(left, low_ref[at], False)
        to_left = dot_bf16(right, high_turned[at], False) + dot_bf16(right, low_turned[at], False)
        to_right = to_right[0:8]
        to_left = to_left[0:8]
        to_right = to_right + pltpu.roll(to_right, 4, 0)
        to_left = to_left + pltpu.roll(to_left, 4, 0)
        slot_out[pl.ds(pl.multiple_of(s * 8, 8), 8), :] = jnp.where(half, to_right, to_left)

    even = (khi_even, klo_even, thi_even, tlo_even)
    odd = (khi_odd, klo_odd, thi_odd, tlo_odd)

    def evaluate_and_multiply(t, carry):
        before = jnp.maximum(t - 1, 0)
        product(2 * before, even, before)
        evaluate(2 * t, even, stage_even, t)
        product(2 * before + 1, odd, before)
        evaluate(jnp.minimum(2 * t + 1, SLOTS - 1), odd, stage_odd, t)
        return carry

    def products(g, carry):
        for u in range(GROUP):
            at = g * GROUP + u
            product(2 * at, even, at)
            product(2 * at + 1, odd, at)
        return carry

    for it in range(ITERS):
        if it == 0:
            lax.fori_loop(0, SLOTS // 2 + 1, evaluate_and_multiply, 0)
        else:
            lax.fori_loop(0, SLOTS // 2 // GROUP, products, 0)
        product(SLOTS - 1, even, SLOTS // 2)
        high, low = split(slot_out[...])
        table = onehot[...]
        added = dot_bf16(table, high, False) + dot_bf16(table, low, False)
        for d in range(9):
            part[it, d] = added[d * ROWS : (d + 1) * ROWS]
        arrive = exchange(
            lambda d: part.at[it, d],
            lambda d, at: got.at[it, at],
            fold_send.at[it],
            fold_recv.at[it],
        )
        image = part[it, 4]
        for at in range(8):
            arrive(at)
            image = image + got[it, at]
        for h in range(2):
            basis[it + 1, h] = image[:, 128 * h : 128 * h + 128]
        if it + 1 < ITERS:
            nearq[it, 4] = image
            arrive = exchange(
                lambda d: nearq.at[it, 4],
                lambda d, at: nearq.at[it, d],
                q_send.at[it],
                q_recv.at[it],
            )

            def refresh(d):
                for k in range(0, BLOCKS, 2):
                    value = nearq[it, d, 4 * k : 4 * k + 8, :]
                    put_pieces(d * BLOCKS + k, 0, value)
                    if k + 1 < BLOCKS:
                        put_pieces(d * BLOCKS + k + 1, 4, value)

            def refresh_next(at, carry):
                arrive(at)
                refresh(at + at // 4)
                return carry

            refresh(4)
            lax.fori_loop(0, 8, refresh_next, 0)

    lane = lax.broadcasted_iota(jnp.int32, (8, 128), 1)
    forward = lax.broadcasted_iota(jnp.int32, (8, 128), 0) % 4 < 2

    def swapped(value):
        return jnp.where(forward, pltpu.roll(value, 6, 0), pltpu.roll(value, 2, 0))

    tiles = [
        [basis[i, h, g : g + 8, :] for h in range(2) for g in range(0, ROWS, 8)]
        for i in range(ITERS + 1)
    ]
    crossed = [[swapped(tile) for tile in row] for row in tiles]
    places = {}
    gram = jnp.zeros((8, 128), F32)
    for i in range(ITERS + 1):
        for j in range(i, ITERS + 1):
            for kind, other in (("same", tiles), ("cross", crossed)):
                total = None
                for mine, theirs in zip(tiles[i], other[j]):
                    term = mine * theirs
                    total = term if total is None else total + term
                column = jnp.sum(total, axis=1, keepdims=True)
                places[kind, i, j] = len(places)
                gram = jnp.where(lane == places[kind, i, j], column, gram)

    for stage, group_peers in enumerate(peers):
        sums[stage] = gram
        copies = []
        for at, device in enumerate(group_peers):
            copy = pltpu.make_async_remote_copy(
                src_ref=sums.at[stage],
                dst_ref=sum_in.at[stage, at],
                send_sem=sum_send.at[stage, at],
                recv_sem=sum_recv.at[stage, at],
                device_id=device,
                device_id_type=MESH,
            )
            copy.start()
            copies.append(copy)
        pending.extend(copies)
        for at, copy in enumerate(copies):
            copy.wait_recv()
            gram = gram + sum_in[stage, at]
    gram = gram + pltpu.roll(gram, 4, 0)

    def entry(kind, i, j, second):
        value = jnp.broadcast_to(gram[:, places[kind, i, j] : places[kind, i, j] + 1], (8, 128))
        return pltpu.roll(value, 6, 0) if second else value

    chain = ITERS + 1
    inner = {}
    for i in range(chain):
        for j in range(chain):
            inner[i, j] = entry("same", min(i, j), max(i, j), False)
            if i < ITERS and j < ITERS:
                inner[chain + i, chain + j] = entry("same", min(i, j), max(i, j), True)
            if j < ITERS:
                cross = entry("cross", min(i, j), max(i, j), i > j)
                inner[i, chain + j] = cross
                inner[chain + j, i] = cross

    def bilinear(first, second):
        total = None
        for i, a in first.items():
            inside = None
            for j, b in second.items():
                term = b * inner[i, j]
                inside = term if inside is None else inside + term
            inside = a * inside
            total = inside if total is None else total + inside
        return total

    def combine(base, scale, other):
        result = dict(base)
        for i, value in other.items():
            result[i] = result[i] + scale * value if i in result else scale * value
        return result

    one = jnp.ones((8, 128), F32)
    in_x, in_r, in_p = {}, {chain: one}, {0: one}
    norm_now = inner[chain, chain]
    for it in range(ITERS):
        image = {i + 1: value for i, value in in_p.items()}
        step = norm_now / bilinear(in_p, image)
        in_x = combine(in_x, step, in_p)
        in_r = combine(in_r, -step, image)
        norm_next = bilinear(in_r, in_r)
        in_p = combine(in_r, norm_next / norm_now, in_p)
        norm_now = norm_next

    for f, h in ((0, 0), (0, 1), (1, 0), (1, 1)):
        lanes = slice(128 * h, 128 * h + 128)
        vectors = {}
        for i in range(chain):
            vectors[i] = basis[i, h, pl.ds(f, BLOCKS, stride=4), :]
            if i < ITERS:
                vectors[chain + i] = basis[i, h, pl.ds(2 + f, BLOCKS, stride=4), :]

        def mixed(total, coefficients):
            for i, value in coefficients.items():
                term = value[f : f + 1, :] * vectors[i]
                total = term if total is None else total + term
            return total

        results = (mixed(None, in_x), mixed(None, in_r), mixed(None, in_p))
        for k in range(BLOCKS):
            at = f * BLOCKS + k
            new_sol_ref[at, :, lanes] = sol_rows[at, :, lanes] + results[0][k : k + 1, :]
            new_res_ref[at, :, lanes] = results[1][k : k + 1, :]
            new_dir_ref[at, :, lanes] = results[2][k : k + 1, :]

    for copy in pending:
        copy.wait_send()


INNER = 29
OUTER = 32
INNER_FOURS = INNER // 4
OUTER_FOURS = OUTER // 4
INNER_WIDTH = 512
FAST_WIDTH = INNER_WIDTH + 8 * OUTER
FAST_TABLE = 64
P_ROWS = 24


def fast_body(
    sizes,
    stages,
    coord_ref,
    sol_ref,
    res_ref,
    dir_ref,
    pairs_hbm_ref,
    count_ref,
    new_sol_ref,
    new_res_ref,
    new_dir_ref,
    flag_ref,
    pairs_out_ref,
    own0,
    near0,
    nearq,
    nearp,
    khi_0,
    khi_1,
    khi_2,
    khi_3,
    klo_0,
    klo_1,
    klo_2,
    klo_3,
    own_pieces,
    pieces,
    slot_out,
    onehot,
    basis,
    sums,
    sum_in,
    raw,
    sol_rows,
    pairs_vec_ref,
    own_columns,
    inner_rows,
    outer_rows,
    inner_entries,
    outer_entries,
    load_sems,
    entry_sems,
    near_send,
    near_recv,
    q_send,
    q_recv,
    sum_send,
    sum_recv,
):
    wide_size, narrow_size = sizes
    wide = lax.axis_index("wide")
    narrow = lax.axis_index("narrow")
    neighbours = []
    for d in range(9):
        if d != 4:
            to_wide = (wide + (d // 3 - 1) + wide_size) % wide_size
            to_narrow = (narrow + (d % 3 - 1) + narrow_size) % narrow_size
            neighbours.append((d, (to_wide, to_narrow)))
    peers = stage_peers(wide, narrow, stages)

    loads = [
        pltpu.make_async_copy(source, landing, load_sems.at[at])
        for at, (source, landing) in enumerate(
            (
                (pairs_hbm_ref, pairs_vec_ref),
                (dir_ref, raw.at[pl.ds(0, 2 * BLOCKS)]),
                (res_ref, raw.at[pl.ds(2 * BLOCKS, 2 * BLOCKS)]),
                (coord_ref, raw.at[pl.ds(4 * BLOCKS, 3 * BLOCKS)]),
                (sol_ref, sol_rows),
            )
        )
    ]
    for load in loads:
        load.start()

    barrier = pltpu.get_barrier_semaphore()
    targets = [device for _, device in neighbours] + [device for group in peers for device in group]
    for device in targets:
        pl.semaphore_signal(barrier, inc=1, device_id=device, device_id_type=MESH)

    for load in loads:
        load.wait()
    pairs_out_ref[...] = pairs_vec_ref[...]
    live = lax.broadcasted_iota(jnp.int32, (2, SLOTS), 1) < count_ref[0:1, 0:1]
    own_list = jnp.where(live, pairs_vec_ref[...], 255).astype(F32)
    own_list = jnp.concatenate([own_list, jnp.full((2, 128 - SLOTS), 255.0, F32)], axis=1)
    for k in range(BLOCKS):
        for c in range(7):
            own0[k, c : c + 1, :] = raw[c * BLOCKS + k]
        own0[k, 7:8, :] = jnp.zeros((1, NODES), F32)
    own0[0, 7:8, 0:128] = own_list[0:1, :]
    own0[0, 7:8, 128:256] = own_list[1:2, :]

    pl.semaphore_wait(barrier, len(targets))

    pending = []

    def exchange(source, landing, send_sem, recv_sem):
        for at in (0, 2, 5, 7, 3, 4, 1, 6):
            d, device = neighbours[at]
            copy = pltpu.make_async_remote_copy(
                src_ref=source,
                dst_ref=landing(8 - d),
                send_sem=send_sem.at[at],
                recv_sem=recv_sem.at[7 - at],
                device_id=device,
                device_id_type=MESH,
            )
            copy.start()
            pending.append(copy)

        def wait(at):
            pltpu.make_async_remote_copy(
                src_ref=source,
                dst_ref=landing(at + at // 4),
                send_sem=send_sem.at[at],
                recv_sem=recv_sem.at[at],
                device_id=neighbours[0][1],
                device_id_type=MESH,
            ).wait_recv()

        return wait

    near_arrive = exchange(
        own0,
        lambda d: near0.at[pl.ds(d * BLOCKS, BLOCKS)],
        near_send,
        near_recv,
    )

    half = lax.broadcasted_iota(jnp.int32, (8, NODES), 0) < 4

    def put_pieces(to, j, rows_at, value):
        high = value.astype(BF16).astype(F32)
        low = value - high
        if rows_at == 0:
            rows = jnp.where(half, high, pltpu.roll(low, 4, 0))
        else:
            rows = jnp.where(half, pltpu.roll(high, 4, 0), low)
        to[j] = jnp.concatenate([rows, rows], axis=0).astype(BF16)

    for h in range(2):
        for k in range(BLOCKS):
            basis[0, h, 4 * k : 4 * k + 4, :] = own0[k, 0:4, 128 * h : 128 * h + 128]
        basis[0, h, 4 * BLOCKS : ROWS, :] = jnp.zeros((ROWS - 4 * BLOCKS, 128), F32)


    before_lane = lax.broadcasted_iota(jnp.int32, (128, 128), 0) < lax.broadcasted_iota(
        jnp.int32, (128, 128), 1
    )
    before_lane = jnp.where(before_lane, 1.0, 0.0).astype(BF16)
    entry_of = lax.broadcasted_iota(jnp.int32, (32, 128), 0).astype(F32)
    row_of = lax.broadcasted_iota(jnp.int32, (8, 128), 0)

    def compact(wanted_rows, codes, rows, most_entries):
        count = wanted_rows.shape[0]
        before_row = lax.broadcasted_iota(jnp.int32, (count, count), 0) > lax.broadcasted_iota(
            jnp.int32, (count, count), 1
        )
        in_row = dot_bf16(wanted_rows.astype(BF16), before_lane, False)
        row_total = jnp.broadcast_to(jnp.sum(wanted_rows, axis=1, keepdims=True), (count, 128))
        rank = in_row + dot_bf16(
            jnp.where(before_row, 1.0, 0.0).astype(BF16), row_total.astype(BF16), False
        )
        everything = jnp.sum(row_total, axis=0, keepdims=True)
        rank = jnp.where(wanted_rows > 0.5, rank, -1.0)
        gathered = jnp.zeros((32, 128), F32)
        for row in rows:
            gathered = gathered + jnp.where(
                entry_of == rank[row : row + 1, :], codes[row : row + 1, :], 0.0
            )
        gathered = jnp.broadcast_to(jnp.sum(gathered, axis=1, keepdims=True), (32, 128))
        gathered = jnp.concatenate([gathered, jnp.zeros((96, 128), F32)], axis=0)
        code = jnp.transpose(gathered)[0:8, :].astype(jnp.int32)
        return code, jnp.where(everything > most_entries + 0.5, 1.0, 0.0)

    def fill_onehot(start, wanted):
        width = wanted.shape[1]
        for first in range(0, FAST_TABLE, CHUNK):
            row = lax.broadcasted_iota(jnp.int32, (CHUNK, width), 0) + first
            lane = lax.broadcasted_iota(jnp.int32, (CHUNK, width), 1)
            second = row - ROWS
            block = jnp.where(row < ROWS, row >> 2, second >> 1)
            vector = jnp.where(row < ROWS, row & 3, second & 1)
            match = (block == wanted) & (vector == (lane & 3))
            onehot[first : first + CHUNK, start : start + width] = jnp.where(
                match, 1.0, 0.0
            ).astype(BF16)

    def spread_over(targets_rows, width, shift):
        entry_row = lax.broadcasted_iota(jnp.int32, (128, width), 0)
        entry_lane = lax.broadcasted_iota(jnp.int32, (128, width), 1) >> shift
        spread = jnp.where(entry_row == entry_lane, 1.0, 0.0).astype(BF16)
        return dot_bf16(targets_rows.astype(F32).astype(BF16), spread, False).astype(jnp.int32)

    own_left = jnp.broadcast_to(own_list[0:1, :], (8, 128)) - 4.0 * BLOCKS
    own_right = jnp.broadcast_to(own_list[1:2, :], (8, 128)) - 4.0 * BLOCKS
    inside = (own_left > -0.5) & (own_left < BLOCKS - 0.5) & (own_right > -0.5) & (own_right < BLOCKS - 0.5)
    code, overflow = compact(
        jnp.where(inside & (row_of == 0), 1.0, 0.0), own_left * 128.0 + own_right + 1.0, (0,), INNER
    )
    filled = code > 0
    code = jnp.maximum(code - 1, 0)
    inner_left, inner_right = code >> 7, code & 127
    inner_rows[...] = jnp.where(row_of == 0, inner_left, inner_right)
    inner_load = pltpu.make_async_copy(inner_rows, inner_entries, entry_sems.at[0])
    inner_load.start()

    def own_block(k, carry):
        value = own0[k]
        put_pieces(own_pieces, k, 0, value)
        turned = jnp.transpose(value)
        for axis in range(3):
            own_columns[k, axis] = jnp.broadcast_to(turned[:, 4 + axis : 5 + axis], (NODES, 128))
        return carry

    lax.fori_loop(0, BLOCKS, own_block, 0)

    ends = jnp.where(row_of == 0, inner_left, inner_right)
    ends = jnp.where(filled & ((row_of == 0) | (inner_left != inner_right)), ends, 200)
    wanted = spread_over(ends, INNER_WIDTH, 4)
    lane = lax.broadcasted_iota(jnp.int32, (1, INNER_WIDTH), 1)
    fill_onehot(0, jnp.where((lane & 8) == 0, wanted[0:1, :], wanted[1:2, :]))
    inner_load.wait()

    def evaluate(block, other, refs, at):
        high_ref, low_ref = refs
        block = jnp.clip(block, 0, BLOCKS - 1)
        for h in range(2):
            lanes = slice(128 * h, 128 * h + 128)
            others = [
                jnp.broadcast_to(other[4 + axis : 5 + axis, lanes], (CHUNK, 128)) for axis in range(3)
            ]
            for first in range(0, NODES, CHUNK):
                squared = None
                for axis in range(3):
                    offset = own_columns[block, axis, first : first + CHUNK, :] - others[axis]
                    squared = offset * offset if squared is None else squared + offset * offset
                squared = jnp.minimum(squared, RADIUS * RADIUS)
                distance = squared * lax.rsqrt(jnp.maximum(squared, 1e-36))
                rest = RADIUS - distance
                rest = rest * rest
                rest = rest * rest
                high, low = split(rest * (PHI_SLOPE * distance + PHI_CONST))
                high_ref[at, first : first + CHUNK, lanes] = high
                low_ref[at, first : first + CHUNK, lanes] = low

    def evaluate_inner(e, refs, at):
        other = own0[jnp.clip(inner_entries[1, e], 0, BLOCKS - 1)]
        evaluate(inner_entries[0, e], other, refs, at)

    def evaluate_outer(e, refs, at):
        other = near0[jnp.clip(outer_entries[1, e], 0, 9 * BLOCKS - 1)]
        evaluate(outer_entries[0, e], other, refs, at)

    def product_inner(e, refs, at):
        high, low = refs[0][at], refs[1][at]
        left = own_pieces[jnp.clip(inner_entries[0, e], 0, BLOCKS - 1)]
        right = own_pieces[jnp.clip(inner_entries[1, e], 0, BLOCKS - 1)]
        to_left = dot_bf16(right, high, True) + dot_bf16(right, low, True)
        to_right = dot_bf16(left, high, False) + dot_bf16(left, low, False)
        start = pl.multiple_of(e * 16, 16)
        slot_out[pl.ds(start, 8), :] = to_left[0:8]
        slot_out[pl.ds(start + 8, 8), :] = to_right[0:8]

    def product_outer(e, refs, at):
        other = pieces[jnp.clip(outer_entries[1, e], 0, 9 * BLOCKS - 1)]
        result = dot_bf16(other, refs[0][at], True) + dot_bf16(other, refs[1][at], True)
        slot_out[pl.ds(pl.multiple_of(INNER_WIDTH + e * 8, 8), 8), :] = result[0:8]

    tiles_of = ((khi_0, klo_0), (khi_1, klo_1), (khi_2, klo_2), (khi_3, klo_3))

    def evaluate_and_multiply(evaluate_one, product_one, start, fours):
        def step(t, carry):
            before = jnp.maximum(t - 1, 0)
            for u, refs in enumerate(tiles_of):
                product_one(4 * before + u, refs, start + before)
                evaluate_one(4 * t + u, refs, start + t)
            return carry

        lax.fori_loop(0, fours, step, 0)

    def last_four(product_one, start, fours):
        for u, refs in enumerate(tiles_of):
            product_one(4 * (fours - 1) + u, refs, start + fours - 1)

    def multiply(product_one, start, fours, group):
        def step(g, carry):
            for at in range(group):
                for u, refs in enumerate(tiles_of):
                    product_one(4 * (g * group + at) + u, refs, start + g * group + at)
            return carry

        lax.fori_loop(0, fours // group, step, 0)

    slot_out[16 * INNER : INNER_WIDTH, :] = jnp.zeros((INNER_WIDTH - 16 * INNER, NODES), F32)
    evaluate_and_multiply(evaluate_inner, product_inner, 0, INNER_FOURS)
    for at in range(8):
        near_arrive(at)
    evaluate_inner(INNER - 1, tiles_of[0], INNER_FOURS)
    last_four(product_inner, 0, INNER_FOURS)

    dead_rows = jnp.full((7, 128), 255.0, F32)
    device_row = lax.broadcasted_iota(jnp.int32, (16, 128), 0)
    add_wide = (device_row * 11 >> 5) - 1
    add_narrow = device_row - (add_wide + 1) * 3 - 1

    def here(row):
        lanes = slice(128 * row, 128 * row + 128)
        rows = [own0[0, 7:8, lanes] if d == 4 else near0[d * BLOCKS, 7:8, lanes] for d in range(9)]
        ids = jnp.concatenate(rows + [dead_rows], axis=0)
        ids = ids.astype(jnp.int32)
        is_live = ids < 200
        ids = jnp.where(is_live, ids, 0)
        device = ids * 7282 >> 16
        within = ids - device * 9
        at_wide = device * 11 >> 5
        at_narrow = device - at_wide * 3 + add_narrow
        at_wide = at_wide + add_wide
        mine = is_live & (at_wide == 1) & (at_narrow == 1)
        return mine, within, at_wide * 27 + at_narrow * 9 + within

    left_mine, left_within, left_here = here(0)
    right_mine, right_within, right_here = here(1)
    wanted_rows = jnp.concatenate(
        [
            jnp.where(left_mine & jnp.logical_not(right_mine), 1.0, 0.0),
            jnp.where(right_mine & jnp.logical_not(left_mine), 1.0, 0.0),
        ],
        axis=0,
    )
    codes = jnp.concatenate(
        [left_within * 128 + right_here + 1, right_within * 128 + left_here + 1], axis=0
    ).astype(F32)
    code, too_many = compact(wanted_rows, codes, (*range(9), *range(16, 25)), OUTER)
    overflow = overflow + too_many
    filled = code > 0
    code = jnp.maximum(code - 1, 0)
    outer_rows[...] = jnp.where(row_of == 0, code >> 7, code & 127)
    outer_load = pltpu.make_async_copy(outer_rows, outer_entries, entry_sems.at[1])
    outer_load.start()
    fill_onehot(INNER_WIDTH, spread_over(jnp.where(filled, code >> 7, 200), 8 * OUTER, 3)[0:1, :])

    product_inner(INNER - 1, tiles_of[0], INNER_FOURS)

    def added(start, end):
        high, low = split(slot_out[start:end, :])
        table = onehot[:, start:end]
        return dot_bf16(table, high, False) + dot_bf16(table, low, False)

    inner_image = added(0, INNER_WIDTH)

    def prepare_next(at, carry):
        for k in range(BLOCKS):
            j = (at + at // 4) * BLOCKS + k
            put_pieces(pieces, j, 0, near0[j])
        return carry

    lax.fori_loop(0, 8, prepare_next, 0)
    outer_load.wait()
    evaluate_and_multiply(evaluate_outer, product_outer, INNER_FOURS + 1, OUTER_FOURS)
    last_four(product_outer, INNER_FOURS + 1, OUTER_FOURS)

    lane = lax.broadcasted_iota(jnp.int32, (8, 128), 1)
    forward = row_of % 4 < 2
    places = {}

    def swapped(value):
        return jnp.where(forward, pltpu.roll(value, 6, 0), pltpu.roll(value, 2, 0))

    def add_products(gram, j):
        tiles = [
            [basis[i, h, g : g + 8, :] for h in range(2) for g in range(0, ROWS, 8)] for i in range(j + 1)
        ]
        crossed = [swapped(tile) for tile in tiles[j]]
        for i in range(j + 1):
            for kind, others in (("same", tiles[j]), ("cross", crossed)):
                total = None
                for mine, theirs in zip(tiles[i], others):
                    term = mine * theirs
                    total = term if total is None else total + term
                column = jnp.sum(total, axis=1, keepdims=True)
                places[kind, i, j] = len(places)
                gram = jnp.where(lane == places[kind, i, j], column, gram)
        return gram

    gram = jnp.zeros((8, 128), F32)
    for it in range(ITERS):
        if it > 0:
            gram = add_products(gram, it - 1)
            if it + 1 == ITERS:
                gram = add_products(gram, it)
            multiply(product_inner, 0, INNER_FOURS, 1)
            product_inner(INNER - 1, tiles_of[0], INNER_FOURS)
            inner_image = added(0, INNER_WIDTH)
            refresh_others()
            multiply(product_outer, INNER_FOURS + 1, OUTER_FOURS, 2)
        image = inner_image + added(INNER_WIDTH, FAST_WIDTH)
        for h in range(2):
            basis[it + 1, h] = image[0:ROWS, 128 * h : 128 * h + 128]
        if it == 0:
            nearq[4] = image[0:ROWS]
            arrive = exchange(nearq.at[4], lambda d: nearq.at[d], q_send.at[it], q_recv.at[it])

            def refresh(d, to, first_block):
                for k in range(0, BLOCKS, 2):
                    value = nearq[d, 4 * k : 4 * k + 8, :]
                    put_pieces(to, first_block + k, 0, value)
                    if k + 1 < BLOCKS:
                        put_pieces(to, first_block + k + 1, 4, value)

            refresh(4, own_pieces, 0)

            def refresh_others(arrive=arrive, refresh=refresh):
                def refresh_next(at, carry):
                    arrive(at)
                    d = at + at // 4
                    refresh(d, pieces, d * BLOCKS)
                    return carry

                lax.fori_loop(0, 8, refresh_next, 0)

        elif it + 1 < ITERS:
            nearp[4] = image[ROWS : ROWS + P_ROWS]
            arrive_p = exchange(nearp.at[4], lambda d: nearp.at[d], q_send.at[it], q_recv.at[it])

            def refresh_p(d, to, first_block):
                for k in range(BLOCKS):
                    value = nearp[d, k // 4 * 8 : k // 4 * 8 + 8, :]
                    if k % 4:
                        value = pltpu.roll(value, 8 - k % 4 * 2, 0)
                    put_pieces(to, first_block + k, 0, value)

            refresh_p(4, own_pieces, 0)

            def refresh_others(arrive=arrive_p, refresh=refresh_p):
                def refresh_next(at, carry):
                    arrive(at)
                    d = at + at // 4
                    refresh(d, pieces, d * BLOCKS)
                    return carry

                lax.fori_loop(0, 8, refresh_next, 0)

    gram = add_products(gram, ITERS)
    gram = jnp.where(lane == 127, overflow, gram)

    for stage, group_peers in enumerate(peers):
        sums[stage] = gram
        copies = []
        count = len(group_peers)
        for at in sorted(range(count), key=lambda at: -min(at + 1, count - at)):
            copy = pltpu.make_async_remote_copy(
                src_ref=sums.at[stage],
                dst_ref=sum_in.at[stage, at],
                send_sem=sum_send.at[stage, at],
                recv_sem=sum_recv.at[stage, at],
                device_id=group_peers[at],
                device_id_type=MESH,
            )
            copy.start()
            copies.append((at, copy))
        copies = [copy for at, copy in sorted(copies, key=lambda pair: pair[0])]
        pending.extend(copies)
        for at, copy in enumerate(copies):
            copy.wait_recv()
            gram = gram + sum_in[stage, at]
    flag_ref[0, 0] = jnp.sum(jnp.where((lane == 127) & (half[:, 0:128]), gram, 0.0))
    gram = gram + pltpu.roll(gram, 4, 0)

    def entry(kind, i, j, second):
        value = jnp.broadcast_to(gram[:, places[kind, i, j] : places[kind, i, j] + 1], (8, 128))
        return pltpu.roll(value, 6, 0) if second else value

    chain = ITERS + 1
    inner = {}
    for i in range(chain):
        for j in range(chain):
            inner[i, j] = entry("same", min(i, j), max(i, j), False)
            if i < ITERS and j < ITERS:
                inner[chain + i, chain + j] = entry("same", min(i, j), max(i, j), True)
            if j < ITERS:
                cross = entry("cross", min(i, j), max(i, j), i > j)
                inner[i, chain + j] = cross
                inner[chain + j, i] = cross

    def bilinear(first, second):
        total = None
        for i, a in first.items():
            inside = None
            for j, b in second.items():
                term = b * inner[i, j]
                inside = term if inside is None else inside + term
            inside = a * inside
            total = inside if total is None else total + inside
        return total

    def combine(base, scale, other):
        result = dict(base)
        for i, value in other.items():
            result[i] = result[i] + scale * value if i in result else scale * value
        return result

    one = jnp.ones((8, 128), F32)
    in_x, in_r, in_p = {}, {chain: one}, {0: one}
    norm_now = inner[chain, chain]
    for it in range(ITERS):
        image = {i + 1: value for i, value in in_p.items()}
        step = norm_now / bilinear(in_p, image)
        in_x = combine(in_x, step, in_p)
        in_r = combine(in_r, -step, image)
        norm_next = bilinear(in_r, in_r)
        in_p = combine(in_r, norm_next / norm_now, in_p)
        norm_now = norm_next

    for f, h in ((0, 0), (0, 1), (1, 0), (1, 1)):
        lanes = slice(128 * h, 128 * h + 128)
        vectors = {}
        for i in range(chain):
            vectors[i] = basis[i, h, pl.ds(f, BLOCKS, stride=4), :]
            if i < ITERS:
                vectors[chain + i] = basis[i, h, pl.ds(2 + f, BLOCKS, stride=4), :]

        def mixed(total, coefficients):
            for i, value in coefficients.items():
                term = value[f : f + 1, :] * vectors[i]
                total = term if total is None else total + term
            return total

        results = (mixed(None, in_x), mixed(None, in_r), mixed(None, in_p))
        for k in range(BLOCKS):
            at = f * BLOCKS + k
            new_sol_ref[at, :, lanes] = sol_rows[at, :, lanes] + results[0][k : k + 1, :]
            new_res_ref[at, :, lanes] = results[1][k : k + 1, :]
            new_dir_ref[at, :, lanes] = results[2][k : k + 1, :]

    for copy in pending:
        copy.wait_send()


def hand_out(*refs):
    sems = refs[6]
    copies = [pltpu.make_async_copy(refs[i], refs[3 + i], sems.at[i]) for i in range(3)]
    for copy in copies:
        copy.start()
    for copy in copies:
        copy.wait()


def solution(mesh):
    sizes = (mesh.shape["wide"], mesh.shape["narrow"])
    if sizes[0] == 64:
        stages = (
            ("narrow", ((1, sizes[1]),)),
            ("wide", ((2, 8),)),
            ("wide", ((16, 4), (1, 2))),
        )
    else:
        stages = (("narrow", ((1, sizes[1]),)), ("wide", ((1, sizes[0]),)))
    most = 0
    for _, places in stages:
        size = 1
        for _, count in places:
            size *= count
        most = max(most, size - 1)

    def on_device(node_coords, solution, residual, direction, tile_pairs, tile_counts):
        full_shape = direction.shape
        fields = jax.ShapeDtypeStruct((2 * BLOCKS, 1, NODES), F32)
        vmem = pl.BlockSpec(memory_space=pltpu.VMEM)
        anywhere = pl.BlockSpec(memory_space=pl.ANY)
        dma = pltpu.SemaphoreType.DMA
        fast = pl.pallas_call(
            functools.partial(fast_body, sizes, stages),
            out_shape=(fields, fields, fields, jax.ShapeDtypeStruct((1, 1), F32), jax.ShapeDtypeStruct((2, SLOTS), jnp.int32)),
            in_specs=[anywhere] * 5 + [vmem],
            out_specs=(vmem, vmem, vmem, pl.BlockSpec(memory_space=pltpu.SMEM), vmem),
            scratch_shapes=[
                pltpu.VMEM((BLOCKS, 8, NODES), F32),
                pltpu.VMEM((9 * BLOCKS, 8, NODES), F32),
                pltpu.VMEM((9, ROWS, NODES), F32),
                pltpu.VMEM((9, P_ROWS, NODES), F32),
                *[pltpu.VMEM((INNER_FOURS + 1 + OUTER_FOURS, NODES, NODES), BF16)] * 8,
                pltpu.VMEM((BLOCKS, 16, NODES), BF16),
                pltpu.VMEM((9 * BLOCKS, 16, NODES), BF16),
                pltpu.VMEM((FAST_WIDTH, NODES), F32),
                pltpu.VMEM((FAST_TABLE, FAST_WIDTH), BF16),
                pltpu.VMEM((ITERS + 1, 2, ROWS, 128), F32),
                pltpu.VMEM((len(stages), 8, 128), F32),
                pltpu.VMEM((len(stages), most, 8, 128), F32),
                pltpu.VMEM((7 * BLOCKS, 1, NODES), F32),
                pltpu.VMEM((2 * BLOCKS, 1, NODES), F32),
                pltpu.VMEM((2, SLOTS), jnp.int32),
                pltpu.VMEM((BLOCKS, 3, NODES, 128), F32),
                pltpu.VMEM((8, 128), jnp.int32),
                pltpu.VMEM((8, 128), jnp.int32),
                pltpu.SMEM((8, 128), jnp.int32),
                pltpu.SMEM((8, 128), jnp.int32),
                dma((5,)),
                dma((2,)),
                dma((8,)),
                dma((8,)),
                dma((ITERS - 1, 8)),
                dma((ITERS - 1, 8)),
                dma((len(stages), most)),
                dma((len(stages), most)),
            ],
            compiler_params=pltpu.CompilerParams(
                collective_id=0, has_side_effects=True, vmem_limit_bytes=60 * 1024 * 1024
            ),
            cost_estimate=pl.CostEstimate(
                flops=81 * 65536 * 40, bytes_accessed=200000, transcendentals=81 * 65536
            ),
        )
        general = pl.pallas_call(
            functools.partial(general_body, sizes, stages),
            out_shape=(fields, fields, fields),
            in_specs=[anywhere] * 5 + [vmem],
            out_specs=(vmem, vmem, vmem),
            scratch_shapes=[
                pltpu.VMEM((9 * BLOCKS, 8, NODES), F32),
                pltpu.VMEM((ITERS - 1, 9, ROWS, NODES), F32),
                pltpu.VMEM((ITERS, 9, ROWS, NODES), F32),
                pltpu.VMEM((ITERS, 8, ROWS, NODES), F32),
                pltpu.VMEM((SLOTS // 2 + 1, NODES, NODES), BF16),
                pltpu.VMEM((SLOTS // 2 + 1, NODES, NODES), BF16),
                pltpu.VMEM((SLOTS // 2 + 1, NODES, NODES), BF16),
                pltpu.VMEM((SLOTS // 2 + 1, NODES, NODES), BF16),
                pltpu.VMEM((SLOTS // 2 + 1, NODES, NODES), BF16),
                pltpu.VMEM((SLOTS // 2 + 1, NODES, NODES), BF16),
                pltpu.VMEM((SLOTS // 2 + 1, NODES, NODES), BF16),
                pltpu.VMEM((SLOTS // 2 + 1, NODES, NODES), BF16),
                pltpu.VMEM((NODES, NODES), F32),
                pltpu.VMEM((NODES, NODES), F32),
                pltpu.VMEM((9 * BLOCKS, 16, NODES), BF16),
                pltpu.VMEM((512, NODES), F32),
                pltpu.VMEM((TABLE, 512), BF16),
                pltpu.VMEM((ITERS + 1, 2, ROWS, 128), F32),
                pltpu.VMEM((len(stages), 8, 128), F32),
                pltpu.VMEM((len(stages), most, 8, 128), F32),
                pltpu.VMEM((7 * BLOCKS, 1, NODES), F32),
                pltpu.VMEM((2 * BLOCKS, 1, NODES), F32),
                pltpu.SMEM((2, SLOTS), jnp.int32),
                pltpu.VMEM((2, SLOTS), jnp.int32),
                pltpu.VMEM((9 * BLOCKS, NODES, 8), F32),
                dma((6,)),
                dma((8,)),
                dma((8,)),
                dma((ITERS - 1, 8)),
                dma((ITERS - 1, 8)),
                dma((ITERS, 8)),
                dma((ITERS, 8)),
                dma((len(stages), most)),
                dma((len(stages), most)),
            ],
            compiler_params=pltpu.CompilerParams(
                collective_id=1, has_side_effects=True, vmem_limit_bytes=60 * 1024 * 1024
            ),
            cost_estimate=pl.CostEstimate(
                flops=61 * 65536 * 40, bytes_accessed=200000, transcendentals=61 * 65536
            ),
        )
        arguments = (
            node_coords.reshape(3 * BLOCKS, 1, NODES),
            solution.reshape(2 * BLOCKS, 1, NODES),
            residual.reshape(2 * BLOCKS, 1, NODES),
            direction.reshape(2 * BLOCKS, 1, NODES),
            tile_pairs.reshape(2, SLOTS),
            tile_counts,
        )
        *outs, flags, pairs = fast(*arguments)
        outs = lax.cond(
            flags[0, 0] > 0.5,
            lambda *a: tuple(general(*a[3:])),
            lambda *a: a[:3],
            *outs,
            *arguments[:4],
            pairs,
            arguments[5],
        )
        outs = pl.pallas_call(
            hand_out,
            out_shape=(fields, fields, fields),
            in_specs=[anywhere] * 3,
            out_specs=(anywhere,) * 3,
            scratch_shapes=[dma((3,))],
        )(*outs)
        return tuple(out.reshape(full_shape) for out in outs)

    fields_spec = P(None, "wide", "narrow", None, None)
    return jax.shard_map(
        on_device,
        mesh=mesh,
        in_specs=(
            fields_spec,
            fields_spec,
            fields_spec,
            fields_spec,
            P("wide", "narrow", None, None),
            P("wide", "narrow"),
        ),
        out_specs=(fields_spec, fields_spec, fields_spec),
        check_vma=False,
    )
```

```python
import functools

import jax
import jax.numpy as jnp
from jax import lax
from jax.experimental import pallas as pl
from jax.experimental.pallas import tpu as pltpu
from jax.sharding import PartitionSpec as P

ITERS = 3
RADIUS = 0.9
MESH = pl.DeviceIdType.MESH
F32 = jnp.float32
BF16 = jnp.bfloat16

BLOCKS = 9
NODES = 256
SLOTS = 61
ROWS = 40
TABLE = 368
GROUP = 3
CHUNK = 16

PHI_SLOPE = 4.0 / RADIUS**5
PHI_CONST = 1.0 / RADIUS**4


def dot_bf16(left, right, transposed):
    dims = (((1,), (1 if transposed else 0,)), ((), ()))
    return lax.dot_general(left, right, dims, preferred_element_type=F32)


def split(value):
    high = value.astype(BF16)
    return high, (value - high.astype(F32)).astype(BF16)


def stage_peers(wide, narrow, stages):
    peers = []
    for axis, places in stages:
        here = wide if axis == "wide" else narrow
        rank, size = 0, 1
        for stride, count in places:
            rank = rank * count + here // stride % count
            size *= count
        group = []
        for step in range(1, size):
            other = (rank + step) % size
            position = here
            left = other
            for stride, count in reversed(places):
                position = position + (left % count - here // stride % count) * stride
                left = left // count
            group.append((position, narrow) if axis == "wide" else (wide, position))
        peers.append(group)
    return peers


def general_body(
    sizes,
    stages,
    coord_ref,
    sol_ref,
    res_ref,
    dir_ref,
    pairs_hbm_ref,
    count_ref,
    new_sol_ref,
    new_res_ref,
    new_dir_ref,
    near0,
    nearq,
    part,
    got,
    khi_even,
    klo_even,
    khi_odd,
    klo_odd,
    thi_even,
    tlo_even,
    thi_odd,
    tlo_odd,
    stage_even,
    stage_odd,
    pieces,
    slot_out,
    onehot,
    basis,
    sums,
    sum_in,
    raw,
    sol_rows,
    pairs_ref,
    pairs_vec_ref,
    cols,
    load_sems,
    near_send,
    near_recv,
    q_send,
    q_recv,
    fold_send,
    fold_recv,
    sum_send,
    sum_recv,
):
    wide_size, narrow_size = sizes
    wide = lax.axis_index("wide")
    narrow = lax.axis_index("narrow")
    neighbours = []
    for d in range(9):
        if d != 4:
            to_wide = (wide + (d // 3 - 1) + wide_size) % wide_size
            to_narrow = (narrow + (d % 3 - 1) + narrow_size) % narrow_size
            neighbours.append((d, (to_wide, to_narrow)))
    peers = stage_peers(wide, narrow, stages)

    loads = [
        pltpu.make_async_copy(source, landing, load_sems.at[at])
        for at, (source, landing) in enumerate(
            (
                (dir_ref, raw.at[pl.ds(0, 2 * BLOCKS)]),
                (res_ref, raw.at[pl.ds(2 * BLOCKS, 2 * BLOCKS)]),
                (coord_ref, raw.at[pl.ds(4 * BLOCKS, 3 * BLOCKS)]),
                (pairs_hbm_ref, pairs_ref),
                (pairs_hbm_ref, pairs_vec_ref),
                (sol_ref, sol_rows),
            )
        )
    ]
    for load in loads:
        load.start()

    barrier = pltpu.get_barrier_semaphore()
    targets = [device for _, device in neighbours] + [device for group in peers for device in group]
    for device in targets:
        pl.semaphore_signal(barrier, inc=1, device_id=device, device_id_type=MESH)

    for load in loads:
        load.wait()
    for k in range(BLOCKS):
        own = 4 * BLOCKS + k
        for c in range(7):
            near0[own, c : c + 1, :] = raw[c * BLOCKS + k]
        near0[own, 7:8, :] = jnp.zeros((1, NODES), F32)

    pl.semaphore_wait(barrier, len(targets))

    pending = []

    def exchange(source, landing, send_sem, recv_sem):
        copies = []
        for at, (d, device) in enumerate(neighbours):
            copy = pltpu.make_async_remote_copy(
                src_ref=source(d),
                dst_ref=landing(8 - d, 7 - at),
                send_sem=send_sem.at[at],
                recv_sem=recv_sem.at[7 - at],
                device_id=device,
                device_id_type=MESH,
            )
            copy.start()
            copies.append(copy)
        pending.extend(copies)

        def wait(at):
            pltpu.make_async_remote_copy(
                src_ref=source(4),
                dst_ref=landing(at + at // 4, at),
                send_sem=send_sem.at[at],
                recv_sem=recv_sem.at[at],
                device_id=neighbours[0][1],
                device_id_type=MESH,
            ).wait_recv()

        return wait

    arrive = exchange(
        lambda d: near0.at[pl.ds(4 * BLOCKS, BLOCKS)],
        lambda d, at: near0.at[pl.ds(d * BLOCKS, BLOCKS)],
        near_send,
        near_recv,
    )

    slot_of = lax.broadcasted_iota(jnp.int32, (64, 512), 0)
    lane_slot = lax.broadcasted_iota(jnp.int32, (64, 512), 1) // 8
    spread = jnp.where(slot_of == lane_slot, 1.0, 0.0).astype(BF16)
    left_id = pairs_vec_ref[0:1, :]
    right_id = pairs_vec_ref[1:2, :]
    live = lax.broadcasted_iota(jnp.int32, (1, SLOTS), 1) < count_ref[0:1, 0:1]
    toward_left = jnp.where(live, left_id, 255)
    toward_right = jnp.where(live & (left_id != right_id), right_id, 255)
    ids = jnp.concatenate([toward_right, toward_left] + [toward_left] * 6, axis=0).astype(F32)
    ids = jnp.concatenate([ids, jnp.full((8, 64 - SLOTS), 255.0, F32)], axis=1)
    wanted = dot_bf16(ids.astype(BF16), spread, False)
    lane = lax.broadcasted_iota(jnp.int32, (8, 512), 1)
    target = jnp.where(lane % 8 < 4, wanted[0:1, :], wanted[1:2, :]).astype(jnp.int32)
    for first in range(0, TABLE, CHUNK):
        row = lax.broadcasted_iota(jnp.int32, (CHUNK, 512), 0) + first
        place = row % ROWS
        block = jnp.where(place < 4 * BLOCKS, row // ROWS * BLOCKS + place // 4, 200)
        match = (block == target[0:1, :]) & (
            row % 4 == lax.broadcasted_iota(jnp.int32, (CHUNK, 512), 1) % 4
        )
        onehot[pl.ds(first, CHUNK), :] = jnp.where(match, 1.0, 0.0).astype(BF16)

    slot_out[pl.ds(8 * SLOTS, 512 - 8 * SLOTS), :] = jnp.zeros((512 - 8 * SLOTS, NODES), F32)
    half = lax.broadcasted_iota(jnp.int32, (8, NODES), 0) < 4

    def put_pieces(j, rows_at, value):
        high = value.astype(BF16).astype(F32)
        low = value - high
        if rows_at == 0:
            rows = jnp.where(half, high, pltpu.roll(low, 4, 0))
        else:
            rows = jnp.where(half, pltpu.roll(high, 4, 0), low)
        pieces[j] = jnp.concatenate([rows, rows], axis=0).astype(BF16)

    for h in range(2):
        for k in range(BLOCKS):
            basis[0, h, 4 * k : 4 * k + 4, :] = near0[4 * BLOCKS + k, 0:4, 128 * h : 128 * h + 128]
        basis[0, h, 4 * BLOCKS : ROWS, :] = jnp.zeros((ROWS - 4 * BLOCKS, 128), F32)

    def prepare(d):
        for k in range(BLOCKS):
            j = d * BLOCKS + k
            value = near0[j]
            put_pieces(j, 0, value)
            cols[j] = jnp.transpose(value)

    def prepare_next(at, carry):
        arrive(at)
        prepare(at + at // 4)
        return carry

    prepare(4)
    lax.fori_loop(0, 8, prepare_next, 0)

    def evaluate(s, refs, stage, at):
        high_ref, low_ref, high_turned, low_turned = refs
        left = cols.at[pairs_ref[0, s]]
        right = near0[pairs_ref[1, s]]
        rights = [jnp.broadcast_to(right[4 + axis : 5 + axis, :], (CHUNK, NODES)) for axis in range(3)]
        for first in range(0, NODES, CHUNK):
            column = left[first : first + CHUNK, :]
            squared = None
            for axis in range(3):
                offset = column[:, 4 + axis : 5 + axis] - rights[axis]
                squared = offset * offset if squared is None else squared + offset * offset
            squared = jnp.minimum(squared, RADIUS * RADIUS)
            distance = squared * lax.rsqrt(jnp.maximum(squared, 1e-36))
            rest = RADIUS - distance
            rest = rest * rest
            rest = rest * rest
            value = rest * (PHI_SLOPE * distance + PHI_CONST)
            high, low = split(value)
            high_ref[at, first : first + CHUNK, :] = high
            low_ref[at, first : first + CHUNK, :] = low
            stage[first : first + CHUNK, :] = value
        for first in range(0, NODES, 128):
            high, low = split(jnp.transpose(stage[first : first + 128, :]))
            high_turned[at, :, first : first + 128] = high
            low_turned[at, :, first : first + 128] = low

    def product(s, refs, at):
        high_ref, low_ref, high_turned, low_turned = refs
        left = pieces[pairs_ref[0, s]]
        right = pieces[pairs_ref[1, s]]
        to_right = dot_bf16(left, high_ref[at], False) + dot_bf16(left, low_ref[at], False)
        to_left = dot_bf16(right, high_turned[at], False) + dot_bf16(right, low_turned[at], False)
        to_right = to_right[0:8]
        to_left = to_left[0:8]
        to_right = to_right + pltpu.roll(to_right, 4, 0)
        to_left = to_left + pltpu.roll(to_left, 4, 0)
        slot_out[pl.ds(pl.multiple_of(s * 8, 8), 8), :] = jnp.where(half, to_right, to_left)

    even = (khi_even, klo_even, thi_even, tlo_even)
    odd = (khi_odd, klo_odd, thi_odd, tlo_odd)

    def evaluate_and_multiply(t, carry):
        before = jnp.maximum(t - 1, 0)
        product(2 * before, even, before)
        evaluate(2 * t, even, stage_even, t)
        product(2 * before + 1, odd, before)
        evaluate(jnp.minimum(2 * t + 1, SLOTS - 1), odd, stage_odd, t)
        return carry

    def products(g, carry):
        for u in range(GROUP):
            at = g * GROUP + u
            product(2 * at, even, at)
            product(2 * at + 1, odd, at)
        return carry

    for it in range(ITERS):
        if it == 0:
            lax.fori_loop(0, SLOTS // 2 + 1, evaluate_and_multiply, 0)
        else:
            lax.fori_loop(0, SLOTS // 2 // GROUP, products, 0)
        product(SLOTS - 1, even, SLOTS // 2)
        high, low = split(slot_out[...])
        table = onehot[...]
        added = dot_bf16(table, high, False) + dot_bf16(table, low, False)
        for d in range(9):
            part[it, d] = added[d * ROWS : (d + 1) * ROWS]
        arrive = exchange(
            lambda d: part.at[it, d],
            lambda d, at: got.at[it, at],
            fold_send.at[it],
            fold_recv.at[it],
        )
        image = part[it, 4]
        for at in range(8):
            arrive(at)
            image = image + got[it, at]
        for h in range(2):
            basis[it + 1, h] = image[:, 128 * h : 128 * h + 128]
        if it + 1 < ITERS:
            nearq[it, 4] = image
            arrive = exchange(
                lambda d: nearq.at[it, 4],
                lambda d, at: nearq.at[it, d],
                q_send.at[it],
                q_recv.at[it],
            )

            def refresh(d):
                for k in range(0, BLOCKS, 2):
                    value = nearq[it, d, 4 * k : 4 * k + 8, :]
                    put_pieces(d * BLOCKS + k, 0, value)
                    if k + 1 < BLOCKS:
                        put_pieces(d * BLOCKS + k + 1, 4, value)

            def refresh_next(at, carry):
                arrive(at)
                refresh(at + at // 4)
                return carry

            refresh(4)
            lax.fori_loop(0, 8, refresh_next, 0)

    lane = lax.broadcasted_iota(jnp.int32, (8, 128), 1)
    forward = lax.broadcasted_iota(jnp.int32, (8, 128), 0) % 4 < 2

    def swapped(value):
        return jnp.where(forward, pltpu.roll(value, 6, 0), pltpu.roll(value, 2, 0))

    tiles = [
        [basis[i, h, g : g + 8, :] for h in range(2) for g in range(0, ROWS, 8)]
        for i in range(ITERS + 1)
    ]
    crossed = [[swapped(tile) for tile in row] for row in tiles]
    places = {}
    gram = jnp.zeros((8, 128), F32)
    for i in range(ITERS + 1):
        for j in range(i, ITERS + 1):
            for kind, other in (("same", tiles), ("cross", crossed)):
                total = None
                for mine, theirs in zip(tiles[i], other[j]):
                    term = mine * theirs
                    total = term if total is None else total + term
                column = jnp.sum(total, axis=1, keepdims=True)
                places[kind, i, j] = len(places)
                gram = jnp.where(lane == places[kind, i, j], column, gram)

    for stage, group_peers in enumerate(peers):
        sums[stage] = gram
        copies = []
        for at, device in enumerate(group_peers):
            copy = pltpu.make_async_remote_copy(
                src_ref=sums.at[stage],
                dst_ref=sum_in.at[stage, at],
                send_sem=sum_send.at[stage, at],
                recv_sem=sum_recv.at[stage, at],
                device_id=device,
                device_id_type=MESH,
            )
            copy.start()
            copies.append(copy)
        pending.extend(copies)
        for at, copy in enumerate(copies):
            copy.wait_recv()
            gram = gram + sum_in[stage, at]
    gram = gram + pltpu.roll(gram, 4, 0)

    def entry(kind, i, j, second):
        value = jnp.broadcast_to(gram[:, places[kind, i, j] : places[kind, i, j] + 1], (8, 128))
        return pltpu.roll(value, 6, 0) if second else value

    chain = ITERS + 1
    inner = {}
    for i in range(chain):
        for j in range(chain):
            inner[i, j] = entry("same", min(i, j), max(i, j), False)
            if i < ITERS and j < ITERS:
                inner[chain + i, chain + j] = entry("same", min(i, j), max(i, j), True)
            if j < ITERS:
                cross = entry("cross", min(i, j), max(i, j), i > j)
                inner[i, chain + j] = cross
                inner[chain + j, i] = cross

    def bilinear(first, second):
        total = None
        for i, a in first.items():
            inside = None
            for j, b in second.items():
                term = b * inner[i, j]
                inside = term if inside is None else inside + term
            inside = a * inside
            total = inside if total is None else total + inside
        return total

    def combine(base, scale, other):
        result = dict(base)
        for i, value in other.items():
            result[i] = result[i] + scale * value if i in result else scale * value
        return result

    one = jnp.ones((8, 128), F32)
    in_x, in_r, in_p = {}, {chain: one}, {0: one}
    norm_now = inner[chain, chain]
    for it in range(ITERS):
        image = {i + 1: value for i, value in in_p.items()}
        step = norm_now / bilinear(in_p, image)
        in_x = combine(in_x, step, in_p)
        in_r = combine(in_r, -step, image)
        norm_next = bilinear(in_r, in_r)
        in_p = combine(in_r, norm_next / norm_now, in_p)
        norm_now = norm_next

    for f, h in ((0, 0), (0, 1), (1, 0), (1, 1)):
        lanes = slice(128 * h, 128 * h + 128)
        vectors = {}
        for i in range(chain):
            vectors[i] = basis[i, h, pl.ds(f, BLOCKS, stride=4), :]
            if i < ITERS:
                vectors[chain + i] = basis[i, h, pl.ds(2 + f, BLOCKS, stride=4), :]

        def mixed(total, coefficients):
            for i, value in coefficients.items():
                term = value[f : f + 1, :] * vectors[i]
                total = term if total is None else total + term
            return total

        results = (mixed(None, in_x), mixed(None, in_r), mixed(None, in_p))
        for k in range(BLOCKS):
            at = f * BLOCKS + k
            new_sol_ref[at, :, lanes] = sol_rows[at, :, lanes] + results[0][k : k + 1, :]
            new_res_ref[at, :, lanes] = results[1][k : k + 1, :]
            new_dir_ref[at, :, lanes] = results[2][k : k + 1, :]

    for copy in pending:
        copy.wait_send()


INNER = 29
OUTER = 32
INNER_FOURS = INNER // 4
OUTER_FOURS = OUTER // 4
INNER_WIDTH = 512
FAST_WIDTH = INNER_WIDTH + 8 * OUTER
FAST_TABLE = 64
P_ROWS = 24


MOST = 31


def two_stage_peers(wide, narrow, narrow_size):
    x, rank = wide // 16, wide % 16
    first = [
        ((wide - rank + (rank + step) % 16, narrow), min(step, 16 - step)) for step in range(1, 16)
    ]
    second = []
    for right in range(4):
        for up in range(narrow_size):
            if right or up:
                device = (rank + (x + right) % 4 * 16, (narrow + up) % narrow_size)
                second.append((device, min(right, 4 - right) + min(up, narrow_size - up)))
    return first, second


def fast_body(
    sizes,
    coord_ref,
    sol_ref,
    res_ref,
    dir_ref,
    pairs_hbm_ref,
    count_ref,
    new_sol_ref,
    new_res_ref,
    new_dir_ref,
    flag_ref,
    pairs_out_ref,
    own0,
    near0,
    nearq,
    nearp,
    khi_0,
    khi_1,
    khi_2,
    khi_3,
    klo_0,
    klo_1,
    klo_2,
    klo_3,
    own_pieces,
    pieces,
    slot_out,
    onehot,
    basis,
    sums,
    sum_in,
    raw,
    sol_rows,
    pairs_vec_ref,
    own_columns,
    inner_rows,
    outer_rows,
    inner_entries,
    outer_entries,
    load_sems,
    entry_sems,
    near_send,
    near_recv,
    q_send,
    q_recv,
    sum_send,
    sum_recv,
):
    wide_size, narrow_size = sizes
    wide = lax.axis_index("wide")
    narrow = lax.axis_index("narrow")
    neighbours = []
    for d in range(9):
        if d != 4:
            to_wide = (wide + (d // 3 - 1) + wide_size) % wide_size
            to_narrow = (narrow + (d % 3 - 1) + narrow_size) % narrow_size
            neighbours.append((d, (to_wide, to_narrow)))
    peers = two_stage_peers(wide, narrow, narrow_size)

    loads = [
        pltpu.make_async_copy(source, landing, load_sems.at[at])
        for at, (source, landing) in enumerate(
            (
                (pairs_hbm_ref, pairs_vec_ref),
                (dir_ref, raw.at[pl.ds(0, 2 * BLOCKS)]),
                (res_ref, raw.at[pl.ds(2 * BLOCKS, 2 * BLOCKS)]),
                (coord_ref, raw.at[pl.ds(4 * BLOCKS, 3 * BLOCKS)]),
                (sol_ref, sol_rows),
            )
        )
    ]
    for load in loads:
        load.start()

    barrier = pltpu.get_barrier_semaphore()
    targets = [device for _, device in neighbours] + [device for group in peers for device, _ in group]
    for device in targets:
        pl.semaphore_signal(barrier, inc=1, device_id=device, device_id_type=MESH)

    for load in loads:
        load.wait()
    pairs_out_ref[...] = pairs_vec_ref[...]
    live = lax.broadcasted_iota(jnp.int32, (2, SLOTS), 1) < count_ref[0:1, 0:1]
    own_list = jnp.where(live, pairs_vec_ref[...], 255).astype(F32)
    own_list = jnp.concatenate([own_list, jnp.full((2, 128 - SLOTS), 255.0, F32)], axis=1)
    for k in range(BLOCKS):
        for c in range(7):
            own0[k, c : c + 1, :] = raw[c * BLOCKS + k]
        own0[k, 7:8, :] = jnp.zeros((1, NODES), F32)
    own0[0, 7:8, 0:128] = own_list[0:1, :]
    own0[0, 7:8, 128:256] = own_list[1:2, :]

    pl.semaphore_wait(barrier, len(targets))

    pending = []

    def exchange(source, landing, send_sem, recv_sem):
        for at in (0, 2, 5, 7, 3, 4, 1, 6):
            d, device = neighbours[at]
            copy = pltpu.make_async_remote_copy(
                src_ref=source,
                dst_ref=landing(8 - d),
                send_sem=send_sem.at[at],
                recv_sem=recv_sem.at[7 - at],
                device_id=device,
                device_id_type=MESH,
            )
            copy.start()
            pending.append(copy)

        def wait(at):
            pltpu.make_async_remote_copy(
                src_ref=source,
                dst_ref=landing(at + at // 4),
                send_sem=send_sem.at[at],
                recv_sem=recv_sem.at[at],
                device_id=neighbours[0][1],
                device_id_type=MESH,
            ).wait_recv()

        return wait

    near_arrive = exchange(
        own0,
        lambda d: near0.at[pl.ds(d * BLOCKS, BLOCKS)],
        near_send,
        near_recv,
    )

    half = lax.broadcasted_iota(jnp.int32, (8, NODES), 0) < 4

    def put_pieces(to, j, rows_at, value):
        high = value.astype(BF16).astype(F32)
        low = value - high
        if rows_at == 0:
            rows = jnp.where(half, high, pltpu.roll(low, 4, 0))
        else:
            rows = jnp.where(half, pltpu.roll(high, 4, 0), low)
        to[j] = jnp.concatenate([rows, rows], axis=0).astype(BF16)

    for h in range(2):
        for k in range(BLOCKS):
            basis[0, h, 4 * k : 4 * k + 4, :] = own0[k, 0:4, 128 * h : 128 * h + 128]
        basis[0, h, 4 * BLOCKS : ROWS, :] = jnp.zeros((ROWS - 4 * BLOCKS, 128), F32)


    before_lane = lax.broadcasted_iota(jnp.int32, (128, 128), 0) < lax.broadcasted_iota(
        jnp.int32, (128, 128), 1
    )
    before_lane = jnp.where(before_lane, 1.0, 0.0).astype(BF16)
    entry_of = lax.broadcasted_iota(jnp.int32, (32, 128), 0).astype(F32)
    row_of = lax.broadcasted_iota(jnp.int32, (8, 128), 0)

    def compact(wanted_rows, codes, rows, most_entries):
        count = wanted_rows.shape[0]
        before_row = lax.broadcasted_iota(jnp.int32, (count, count), 0) > lax.broadcasted_iota(
            jnp.int32, (count, count), 1
        )
        in_row = dot_bf16(wanted_rows.astype(BF16), before_lane, False)
        row_total = jnp.broadcast_to(jnp.sum(wanted_rows, axis=1, keepdims=True), (count, 128))
        rank = in_row + dot_bf16(
            jnp.where(before_row, 1.0, 0.0).astype(BF16), row_total.astype(BF16), False
        )
        everything = jnp.sum(row_total, axis=0, keepdims=True)
        rank = jnp.where(wanted_rows > 0.5, rank, -1.0)
        gathered = jnp.zeros((32, 128), F32)
        for row in rows:
            gathered = gathered + jnp.where(
                entry_of == rank[row : row + 1, :], codes[row : row + 1, :], 0.0
            )
        gathered = jnp.broadcast_to(jnp.sum(gathered, axis=1, keepdims=True), (32, 128))
        gathered = jnp.concatenate([gathered, jnp.zeros((96, 128), F32)], axis=0)
        code = jnp.transpose(gathered)[0:8, :].astype(jnp.int32)
        return code, jnp.where(everything > most_entries + 0.5, 1.0, 0.0)

    def fill_onehot(start, wanted):
        width = wanted.shape[1]
        for first in range(0, FAST_TABLE, CHUNK):
            row = lax.broadcasted_iota(jnp.int32, (CHUNK, width), 0) + first
            lane = lax.broadcasted_iota(jnp.int32, (CHUNK, width), 1)
            second = row - ROWS
            block = jnp.where(row < ROWS, row >> 2, second >> 1)
            vector = jnp.where(row < ROWS, row & 3, second & 1)
            match = (block == wanted) & (vector == (lane & 3))
            onehot[first : first + CHUNK, start : start + width] = jnp.where(
                match, 1.0, 0.0
            ).astype(BF16)

    def spread_over(targets_rows, width, shift):
        entry_row = lax.broadcasted_iota(jnp.int32, (128, width), 0)
        entry_lane = lax.broadcasted_iota(jnp.int32, (128, width), 1) >> shift
        spread = jnp.where(entry_row == entry_lane, 1.0, 0.0).astype(BF16)
        return dot_bf16(targets_rows.astype(F32).astype(BF16), spread, False).astype(jnp.int32)

    own_left = jnp.broadcast_to(own_list[0:1, :], (8, 128)) - 4.0 * BLOCKS
    own_right = jnp.broadcast_to(own_list[1:2, :], (8, 128)) - 4.0 * BLOCKS
    inside = (own_left > -0.5) & (own_left < BLOCKS - 0.5) & (own_right > -0.5) & (own_right < BLOCKS - 0.5)
    code, overflow = compact(
        jnp.where(inside & (row_of == 0), 1.0, 0.0), own_left * 128.0 + own_right + 1.0, (0,), INNER
    )
    filled = code > 0
    code = jnp.maximum(code - 1, 0)
    inner_left, inner_right = code >> 7, code & 127
    inner_rows[...] = jnp.where(row_of == 0, inner_left, inner_right)
    inner_load = pltpu.make_async_copy(inner_rows, inner_entries, entry_sems.at[0])
    inner_load.start()

    def own_block(k, carry):
        value = own0[k]
        put_pieces(own_pieces, k, 0, value)
        turned = jnp.transpose(value)
        for axis in range(3):
            own_columns[k, axis] = jnp.broadcast_to(turned[:, 4 + axis : 5 + axis], (NODES, 128))
        return carry

    lax.fori_loop(0, BLOCKS, own_block, 0)

    ends = jnp.where(row_of == 0, inner_left, inner_right)
    ends = jnp.where(filled & ((row_of == 0) | (inner_left != inner_right)), ends, 200)
    wanted = spread_over(ends, INNER_WIDTH, 4)
    lane = lax.broadcasted_iota(jnp.int32, (1, INNER_WIDTH), 1)
    fill_onehot(0, jnp.where((lane & 8) == 0, wanted[0:1, :], wanted[1:2, :]))
    inner_load.wait()

    def evaluate(block, other, refs, at):
        high_ref, low_ref = refs
        block = jnp.clip(block, 0, BLOCKS - 1)
        for h in range(2):
            lanes = slice(128 * h, 128 * h + 128)
            others = [
                jnp.broadcast_to(other[4 + axis : 5 + axis, lanes], (CHUNK, 128)) for axis in range(3)
            ]
            for first in range(0, NODES, CHUNK):
                squared = None
                for axis in range(3):
                    offset = own_columns[block, axis, first : first + CHUNK, :] - others[axis]
                    squared = offset * offset if squared is None else squared + offset * offset
                squared = jnp.minimum(squared, RADIUS * RADIUS)
                distance = squared * lax.rsqrt(jnp.maximum(squared, 1e-36))
                rest = RADIUS - distance
                rest = rest * rest
                rest = rest * rest
                high, low = split(rest * (PHI_SLOPE * distance + PHI_CONST))
                high_ref[at, first : first + CHUNK, lanes] = high
                low_ref[at, first : first + CHUNK, lanes] = low

    def evaluate_inner(e, refs, at):
        other = own0[jnp.clip(inner_entries[1, e], 0, BLOCKS - 1)]
        evaluate(inner_entries[0, e], other, refs, at)

    def evaluate_outer(e, refs, at):
        other = near0[jnp.clip(outer_entries[1, e], 0, 9 * BLOCKS - 1)]
        evaluate(outer_entries[0, e], other, refs, at)

    def product_inner(e, refs, at):
        high, low = refs[0][at], refs[1][at]
        left = own_pieces[jnp.clip(inner_entries[0, e], 0, BLOCKS - 1)]
        right = own_pieces[jnp.clip(inner_entries[1, e], 0, BLOCKS - 1)]
        to_left = dot_bf16(right, high, True) + dot_bf16(right, low, True)
        to_right = dot_bf16(left, high, False) + dot_bf16(left, low, False)
        start = pl.multiple_of(e * 16, 16)
        slot_out[pl.ds(start, 8), :] = to_left[0:8]
        slot_out[pl.ds(start + 8, 8), :] = to_right[0:8]

    def product_outer(e, refs, at):
        other = pieces[jnp.clip(outer_entries[1, e], 0, 9 * BLOCKS - 1)]
        result = dot_bf16(other, refs[0][at], True) + dot_bf16(other, refs[1][at], True)
        slot_out[pl.ds(pl.multiple_of(INNER_WIDTH + e * 8, 8), 8), :] = result[0:8]

    tiles_of = ((khi_0, klo_0), (khi_1, klo_1), (khi_2, klo_2), (khi_3, klo_3))

    def evaluate_and_multiply(evaluate_one, product_one, start, fours):
        def step(t, carry):
            before = jnp.maximum(t - 1, 0)
            for u, refs in enumerate(tiles_of):
                product_one(4 * before + u, refs, start + before)
                evaluate_one(4 * t + u, refs, start + t)
            return carry

        lax.fori_loop(0, fours, step, 0)

    def last_four(product_one, start, fours):
        for u, refs in enumerate(tiles_of):
            product_one(4 * (fours - 1) + u, refs, start + fours - 1)

    def multiply(product_one, start, fours, group):
        def step(g, carry):
            for at in range(group):
                for u, refs in enumerate(tiles_of):
                    product_one(4 * (g * group + at) + u, refs, start + g * group + at)
            return carry

        lax.fori_loop(0, fours // group, step, 0)

    slot_out[16 * INNER : INNER_WIDTH, :] = jnp.zeros((INNER_WIDTH - 16 * INNER, NODES), F32)
    evaluate_and_multiply(evaluate_inner, product_inner, 0, INNER_FOURS)
    for at in range(8):
        near_arrive(at)
    evaluate_inner(INNER - 1, tiles_of[0], INNER_FOURS)
    last_four(product_inner, 0, INNER_FOURS)

    dead_rows = jnp.full((7, 128), 255.0, F32)
    device_row = lax.broadcasted_iota(jnp.int32, (16, 128), 0)
    add_wide = (device_row * 11 >> 5) - 1
    add_narrow = device_row - (add_wide + 1) * 3 - 1

    def here(row):
        lanes = slice(128 * row, 128 * row + 128)
        rows = [own0[0, 7:8, lanes] if d == 4 else near0[d * BLOCKS, 7:8, lanes] for d in range(9)]
        ids = jnp.concatenate(rows + [dead_rows], axis=0)
        ids = ids.astype(jnp.int32)
        is_live = ids < 200
        ids = jnp.where(is_live, ids, 0)
        device = ids * 7282 >> 16
        within = ids - device * 9
        at_wide = device * 11 >> 5
        at_narrow = device - at_wide * 3 + add_narrow
        at_wide = at_wide + add_wide
        mine = is_live & (at_wide == 1) & (at_narrow == 1)
        return mine, within, at_wide * 27 + at_narrow * 9 + within

    left_mine, left_within, left_here = here(0)
    right_mine, right_within, right_here = here(1)
    wanted_rows = jnp.concatenate(
        [
            jnp.where(left_mine & jnp.logical_not(right_mine), 1.0, 0.0),
            jnp.where(right_mine & jnp.logical_not(left_mine), 1.0, 0.0),
        ],
        axis=0,
    )
    codes = jnp.concatenate(
        [left_within * 128 + right_here + 1, right_within * 128 + left_here + 1], axis=0
    ).astype(F32)
    code, too_many = compact(wanted_rows, codes, (*range(9), *range(16, 25)), OUTER)
    overflow = overflow + too_many
    filled = code > 0
    code = jnp.maximum(code - 1, 0)
    outer_rows[...] = jnp.where(row_of == 0, code >> 7, code & 127)
    outer_load = pltpu.make_async_copy(outer_rows, outer_entries, entry_sems.at[1])
    outer_load.start()
    fill_onehot(INNER_WIDTH, spread_over(jnp.where(filled, code >> 7, 200), 8 * OUTER, 3)[0:1, :])

    product_inner(INNER - 1, tiles_of[0], INNER_FOURS)

    def added(start, end):
        high, low = split(slot_out[start:end, :])
        table = onehot[:, start:end]
        return dot_bf16(table, high, False) + dot_bf16(table, low, False)

    inner_image = added(0, INNER_WIDTH)

    def prepare_next(at, carry):
        for k in range(BLOCKS):
            j = (at + at // 4) * BLOCKS + k
            put_pieces(pieces, j, 0, near0[j])
        return carry

    lax.fori_loop(0, 8, prepare_next, 0)
    outer_load.wait()
    evaluate_and_multiply(evaluate_outer, product_outer, INNER_FOURS + 1, OUTER_FOURS)
    last_four(product_outer, INNER_FOURS + 1, OUTER_FOURS)

    lane = lax.broadcasted_iota(jnp.int32, (8, 128), 1)
    forward = row_of % 4 < 2
    places = {}

    def swapped(value):
        return jnp.where(forward, pltpu.roll(value, 6, 0), pltpu.roll(value, 2, 0))

    def add_products(gram, j):
        tiles = [
            [basis[i, h, g : g + 8, :] for h in range(2) for g in range(0, ROWS, 8)] for i in range(j + 1)
        ]
        crossed = [swapped(tile) for tile in tiles[j]]
        for i in range(j + 1):
            for kind, others in (("same", tiles[j]), ("cross", crossed)):
                total = None
                for mine, theirs in zip(tiles[i], others):
                    term = mine * theirs
                    total = term if total is None else total + term
                column = jnp.sum(total, axis=1, keepdims=True)
                places[kind, i, j] = len(places)
                gram = jnp.where(lane == places[kind, i, j], column, gram)
        return gram

    gram = jnp.zeros((8, 128), F32)
    for it in range(ITERS):
        if it > 0:
            gram = add_products(gram, it - 1)
            if it + 1 == ITERS:
                gram = add_products(gram, it)
            multiply(product_inner, 0, INNER_FOURS, 1)
            product_inner(INNER - 1, tiles_of[0], INNER_FOURS)
            inner_image = added(0, INNER_WIDTH)
            refresh_others()
            multiply(product_outer, INNER_FOURS + 1, OUTER_FOURS, 2)
        image = inner_image + added(INNER_WIDTH, FAST_WIDTH)
        for h in range(2):
            basis[it + 1, h] = image[0:ROWS, 128 * h : 128 * h + 128]
        if it == 0:
            nearq[4] = image[0:ROWS]
            arrive = exchange(nearq.at[4], lambda d: nearq.at[d], q_send.at[it], q_recv.at[it])

            def refresh(d, to, first_block):
                for k in range(0, BLOCKS, 2):
                    value = nearq[d, 4 * k : 4 * k + 8, :]
                    put_pieces(to, first_block + k, 0, value)
                    if k + 1 < BLOCKS:
                        put_pieces(to, first_block + k + 1, 4, value)

            refresh(4, own_pieces, 0)

            def refresh_others(arrive=arrive, refresh=refresh):
                def refresh_next(at, carry):
                    arrive(at)
                    d = at + at // 4
                    refresh(d, pieces, d * BLOCKS)
                    return carry

                lax.fori_loop(0, 8, refresh_next, 0)

        elif it + 1 < ITERS:
            nearp[4] = image[ROWS : ROWS + P_ROWS]
            arrive_p = exchange(nearp.at[4], lambda d: nearp.at[d], q_send.at[it], q_recv.at[it])

            def refresh_p(d, to, first_block):
                for k in range(BLOCKS):
                    value = nearp[d, k // 4 * 8 : k // 4 * 8 + 8, :]
                    if k % 4:
                        value = pltpu.roll(value, 8 - k % 4 * 2, 0)
                    put_pieces(to, first_block + k, 0, value)

            refresh_p(4, own_pieces, 0)

            def refresh_others(arrive=arrive_p, refresh=refresh_p):
                def refresh_next(at, carry):
                    arrive(at)
                    d = at + at // 4
                    refresh(d, pieces, d * BLOCKS)
                    return carry

                lax.fori_loop(0, 8, refresh_next, 0)

    gram = add_products(gram, ITERS)
    gram = jnp.where(lane == 127, overflow, gram)

    for stage, group_peers in enumerate(peers):
        sums[stage] = gram
        copies = []
        for at in sorted(range(len(group_peers)), key=lambda at: -group_peers[at][1]):
            copy = pltpu.make_async_remote_copy(
                src_ref=sums.at[stage],
                dst_ref=sum_in.at[stage, at],
                send_sem=sum_send.at[stage, at],
                recv_sem=sum_recv.at[stage, at],
                device_id=group_peers[at][0],
                device_id_type=MESH,
            )
            copy.start()
            copies.append((at, copy))
        copies = [copy for at, copy in sorted(copies, key=lambda pair: pair[0])]
        pending.extend(copies)
        for at, copy in enumerate(copies):
            copy.wait_recv()
            gram = gram + sum_in[stage, at]
    flag_ref[0, 0] = jnp.sum(jnp.where((lane == 127) & (half[:, 0:128]), gram, 0.0))
    gram = gram + pltpu.roll(gram, 4, 0)

    def entry(kind, i, j, second):
        value = jnp.broadcast_to(gram[:, places[kind, i, j] : places[kind, i, j] + 1], (8, 128))
        return pltpu.roll(value, 6, 0) if second else value

    chain = ITERS + 1
    inner = {}
    for i in range(chain):
        for j in range(chain):
            inner[i, j] = entry("same", min(i, j), max(i, j), False)
            if i < ITERS and j < ITERS:
                inner[chain + i, chain + j] = entry("same", min(i, j), max(i, j), True)
            if j < ITERS:
                cross = entry("cross", min(i, j), max(i, j), i > j)
                inner[i, chain + j] = cross
                inner[chain + j, i] = cross

    def bilinear(first, second):
        total = None
        for i, a in first.items():
            inside = None
            for j, b in second.items():
                term = b * inner[i, j]
                inside = term if inside is None else inside + term
            inside = a * inside
            total = inside if total is None else total + inside
        return total

    def combine(base, scale, other):
        result = dict(base)
        for i, value in other.items():
            result[i] = result[i] + scale * value if i in result else scale * value
        return result

    one = jnp.ones((8, 128), F32)
    in_x, in_r, in_p = {}, {chain: one}, {0: one}
    norm_now = inner[chain, chain]
    for it in range(ITERS):
        image = {i + 1: value for i, value in in_p.items()}
        step = norm_now / bilinear(in_p, image)
        in_x = combine(in_x, step, in_p)
        in_r = combine(in_r, -step, image)
        norm_next = bilinear(in_r, in_r)
        in_p = combine(in_r, norm_next / norm_now, in_p)
        norm_now = norm_next

    for f, h in ((0, 0), (0, 1), (1, 0), (1, 1)):
        lanes = slice(128 * h, 128 * h + 128)
        vectors = {}
        for i in range(chain):
            vectors[i] = basis[i, h, pl.ds(f, BLOCKS, stride=4), :]
            if i < ITERS:
                vectors[chain + i] = basis[i, h, pl.ds(2 + f, BLOCKS, stride=4), :]

        def mixed(total, coefficients):
            for i, value in coefficients.items():
                term = value[f : f + 1, :] * vectors[i]
                total = term if total is None else total + term
            return total

        results = (mixed(None, in_x), mixed(None, in_r), mixed(None, in_p))
        for k in range(BLOCKS):
            at = f * BLOCKS + k
            new_sol_ref[at, :, lanes] = sol_rows[at, :, lanes] + results[0][k : k + 1, :]
            new_res_ref[at, :, lanes] = results[1][k : k + 1, :]
            new_dir_ref[at, :, lanes] = results[2][k : k + 1, :]

    for copy in pending:
        copy.wait_send()


def hand_out(*refs):
    sems = refs[6]
    copies = [pltpu.make_async_copy(refs[i], refs[3 + i], sems.at[i]) for i in range(3)]
    for copy in copies:
        copy.start()
    for copy in copies:
        copy.wait()


def solution(mesh):
    sizes = (mesh.shape["wide"], mesh.shape["narrow"])
    if sizes[0] == 64:
        stages = (
            ("narrow", ((1, sizes[1]),)),
            ("wide", ((2, 8),)),
            ("wide", ((16, 4), (1, 2))),
        )
    else:
        stages = (("narrow", ((1, sizes[1]),)), ("wide", ((1, sizes[0]),)))
    most = 0
    for _, places in stages:
        size = 1
        for _, count in places:
            size *= count
        most = max(most, size - 1)

    def on_device(node_coords, solution, residual, direction, tile_pairs, tile_counts):
        full_shape = direction.shape
        fields = jax.ShapeDtypeStruct((2 * BLOCKS, 1, NODES), F32)
        vmem = pl.BlockSpec(memory_space=pltpu.VMEM)
        anywhere = pl.BlockSpec(memory_space=pl.ANY)
        dma = pltpu.SemaphoreType.DMA
        fast = pl.pallas_call(
            functools.partial(fast_body, sizes),
            out_shape=(fields, fields, fields, jax.ShapeDtypeStruct((1, 1), F32), jax.ShapeDtypeStruct((2, SLOTS), jnp.int32)),
            in_specs=[anywhere] * 5 + [vmem],
            out_specs=(vmem, vmem, vmem, pl.BlockSpec(memory_space=pltpu.SMEM), vmem),
            scratch_shapes=[
                pltpu.VMEM((BLOCKS, 8, NODES), F32),
                pltpu.VMEM((9 * BLOCKS, 8, NODES), F32),
                pltpu.VMEM((9, ROWS, NODES), F32),
                pltpu.VMEM((9, P_ROWS, NODES), F32),
                *[pltpu.VMEM((INNER_FOURS + 1 + OUTER_FOURS, NODES, NODES), BF16)] * 8,
                pltpu.VMEM((BLOCKS, 16, NODES), BF16),
                pltpu.VMEM((9 * BLOCKS, 16, NODES), BF16),
                pltpu.VMEM((FAST_WIDTH, NODES), F32),
                pltpu.VMEM((FAST_TABLE, FAST_WIDTH), BF16),
                pltpu.VMEM((ITERS + 1, 2, ROWS, 128), F32),
                pltpu.VMEM((2, 8, 128), F32),
                pltpu.VMEM((2, MOST, 8, 128), F32),
                pltpu.VMEM((7 * BLOCKS, 1, NODES), F32),
                pltpu.VMEM((2 * BLOCKS, 1, NODES), F32),
                pltpu.VMEM((2, SLOTS), jnp.int32),
                pltpu.VMEM((BLOCKS, 3, NODES, 128), F32),
                pltpu.VMEM((8, 128), jnp.int32),
                pltpu.VMEM((8, 128), jnp.int32),
                pltpu.SMEM((8, 128), jnp.int32),
                pltpu.SMEM((8, 128), jnp.int32),
                dma((5,)),
                dma((2,)),
                dma((8,)),
                dma((8,)),
                dma((ITERS - 1, 8)),
                dma((ITERS - 1, 8)),
                dma((2, MOST)),
                dma((2, MOST)),
            ],
            compiler_params=pltpu.CompilerParams(
                collective_id=0, has_side_effects=True, vmem_limit_bytes=60 * 1024 * 1024
            ),
            cost_estimate=pl.CostEstimate(
                flops=81 * 65536 * 40, bytes_accessed=200000, transcendentals=81 * 65536
            ),
        )
        general = pl.pallas_call(
            functools.partial(general_body, sizes, stages),
            out_shape=(fields, fields, fields),
            in_specs=[anywhere] * 5 + [vmem],
            out_specs=(vmem, vmem, vmem),
            scratch_shapes=[
                pltpu.VMEM((9 * BLOCKS, 8, NODES), F32),
                pltpu.VMEM((ITERS - 1, 9, ROWS, NODES), F32),
                pltpu.VMEM((ITERS, 9, ROWS, NODES), F32),
                pltpu.VMEM((ITERS, 8, ROWS, NODES), F32),
                pltpu.VMEM((SLOTS // 2 + 1, NODES, NODES), BF16),
                pltpu.VMEM((SLOTS // 2 + 1, NODES, NODES), BF16),
                pltpu.VMEM((SLOTS // 2 + 1, NODES, NODES), BF16),
                pltpu.VMEM((SLOTS // 2 + 1, NODES, NODES), BF16),
                pltpu.VMEM((SLOTS // 2 + 1, NODES, NODES), BF16),
                pltpu.VMEM((SLOTS // 2 + 1, NODES, NODES), BF16),
                pltpu.VMEM((SLOTS // 2 + 1, NODES, NODES), BF16),
                pltpu.VMEM((SLOTS // 2 + 1, NODES, NODES), BF16),
                pltpu.VMEM((NODES, NODES), F32),
                pltpu.VMEM((NODES, NODES), F32),
                pltpu.VMEM((9 * BLOCKS, 16, NODES), BF16),
                pltpu.VMEM((512, NODES), F32),
                pltpu.VMEM((TABLE, 512), BF16),
                pltpu.VMEM((ITERS + 1, 2, ROWS, 128), F32),
                pltpu.VMEM((len(stages), 8, 128), F32),
                pltpu.VMEM((len(stages), most, 8, 128), F32),
                pltpu.VMEM((7 * BLOCKS, 1, NODES), F32),
                pltpu.VMEM((2 * BLOCKS, 1, NODES), F32),
                pltpu.SMEM((2, SLOTS), jnp.int32),
                pltpu.VMEM((2, SLOTS), jnp.int32),
                pltpu.VMEM((9 * BLOCKS, NODES, 8), F32),
                dma((6,)),
                dma((8,)),
                dma((8,)),
                dma((ITERS - 1, 8)),
                dma((ITERS - 1, 8)),
                dma((ITERS, 8)),
                dma((ITERS, 8)),
                dma((len(stages), most)),
                dma((len(stages), most)),
            ],
            compiler_params=pltpu.CompilerParams(
                collective_id=1, has_side_effects=True, vmem_limit_bytes=60 * 1024 * 1024
            ),
            cost_estimate=pl.CostEstimate(
                flops=61 * 65536 * 40, bytes_accessed=200000, transcendentals=61 * 65536
            ),
        )
        arguments = (
            node_coords.reshape(3 * BLOCKS, 1, NODES),
            solution.reshape(2 * BLOCKS, 1, NODES),
            residual.reshape(2 * BLOCKS, 1, NODES),
            direction.reshape(2 * BLOCKS, 1, NODES),
            tile_pairs.reshape(2, SLOTS),
            tile_counts,
        )
        *outs, flags, pairs = fast(*arguments)
        outs = lax.cond(
            flags[0, 0] > 0.5,
            lambda *a: tuple(general(*a[3:])),
            lambda *a: a[:3],
            *outs,
            *arguments[:4],
            pairs,
            arguments[5],
        )
        outs = pl.pallas_call(
            hand_out,
            out_shape=(fields, fields, fields),
            in_specs=[anywhere] * 3,
            out_specs=(anywhere,) * 3,
            scratch_shapes=[dma((3,))],
        )(*outs)
        return tuple(out.reshape(full_shape) for out in outs)

    fields_spec = P(None, "wide", "narrow", None, None)
    return jax.shard_map(
        on_device,
        mesh=mesh,
        in_specs=(
            fields_spec,
            fields_spec,
            fields_spec,
            fields_spec,
            P("wide", "narrow", None, None),
            P("wide", "narrow"),
        ),
        out_specs=(fields_spec, fields_spec, fields_spec),
        check_vma=False,
    )
```

```python
import functools

import jax
import jax.numpy as jnp
from jax import lax
from jax.experimental import pallas as pl
from jax.experimental.pallas import tpu as pltpu
from jax.sharding import PartitionSpec as P

ITERS = 3
RADIUS = 0.9
MESH = pl.DeviceIdType.MESH
F32 = jnp.float32
BF16 = jnp.bfloat16

BLOCKS = 9
NODES = 256
SLOTS = 61
ROWS = 40
TABLE = 368
GROUP = 3
CHUNK = 16

PHI_SLOPE = 4.0 / RADIUS**5
PHI_CONST = 1.0 / RADIUS**4


def dot_bf16(left, right, transposed):
    dims = (((1,), (1 if transposed else 0,)), ((), ()))
    return lax.dot_general(left, right, dims, preferred_element_type=F32)


def split(value):
    high = value.astype(BF16)
    return high, (value - high.astype(F32)).astype(BF16)


def stage_peers(wide, narrow, stages):
    peers = []
    for axis, places in stages:
        here = wide if axis == "wide" else narrow
        rank, size = 0, 1
        for stride, count in places:
            rank = rank * count + here // stride % count
            size *= count
        group = []
        for step in range(1, size):
            other = (rank + step) % size
            position = here
            left = other
            for stride, count in reversed(places):
                position = position + (left % count - here // stride % count) * stride
                left = left // count
            group.append((position, narrow) if axis == "wide" else (wide, position))
        peers.append(group)
    return peers


def general_body(
    sizes,
    stages,
    coord_ref,
    sol_ref,
    res_ref,
    dir_ref,
    pairs_hbm_ref,
    count_ref,
    new_sol_ref,
    new_res_ref,
    new_dir_ref,
    near0,
    nearq,
    part,
    got,
    khi_even,
    klo_even,
    khi_odd,
    klo_odd,
    thi_even,
    tlo_even,
    thi_odd,
    tlo_odd,
    stage_even,
    stage_odd,
    pieces,
    slot_out,
    onehot,
    basis,
    sums,
    sum_in,
    raw,
    sol_rows,
    pairs_ref,
    pairs_vec_ref,
    cols,
    load_sems,
    near_send,
    near_recv,
    q_send,
    q_recv,
    fold_send,
    fold_recv,
    sum_send,
    sum_recv,
):
    wide_size, narrow_size = sizes
    wide = lax.axis_index("wide")
    narrow = lax.axis_index("narrow")
    neighbours = []
    for d in range(9):
        if d != 4:
            to_wide = (wide + (d // 3 - 1) + wide_size) % wide_size
            to_narrow = (narrow + (d % 3 - 1) + narrow_size) % narrow_size
            neighbours.append((d, (to_wide, to_narrow)))
    peers = stage_peers(wide, narrow, stages)

    loads = [
        pltpu.make_async_copy(source, landing, load_sems.at[at])
        for at, (source, landing) in enumerate(
            (
                (dir_ref, raw.at[pl.ds(0, 2 * BLOCKS)]),
                (res_ref, raw.at[pl.ds(2 * BLOCKS, 2 * BLOCKS)]),
                (coord_ref, raw.at[pl.ds(4 * BLOCKS, 3 * BLOCKS)]),
                (pairs_hbm_ref, pairs_ref),
                (pairs_hbm_ref, pairs_vec_ref),
                (sol_ref, sol_rows),
            )
        )
    ]
    for load in loads:
        load.start()

    barrier = pltpu.get_barrier_semaphore()
    targets = [device for _, device in neighbours] + [device for group in peers for device in group]
    for device in targets:
        pl.semaphore_signal(barrier, inc=1, device_id=device, device_id_type=MESH)

    for load in loads:
        load.wait()
    for k in range(BLOCKS):
        own = 4 * BLOCKS + k
        for c in range(7):
            near0[own, c : c + 1, :] = raw[c * BLOCKS + k]
        near0[own, 7:8, :] = jnp.zeros((1, NODES), F32)

    pl.semaphore_wait(barrier, len(targets))

    pending = []

    def exchange(source, landing, send_sem, recv_sem):
        copies = []
        for at, (d, device) in enumerate(neighbours):
            copy = pltpu.make_async_remote_copy(
                src_ref=source(d),
                dst_ref=landing(8 - d, 7 - at),
                send_sem=send_sem.at[at],
                recv_sem=recv_sem.at[7 - at],
                device_id=device,
                device_id_type=MESH,
            )
            copy.start()
            copies.append(copy)
        pending.extend(copies)

        def wait(at):
            pltpu.make_async_remote_copy(
                src_ref=source(4),
                dst_ref=landing(at + at // 4, at),
                send_sem=send_sem.at[at],
                recv_sem=recv_sem.at[at],
                device_id=neighbours[0][1],
                device_id_type=MESH,
            ).wait_recv()

        return wait

    arrive = exchange(
        lambda d: near0.at[pl.ds(4 * BLOCKS, BLOCKS)],
        lambda d, at: near0.at[pl.ds(d * BLOCKS, BLOCKS)],
        near_send,
        near_recv,
    )

    slot_of = lax.broadcasted_iota(jnp.int32, (64, 512), 0)
    lane_slot = lax.broadcasted_iota(jnp.int32, (64, 512), 1) // 8
    spread = jnp.where(slot_of == lane_slot, 1.0, 0.0).astype(BF16)
    left_id = pairs_vec_ref[0:1, :]
    right_id = pairs_vec_ref[1:2, :]
    live = lax.broadcasted_iota(jnp.int32, (1, SLOTS), 1) < count_ref[0:1, 0:1]
    toward_left = jnp.where(live, left_id, 255)
    toward_right = jnp.where(live & (left_id != right_id), right_id, 255)
    ids = jnp.concatenate([toward_right, toward_left] + [toward_left] * 6, axis=0).astype(F32)
    ids = jnp.concatenate([ids, jnp.full((8, 64 - SLOTS), 255.0, F32)], axis=1)
    wanted = dot_bf16(ids.astype(BF16), spread, False)
    lane = lax.broadcasted_iota(jnp.int32, (8, 512), 1)
    target = jnp.where(lane % 8 < 4, wanted[0:1, :], wanted[1:2, :]).astype(jnp.int32)
    for first in range(0, TABLE, CHUNK):
        row = lax.broadcasted_iota(jnp.int32, (CHUNK, 512), 0) + first
        place = row % ROWS
        block = jnp.where(place < 4 * BLOCKS, row // ROWS * BLOCKS + place // 4, 200)
        match = (block == target[0:1, :]) & (
            row % 4 == lax.broadcasted_iota(jnp.int32, (CHUNK, 512), 1) % 4
        )
        onehot[pl.ds(first, CHUNK), :] = jnp.where(match, 1.0, 0.0).astype(BF16)

    slot_out[pl.ds(8 * SLOTS, 512 - 8 * SLOTS), :] = jnp.zeros((512 - 8 * SLOTS, NODES), F32)
    half = lax.broadcasted_iota(jnp.int32, (8, NODES), 0) < 4

    def put_pieces(j, rows_at, value):
        high = value.astype(BF16).astype(F32)
        low = value - high
        if rows_at == 0:
            rows = jnp.where(half, high, pltpu.roll(low, 4, 0))
        else:
            rows = jnp.where(half, pltpu.roll(high, 4, 0), low)
        pieces[j] = jnp.concatenate([rows, rows], axis=0).astype(BF16)

    for h in range(2):
        for k in range(BLOCKS):
            basis[0, h, 4 * k : 4 * k + 4, :] = near0[4 * BLOCKS + k, 0:4, 128 * h : 128 * h + 128]
        basis[0, h, 4 * BLOCKS : ROWS, :] = jnp.zeros((ROWS - 4 * BLOCKS, 128), F32)

    def prepare(d):
        for k in range(BLOCKS):
            j = d * BLOCKS + k
            value = near0[j]
            put_pieces(j, 0, value)
            cols[j] = jnp.transpose(value)

    def prepare_next(at, carry):
        arrive(at)
        prepare(at + at // 4)
        return carry

    prepare(4)
    lax.fori_loop(0, 8, prepare_next, 0)

    def evaluate(s, refs, stage, at):
        high_ref, low_ref, high_turned, low_turned = refs
        left = cols.at[pairs_ref[0, s]]
        right = near0[pairs_ref[1, s]]
        rights = [jnp.broadcast_to(right[4 + axis : 5 + axis, :], (CHUNK, NODES)) for axis in range(3)]
        for first in range(0, NODES, CHUNK):
            column = left[first : first + CHUNK, :]
            squared = None
            for axis in range(3):
                offset = column[:, 4 + axis : 5 + axis] - rights[axis]
                squared = offset * offset if squared is None else squared + offset * offset
            squared = jnp.minimum(squared, RADIUS * RADIUS)
            distance = squared * lax.rsqrt(jnp.maximum(squared, 1e-36))
            rest = RADIUS - distance
            rest = rest * rest
            rest = rest * rest
            value = rest * (PHI_SLOPE * distance + PHI_CONST)
            high, low = split(value)
            high_ref[at, first : first + CHUNK, :] = high
            low_ref[at, first : first + CHUNK, :] = low
            stage[first : first + CHUNK, :] = value
        for first in range(0, NODES, 128):
            high, low = split(jnp.transpose(stage[first : first + 128, :]))
            high_turned[at, :, first : first + 128] = high
            low_turned[at, :, first : first + 128] = low

    def product(s, refs, at):
        high_ref, low_ref, high_turned, low_turned = refs
        left = pieces[pairs_ref[0, s]]
        right = pieces[pairs_ref[1, s]]
        to_right = dot_bf16(left, high_ref[at], False) + dot_bf16(left, low_ref[at], False)
        to_left = dot_bf16(right, high_turned[at], False) + dot_bf16(right, low_turned[at], False)
        to_right = to_right[0:8]
        to_left = to_left[0:8]
        to_right = to_right + pltpu.roll(to_right, 4, 0)
        to_left = to_left + pltpu.roll(to_left, 4, 0)
        slot_out[pl.ds(pl.multiple_of(s * 8, 8), 8), :] = jnp.where(half, to_right, to_left)

    even = (khi_even, klo_even, thi_even, tlo_even)
    odd = (khi_odd, klo_odd, thi_odd, tlo_odd)

    def evaluate_and_multiply(t, carry):
        before = jnp.maximum(t - 1, 0)
        product(2 * before, even, before)
        evaluate(2 * t, even, stage_even, t)
        product(2 * before + 1, odd, before)
        evaluate(jnp.minimum(2 * t + 1, SLOTS - 1), odd, stage_odd, t)
        return carry

    def products(g, carry):
        for u in range(GROUP):
            at = g * GROUP + u
            product(2 * at, even, at)
            product(2 * at + 1, odd, at)
        return carry

    for it in range(ITERS):
        if it == 0:
            lax.fori_loop(0, SLOTS // 2 + 1, evaluate_and_multiply, 0)
        else:
            lax.fori_loop(0, SLOTS // 2 // GROUP, products, 0)
        product(SLOTS - 1, even, SLOTS // 2)
        high, low = split(slot_out[...])
        table = onehot[...]
        added = dot_bf16(table, high, False) + dot_bf16(table, low, False)
        for d in range(9):
            part[it, d] = added[d * ROWS : (d + 1) * ROWS]
        arrive = exchange(
            lambda d: part.at[it, d],
            lambda d, at: got.at[it, at],
            fold_send.at[it],
            fold_recv.at[it],
        )
        image = part[it, 4]
        for at in range(8):
            arrive(at)
            image = image + got[it, at]
        for h in range(2):
            basis[it + 1, h] = image[:, 128 * h : 128 * h + 128]
        if it + 1 < ITERS:
            nearq[it, 4] = image
            arrive = exchange(
                lambda d: nearq.at[it, 4],
                lambda d, at: nearq.at[it, d],
                q_send.at[it],
                q_recv.at[it],
            )

            def refresh(d):
                for k in range(0, BLOCKS, 2):
                    value = nearq[it, d, 4 * k : 4 * k + 8, :]
                    put_pieces(d * BLOCKS + k, 0, value)
                    if k + 1 < BLOCKS:
                        put_pieces(d * BLOCKS + k + 1, 4, value)

            def refresh_next(at, carry):
                arrive(at)
                refresh(at + at // 4)
                return carry

            refresh(4)
            lax.fori_loop(0, 8, refresh_next, 0)

    lane = lax.broadcasted_iota(jnp.int32, (8, 128), 1)
    forward = lax.broadcasted_iota(jnp.int32, (8, 128), 0) % 4 < 2

    def swapped(value):
        return jnp.where(forward, pltpu.roll(value, 6, 0), pltpu.roll(value, 2, 0))

    tiles = [
        [basis[i, h, g : g + 8, :] for h in range(2) for g in range(0, ROWS, 8)]
        for i in range(ITERS + 1)
    ]
    crossed = [[swapped(tile) for tile in row] for row in tiles]
    places = {}
    gram = jnp.zeros((8, 128), F32)
    for i in range(ITERS + 1):
        for j in range(i, ITERS + 1):
            for kind, other in (("same", tiles), ("cross", crossed)):
                total = None
                for mine, theirs in zip(tiles[i], other[j]):
                    term = mine * theirs
                    total = term if total is None else total + term
                column = jnp.sum(total, axis=1, keepdims=True)
                places[kind, i, j] = len(places)
                gram = jnp.where(lane == places[kind, i, j], column, gram)

    for stage, group_peers in enumerate(peers):
        sums[stage] = gram
        copies = []
        for at, device in enumerate(group_peers):
            copy = pltpu.make_async_remote_copy(
                src_ref=sums.at[stage],
                dst_ref=sum_in.at[stage, at],
                send_sem=sum_send.at[stage, at],
                recv_sem=sum_recv.at[stage, at],
                device_id=device,
                device_id_type=MESH,
            )
            copy.start()
            copies.append(copy)
        pending.extend(copies)
        for at, copy in enumerate(copies):
            copy.wait_recv()
            gram = gram + sum_in[stage, at]
    gram = gram + pltpu.roll(gram, 4, 0)

    def entry(kind, i, j, second):
        value = jnp.broadcast_to(gram[:, places[kind, i, j] : places[kind, i, j] + 1], (8, 128))
        return pltpu.roll(value, 6, 0) if second else value

    chain = ITERS + 1
    inner = {}
    for i in range(chain):
        for j in range(chain):
            inner[i, j] = entry("same", min(i, j), max(i, j), False)
            if i < ITERS and j < ITERS:
                inner[chain + i, chain + j] = entry("same", min(i, j), max(i, j), True)
            if j < ITERS:
                cross = entry("cross", min(i, j), max(i, j), i > j)
                inner[i, chain + j] = cross
                inner[chain + j, i] = cross

    def bilinear(first, second):
        total = None
        for i, a in first.items():
            inside = None
            for j, b in second.items():
                term = b * inner[i, j]
                inside = term if inside is None else inside + term
            inside = a * inside
            total = inside if total is None else total + inside
        return total

    def combine(base, scale, other):
        result = dict(base)
        for i, value in other.items():
            result[i] = result[i] + scale * value if i in result else scale * value
        return result

    one = jnp.ones((8, 128), F32)
    in_x, in_r, in_p = {}, {chain: one}, {0: one}
    norm_now = inner[chain, chain]
    for it in range(ITERS):
        image = {i + 1: value for i, value in in_p.items()}
        step = norm_now / bilinear(in_p, image)
        in_x = combine(in_x, step, in_p)
        in_r = combine(in_r, -step, image)
        norm_next = bilinear(in_r, in_r)
        in_p = combine(in_r, norm_next / norm_now, in_p)
        norm_now = norm_next

    for f, h in ((0, 0), (0, 1), (1, 0), (1, 1)):
        lanes = slice(128 * h, 128 * h + 128)
        vectors = {}
        for i in range(chain):
            vectors[i] = basis[i, h, pl.ds(f, BLOCKS, stride=4), :]
            if i < ITERS:
                vectors[chain + i] = basis[i, h, pl.ds(2 + f, BLOCKS, stride=4), :]

        def mixed(total, coefficients):
            for i, value in coefficients.items():
                term = value[f : f + 1, :] * vectors[i]
                total = term if total is None else total + term
            return total

        results = (mixed(None, in_x), mixed(None, in_r), mixed(None, in_p))
        for k in range(BLOCKS):
            at = f * BLOCKS + k
            new_sol_ref[at, :, lanes] = sol_rows[at, :, lanes] + results[0][k : k + 1, :]
            new_res_ref[at, :, lanes] = results[1][k : k + 1, :]
            new_dir_ref[at, :, lanes] = results[2][k : k + 1, :]

    for copy in pending:
        copy.wait_send()


INNER = 29
OUTER = 32
INNER_FOURS = INNER // 4
OUTER_FOURS = OUTER // 4
INNER_WIDTH = 512
FAST_WIDTH = INNER_WIDTH + 8 * OUTER
FAST_TABLE = 64
P_ROWS = 24


MOST = 31


def two_stage_peers(wide, narrow, narrow_size):
    x, rank = wide // 16, wide % 16
    first = [
        ((wide - rank + (rank + step) % 16, narrow), min(step, 16 - step)) for step in range(1, 16)
    ]
    second = []
    for right in range(4):
        for up in range(narrow_size):
            if right or up:
                device = (rank + (x + right) % 4 * 16, (narrow + up) % narrow_size)
                second.append((device, min(right, 4 - right) + min(up, narrow_size - up)))
    return first, second


def fast_body(
    sizes,
    coord_ref,
    sol_ref,
    res_ref,
    dir_ref,
    pairs_hbm_ref,
    count_ref,
    new_sol_ref,
    new_res_ref,
    new_dir_ref,
    flag_ref,
    pairs_out_ref,
    own0,
    near0,
    nearq,
    nearp,
    khi_0,
    khi_1,
    khi_2,
    khi_3,
    klo_0,
    klo_1,
    klo_2,
    klo_3,
    own_pieces,
    pieces,
    slot_out,
    onehot,
    basis,
    sums,
    sum_in,
    raw,
    sol_rows,
    pairs_vec_ref,
    own_columns,
    inner_rows,
    outer_rows,
    inner_entries,
    outer_entries,
    load_sems,
    entry_sems,
    near_send,
    near_recv,
    q_send,
    q_recv,
    sum_send,
    sum_recv,
):
    wide_size, narrow_size = sizes
    wide = lax.axis_index("wide")
    narrow = lax.axis_index("narrow")
    neighbours = []
    for d in range(9):
        if d != 4:
            to_wide = (wide + (d // 3 - 1) + wide_size) % wide_size
            to_narrow = (narrow + (d % 3 - 1) + narrow_size) % narrow_size
            neighbours.append((d, (to_wide, to_narrow)))
    peers = two_stage_peers(wide, narrow, narrow_size)

    loads = [
        pltpu.make_async_copy(source, landing, load_sems.at[at])
        for at, (source, landing) in enumerate(
            (
                (pairs_hbm_ref, pairs_vec_ref),
                (dir_ref, raw.at[pl.ds(0, 2 * BLOCKS)]),
                (res_ref, raw.at[pl.ds(2 * BLOCKS, 2 * BLOCKS)]),
                (coord_ref, raw.at[pl.ds(4 * BLOCKS, 3 * BLOCKS)]),
                (sol_ref, sol_rows),
            )
        )
    ]
    for load in loads:
        load.start()

    barrier = pltpu.get_barrier_semaphore()
    targets = [device for _, device in neighbours] + [device for group in peers for device, _ in group]
    for device in targets:
        pl.semaphore_signal(barrier, inc=1, device_id=device, device_id_type=MESH)

    for load in loads:
        load.wait()
    pairs_out_ref[...] = pairs_vec_ref[...]
    live = lax.broadcasted_iota(jnp.int32, (2, SLOTS), 1) < count_ref[0:1, 0:1]
    own_list = jnp.where(live, pairs_vec_ref[...], 255).astype(F32)
    own_list = jnp.concatenate([own_list, jnp.full((2, 128 - SLOTS), 255.0, F32)], axis=1)
    for k in range(BLOCKS):
        for c in range(7):
            own0[k, c : c + 1, :] = raw[c * BLOCKS + k]
        own0[k, 7:8, :] = jnp.zeros((1, NODES), F32)
    own0[0, 7:8, 0:128] = own_list[0:1, :]
    own0[0, 7:8, 128:256] = own_list[1:2, :]

    pl.semaphore_wait(barrier, len(targets))

    pending = []

    def exchange(source, landing, send_sem, recv_sem):
        for at in (0, 2, 5, 7, 3, 4, 1, 6):
            d, device = neighbours[at]
            copy = pltpu.make_async_remote_copy(
                src_ref=source,
                dst_ref=landing(8 - d),
                send_sem=send_sem.at[at],
                recv_sem=recv_sem.at[7 - at],
                device_id=device,
                device_id_type=MESH,
            )
            copy.start()
            pending.append(copy)

        def wait(at):
            pltpu.make_async_remote_copy(
                src_ref=source,
                dst_ref=landing(at + at // 4),
                send_sem=send_sem.at[at],
                recv_sem=recv_sem.at[at],
                device_id=neighbours[0][1],
                device_id_type=MESH,
            ).wait_recv()

        return wait

    near_arrive = exchange(
        own0,
        lambda d: near0.at[pl.ds(d * BLOCKS, BLOCKS)],
        near_send,
        near_recv,
    )

    half = lax.broadcasted_iota(jnp.int32, (8, NODES), 0) < 4

    def put_pieces(to, j, rows_at, value):
        high = value.astype(BF16).astype(F32)
        low = value - high
        if rows_at == 0:
            rows = jnp.where(half, high, pltpu.roll(low, 4, 0))
        else:
            rows = jnp.where(half, pltpu.roll(high, 4, 0), low)
        to[j] = jnp.concatenate([rows, rows], axis=0).astype(BF16)

    for h in range(2):
        for k in range(BLOCKS):
            basis[0, h, 4 * k : 4 * k + 4, :] = own0[k, 0:4, 128 * h : 128 * h + 128]
        basis[0, h, 4 * BLOCKS : ROWS, :] = jnp.zeros((ROWS - 4 * BLOCKS, 128), F32)


    before_lane = lax.broadcasted_iota(jnp.int32, (128, 128), 0) < lax.broadcasted_iota(
        jnp.int32, (128, 128), 1
    )
    before_lane = jnp.where(before_lane, 1.0, 0.0).astype(BF16)
    entry_of = lax.broadcasted_iota(jnp.int32, (32, 128), 0).astype(F32)
    row_of = lax.broadcasted_iota(jnp.int32, (8, 128), 0)

    def compact(wanted_rows, codes, rows, most_entries):
        count = wanted_rows.shape[0]
        before_row = lax.broadcasted_iota(jnp.int32, (count, count), 0) > lax.broadcasted_iota(
            jnp.int32, (count, count), 1
        )
        in_row = dot_bf16(wanted_rows.astype(BF16), before_lane, False)
        row_total = jnp.broadcast_to(jnp.sum(wanted_rows, axis=1, keepdims=True), (count, 128))
        rank = in_row + dot_bf16(
            jnp.where(before_row, 1.0, 0.0).astype(BF16), row_total.astype(BF16), False
        )
        everything = jnp.sum(row_total, axis=0, keepdims=True)
        rank = jnp.where(wanted_rows > 0.5, rank, -1.0)
        gathered = jnp.zeros((32, 128), F32)
        for row in rows:
            gathered = gathered + jnp.where(
                entry_of == rank[row : row + 1, :], codes[row : row + 1, :], 0.0
            )
        gathered = jnp.broadcast_to(jnp.sum(gathered, axis=1, keepdims=True), (32, 128))
        gathered = jnp.concatenate([gathered, jnp.zeros((96, 128), F32)], axis=0)
        code = jnp.transpose(gathered)[0:8, :].astype(jnp.int32)
        return code, jnp.where(everything > most_entries + 0.5, 1.0, 0.0)

    def fill_onehot(start, wanted):
        width = wanted.shape[1]
        for first in range(0, FAST_TABLE, CHUNK):
            row = lax.broadcasted_iota(jnp.int32, (CHUNK, width), 0) + first
            lane = lax.broadcasted_iota(jnp.int32, (CHUNK, width), 1)
            second = row - ROWS
            block = jnp.where(row < ROWS, row >> 2, second >> 1)
            vector = jnp.where(row < ROWS, row & 3, second & 1)
            match = (block == wanted) & (vector == (lane & 3))
            onehot[first : first + CHUNK, start : start + width] = jnp.where(
                match, 1.0, 0.0
            ).astype(BF16)

    def spread_over(targets_rows, width, shift):
        entry_row = lax.broadcasted_iota(jnp.int32, (128, width), 0)
        entry_lane = lax.broadcasted_iota(jnp.int32, (128, width), 1) >> shift
        spread = jnp.where(entry_row == entry_lane, 1.0, 0.0).astype(BF16)
        return dot_bf16(targets_rows.astype(F32).astype(BF16), spread, False).astype(jnp.int32)

    own_left = jnp.broadcast_to(own_list[0:1, :], (8, 128)) - 4.0 * BLOCKS
    own_right = jnp.broadcast_to(own_list[1:2, :], (8, 128)) - 4.0 * BLOCKS
    inside = (own_left > -0.5) & (own_left < BLOCKS - 0.5) & (own_right > -0.5) & (own_right < BLOCKS - 0.5)
    code, overflow = compact(
        jnp.where(inside & (row_of == 0), 1.0, 0.0), own_left * 128.0 + own_right + 1.0, (0,), INNER
    )
    filled = code > 0
    code = jnp.maximum(code - 1, 0)
    inner_left, inner_right = code >> 7, code & 127
    inner_rows[...] = jnp.where(row_of == 0, inner_left, inner_right)
    inner_load = pltpu.make_async_copy(inner_rows, inner_entries, entry_sems.at[0])
    inner_load.start()

    def own_block(k, carry):
        value = own0[k]
        put_pieces(own_pieces, k, 0, value)
        turned = jnp.transpose(value)
        for axis in range(3):
            own_columns[k, axis] = jnp.broadcast_to(turned[:, 4 + axis : 5 + axis], (NODES, 128))
        return carry

    lax.fori_loop(0, BLOCKS, own_block, 0)

    ends = jnp.where(row_of == 0, inner_left, inner_right)
    ends = jnp.where(filled & ((row_of == 0) | (inner_left != inner_right)), ends, 200)
    wanted = spread_over(ends, INNER_WIDTH, 4)
    lane = lax.broadcasted_iota(jnp.int32, (1, INNER_WIDTH), 1)
    fill_onehot(0, jnp.where((lane & 8) == 0, wanted[0:1, :], wanted[1:2, :]))
    inner_load.wait()

    def evaluate(block, other, refs, at):
        high_ref, low_ref = refs
        block = jnp.clip(block, 0, BLOCKS - 1)
        others = [jnp.broadcast_to(other[4 + axis : 5 + axis, :], (CHUNK, NODES)) for axis in range(3)]
        for first in range(0, NODES, CHUNK):
            columns = [own_columns[block, axis, first : first + CHUNK, :] for axis in range(3)]
            for h in range(2):
                lanes = slice(128 * h, 128 * h + 128)
                squared = None
                for axis in range(3):
                    offset = columns[axis] - others[axis][:, lanes]
                    squared = offset * offset if squared is None else squared + offset * offset
                squared = jnp.minimum(squared, RADIUS * RADIUS)
                distance = squared * lax.rsqrt(jnp.maximum(squared, 1e-36))
                rest = RADIUS - distance
                rest = rest * rest
                rest = rest * rest
                high, low = split(rest * (PHI_SLOPE * distance + PHI_CONST))
                high_ref[at, first : first + CHUNK, lanes] = high
                low_ref[at, first : first + CHUNK, lanes] = low

    def evaluate_inner(e, refs, at):
        other = own0[jnp.clip(inner_entries[1, e], 0, BLOCKS - 1)]
        evaluate(inner_entries[0, e], other, refs, at)

    def evaluate_outer(e, refs, at):
        other = near0[jnp.clip(outer_entries[1, e], 0, 9 * BLOCKS - 1)]
        evaluate(outer_entries[0, e], other, refs, at)

    def product_inner(e, refs, at):
        high, low = refs[0][at], refs[1][at]
        left = own_pieces[jnp.clip(inner_entries[0, e], 0, BLOCKS - 1)]
        right = own_pieces[jnp.clip(inner_entries[1, e], 0, BLOCKS - 1)]
        to_left = dot_bf16(right, high, True) + dot_bf16(right, low, True)
        to_right = dot_bf16(left, high, False) + dot_bf16(left, low, False)
        start = pl.multiple_of(e * 16, 16)
        slot_out[pl.ds(start, 8), :] = to_left[0:8]
        slot_out[pl.ds(start + 8, 8), :] = to_right[0:8]

    def product_outer(e, refs, at):
        other = pieces[jnp.clip(outer_entries[1, e], 0, 9 * BLOCKS - 1)]
        result = dot_bf16(other, refs[0][at], True) + dot_bf16(other, refs[1][at], True)
        slot_out[pl.ds(pl.multiple_of(INNER_WIDTH + e * 8, 8), 8), :] = result[0:8]

    tiles_of = ((khi_0, klo_0), (khi_1, klo_1), (khi_2, klo_2), (khi_3, klo_3))

    def evaluate_and_multiply(evaluate_one, product_one, start, fours):
        def step(t, carry):
            before = jnp.maximum(t - 1, 0)
            for u, refs in enumerate(tiles_of):
                product_one(4 * before + u, refs, start + before)
                evaluate_one(4 * t + u, refs, start + t)
            return carry

        lax.fori_loop(0, fours, step, 0)

    def last_four(product_one, start, fours):
        for u, refs in enumerate(tiles_of):
            product_one(4 * (fours - 1) + u, refs, start + fours - 1)

    def multiply(product_one, start, fours, group):
        def step(g, carry):
            for at in range(group):
                for u, refs in enumerate(tiles_of):
                    product_one(4 * (g * group + at) + u, refs, start + g * group + at)
            return carry

        lax.fori_loop(0, fours // group, step, 0)

    slot_out[16 * INNER : INNER_WIDTH, :] = jnp.zeros((INNER_WIDTH - 16 * INNER, NODES), F32)
    evaluate_and_multiply(evaluate_inner, product_inner, 0, INNER_FOURS)
    for at in range(8):
        near_arrive(at)
    evaluate_inner(INNER - 1, tiles_of[0], INNER_FOURS)
    last_four(product_inner, 0, INNER_FOURS)

    dead_rows = jnp.full((7, 128), 255.0, F32)
    device_row = lax.broadcasted_iota(jnp.int32, (16, 128), 0)
    add_wide = (device_row * 11 >> 5) - 1
    add_narrow = device_row - (add_wide + 1) * 3 - 1

    def here(row):
        lanes = slice(128 * row, 128 * row + 128)
        rows = [own0[0, 7:8, lanes] if d == 4 else near0[d * BLOCKS, 7:8, lanes] for d in range(9)]
        ids = jnp.concatenate(rows + [dead_rows], axis=0)
        ids = ids.astype(jnp.int32)
        is_live = ids < 200
        ids = jnp.where(is_live, ids, 0)
        device = ids * 7282 >> 16
        within = ids - device * 9
        at_wide = device * 11 >> 5
        at_narrow = device - at_wide * 3 + add_narrow
        at_wide = at_wide + add_wide
        mine = is_live & (at_wide == 1) & (at_narrow == 1)
        return mine, within, at_wide * 27 + at_narrow * 9 + within

    left_mine, left_within, left_here = here(0)
    right_mine, right_within, right_here = here(1)
    wanted_rows = jnp.concatenate(
        [
            jnp.where(left_mine & jnp.logical_not(right_mine), 1.0, 0.0),
            jnp.where(right_mine & jnp.logical_not(left_mine), 1.0, 0.0),
        ],
        axis=0,
    )
    codes = jnp.concatenate(
        [left_within * 128 + right_here + 1, right_within * 128 + left_here + 1], axis=0
    ).astype(F32)
    code, too_many = compact(wanted_rows, codes, (*range(9), *range(16, 25)), OUTER)
    overflow = overflow + too_many
    filled = code > 0
    code = jnp.maximum(code - 1, 0)
    outer_rows[...] = jnp.where(row_of == 0, code >> 7, code & 127)
    outer_load = pltpu.make_async_copy(outer_rows, outer_entries, entry_sems.at[1])
    outer_load.start()
    fill_onehot(INNER_WIDTH, spread_over(jnp.where(filled, code >> 7, 200), 8 * OUTER, 3)[0:1, :])

    product_inner(INNER - 1, tiles_of[0], INNER_FOURS)

    def added(start, end):
        high, low = split(slot_out[start:end, :])
        table = onehot[:, start:end]
        return dot_bf16(table, high, False) + dot_bf16(table, low, False)

    inner_image = added(0, INNER_WIDTH)

    def prepare_next(at, carry):
        for k in range(BLOCKS):
            j = (at + at // 4) * BLOCKS + k
            put_pieces(pieces, j, 0, near0[j])
        return carry

    lax.fori_loop(0, 8, prepare_next, 0)
    outer_load.wait()
    evaluate_and_multiply(evaluate_outer, product_outer, INNER_FOURS + 1, OUTER_FOURS)
    last_four(product_outer, INNER_FOURS + 1, OUTER_FOURS)

    lane = lax.broadcasted_iota(jnp.int32, (8, 128), 1)
    forward = row_of % 4 < 2
    places = {}

    def swapped(value):
        return jnp.where(forward, pltpu.roll(value, 6, 0), pltpu.roll(value, 2, 0))

    def add_products(gram, j):
        tiles = [
            [basis[i, h, g : g + 8, :] for h in range(2) for g in range(0, ROWS, 8)] for i in range(j + 1)
        ]
        crossed = [swapped(tile) for tile in tiles[j]]
        for i in range(j + 1):
            for kind, others in (("same", tiles[j]), ("cross", crossed)):
                total = None
                for mine, theirs in zip(tiles[i], others):
                    term = mine * theirs
                    total = term if total is None else total + term
                column = jnp.sum(total, axis=1, keepdims=True)
                places[kind, i, j] = len(places)
                gram = jnp.where(lane == places[kind, i, j], column, gram)
        return gram

    gram = jnp.zeros((8, 128), F32)
    for it in range(ITERS):
        if it > 0:
            gram = add_products(gram, it - 1)
            if it + 1 == ITERS:
                gram = add_products(gram, it)
            multiply(product_inner, 0, INNER_FOURS, 1)
            product_inner(INNER - 1, tiles_of[0], INNER_FOURS)
            inner_image = added(0, INNER_WIDTH)
            refresh_others()
            multiply(product_outer, INNER_FOURS + 1, OUTER_FOURS, 2)
        image = inner_image + added(INNER_WIDTH, FAST_WIDTH)
        for h in range(2):
            basis[it + 1, h] = image[0:ROWS, 128 * h : 128 * h + 128]
        if it == 0:
            nearq[4] = image[0:ROWS]
            arrive = exchange(nearq.at[4], lambda d: nearq.at[d], q_send.at[it], q_recv.at[it])

            def refresh(d, to, first_block):
                for k in range(0, BLOCKS, 2):
                    value = nearq[d, 4 * k : 4 * k + 8, :]
                    put_pieces(to, first_block + k, 0, value)
                    if k + 1 < BLOCKS:
                        put_pieces(to, first_block + k + 1, 4, value)

            refresh(4, own_pieces, 0)

            def refresh_others(arrive=arrive, refresh=refresh):
                def refresh_next(at, carry):
                    arrive(at)
                    d = at + at // 4
                    refresh(d, pieces, d * BLOCKS)
                    return carry

                lax.fori_loop(0, 8, refresh_next, 0)

        elif it + 1 < ITERS:
            nearp[4] = image[ROWS : ROWS + P_ROWS]
            arrive_p = exchange(nearp.at[4], lambda d: nearp.at[d], q_send.at[it], q_recv.at[it])

            def refresh_p(d, to, first_block):
                for k in range(BLOCKS):
                    value = nearp[d, k // 4 * 8 : k // 4 * 8 + 8, :]
                    if k % 4:
                        value = pltpu.roll(value, 8 - k % 4 * 2, 0)
                    put_pieces(to, first_block + k, 0, value)

            refresh_p(4, own_pieces, 0)

            def refresh_others(arrive=arrive_p, refresh=refresh_p):
                def refresh_next(at, carry):
                    arrive(at)
                    d = at + at // 4
                    refresh(d, pieces, d * BLOCKS)
                    return carry

                lax.fori_loop(0, 8, refresh_next, 0)

    gram = add_products(gram, ITERS)
    gram = jnp.where(lane == 127, overflow, gram)

    for stage, group_peers in enumerate(peers):
        sums[stage] = gram
        copies = []
        for at in sorted(range(len(group_peers)), key=lambda at: -group_peers[at][1]):
            copy = pltpu.make_async_remote_copy(
                src_ref=sums.at[stage],
                dst_ref=sum_in.at[stage, at],
                send_sem=sum_send.at[stage, at],
                recv_sem=sum_recv.at[stage, at],
                device_id=group_peers[at][0],
                device_id_type=MESH,
            )
            copy.start()
            copies.append((at, copy))
        copies = [copy for at, copy in sorted(copies, key=lambda pair: pair[0])]
        pending.extend(copies)
        for at, copy in enumerate(copies):
            copy.wait_recv()
            gram = gram + sum_in[stage, at]
    flag_ref[0, 0] = jnp.sum(jnp.where((lane == 127) & (half[:, 0:128]), gram, 0.0))
    gram = gram + pltpu.roll(gram, 4, 0)

    def entry(kind, i, j, second):
        value = jnp.broadcast_to(gram[:, places[kind, i, j] : places[kind, i, j] + 1], (8, 128))
        return pltpu.roll(value, 6, 0) if second else value

    chain = ITERS + 1
    inner = {}
    for i in range(chain):
        for j in range(chain):
            inner[i, j] = entry("same", min(i, j), max(i, j), False)
            if i < ITERS and j < ITERS:
                inner[chain + i, chain + j] = entry("same", min(i, j), max(i, j), True)
            if j < ITERS:
                cross = entry("cross", min(i, j), max(i, j), i > j)
                inner[i, chain + j] = cross
                inner[chain + j, i] = cross

    def bilinear(first, second):
        total = None
        for i, a in first.items():
            inside = None
            for j, b in second.items():
                term = b * inner[i, j]
                inside = term if inside is None else inside + term
            inside = a * inside
            total = inside if total is None else total + inside
        return total

    def combine(base, scale, other):
        result = dict(base)
        for i, value in other.items():
            result[i] = result[i] + scale * value if i in result else scale * value
        return result

    one = jnp.ones((8, 128), F32)
    in_x, in_r, in_p = {}, {chain: one}, {0: one}
    norm_now = inner[chain, chain]
    for it in range(ITERS):
        image = {i + 1: value for i, value in in_p.items()}
        step = norm_now / bilinear(in_p, image)
        in_x = combine(in_x, step, in_p)
        in_r = combine(in_r, -step, image)
        norm_next = bilinear(in_r, in_r)
        in_p = combine(in_r, norm_next / norm_now, in_p)
        norm_now = norm_next

    for f, h in ((0, 0), (0, 1), (1, 0), (1, 1)):
        lanes = slice(128 * h, 128 * h + 128)
        vectors = {}
        for i in range(chain):
            vectors[i] = basis[i, h, pl.ds(f, BLOCKS, stride=4), :]
            if i < ITERS:
                vectors[chain + i] = basis[i, h, pl.ds(2 + f, BLOCKS, stride=4), :]

        def mixed(total, coefficients):
            for i, value in coefficients.items():
                term = value[f : f + 1, :] * vectors[i]
                total = term if total is None else total + term
            return total

        results = (mixed(None, in_x), mixed(None, in_r), mixed(None, in_p))
        for k in range(BLOCKS):
            at = f * BLOCKS + k
            new_sol_ref[at, :, lanes] = sol_rows[at, :, lanes] + results[0][k : k + 1, :]
            new_res_ref[at, :, lanes] = results[1][k : k + 1, :]
            new_dir_ref[at, :, lanes] = results[2][k : k + 1, :]

    for copy in pending:
        copy.wait_send()


def hand_out(*refs):
    sems = refs[6]
    copies = [pltpu.make_async_copy(refs[i], refs[3 + i], sems.at[i]) for i in range(3)]
    for copy in copies:
        copy.start()
    for copy in copies:
        copy.wait()


def solution(mesh):
    sizes = (mesh.shape["wide"], mesh.shape["narrow"])
    if sizes[0] == 64:
        stages = (
            ("narrow", ((1, sizes[1]),)),
            ("wide", ((2, 8),)),
            ("wide", ((16, 4), (1, 2))),
        )
    else:
        stages = (("narrow", ((1, sizes[1]),)), ("wide", ((1, sizes[0]),)))
    most = 0
    for _, places in stages:
        size = 1
        for _, count in places:
            size *= count
        most = max(most, size - 1)

    def on_device(node_coords, solution, residual, direction, tile_pairs, tile_counts):
        full_shape = direction.shape
        fields = jax.ShapeDtypeStruct((2 * BLOCKS, 1, NODES), F32)
        vmem = pl.BlockSpec(memory_space=pltpu.VMEM)
        anywhere = pl.BlockSpec(memory_space=pl.ANY)
        dma = pltpu.SemaphoreType.DMA
        fast = pl.pallas_call(
            functools.partial(fast_body, sizes),
            out_shape=(fields, fields, fields, jax.ShapeDtypeStruct((1, 1), F32), jax.ShapeDtypeStruct((2, SLOTS), jnp.int32)),
            in_specs=[anywhere] * 5 + [vmem],
            out_specs=(vmem, vmem, vmem, pl.BlockSpec(memory_space=pltpu.SMEM), vmem),
            scratch_shapes=[
                pltpu.VMEM((BLOCKS, 8, NODES), F32),
                pltpu.VMEM((9 * BLOCKS, 8, NODES), F32),
                pltpu.VMEM((9, ROWS, NODES), F32),
                pltpu.VMEM((9, P_ROWS, NODES), F32),
                *[pltpu.VMEM((INNER_FOURS + 1 + OUTER_FOURS, NODES, NODES), BF16)] * 8,
                pltpu.VMEM((BLOCKS, 16, NODES), BF16),
                pltpu.VMEM((9 * BLOCKS, 16, NODES), BF16),
                pltpu.VMEM((FAST_WIDTH, NODES), F32),
                pltpu.VMEM((FAST_TABLE, FAST_WIDTH), BF16),
                pltpu.VMEM((ITERS + 1, 2, ROWS, 128), F32),
                pltpu.VMEM((2, 8, 128), F32),
                pltpu.VMEM((2, MOST, 8, 128), F32),
                pltpu.VMEM((7 * BLOCKS, 1, NODES), F32),
                pltpu.VMEM((2 * BLOCKS, 1, NODES), F32),
                pltpu.VMEM((2, SLOTS), jnp.int32),
                pltpu.VMEM((BLOCKS, 3, NODES, 128), F32),
                pltpu.VMEM((8, 128), jnp.int32),
                pltpu.VMEM((8, 128), jnp.int32),
                pltpu.SMEM((8, 128), jnp.int32),
                pltpu.SMEM((8, 128), jnp.int32),
                dma((5,)),
                dma((2,)),
                dma((8,)),
                dma((8,)),
                dma((ITERS - 1, 8)),
                dma((ITERS - 1, 8)),
                dma((2, MOST)),
                dma((2, MOST)),
            ],
            compiler_params=pltpu.CompilerParams(
                collective_id=0, has_side_effects=True, vmem_limit_bytes=60 * 1024 * 1024
            ),
            cost_estimate=pl.CostEstimate(
                flops=81 * 65536 * 40, bytes_accessed=200000, transcendentals=81 * 65536
            ),
        )
        general = pl.pallas_call(
            functools.partial(general_body, sizes, stages),
            out_shape=(fields, fields, fields),
            in_specs=[anywhere] * 5 + [vmem],
            out_specs=(vmem, vmem, vmem),
            scratch_shapes=[
                pltpu.VMEM((9 * BLOCKS, 8, NODES), F32),
                pltpu.VMEM((ITERS - 1, 9, ROWS, NODES), F32),
                pltpu.VMEM((ITERS, 9, ROWS, NODES), F32),
                pltpu.VMEM((ITERS, 8, ROWS, NODES), F32),
                pltpu.VMEM((SLOTS // 2 + 1, NODES, NODES), BF16),
                pltpu.VMEM((SLOTS // 2 + 1, NODES, NODES), BF16),
                pltpu.VMEM((SLOTS // 2 + 1, NODES, NODES), BF16),
                pltpu.VMEM((SLOTS // 2 + 1, NODES, NODES), BF16),
                pltpu.VMEM((SLOTS // 2 + 1, NODES, NODES), BF16),
                pltpu.VMEM((SLOTS // 2 + 1, NODES, NODES), BF16),
                pltpu.VMEM((SLOTS // 2 + 1, NODES, NODES), BF16),
                pltpu.VMEM((SLOTS // 2 + 1, NODES, NODES), BF16),
                pltpu.VMEM((NODES, NODES), F32),
                pltpu.VMEM((NODES, NODES), F32),
                pltpu.VMEM((9 * BLOCKS, 16, NODES), BF16),
                pltpu.VMEM((512, NODES), F32),
                pltpu.VMEM((TABLE, 512), BF16),
                pltpu.VMEM((ITERS + 1, 2, ROWS, 128), F32),
                pltpu.VMEM((len(stages), 8, 128), F32),
                pltpu.VMEM((len(stages), most, 8, 128), F32),
                pltpu.VMEM((7 * BLOCKS, 1, NODES), F32),
                pltpu.VMEM((2 * BLOCKS, 1, NODES), F32),
                pltpu.SMEM((2, SLOTS), jnp.int32),
                pltpu.VMEM((2, SLOTS), jnp.int32),
                pltpu.VMEM((9 * BLOCKS, NODES, 8), F32),
                dma((6,)),
                dma((8,)),
                dma((8,)),
                dma((ITERS - 1, 8)),
                dma((ITERS - 1, 8)),
                dma((ITERS, 8)),
                dma((ITERS, 8)),
                dma((len(stages), most)),
                dma((len(stages), most)),
            ],
            compiler_params=pltpu.CompilerParams(
                collective_id=1, has_side_effects=True, vmem_limit_bytes=60 * 1024 * 1024
            ),
            cost_estimate=pl.CostEstimate(
                flops=61 * 65536 * 40, bytes_accessed=200000, transcendentals=61 * 65536
            ),
        )
        arguments = (
            node_coords.reshape(3 * BLOCKS, 1, NODES),
            solution.reshape(2 * BLOCKS, 1, NODES),
            residual.reshape(2 * BLOCKS, 1, NODES),
            direction.reshape(2 * BLOCKS, 1, NODES),
            tile_pairs.reshape(2, SLOTS),
            tile_counts,
        )
        *outs, flags, pairs = fast(*arguments)
        outs = lax.cond(
            flags[0, 0] > 0.5,
            lambda *a: tuple(general(*a[3:])),
            lambda *a: a[:3],
            *outs,
            *arguments[:4],
            pairs,
            arguments[5],
        )
        outs = pl.pallas_call(
            hand_out,
            out_shape=(fields, fields, fields),
            in_specs=[anywhere] * 3,
            out_specs=(anywhere,) * 3,
            scratch_shapes=[dma((3,))],
        )(*outs)
        return tuple(out.reshape(full_shape) for out in outs)

    fields_spec = P(None, "wide", "narrow", None, None)
    return jax.shard_map(
        on_device,
        mesh=mesh,
        in_specs=(
            fields_spec,
            fields_spec,
            fields_spec,
            fields_spec,
            P("wide", "narrow", None, None),
            P("wide", "narrow"),
        ),
        out_specs=(fields_spec, fields_spec, fields_spec),
        check_vma=False,
    )
```
